32 devices in a mesh: seq: 8 (over z, x), dp: 4 (over y, core).
Axes of the slice: x: 2, y: 2, z: 4, core: 2. Of those that a mesh axis runs over, the one named last changes fastest.
Arguments:
- byte_rows: bfloat16 [4, 8192, 768], P('dp', 'seq'), may hold values from -6 to 6
- starts: int32 [4, 8192], P('dp', 'seq'), may hold values from 0 to 1, as said below
- doc_ids: int32 [4, 8192], P('dp', 'seq'), may hold values from 0 to 5, as said below
- out_cotangent: bfloat16 [4, 8192, 768], P('dp', 'seq'), may hold values from -6 to 6
- widen_master: float32 [768, 1536], P(('seq', 'dp')), may hold values from -0.21875 to 0.21875
- widen_first: float32 [768, 1536], P(('seq', 'dp')), may hold values from -0.00015258789 to 0.00015258789
- widen_second: float32 [768, 1536], P(('seq', 'dp')), may hold values from 2.8080411e-09 to 1.11262e-08
- triple_master: float32 [1536, 4608], P(('seq', 'dp')), may hold values from -0.15625 to 0.15625
- triple_first: float32 [1536, 4608], P(('seq', 'dp')), may hold values from -0.00012207031 to 0.00012207031
- triple_second: float32 [1536, 4608], P(('seq', 'dp')), may hold values from 1.8013848e-09 to 7.2055393e-09
- mixing_master: float32 [1536, 1536], P(('seq', 'dp')), may hold values from -0.875 to 0.875
- mixing_first: float32 [1536, 1536], P(('seq', 'dp')), may hold values from -2.2888184e-05 to 2.2888184e-05
- mixing_second: float32 [1536, 1536], P(('seq', 'dp')), may hold values from 6.357829e-11 to 2.5431315e-10
- expand_master: float32 [1536, 6144], P(('seq', 'dp')), may hold values from -0.15625 to 0.15625
- expand_first: float32 [1536, 6144], P(('seq', 'dp')), may hold values from -0.00010681152 to 0.00010681152
- expand_second: float32 [1536, 6144], P(('seq', 'dp')), may hold values from 2.6490954e-10 to 1.0596382e-09
- shrink_master: float32 [6144, 1536], P(('seq', 'dp')), may hold values from -0.078125 to 0.078125
- shrink_first: float32 [6144, 1536], P(('seq', 'dp')), may hold values from -9.1552734e-05 to 9.1552734e-05
- shrink_second: float32 [6144, 1536], P(('seq', 'dp')), may hold values from 8.7949964e-10 to 3.4968057e-09
- narrow_master: float32 [1536, 768], P(('seq', 'dp')), may hold values from -0.15625 to 0.15625
- narrow_first: float32 [1536, 768], P(('seq', 'dp')), may hold values from -0.00024414062 to 0.00024414062
- narrow_second: float32 [1536, 768], P(('seq', 'dp')), may hold values from 8.106232e-09 to 3.231896e-08
- gains_master: float32 [2, 1536], P(None, ('seq', 'dp')), may hold values from 0.3 to 3
- gains_first: float32 [2, 1536], P(None, ('seq', 'dp')), may hold values from -9.1552734e-05 to 9.1552734e-05
- gains_second: float32 [2, 1536], P(None, ('seq', 'dp')), may hold values from 1.0066562e-09 to 4.026625e-09
Outputs:
- new_rows: bfloat16 [4, 8192, 768], P('dp', 'seq')
- byte_grad: bfloat16 [4, 8192, 768], P('dp', 'seq')
- grad_norm: float32 [], replicated
- widen_weight: float32 [768, 1536], P(('seq', 'dp'))
- widen_moment: float32 [768, 1536], P(('seq', 'dp'))
- widen_square: float32 [768, 1536], P(('seq', 'dp'))
- triple_weight: float32 [1536, 4608], P(('seq', 'dp'))
- triple_moment: float32 [1536, 4608], P(('seq', 'dp'))
- triple_square: float32 [1536, 4608], P(('seq', 'dp'))
- mixing_weight: float32 [1536, 1536], P(('seq', 'dp'))
- mixing_moment: float32 [1536, 1536], P(('seq', 'dp'))
- mixing_square: float32 [1536, 1536], P(('seq', 'dp'))
- expand_weight: float32 [1536, 6144], P(('seq', 'dp'))
- expand_moment: float32 [1536, 6144], P(('seq', 'dp'))
- expand_square: float32 [1536, 6144], P(('seq', 'dp'))
- shrink_weight: float32 [6144, 1536], P(('seq', 'dp'))
- shrink_moment: float32 [6144, 1536], P(('seq', 'dp'))
- shrink_square: float32 [6144, 1536], P(('seq', 'dp'))
- narrow_weight: float32 [1536, 768], P(('seq', 'dp'))
- narrow_moment: float32 [1536, 768], P(('seq', 'dp'))
- narrow_square: float32 [1536, 768], P(('seq', 'dp'))
- gains_weight: float32 [2, 1536], P(None, ('seq', 'dp'))
- gains_moment: float32 [2, 1536], P(None, ('seq', 'dp'))
- gains_square: float32 [2, 1536], P(None, ('seq', 'dp'))
The draws below stay inside these ranges and needn't reach their ends.
Inputs may be any that keep to these rules, and one draw needn't show every extreme that they name: `starts`: each sequence has exactly 1536 ones; the 1024 bytes of one device hold 96 to 288 of them, and some device of every sequence holds 288. `doc_ids`: ids never fall along a sequence; in every sequence one document begins among the bytes of its first device and ends among those of its last.
All inputs are finite; a program needn't handle non-finite values.
Results may differ from the reference program's by a relative error of at most 0.024.
Values may be sent and summed in bfloat16 or wider, within the bound.
No kernel may reach another device: no remote copies, remote signals or barrier semaphores. Data moves between devices by JAX's collectives and lax.ppermute only.
A program may use at most 448 MiB of HBM per device.

```python
import math
import jax
import jax.numpy as jnp
from jax import lax

D_BYTE = 768
D = 1536
HEADS = 24
HEAD_DIM = 64
FF = 6144
BYTE_DEV = 1024
STEP = 10
PATCH_DEV = 192
LENGTH = 8192
PATCHES = 1536
SEQS = 4
N_SEQ = 8


def starts_one(subkey):
    order_key, moving_key, place_key = jax.random.split(subkey, 3)
    ordering = jax.random.permutation(order_key, N_SEQ)
    paired = N_SEQ // 2
    moving = jax.random.randint(moving_key, (paired,), 0, PATCH_DEV // 2 + 1)
    moving = moving.at[0].set(PATCH_DEV // 2)
    counts = jnp.full((N_SEQ,), PATCH_DEV, jnp.int32)
    counts = counts.at[ordering[:paired]].add(moving)
    counts = counts.at[ordering[paired:]].add(-moving)
    ranking = jax.vmap(lambda device_key: jax.random.permutation(device_key, BYTE_DEV))(jax.random.split(place_key, N_SEQ))
    return (ranking < counts[:, None]).astype(jnp.int32).reshape(LENGTH)


def draw_starts(key, part):
    key = jax.random.fold_in(key, 11)
    return jax.vmap(starts_one)(jax.random.split(key, SEQS))


def documents_one(subkey):
    subkeys = jax.random.split(subkey, 5)
    begin = jax.random.randint(subkeys[0], (), 1, BYTE_DEV)
    finish = LENGTH - jax.random.randint(subkeys[1], (), 1, BYTE_DEV)
    early_one = jax.random.randint(subkeys[2], (), 1, begin + 1)
    early_two = jax.random.randint(subkeys[3], (), 1, begin + 1)
    latest = jax.random.randint(subkeys[4], (), finish, LENGTH)
    places = jnp.arange(LENGTH, dtype=jnp.int32)
    result = (places >= early_one).astype(jnp.int32) + (places >= early_two).astype(jnp.int32)
    result = result + (places >= begin).astype(jnp.int32) + (places >= finish).astype(jnp.int32)
    return result + (places >= latest).astype(jnp.int32)


def draw_doc_ids(key, part):
    key = jax.random.fold_in(key, 12)
    return jax.vmap(documents_one)(jax.random.split(key, SEQS))


def draw_gains_master(key, part):
    key = jax.random.fold_in(key, 13)
    incline = jnp.arange(D, dtype=jnp.float32) / (D - 1)
    jitter = jax.random.uniform(key, (2, D), jnp.float32, 0.85, 1.15)
    return 0.6 * (1.0 + 2.0 * incline)[None, :] * jitter


def block_levels(key, dims, shards, smallest, largest):
    def one(dim, blocks):
        draws = jax.random.uniform(jax.random.fold_in(jax.random.fold_in(key, 6), dim), (blocks,), jnp.float32, smallest / len(shards), largest / len(shards))
        return jnp.repeat(jnp.exp(draws), dims[dim] // blocks).reshape((-1,) + (1,) * (len(dims) - dim - 1))

    loudness = one(*shards[0])
    for cut in shards[1:]:
        loudness = loudness * one(*cut)
    return loudness


def normal_values(stream_key, shape, spread, bound, cuts=(), held_as=jnp.bfloat16):
    factor_of = block_levels(stream_key, shape, cuts, -0.22, 0.18) if cuts else 1.0
    entries = jax.random.normal(stream_key, shape, jnp.float32) * spread * factor_of
    return jnp.minimum(jnp.maximum(entries, -bound), bound).astype(held_as)


def setup_inputs(seed: int = 0) -> dict:
    keys = jax.random.split(jax.random.key(seed), 26)
    byte_rows = normal_values(keys[0], (SEQS, LENGTH, D_BYTE), 1.0, 6.0, ((0, 4), (1, 8)))
    starts = draw_starts(jax.random.fold_in(keys[25], 71), 0)
    doc_ids = draw_doc_ids(jax.random.fold_in(keys[25], 71), 0)
    out_cotangent = normal_values(keys[3], (SEQS, LENGTH, D_BYTE), 1.0, 6.0, ((0, 4), (1, 8)))
    widen_master = normal_values(keys[4], (D_BYTE, D), D_BYTE ** -0.5, 0.21875, ((0, 32),), jnp.float32)
    widen_first = normal_values(keys[5], (D_BYTE, D), (0.11 * (4 * D_BYTE * D + 2 * D * D + D * FF) ** -0.5), 0.00015258789, ((0, 32),), jnp.float32)
    widen_second = jnp.clip(jnp.exp(math.log(1.1126200405442432e-08) - 1.3768156 * jax.random.uniform(keys[6], (D_BYTE, D), jnp.float32) ** block_levels(keys[6], (D_BYTE, D), ((0, 32),), -0.2, 0.2)), 2.808041132951189e-09, 1.1126200405442432e-08)
    triple_master = normal_values(keys[7], (D, 3 * D), D ** -0.5, 0.15625, ((0, 32),), jnp.float32)
    triple_first = normal_values(keys[8], (D, 3 * D), (0.088 * (4 * D_BYTE * D + 2 * D * D + D * FF) ** -0.5), 0.00012207031, ((0, 32),), jnp.float32)
    triple_second = jnp.clip(jnp.exp(math.log(7.205539276355921e-09) - 1.3862944 * jax.random.uniform(keys[9], (D, 3 * D), jnp.float32) ** block_levels(keys[9], (D, 3 * D), ((0, 32),), -0.2, 0.2)), 1.8013848190889803e-09, 7.205539276355921e-09)
    mixing_master = normal_values(keys[10], (D, D), (max(1, D * 48 // (PATCH_DEV * N_SEQ))) ** -0.5, 0.875, ((0, 32),), jnp.float32)
    mixing_first = normal_values(keys[11], (D, D), (0.0165 * (4 * D_BYTE * D + 2 * D * D + D * FF) ** -0.5), 2.288818359375e-05, ((0, 32),), jnp.float32)
    mixing_second = jnp.clip(jnp.exp(math.log(2.5431315386903464e-10) - 1.3862944 * jax.random.uniform(keys[12], (D, D), jnp.float32) ** block_levels(keys[12], (D, D), ((0, 32),), -0.2, 0.2)), 6.357828846725866e-11, 2.5431315386903464e-10)
    expand_master = normal_values(keys[13], (D, FF), D ** -0.5, 0.15625, ((0, 32),), jnp.float32)
    expand_first = normal_values(keys[14], (D, FF), (0.077 * (4 * D_BYTE * D + 2 * D * D + D * FF) ** -0.5), 0.00010681152, ((0, 32),), jnp.float32)
    expand_second = jnp.clip(jnp.exp(math.log(1.0596381549987655e-09) - 1.3862944 * jax.random.uniform(keys[15], (D, FF), jnp.float32) ** block_levels(keys[15], (D, FF), ((0, 32),), -0.2, 0.2)), 2.6490953874969136e-10, 1.0596381549987655e-09)
    shrink_master = normal_values(keys[16], (FF, D), FF ** -0.5, 0.078125, ((0, 32),), jnp.float32)
    shrink_first = normal_values(keys[17], (FF, D), (0.062 * (4 * D_BYTE * D + 2 * D * D + D * FF) ** -0.5), 9.1552734375e-05, ((0, 32),), jnp.float32)
    shrink_second = jnp.clip(jnp.exp(math.log(3.496805733860242e-09) - 1.380252 * jax.random.uniform(keys[18], (FF, D), jnp.float32) ** block_levels(keys[18], (FF, D), ((0, 32),), -0.2, 0.2)), 8.794996397831767e-10, 3.496805733860242e-09)
    narrow_master = normal_values(keys[19], (D, D_BYTE), D ** -0.5, 0.15625, ((0, 32),), jnp.float32)
    narrow_first = normal_values(keys[20], (D, D_BYTE), (0.19 * (4 * D_BYTE * D + 2 * D * D + D * FF) ** -0.5), 0.00024414062, ((0, 32),), jnp.float32)
    narrow_second = jnp.clip(jnp.exp(math.log(3.23189617290609e-08) - 1.383021 * jax.random.uniform(keys[21], (D, D_BYTE), jnp.float32) ** block_levels(keys[21], (D, D_BYTE), ((0, 32),), -0.2, 0.2)), 8.106232129989621e-09, 3.23189617290609e-08)
    gains_master = draw_gains_master(jax.random.fold_in(keys[25], 71), 0)
    gains_first = normal_values(keys[23], (2, D), (0.066 * (4 * D_BYTE * D + 2 * D * D + D * FF) ** -0.5), 9.1552734375e-05, ((1, 32),), jnp.float32)
    gains_second = jnp.clip(jnp.exp(math.log(4.026624811359625e-09) - 1.3862944 * jax.random.uniform(keys[24], (2, D), jnp.float32) ** block_levels(keys[24], (2, D), ((1, 32),), -0.2, 0.2)), 1.0066562028399062e-09, 4.026624811359625e-09)
    return {"byte_rows": byte_rows, "starts": starts, "doc_ids": doc_ids, "out_cotangent": out_cotangent, "widen_master": widen_master, "widen_first": widen_first, "widen_second": widen_second, "triple_master": triple_master, "triple_first": triple_first, "triple_second": triple_second, "mixing_master": mixing_master, "mixing_first": mixing_first, "mixing_second": mixing_second, "expand_master": expand_master, "expand_first": expand_first, "expand_second": expand_second, "shrink_master": shrink_master, "shrink_first": shrink_first, "shrink_second": shrink_second, "narrow_master": narrow_master, "narrow_first": narrow_first, "narrow_second": narrow_second, "gains_master": gains_master, "gains_first": gains_first, "gains_second": gains_second}


NORM_EPS = 1e-05
SCORE_SCALE = 0.125
MASK_FILL = -1e+30
BETA_ONE = 0.9
BETA_TWO = 0.95
ADAM_EPS = 1e-08
DECAY_RATE = 0.1
CLIP_NORM = 1.0

@jax.custom_vjp
def low(v):
    return lax.optimization_barrier(v.astype(jnp.bfloat16)).astype(jnp.float32)

@jax.custom_vjp
def low_back(v):
    return v

def low_keep(v):
    return (low(v), None)

def low_pass(kept, grad):
    return (grad,)

def back_keep(v):
    return (v, None)

def back_low(kept, grad):
    return (low(grad),)
low.defvjp(low_keep, low_pass)
low_back.defvjp(back_keep, back_low)

def product(left, right):
    return jnp.dot(left, right, precision=lax.Precision.HIGHEST, preferred_element_type=jnp.float32)

def normalize(values, gain):
    inverse = lax.rsqrt(lax.optimization_barrier(jnp.mean(values * values, axis=-1, keepdims=True)) + NORM_EPS)
    return values * inverse * gain

def attention(queries, key_rows, value_rows, patch_docs):
    total_rows = queries.shape[0]
    block_len = 512 if total_rows % 512 == 0 else total_rows
    number = total_rows // block_len
    positions = jnp.arange(total_rows, dtype=jnp.int32)

    def one_block(inputs):
        block_queries, block_docs, block_pos = inputs
        scores = jnp.einsum('qhd,khd->hqk', block_queries, key_rows, precision=lax.Precision.HIGHEST) * SCORE_SCALE
        scores = low_back(scores)
        allowed = (block_docs[:, None] == patch_docs[None, :]) & (positions[None, :] <= block_pos[:, None])
        masked = jnp.where(allowed[None], scores, MASK_FILL)
        running_top = lax.optimization_barrier(jnp.max(masked, axis=-1, keepdims=True))
        powers = jnp.where(allowed[None], jnp.exp(masked - running_top), 0.0)
        probs = low(powers / lax.optimization_barrier(jnp.sum(powers, axis=-1, keepdims=True)))
        return jnp.einsum('hqk,khd->qhd', probs, value_rows, precision=lax.Precision.HIGHEST)
    outputs = lax.map(jax.checkpoint(one_block), (queries.reshape(number, block_len, HEADS, HEAD_DIM), patch_docs.reshape(number, block_len), positions.reshape(number, block_len)))
    return outputs.reshape(total_rows, HEADS * HEAD_DIM)

def block_forward(params, byte_block, where_rows, patch_docs):
    widen_full, triple_full, mixing_full, expand_full, shrink_full, narrow_full, gains_full = params
    model_width = HEADS * HEAD_DIM
    patch_rows = low_back(byte_block[where_rows])
    widened = low_back(product(patch_rows, widen_full))
    first_low = low(normalize(widened, gains_full[0]))
    projected = low(low_back(product(first_low, triple_full)))
    queries = projected[:, :model_width].reshape(PATCHES, HEADS, HEAD_DIM)
    key_rows = projected[:, model_width:2 * model_width].reshape(PATCHES, HEADS, HEAD_DIM)
    value_rows = projected[:, 2 * model_width:].reshape(PATCHES, HEADS, HEAD_DIM)
    attended = low(low_back(attention(queries, key_rows, value_rows, patch_docs)))
    resid_one = widened + low_back(product(attended, mixing_full))
    second_low = low(normalize(resid_one, gains_full[1]))
    expanded = low_back(product(second_low, expand_full))
    active_low = low(jax.nn.gelu(expanded))
    resid_two = resid_one + low_back(product(active_low, shrink_full))
    narrow_low = low(product(low(resid_two), narrow_full))
    return byte_block.at[where_rows].add(narrow_low)

def adam_update(master, first_old, second_old, gradient, clip_factor, learn_rate, weight_decay):
    clipped = gradient * clip_factor
    moment = BETA_ONE * first_old + (1.0 - BETA_ONE) * clipped
    square = BETA_TWO * second_old + (1.0 - BETA_TWO) * clipped * clipped
    corrected = moment / (1.0 - BETA_ONE ** STEP) / (jnp.sqrt(square / (1.0 - BETA_TWO ** STEP)) + ADAM_EPS)
    weight = master - learn_rate * (corrected + weight_decay * master)
    return (weight, moment, square)

def reference(byte_rows, starts, doc_ids, out_cotangent, widen_master, widen_first, widen_second, triple_master, triple_first, triple_second, mixing_master, mixing_first, mixing_second, expand_master, expand_first, expand_second, shrink_master, shrink_first, shrink_second, narrow_master, narrow_first, narrow_second, gains_master, gains_first, gains_second):
    masters = (widen_master, triple_master, mixing_master, expand_master, shrink_master, narrow_master, gains_master)
    firsts = (widen_first, triple_first, mixing_first, expand_first, shrink_first, narrow_first, gains_first)
    seconds = (widen_second, triple_second, mixing_second, expand_second, shrink_second, narrow_second, gains_second)
    params = tuple((master.astype(jnp.bfloat16).astype(jnp.float32) for master in masters))

    def one_sequence(totals, inputs):
        byte_block, start_flags, doc_local, cotangent_rows = inputs
        where_rows = jnp.nonzero(start_flags, size=PATCHES)[0].astype(jnp.int32)
        patch_docs = doc_local[where_rows]

        def forward(weights, rows_in):
            return block_forward(weights, rows_in, where_rows, patch_docs)
        new_block, pull_back = jax.vjp(forward, params, byte_block.astype(jnp.float32))
        weight_grads, grad_block = pull_back(cotangent_rows.astype(jnp.float32))
        totals = jax.tree.map(jnp.add, totals, weight_grads)
        return (totals, (new_block.astype(jnp.bfloat16), grad_block.astype(jnp.bfloat16)))
    initial = tuple((jnp.zeros_like(weight) for weight in params))
    summed, (new_rows, byte_grad) = lax.scan(one_sequence, initial, (byte_rows, starts, doc_ids, out_cotangent))
    squares = jnp.float32(0.0)
    for member in summed:
        squares = squares + jnp.sum(member * member)
    grad_norm = jnp.sqrt(squares)
    factor = CLIP_NORM / jnp.maximum(grad_norm, CLIP_NORM)
    rates = (2.0 * D_BYTE ** (-0.5), 2.0 * D ** (-0.5), 0.4, 2.0 * D ** (-0.5), 2.0 * FF ** (-0.5), 2.0 * D ** (-0.5), 0.6)
    decays = (DECAY_RATE, DECAY_RATE, DECAY_RATE, DECAY_RATE, DECAY_RATE, DECAY_RATE, 0.0)
    updates = [adam_update(masters[index], firsts[index], seconds[index], summed[index], factor, rates[index], decays[index]) for index in range(7)]
    return (new_rows, byte_grad, grad_norm, updates[0][0], updates[0][1], updates[0][2], updates[1][0], updates[1][1], updates[1][2], updates[2][0], updates[2][1], updates[2][2], updates[3][0], updates[3][1], updates[3][2], updates[4][0], updates[4][1], updates[4][2], updates[5][0], updates[5][1], updates[5][2], updates[6][0], updates[6][1], updates[6][2])
```

```python
import jax
import jax.numpy as jnp
import numpy as np
from jax import lax
from jax.experimental import pallas as pl
from jax.experimental.pallas import tpu as pltpu
from jax.sharding import Mesh, PartitionSpec as P

D_BYTE = 768
D = 1536
HEADS = 24
HEAD_DIM = 64
FF = 6144
STEP = 10


NORM_EPS = 1e-05
SCORE_SCALE = 0.125
MASK_FILL = -1e30
BETA_ONE = 0.9
BETA_TWO = 0.95
ADAM_EPS = 1e-08
DECAY_RATE = 0.1
CLIP_NORM = 1.0


def prefix(part, axis, combine, identity):
    place = lax.axis_index(axis)
    gathered = lax.all_gather(part, axis)
    state = jnp.zeros_like(part) + jnp.asarray(identity, part.dtype)

    def one(hop, state):
        return combine(state, lax.dynamic_index_in_dim(gathered, hop, 0, False))

    return lax.fori_loop(0, place, one, state)


def normalize(values, gain):
    inverse = lax.rsqrt(jnp.mean(values * values, axis=-1, keepdims=True) + NORM_EPS)
    return values * inverse * gain


def add_counts(earlier, later):
    return earlier + later


def block_rows(amount):
    for option in (1024, 768, 512, 384, 256):
        if amount >= option and amount % option == 0:
            return option
    return amount


def spread_positions(first_row, amount, patch_dev, devices):
    whole_rows = first_row + jnp.arange(amount, dtype=jnp.int32)
    return whole_rows % patch_dev * devices + whole_rows // patch_dev


def make_attend(queries, patch_docs, patch_pos, patch_dev, devices):

    def attend(running, shards, offset):
        piece_keys, piece_values, piece_docs = shards
        amount = piece_keys.shape[0]
        span_rows = block_rows(amount)
        number = amount // span_rows
        key_blocks = piece_keys.reshape(number, span_rows, HEADS, HEAD_DIM)
        value_blocks = piece_values.reshape(number, span_rows, HEADS, HEAD_DIM)
        doc_blocks = piece_docs.reshape(number, span_rows)
        firsts = span_rows * jnp.arange(number, dtype=jnp.int32)

        def advance(status, section):
            block_keys, block_values, block_docs, block_first = section
            running_top, running_sum, running_out = status
            scores = (
                jnp.einsum("phd,khd->hpk", queries, block_keys, preferred_element_type=jnp.float32)
                * SCORE_SCALE
            )
            key_pos = spread_positions(block_first, span_rows, patch_dev, devices)
            allowed = (patch_docs[:, None] == block_docs[None, :]) & (
                key_pos[None, :] <= patch_pos[:, None]
            )
            masked = jnp.where(allowed[None], scores, MASK_FILL)
            new_top = jnp.maximum(running_top, jnp.max(masked, axis=-1))
            weights = jnp.where(allowed[None], jnp.exp(masked - new_top[..., None]), 0.0)
            rescale = jnp.exp(running_top - new_top)
            running_sum = running_sum * rescale + jnp.sum(weights, axis=-1)
            running_out = running_out * rescale[..., None] + jnp.einsum(
                "hpk,khd->hpd",
                weights.astype(jnp.bfloat16),
                block_values,
                preferred_element_type=jnp.float32,
            )
            return ((new_top, running_sum, running_out), None)

        running, _ = lax.scan(advance, running, (key_blocks, value_blocks, doc_blocks, firsts))
        return running

    return attend


def outer_sum(left, right):
    return jnp.einsum("pi,pj->ij", left, right, preferred_element_type=jnp.float32)


def back_product(grads, weight):
    return jnp.einsum("pj,ij->pi", grads, weight, preferred_element_type=jnp.float32)


def adam_update(master, first_old, second_old, gradient, clip_factor, learn_rate, weight_decay):
    clipped = gradient * clip_factor
    moment = BETA_ONE * first_old + (1.0 - BETA_ONE) * clipped
    square = BETA_TWO * second_old + (1.0 - BETA_TWO) * clipped * clipped
    corrected = (
        moment / (1.0 - BETA_ONE**STEP) / (jnp.sqrt(square / (1.0 - BETA_TWO**STEP)) + ADAM_EPS)
    )
    weight = master - learn_rate * (corrected + weight_decay * master)
    return (weight, moment, square)


def per_device(
    byte_rows,
    starts,
    doc_ids,
    out_cotangent,
    widen_master,
    widen_first,
    widen_second,
    triple_master,
    triple_first,
    triple_second,
    mixing_master,
    mixing_first,
    mixing_second,
    expand_master,
    expand_first,
    expand_second,
    shrink_master,
    shrink_first,
    shrink_second,
    narrow_master,
    narrow_first,
    narrow_second,
    gains_master,
    gains_first,
    gains_second,
):
    widen_full, triple_full, mixing_full, expand_full, shrink_full, narrow_full, gains_full = (
        lax.all_gather(widen_master.astype(jnp.bfloat16), ("seq", "dp"), axis=0, tiled=True),
        lax.all_gather(triple_master.astype(jnp.bfloat16), ("seq", "dp"), axis=0, tiled=True),
        lax.all_gather(mixing_master.astype(jnp.bfloat16), ("seq", "dp"), axis=0, tiled=True),
        lax.all_gather(expand_master.astype(jnp.bfloat16), ("seq", "dp"), axis=0, tiled=True),
        lax.all_gather(shrink_master.astype(jnp.bfloat16), ("seq", "dp"), axis=0, tiled=True),
        lax.all_gather(narrow_master.astype(jnp.bfloat16), ("seq", "dp"), axis=0, tiled=True),
        lax.all_gather(gains_master.astype(jnp.bfloat16), ("seq", "dp"), axis=1, tiled=True),
    )
    gain_one = gains_full[0].astype(jnp.float32)
    gain_two = gains_full[1].astype(jnp.float32)
    devices = lax.axis_size("seq")
    seq_place = lax.axis_index("seq")
    byte_block = byte_rows[0]
    start_flags = starts[0]
    doc_local = doc_ids[0]
    cotangent_rows = out_cotangent[0]
    byte_width = byte_block.shape[1]
    patch_dev = 3 * byte_block.shape[0] // 16
    capacity = patch_dev + patch_dev // 2
    slot_count = (capacity + devices - 2) // devices + 1
    buffer_rows = devices * slot_count
    amount = jnp.sum(start_flags)
    offset = prefix(amount, "seq", add_counts, jnp.int32(0))
    ranking = jnp.cumsum(start_flags) - start_flags
    patch_index = offset + ranking
    owners = patch_index % devices
    local_row = patch_index // devices
    slot_index = local_row - offset // devices
    target_slot = jnp.where(start_flags == 1, owners * slot_count + slot_index, buffer_rows)
    send_rows = (
        jnp.zeros((buffer_rows, byte_width), jnp.bfloat16)
        .at[target_slot]
        .set(byte_block, mode="drop")
    )
    send_meta = (
        jnp.full((buffer_rows, 2), patch_dev, jnp.int32)
        .at[target_slot]
        .set(jnp.stack([local_row, doc_local], axis=-1), mode="drop")
    )
    send_grad = (
        jnp.zeros((buffer_rows, byte_width), jnp.bfloat16)
        .at[target_slot]
        .set(cotangent_rows, mode="drop")
    )
    arrived_rows, arrived_meta = (
        lax.all_to_all(send_rows, "seq", split_axis=0, concat_axis=0, tiled=True),
        lax.all_to_all(send_meta, "seq", split_axis=0, concat_axis=0, tiled=True),
    )
    target = arrived_meta[:, 0]
    valid_slot = target < patch_dev
    patch_rows = (
        jnp.zeros((patch_dev, byte_width), jnp.bfloat16).at[target].set(arrived_rows, mode="drop")
    )
    patch_docs = jnp.zeros((patch_dev,), jnp.int32).at[target].set(arrived_meta[:, 1], mode="drop")
    patch_pos = seq_place + devices * jnp.arange(patch_dev, dtype=jnp.int32)
    widened = jnp.dot(patch_rows, widen_full, preferred_element_type=jnp.float32)
    model_width = widened.shape[1]
    first_low = normalize(widened, gain_one).astype(jnp.bfloat16)
    projected = jnp.dot(first_low, triple_full, preferred_element_type=jnp.float32).astype(
        jnp.bfloat16
    )
    queries = projected[:, :model_width].reshape(patch_dev, HEADS, HEAD_DIM)
    key_rows = projected[:, model_width : 2 * model_width]
    value_rows = projected[:, 2 * model_width :]
    initial = (
        jnp.full((HEADS, patch_dev), MASK_FILL, jnp.float32),
        jnp.zeros((HEADS, patch_dev), jnp.float32),
        jnp.zeros((HEADS, patch_dev, HEAD_DIM), jnp.float32),
    )
    attend = make_attend(queries, patch_docs, patch_pos, patch_dev, devices)
    running = attend(
        initial,
        (
            lax.all_gather(key_rows, "seq", axis=0, tiled=True),
            lax.all_gather(value_rows, "seq", axis=0, tiled=True),
            lax.all_gather(patch_docs, "seq", axis=0, tiled=True),
        ),
        jnp.int32(0),
    )
    running_top, running_sum, running_out = running
    attended = running_out / running_sum[..., None]
    log_total = running_top + jnp.log(running_sum)
    attended_low = (
        jnp.transpose(attended, (1, 0, 2)).reshape(patch_dev, model_width).astype(jnp.bfloat16)
    )
    resid_one = widened + jnp.dot(attended_low, mixing_full, preferred_element_type=jnp.float32)
    second_low = normalize(resid_one, gain_two).astype(jnp.bfloat16)
    expanded = jnp.dot(second_low, expand_full, preferred_element_type=jnp.float32)
    active_low = jax.nn.gelu(expanded).astype(jnp.bfloat16)
    resid_two = resid_one + jnp.dot(active_low, shrink_full, preferred_element_type=jnp.float32)
    resid_low = resid_two.astype(jnp.bfloat16)
    narrow_low = jnp.dot(resid_low, narrow_full, preferred_element_type=jnp.float32).astype(
        jnp.bfloat16
    )
    returned = jnp.where(valid_slot[:, None], jnp.take(narrow_low, target, axis=0, mode="clip"), 0)
    back_rows = lax.all_to_all(returned, "seq", split_axis=0, concat_axis=0, tiled=True)
    added = jnp.take(back_rows, target_slot, axis=0, mode="clip").astype(jnp.float32)
    new_block = byte_block.astype(jnp.float32) + jnp.where(start_flags[:, None] == 1, added, 0.0)
    arrived_grad = lax.all_to_all(send_grad, "seq", split_axis=0, concat_axis=0, tiled=True)
    narrow_back = (
        jnp.zeros((patch_dev, byte_width), jnp.bfloat16).at[target].set(arrived_grad, mode="drop")
    )
    narrow_grad = outer_sum(resid_low, narrow_back)
    upper_back = back_product(narrow_back, narrow_full)
    shrink_back = upper_back.astype(jnp.bfloat16)
    shrink_grad = outer_sum(active_low, shrink_back)
    active_back = back_product(shrink_back, shrink_full)
    _, gelu_pull = jax.vjp(jax.nn.gelu, expanded)
    expand_back = gelu_pull(active_back)[0].astype(jnp.bfloat16)
    expand_grad = outer_sum(second_low, expand_back)
    second_back = back_product(expand_back, expand_full)
    _, second_pull = jax.vjp(normalize, resid_one, gain_two)
    second_part, second_gain = second_pull(second_back)
    lower_back = upper_back + second_part
    mixed_back = lower_back.astype(jnp.bfloat16)
    mixing_grad = outer_sum(attended_low, mixed_back)
    attend_back = (
        back_product(mixed_back, mixing_full)
        .astype(jnp.bfloat16)
        .reshape(patch_dev, HEADS, HEAD_DIM)
    )
    delta_rows = jnp.einsum("phd,hpd->hp", attend_back.astype(jnp.float32), attended)
    all_keys, all_values, all_docs = (
        lax.all_gather(key_rows, "seq", axis=0, tiled=True),
        lax.all_gather(value_rows, "seq", axis=0, tiled=True),
        lax.all_gather(patch_docs, "seq", axis=0, tiled=True),
    )
    total_keys = all_keys.shape[0]
    span_rows = block_rows(total_keys)
    number = total_keys // span_rows
    key_blocks = all_keys.reshape(number, span_rows, HEADS, HEAD_DIM)
    value_blocks = all_values.reshape(number, span_rows, HEADS, HEAD_DIM)
    doc_blocks = all_docs.reshape(number, span_rows)
    firsts = span_rows * jnp.arange(number, dtype=jnp.int32)
    query_start = jnp.zeros((patch_dev, HEADS, HEAD_DIM), jnp.float32)

    def backstep(query_back, section):
        block_keys, block_values, block_docs, block_first = section
        scores = (
            jnp.einsum("phd,khd->hpk", queries, block_keys, preferred_element_type=jnp.float32)
            * SCORE_SCALE
        )
        key_pos = spread_positions(block_first, span_rows, patch_dev, devices)
        allowed = (patch_docs[:, None] == block_docs[None, :]) & (
            key_pos[None, :] <= patch_pos[:, None]
        )
        probs = jnp.where(allowed[None], jnp.exp(scores - log_total[..., None]), 0.0)
        prob_back = jnp.einsum(
            "phd,khd->hpk", attend_back, block_values, preferred_element_type=jnp.float32
        )
        score_back = (probs * (prob_back - delta_rows[..., None])).astype(jnp.bfloat16)
        query_back = (
            query_back
            + jnp.einsum("hpk,khd->phd", score_back, block_keys, preferred_element_type=jnp.float32)
            * SCORE_SCALE
        )
        keys_part = (
            jnp.einsum("hpk,phd->khd", score_back, queries, preferred_element_type=jnp.float32)
            * SCORE_SCALE
        )
        values_part = jnp.einsum(
            "hpk,phd->khd",
            probs.astype(jnp.bfloat16),
            attend_back,
            preferred_element_type=jnp.float32,
        )
        return (
            query_back,
            (
                keys_part.reshape(span_rows, model_width),
                values_part.reshape(span_rows, model_width),
            ),
        )

    query_back, (keys_back, values_back) = lax.scan(
        backstep, query_start, (key_blocks, value_blocks, doc_blocks, firsts)
    )
    keys_own, values_own = (
        lax.psum_scatter(
            keys_back.reshape(total_keys, model_width).astype(jnp.bfloat16),
            "seq",
            scatter_dimension=0,
            tiled=True,
        ).astype(jnp.float32),
        lax.psum_scatter(
            values_back.reshape(total_keys, model_width).astype(jnp.bfloat16),
            "seq",
            scatter_dimension=0,
            tiled=True,
        ).astype(jnp.float32),
    )
    triple_back = jnp.concatenate(
        [query_back.reshape(patch_dev, model_width), keys_own, values_own], axis=1
    ).astype(jnp.bfloat16)
    triple_grad = outer_sum(first_low, triple_back)
    first_back = back_product(triple_back, triple_full)
    _, first_pull = jax.vjp(normalize, widened, gain_one)
    first_part, first_gain = first_pull(first_back)
    base_low = (lower_back + first_part).astype(jnp.bfloat16)
    widen_grad = outer_sum(patch_rows, base_low)
    patch_back = back_product(base_low, widen_full).astype(jnp.bfloat16)
    grad_slots = jnp.where(
        valid_slot[:, None], jnp.take(patch_back, target, axis=0, mode="clip"), 0
    )
    grad_rows = lax.all_to_all(grad_slots, "seq", split_axis=0, concat_axis=0, tiled=True)
    coming = jnp.take(grad_rows, target_slot, axis=0, mode="clip").astype(jnp.float32)
    grad_block = cotangent_rows.astype(jnp.float32) + jnp.where(
        start_flags[:, None] == 1, coming, 0.0
    )
    gains_grad = jnp.stack([first_gain, second_gain], axis=0)
    reduced = (
        lax.psum_scatter(widen_grad, ("seq", "dp"), scatter_dimension=0, tiled=True),
        lax.psum_scatter(triple_grad, ("seq", "dp"), scatter_dimension=0, tiled=True),
        lax.psum_scatter(mixing_grad, ("seq", "dp"), scatter_dimension=0, tiled=True),
        lax.psum_scatter(expand_grad, ("seq", "dp"), scatter_dimension=0, tiled=True),
        lax.psum_scatter(shrink_grad, ("seq", "dp"), scatter_dimension=0, tiled=True),
        lax.psum_scatter(narrow_grad, ("seq", "dp"), scatter_dimension=0, tiled=True),
        lax.psum_scatter(gains_grad, ("seq", "dp"), scatter_dimension=1, tiled=True),
    )
    local_squares = jnp.float32(0.0)
    for member in reduced:
        local_squares = local_squares + jnp.sum(member * member)
    norm_squared = lax.psum(local_squares, ("seq", "dp"))
    grad_norm = jnp.sqrt(norm_squared)
    factor = CLIP_NORM / jnp.maximum(grad_norm, CLIP_NORM)
    masters = (
        widen_master,
        triple_master,
        mixing_master,
        expand_master,
        shrink_master,
        narrow_master,
        gains_master,
    )
    firsts_old = (
        widen_first,
        triple_first,
        mixing_first,
        expand_first,
        shrink_first,
        narrow_first,
        gains_first,
    )
    seconds_old = (
        widen_second,
        triple_second,
        mixing_second,
        expand_second,
        shrink_second,
        narrow_second,
        gains_second,
    )
    rates = (
        2.0 * D_BYTE ** (-0.5),
        2.0 * D ** (-0.5),
        0.4,
        2.0 * D ** (-0.5),
        2.0 * FF ** (-0.5),
        2.0 * D ** (-0.5),
        0.6,
    )
    decays = (DECAY_RATE, DECAY_RATE, DECAY_RATE, DECAY_RATE, DECAY_RATE, DECAY_RATE, 0.0)
    updates = [
        adam_update(
            masters[index],
            firsts_old[index],
            seconds_old[index],
            reduced[index],
            factor,
            rates[index],
            decays[index],
        )
        for index in range(7)
    ]
    return (
        new_block.astype(jnp.bfloat16)[None],
        grad_block.astype(jnp.bfloat16)[None],
        grad_norm,
        updates[0][0],
        updates[0][1],
        updates[0][2],
        updates[1][0],
        updates[1][1],
        updates[1][2],
        updates[2][0],
        updates[2][1],
        updates[2][2],
        updates[3][0],
        updates[3][1],
        updates[3][2],
        updates[4][0],
        updates[4][1],
        updates[4][2],
        updates[5][0],
        updates[5][1],
        updates[5][2],
        updates[6][0],
        updates[6][1],
        updates[6][2],
    )


PLANES = 4
TEAM = 8
CORE_BIT, Y_BIT, X_BIT = 1, 2, 4
AXES = ("z", "x", "y", "c")
TEAM_AXES = ("x", "y", "c")
LOW = jnp.bfloat16
WIDE = jnp.float32
VMEM_LIMIT = 56 * 1024 * 1024
LOG2_E = 1.4426950408889634
TILE = 256
GELU_A = 0.7978845608028654
GELU_B = 0.044715


def plane_fits(mesh):
    return mesh.shape["seq"] == 2 * PLANES and mesh.shape["dp"] == PLANES


def flip(value, bit):
    pairs = [(place, place ^ bit) for place in range(PLANES * TEAM)]
    return lax.ppermute(value, AXES, pairs)


def shift_plane(value, hop):
    pairs = [
        (plane * TEAM + t, (plane + hop) % PLANES * TEAM + t)
        for plane in range(PLANES)
        for t in range(TEAM)
    ]
    return lax.ppermute(value, AXES, pairs)


def source_of(plane, t):
    core = t % 2
    return (t // 2 - plane - 2 * core) % PLANES * 2 + core


def byte_pairs():
    return [
        (source_of(plane, t) * PLANES + plane, plane * TEAM + t)
        for plane in range(PLANES)
        for t in range(TEAM)
    ]


def to_plane(value):
    return lax.ppermute(value, AXES, byte_pairs())


def from_plane(value):
    return lax.ppermute(value, AXES, [(there, here) for here, there in byte_pairs()])


def team_gather(block, cut=None):
    cut = block.shape[0] // 2 if cut is None else cut
    from_x = flip(block, X_BIT)
    from_y = flip(block, Y_BIT)
    from_core = flip(block, CORE_BIT)
    upper = flip(from_y[:cut], X_BIT)
    lower = flip(from_x[cut:], Y_BIT)
    y_core = flip(from_y, CORE_BIT)
    x_core = flip(from_x, CORE_BIT)
    diagonal = jnp.concatenate([upper, lower], axis=0)
    return [block, from_core, from_y, y_core, from_x, x_core, diagonal, flip(diagonal, CORE_BIT)]


def team_scatter(pieces):
    sums = {}
    for k in (3, 2, 1, 0):
        piece = pieces(k)
        half = piece.shape[0] // 2
        sums[k] = piece[:half] + flip(piece[half:].astype(LOW), CORE_BIT).astype(WIDE)
        if k == 3:
            cut = half // 2
            diagonal = sums[3].astype(LOW)
            upper = flip(diagonal[:cut], X_BIT).astype(WIDE)
            lower = flip(diagonal[cut:], Y_BIT).astype(WIDE)
        if k == 2:
            sums[2] = jnp.concatenate([sums[2][:cut], sums[2][cut:] + lower], axis=0)
            from_x = flip(sums[2].astype(LOW), X_BIT).astype(WIDE)
        if k == 1:
            sums[1] = jnp.concatenate([sums[1][:cut] + upper, sums[1][cut:]], axis=0)
            from_y = flip(sums[1].astype(LOW), Y_BIT).astype(WIDE)
    return sums[0] + from_x + from_y


def plane_gather_small(block, plane):
    out = jnp.zeros((PLANES,) + block.shape, block.dtype)
    out = lax.dynamic_update_index_in_dim(out, block, plane, 0)
    for hop in (1, 2, 3):
        out = lax.dynamic_update_index_in_dim(
            out, shift_plane(block, hop), (plane - hop) % PLANES, 0
        )
    return out


def plane_scatter_small(stack, plane):
    total = lax.dynamic_index_in_dim(stack, plane, 0, False).astype(WIDE)
    for hop in (1, 2, 3):
        part = lax.dynamic_index_in_dim(stack, (plane + hop) % PLANES, 0, False)
        total = total + shift_plane(part, hop).astype(WIDE)
    return total


def team_exchange(value):
    return lax.all_to_all(value, TEAM_AXES, split_axis=0, concat_axis=0, tiled=True)


def pick(value, place, axis):
    return lax.dynamic_index_in_dim(value, place, axis, False)


def join(mine, other, place, axis):
    return jnp.where(
        place == 0, jnp.stack([mine, other], axis=axis), jnp.stack([other, mine], axis=axis)
    )


def mixing_exchange(stack, x, y, core):
    rows, width = stack.shape[1:]
    cube = stack.reshape(2, 2, rows, width)
    cube = join(pick(cube, x, 0), flip(pick(cube, 1 - x, 0), X_BIT), x, 0)
    cube = join(pick(cube, y, 1), flip(pick(cube, 1 - y, 1), Y_BIT), y, 0)
    cube = join(pick(cube, core, 1), flip(pick(cube, 1 - core, 1), CORE_BIT), core, 1)
    return cube.reshape(4 * rows, width)


def mixing_return(block, x, y, core):
    rows, width = block.shape[0] // 4, block.shape[1]
    cube = block.reshape(2, 2, rows, width)
    cube = join(pick(cube, core, 1), flip(pick(cube, 1 - core, 1), CORE_BIT), core, 0)
    cube = join(pick(cube, y, 1), flip(pick(cube, 1 - y, 1), Y_BIT), y, 0)
    cube = join(pick(cube, x, 1), flip(pick(cube, 1 - x, 1), X_BIT), x, 0)
    return cube.reshape(4, rows, width)


def in_vmem():
    return pl.BlockSpec(memory_space=pltpu.VMEM)


def in_smem():
    return pl.BlockSpec(memory_space=pltpu.SMEM)


def params():
    return pltpu.CompilerParams(vmem_limit_bytes=VMEM_LIMIT)


def nn(left, right):
    return lax.dot_general(left, right, (((1,), (0,)), ((), ())), preferred_element_type=WIDE)


def nt(left, right):
    return lax.dot_general(left, right, (((1,), (1,)), ((), ())), preferred_element_type=WIDE)


def tn(left, right):
    return lax.dot_general(left, right, (((0,), (0,)), ((), ())), preferred_element_type=WIDE)


def slot_matrix(flags, slots):
    amount = flags.shape[1]
    row = lax.broadcasted_iota(jnp.int32, (amount, amount), 0)
    column = lax.broadcasted_iota(jnp.int32, (amount, amount), 1)
    before = jnp.where(row < column, 1.0, 0.0).astype(LOW)
    rank = nn(jnp.broadcast_to(flags, (8, amount)).astype(LOW), before)[:1]
    rank = jnp.where(flags > 0.5, rank, -1.0)
    slot = lax.broadcasted_iota(jnp.int32, (slots, amount), 0).astype(WIDE)
    return jnp.where(slot == rank, 1.0, 0.0).astype(LOW)


def pack_kernel(starts_ref, docs_ref, rows_ref, cotangent_ref, rows_out, cotangent_out):
    capacity, width = cotangent_out.shape
    flags = starts_ref[...].astype(WIDE)
    chosen = slot_matrix(flags, 384)
    amount = jnp.sum(flags)
    docs = nt(jnp.broadcast_to(docs_ref[...].astype(WIDE), (16, flags.shape[1])).astype(LOW), chosen)
    docs = jnp.concatenate([docs, jnp.zeros((16, width - 384), WIDE)], axis=1)
    row = lax.broadcasted_iota(jnp.int32, (16, width), 0)
    high = jnp.floor(amount * 0.5)
    meta = jnp.where(row == 0, docs, jnp.where(row == 1, high, amount - 2.0 * high))
    chosen = chosen[:capacity]
    rows_out[:capacity] = nn(chosen, rows_ref[...]).astype(LOW)
    rows_out[capacity:] = meta.astype(LOW)
    cotangent_out[...] = nn(chosen, cotangent_ref[...]).astype(LOW)


def pack(starts, docs, rows, cotangent, capacity):
    width = rows.shape[1]
    return pl.pallas_call(
        pack_kernel,
        out_shape=(
            jax.ShapeDtypeStruct((capacity + 16, width), LOW),
            jax.ShapeDtypeStruct((capacity, width), LOW),
        ),
        in_specs=[in_vmem()] * 4,
        out_specs=(in_vmem(), in_vmem()),
        compiler_params=params(),
        name="pack",
    )(starts, docs, rows, cotangent)


def unpack_kernel(starts_ref, rows_ref, back_ref, out_ref):
    flags = starts_ref[...].astype(WIDE)
    chosen = slot_matrix(flags, back_ref.shape[0])
    added = tn(chosen, back_ref[...])
    out_ref[...] = (rows_ref[...].astype(WIDE) + added).astype(LOW)


def unpack(starts, rows, back):
    return pl.pallas_call(
        unpack_kernel,
        out_shape=jax.ShapeDtypeStruct(rows.shape, LOW),
        in_specs=[in_vmem()] * 3,
        out_specs=in_vmem(),
        compiler_params=params(),
        name="unpack",
    )(starts, rows, back)


def window_matrix(first, amount, capacity):
    target = lax.broadcasted_iota(jnp.int32, (capacity + 16, capacity), 0)
    source = lax.broadcasted_iota(jnp.int32, (capacity + 16, capacity), 1)
    moved = (target == source + first % 16) & (source < amount)
    return jnp.where(moved, 1.0, 0.0).astype(LOW)


def enter_kernel(
    capacity,
    place_ref,
    gain_ref,
    *refs,
):
    blocks = refs[:TEAM]
    low_out, own_wide, own_rows, doc_column, doc_row, widen_out, spans = refs[TEAM : TEAM + 7]
    rows, docs, widen_wide = refs[TEAM + 7 :]
    plane, t = place_ref[0], place_ref[1]
    member_rows = own_rows.shape[0]
    total = low_out.shape[0]
    width = own_rows.shape[1]
    shard = widen_out.shape[0] // (PLANES * TEAM)

    amounts, sources = [], []
    for m in range(TEAM):
        meta = blocks[m][capacity : capacity + 16].astype(WIDE)
        row = lax.broadcasted_iota(jnp.int32, meta.shape, 0)
        lane = lax.broadcasted_iota(jnp.int32, meta.shape, 1)
        picked = jnp.where(lane == 0, jnp.where(row == 1, 2.0 * meta, jnp.where(row == 2, meta, 0.0)), 0.0)
        amounts.append(jnp.sum(picked).astype(jnp.int32))
        member = t ^ m
        core = member % 2
        sources.append((member // 2 - plane - 2 * core + 2 * PLANES) % PLANES * 2 + core)
    firsts = []
    for m in range(TEAM):
        first = jnp.int32(0)
        for other in range(TEAM):
            if other != m:
                first = first + jnp.where(sources[other] < sources[m], amounts[other], 0)
        firsts.append(first)
        spans[m] = first
        spans[TEAM + m] = amounts[m]

    for m in range(TEAM):
        member = t ^ m
        for source in range(PLANES):
            base = capacity + 16 + source * 64
            at = pl.multiple_of((source * TEAM + member) * shard, 8)
            widen_wide[pl.ds(at, shard), :width] = blocks[m][base : base + 32].astype(WIDE)[:shard]
            widen_wide[pl.ds(at, shard), width:] = blocks[m][base + 32 : base + 64].astype(WIDE)[:shard]
    widen_out[...] = widen_wide[...].astype(LOW)

    rows[...] = jnp.zeros_like(rows)
    docs[...] = jnp.zeros_like(docs)
    for m in range(TEAM):
        moving = window_matrix(firsts[m], amounts[m], capacity)
        at = pl.ds(pl.multiple_of(firsts[m] // 16 * 16, 16), capacity + 16)
        rows[at] = rows[at] + nn(moving, blocks[m][:capacity]).astype(LOW)
        names = blocks[m][capacity : capacity + 16][:1, :384]
        names = jnp.broadcast_to(names, (128, 384))[:, :capacity]
        docs[at] = docs[at] + nt(moving, names)

    doc_column[...] = docs[:total]
    select = jnp.where(lax.broadcasted_iota(jnp.int32, (8, 128), 1) == 0, 1.0, 0.0).astype(LOW)
    doc_row[...] = nt(select, docs[:total].astype(LOW))

    def one(member, carry):
        at = pl.ds(pl.multiple_of(member * member_rows, 16), member_rows)
        here = rows[at]
        wide = nn(here, widen_out[...])
        inverse = lax.rsqrt(jnp.mean(wide * wide, axis=-1, keepdims=True) + NORM_EPS)
        low_out[at] = (wide * inverse * gain_ref[...]).astype(LOW)

        @pl.when(member == t)
        def _():
            own_wide[...] = wide
            own_rows[...] = here

        return carry

    lax.fori_loop(0, TEAM, one, 0)


def enter(place, gain, blocks, capacity, member_rows, shard):
    width = blocks[0].shape[1]
    model = gain.shape[1]
    total = member_rows * TEAM
    padded = total + capacity + 16
    return pl.pallas_call(
        lambda *refs: enter_kernel(capacity, *refs),
        out_shape=(
            jax.ShapeDtypeStruct((total, model), LOW),
            jax.ShapeDtypeStruct((member_rows, model), WIDE),
            jax.ShapeDtypeStruct((member_rows, width), LOW),
            jax.ShapeDtypeStruct((total, 128), WIDE),
            jax.ShapeDtypeStruct((8, total), WIDE),
            jax.ShapeDtypeStruct((shard * PLANES * TEAM, model), LOW),
            jax.ShapeDtypeStruct((2 * TEAM,), jnp.int32),
        ),
        in_specs=[in_smem(), in_vmem()] + [in_vmem()] * TEAM,
        out_specs=(in_vmem(),) * 6 + (in_smem(),),
        scratch_shapes=[
            pltpu.VMEM((padded, width), LOW),
            pltpu.VMEM((padded, 128), WIDE),
            pltpu.VMEM((shard * PLANES * TEAM, model), WIDE),
        ],
        compiler_params=params(),
        name="enter",
    )(place, gain, *blocks)


def cotangent_kernel(capacity, place_ref, spans_ref, *refs):
    blocks = refs[:TEAM]
    low_out, own_wide, own_rows, narrow_out = refs[TEAM : TEAM + 4]
    (rows,) = refs[TEAM + 4 :]
    t = place_ref[1]
    member_rows = own_rows.shape[0]
    shard = narrow_out.shape[0] // (PLANES * TEAM)
    for m in range(TEAM):
        member = t ^ m
        for source in range(PLANES):
            at = pl.multiple_of((source * TEAM + member) * shard, 16)
            base = capacity + source * shard
            narrow_out[pl.ds(at, shard)] = blocks[m][base : base + shard]
    rows[...] = jnp.zeros_like(rows)
    for m in range(TEAM):
        first = spans_ref[m]
        moving = window_matrix(first, spans_ref[TEAM + m], capacity)
        at = pl.ds(pl.multiple_of(first // 16 * 16, 16), capacity + 16)
        rows[at] = rows[at] + nn(moving, blocks[m][:capacity]).astype(LOW)

    def one(m, carry):
        at = pl.ds(pl.multiple_of((t ^ m) * member_rows, 16), member_rows)
        here = rows[at]
        wide = nt(here, narrow_out[...])
        low_out[pl.ds(pl.multiple_of(m * member_rows, 16), member_rows)] = wide.astype(LOW)

        @pl.when(m == 0)
        def _():
            own_wide[...] = wide
            own_rows[...] = here

        return carry

    lax.fori_loop(0, TEAM, one, 0)


def cotangent(place, spans, blocks, capacity, member_rows, model):
    width = blocks[0].shape[1]
    total = member_rows * TEAM
    return pl.pallas_call(
        lambda *refs: cotangent_kernel(capacity, *refs),
        out_shape=(
            jax.ShapeDtypeStruct((total, model), LOW),
            jax.ShapeDtypeStruct((member_rows, model), WIDE),
            jax.ShapeDtypeStruct((member_rows, width), LOW),
            jax.ShapeDtypeStruct((model, width), LOW),
        ),
        in_specs=[in_smem(), in_smem()] + [in_vmem()] * TEAM,
        out_specs=(in_vmem(),) * 4,
        scratch_shapes=[pltpu.VMEM((total + capacity + 16, width), LOW)],
        compiler_params=params(),
        name="cotangent",
    )(place, spans, *blocks)


def leave_kernel(place_ref, spans_ref, *refs):
    blocks, out_ref = refs[:TEAM], refs[TEAM]
    t = place_ref[1]
    first = spans_ref[0]
    capacity = out_ref.shape[0]
    rows = blocks[0].shape[0]
    total = jnp.zeros(out_ref.shape, WIDE)
    for m in range(TEAM):
        target = lax.broadcasted_iota(jnp.int32, (capacity, rows), 0)
        source = lax.broadcasted_iota(jnp.int32, (capacity, rows), 1) + ((t ^ m) * rows - first)
        total = total + nn(jnp.where(target == source, 1.0, 0.0).astype(LOW), blocks[m][...])
    out_ref[...] = total.astype(LOW)


def leave(place, spans, blocks, capacity):
    return pl.pallas_call(
        leave_kernel,
        out_shape=jax.ShapeDtypeStruct((capacity, blocks[0].shape[1]), LOW),
        in_specs=[in_smem(), in_smem()] + [in_vmem()] * TEAM,
        out_specs=in_vmem(),
        compiler_params=params(),
        name="leave",
    )(place, spans, *blocks)


def attend_kernel(own, projected_ref, doc_column, doc_row, flat_out, low_out, total_out, queries, keys, values):
    rows = projected_ref.shape[0]
    width = own * HEAD_DIM
    for h in range(own):
        lanes = slice(h * HEAD_DIM, (h + 1) * HEAD_DIM)
        queries[h] = projected_ref[:, :width][:, lanes]
        keys[h] = projected_ref[:, width : 2 * width][:, lanes]
        values[h] = jnp.transpose(
            projected_ref[:, 2 * width :][:, lanes].astype(WIDE)
        ).astype(LOW)
    total_out[...] = jnp.zeros_like(total_out)
    scale = SCORE_SCALE * LOG2_E
    causal = lax.broadcasted_iota(jnp.int32, (TILE, TILE), 0) <= lax.broadcasted_iota(
        jnp.int32, (TILE, TILE), 1
    )

    def one_query(j, carry):
        at_query = pl.ds(pl.multiple_of(j * TILE, TILE), TILE)
        query_docs = doc_row[:1, at_query]

        def one_key(i, status, diagonal):
            at_key = pl.ds(pl.multiple_of(i * TILE, TILE), TILE)
            allowed = doc_column[at_key, :1] == query_docs
            if diagonal:
                allowed = allowed & causal
            result = []
            for h in range(own):
                scores = nt(keys[h, at_key], queries[h, at_query]) * scale
                masked = jnp.where(allowed, scores, MASK_FILL)
                best = jnp.max(masked, axis=0, keepdims=True)
                if diagonal:
                    top = best
                    weights = jnp.exp2(masked - top)
                    summed = jnp.sum(weights, axis=0, keepdims=True)
                    out = nn(values[h, :, at_key], weights.astype(LOW))
                else:
                    old_top, old_sum, old_out = status[h]
                    top = jnp.maximum(old_top, best)
                    weights = jnp.exp2(masked - top)
                    rescale = jnp.exp2(old_top - top)
                    summed = old_sum * rescale + jnp.sum(weights, axis=0, keepdims=True)
                    out = old_out * rescale + nn(values[h, :, at_key], weights.astype(LOW))
                result.append((top, summed, out))
            return tuple(result)

        status = one_key(j, None, True)
        status = lax.fori_loop(0, j, lambda i, now: one_key(i, now, False), status)
        for h in range(own):
            top, summed, out = status[h]
            done = out / summed
            flat_out[h * HEAD_DIM : (h + 1) * HEAD_DIM, at_query] = done
            total_out[h : h + 1, at_query] = top + jnp.log2(summed)
        return carry

    lax.fori_loop(0, rows // TILE, one_query, 0)
    low_out[...] = jnp.transpose(flat_out[...]).astype(LOW)


def attend_team(projected, doc_column, doc_row, own):
    rows = projected.shape[0]
    width = own * HEAD_DIM
    return pl.pallas_call(
        lambda *refs: attend_kernel(own, *refs),
        out_shape=(
            jax.ShapeDtypeStruct((width, rows), WIDE),
            jax.ShapeDtypeStruct((rows, width), LOW),
            jax.ShapeDtypeStruct((8, rows), WIDE),
        ),
        in_specs=[in_vmem()] * 3,
        out_specs=(in_vmem(),) * 3,
        scratch_shapes=[
            pltpu.VMEM((own, rows, HEAD_DIM), LOW),
            pltpu.VMEM((own, rows, HEAD_DIM), LOW),
            pltpu.VMEM((own, HEAD_DIM, rows), LOW),
        ],
        compiler_params=params(),
        name="attend",
    )(projected, doc_column, doc_row)


def attend_back_kernel(
    own,
    projected_ref,
    flat_ref,
    total_ref,
    back_ref,
    doc_column,
    doc_row,
    out_ref,
    queries,
    keys,
    values,
    backs,
    keys_flat,
    backs_flat,
    deltas,
    query_back,
):
    rows = projected_ref.shape[0]
    width = own * HEAD_DIM
    for h in range(own):
        lanes = slice(h * HEAD_DIM, (h + 1) * HEAD_DIM)
        key = projected_ref[:, width : 2 * width][:, lanes]
        back = back_ref[:, lanes]
        back_flat = jnp.transpose(back.astype(WIDE))
        queries[h] = projected_ref[:, :width][:, lanes]
        keys[h] = key
        values[h] = projected_ref[:, 2 * width :][:, lanes]
        backs[h] = back
        keys_flat[h] = jnp.transpose(key.astype(WIDE)).astype(LOW)
        backs_flat[h] = back_flat.astype(LOW)
        deltas[h : h + 1] = jnp.sum(back_flat * flat_ref[lanes], axis=0, keepdims=True)
    query_back[...] = jnp.zeros_like(query_back)
    scale = SCORE_SCALE * LOG2_E
    causal = lax.broadcasted_iota(jnp.int32, (TILE, TILE), 0) <= lax.broadcasted_iota(
        jnp.int32, (TILE, TILE), 1
    )

    def one_key(i, carry):
        at_key = pl.ds(pl.multiple_of(i * TILE, TILE), TILE)

        def one_query(j, status, diagonal):
            at_query = pl.ds(pl.multiple_of(j * TILE, TILE), TILE)
            allowed = doc_column[at_key, :1] == doc_row[:1, at_query]
            if diagonal:
                allowed = allowed & causal
            result = []
            for h in range(own):
                scores = nt(keys[h, at_key], queries[h, at_query]) * scale
                probs = jnp.where(allowed, jnp.exp2(scores - total_ref[h : h + 1, at_query]), 0.0)
                prob_back = nn(values[h, at_key], backs_flat[h, :, at_query])
                score_back = (probs * (prob_back - deltas[h : h + 1, at_query])).astype(LOW)
                value_part = nn(probs.astype(LOW), backs[h, at_query])
                key_part = nn(score_back, queries[h, at_query])
                query_back[h, :, at_query] += nn(keys_flat[h, :, at_key], score_back)
                if diagonal:
                    result.append((key_part, value_part))
                else:
                    result.append((status[h][0] + key_part, status[h][1] + value_part))
            return tuple(result)

        status = one_query(i, None, True)
        status = lax.fori_loop(
            i + 1, rows // TILE, lambda j, now: one_query(j, now, False), status
        )
        key_all = jnp.concatenate([status[h][0] * SCORE_SCALE for h in range(own)], axis=1)
        value_all = jnp.concatenate([status[h][1] for h in range(own)], axis=1)
        out_ref[at_key, width : 3 * width] = jnp.concatenate([key_all, value_all], axis=1).astype(LOW)
        return carry

    lax.fori_loop(0, rows // TILE, one_key, 0)
    flat = jnp.concatenate([query_back[h] for h in range(own)], axis=0) * SCORE_SCALE
    out_ref[:, :width] = jnp.transpose(flat).astype(LOW)


def attend_back_team(projected, flat, totals, back, doc_column, doc_row, own):
    rows = projected.shape[0]
    tall = pltpu.VMEM((own, rows, HEAD_DIM), LOW)
    long = pltpu.VMEM((own, HEAD_DIM, rows), LOW)
    return pl.pallas_call(
        lambda *refs: attend_back_kernel(own, *refs),
        out_shape=jax.ShapeDtypeStruct(projected.shape, LOW),
        in_specs=[in_vmem()] * 6,
        out_specs=in_vmem(),
        scratch_shapes=[
            tall,
            tall,
            tall,
            tall,
            long,
            long,
            pltpu.VMEM((8, rows), WIDE),
            pltpu.VMEM((own, HEAD_DIM, rows), WIDE),
        ],
        compiler_params=params(),
        name="attend_back",
    )(projected, flat, totals, back, doc_column, doc_row)


def per_member(
    byte_rows,
    starts,
    doc_ids,
    out_cotangent,
    widen_master,
    widen_first,
    widen_second,
    triple_master,
    triple_first,
    triple_second,
    mixing_master,
    mixing_first,
    mixing_second,
    expand_master,
    expand_first,
    expand_second,
    shrink_master,
    shrink_first,
    shrink_second,
    narrow_master,
    narrow_first,
    narrow_second,
    gains_master,
    gains_first,
    gains_second,
):
    plane = lax.axis_index("z")
    x, y, core = lax.axis_index("x"), lax.axis_index("y"), lax.axis_index("c")
    t = 4 * x + 2 * y + core
    place = jnp.stack([plane, t]).astype(jnp.int32)
    byte_block, cotangent_rows = byte_rows[0], out_cotangent[0]
    bytes_dev, byte_width = byte_block.shape
    model = triple_master.shape[1] // 3
    hidden = expand_master.shape[1]
    shard = triple_master.shape[0]
    widen_shard = widen_master.shape[0]
    member_rows = 3 * bytes_dev // 16
    capacity = member_rows + member_rows // 2
    total = TEAM * member_rows
    own = HEADS // TEAM
    own_width = model // TEAM
    own_hidden = hidden // TEAM
    piece_hidden = own_hidden // PLANES

    row_buffer, cotangent_buffer = pack(
        starts, doc_ids, byte_block, cotangent_rows, capacity
    )
    row_buffer = to_plane(row_buffer)

    widen_low = widen_master.astype(LOW)
    gains_low = gains_master.astype(LOW)
    gain_rows = jnp.pad(gains_low, ((0, 32 - widen_shard - 2), (0, byte_width - shard)))
    small = jnp.concatenate(
        [
            widen_low[:, :byte_width],
            gain_rows,
            widen_low[:, byte_width:],
            jnp.zeros((32 - widen_shard, byte_width), LOW),
        ],
        axis=0,
    )
    small = plane_gather_small(small, plane).reshape(PLANES * 64, byte_width)
    triple_own = triple_master.astype(LOW).reshape(shard, 3, TEAM, own_width)
    triple_own = team_exchange(
        jnp.transpose(triple_own, (2, 0, 1, 3)).reshape(TEAM, shard, 3 * own_width)
    )
    triple_own = lax.all_gather(
        triple_own.reshape(TEAM * shard, 3 * own_width), "z", axis=0, tiled=True
    )

    entering = team_gather(jnp.concatenate([row_buffer, small], axis=0))
    gains_full = jnp.stack(
        [
            block[capacity + 16 :].reshape(PLANES, 64, byte_width)[:, widen_shard : widen_shard + 2, :shard]
            for block in entering
        ]
    )
    gains_full = jnp.take(gains_full, t ^ jnp.arange(TEAM, dtype=jnp.int32), axis=0)
    gains_full = jnp.transpose(gains_full, (2, 1, 0, 3)).reshape(2, model).astype(WIDE)
    gain_one, gain_two = gains_full[:1], gains_full[1:]

    first_low, widened, patch_rows, doc_column, doc_row, widen_full, spans = enter(
        place, gain_one, entering, capacity, member_rows, widen_shard
    )

    expand_own = expand_master.astype(LOW).reshape(shard, PLANES, TEAM, piece_hidden)
    expand_own = team_exchange(
        jnp.transpose(expand_own, (2, 0, 1, 3)).reshape(TEAM, shard, own_hidden)
    )
    expand_own = lax.all_gather(
        expand_own.reshape(TEAM * shard, own_hidden), "z", axis=0, tiled=True
    )
    shrink_own = lax.all_gather(shrink_master.astype(LOW), "z", axis=0, tiled=True)
    mixing_own = mixing_exchange(
        plane_gather_small(mixing_master.astype(LOW), plane), x, y, core
    )

    narrow_stack = plane_gather_small(narrow_master.astype(LOW), plane)
    leaving = team_gather(
        jnp.concatenate(
            [to_plane(cotangent_buffer), narrow_stack.reshape(PLANES * shard, byte_width)], axis=0
        )
    )
    shrink_back, upper_back, narrow_back, narrow_full = cotangent(
        place, spans, leaving, capacity, member_rows, model
    )

    projected = nn(first_low, triple_own).astype(LOW)
    flat, attended_low, totals = attend_team(projected, doc_column, doc_row, own)

    def relative(value):
        return jnp.concatenate(
            [
                lax.dynamic_slice_in_dim(value, (t ^ m) * member_rows, member_rows, 0)
                for m in range(TEAM)
            ],
            axis=0,
        )

    natural = relative
    pair = 2 * member_rows
    attended_low = relative(attended_low)
    resid_one = widened + team_scatter(
        lambda k: nn(attended_low[k * pair : (k + 1) * pair], mixing_own)
    )
    second_low = jnp.concatenate(team_gather(normalize(resid_one, gain_two).astype(LOW)), axis=0)

    expanded = nn(second_low, expand_own)
    active_low = jax.nn.gelu(expanded).astype(LOW)
    active_back = nt(shrink_back, shrink_own)
    _, gelu_pull = jax.vjp(jax.nn.gelu, expanded)
    expand_back = gelu_pull(active_back)[0].astype(LOW)
    second_back = team_scatter(
        lambda k: nt(expand_back[k * pair : (k + 1) * pair], expand_own)
    )
    _, second_pull = jax.vjp(normalize, resid_one, gain_two)
    second_part, second_gain = second_pull(second_back)
    lower_back = upper_back + second_part
    mixed_back = jnp.concatenate(team_gather(lower_back.astype(LOW)), axis=0)

    shrink_grad = tn(active_low, shrink_back).astype(LOW)
    shrink_sum = lax.psum_scatter(shrink_grad, "z", scatter_dimension=0, tiled=True)
    expand_grad = tn(second_low, expand_back).astype(LOW)
    expand_sum = lax.psum_scatter(expand_grad, "z", scatter_dimension=0, tiled=True)

    attend_back = natural(nt(mixed_back, mixing_own).astype(LOW))
    triple_back = attend_back_team(
        projected, flat, totals, attend_back, doc_column, doc_row, own
    )
    triple_back_relative = relative(triple_back)
    first_back = team_scatter(
        lambda k: nt(triple_back_relative[k * pair : (k + 1) * pair], triple_own)
    )
    triple_grad = tn(first_low, triple_back).astype(LOW)
    triple_sum = lax.psum_scatter(triple_grad, "z", scatter_dimension=0, tiled=True)
    mixing_grad = tn(attended_low, mixed_back).astype(LOW)
    mixing_sum = plane_scatter_small(mixing_return(mixing_grad, x, y, core), plane)

    resid_two = resid_one + team_scatter(
        lambda k: nn(active_low[k * pair : (k + 1) * pair], shrink_own)
    )
    resid_low = resid_two.astype(LOW)
    narrow_low = nn(resid_low, narrow_full).astype(LOW)
    narrow_buffer = from_plane(leave(place, spans, team_gather(narrow_low), capacity))
    new_block = unpack(starts, byte_block, narrow_buffer)
    narrow_grad = tn(resid_low, narrow_back)

    _, first_pull = jax.vjp(normalize, widened, gain_one)
    first_part, first_gain = first_pull(first_back)
    base_low = (lower_back + first_part).astype(LOW)
    widen_grad = tn(patch_rows, base_low)
    patch_back = nt(base_low, widen_full).astype(LOW)
    patch_buffer = from_plane(leave(place, spans, team_gather(patch_back), capacity))
    grad_block = unpack(starts, cotangent_rows, patch_buffer)

    def by_target(gradient, rows):
        width = gradient.shape[1]
        blocks = gradient.reshape(PLANES, TEAM, rows, width)
        blocks = jnp.transpose(blocks, (1, 0, 2, 3)).reshape(TEAM * PLANES * rows, width)
        return jnp.concatenate(
            [
                lax.dynamic_slice_in_dim(blocks, (t ^ m) * PLANES * rows, PLANES * rows, 0)
                for m in range(TEAM)
            ],
            axis=0,
        )

    gains_grad = jnp.concatenate([first_gain, second_gain], axis=0)
    gains_grad = jnp.transpose(gains_grad.reshape(2, PLANES, TEAM, shard), (1, 2, 0, 3))
    gains_grad = jnp.pad(
        gains_grad.reshape(PLANES * TEAM, 2, shard), ((0, 0), (0, 6), (0, model - shard))
    )
    widen_grad = jnp.concatenate(
        [widen_grad.reshape(PLANES * TEAM, widen_shard, model), gains_grad], axis=1
    ).reshape(-1, model)
    widen_ready = by_target(widen_grad, widen_shard + 8)
    block = 2 * PLANES * (widen_shard + 8)
    widen_sum = team_scatter(lambda k: widen_ready[k * block : (k + 1) * block]).astype(LOW)
    widen_sum = plane_scatter_small(
        widen_sum.reshape(PLANES, widen_shard + 8, model), plane
    )
    gains_sum = widen_sum[widen_shard : widen_shard + 2, :shard]
    widen_sum = widen_sum[:widen_shard]
    narrow_ready = by_target(narrow_grad, shard)
    narrow_block = 2 * PLANES * shard
    narrow_sum = team_scatter(
        lambda k: narrow_ready[k * narrow_block : (k + 1) * narrow_block]
    ).astype(LOW)
    narrow_sum = plane_scatter_small(narrow_sum.reshape(PLANES, shard, byte_width), plane)

    triple_sum = team_exchange(triple_sum.reshape(TEAM, shard, 3 * own_width))
    triple_sum = triple_sum.reshape(TEAM, shard, 3, own_width)
    triple_sum = jnp.transpose(triple_sum, (1, 2, 0, 3)).reshape(shard, 3 * model).astype(WIDE)
    expand_sum = team_exchange(expand_sum.reshape(TEAM, shard, own_hidden))
    expand_sum = expand_sum.reshape(TEAM, shard, PLANES, piece_hidden)
    expand_sum = jnp.transpose(expand_sum, (1, 2, 0, 3)).reshape(shard, hidden).astype(WIDE)
    shrink_sum = shrink_sum.astype(WIDE)

    reduced = (widen_sum, triple_sum, mixing_sum, expand_sum, shrink_sum, narrow_sum, gains_sum)
    squares = jnp.float32(0.0)
    for gradient in reduced:
        squares = squares + jnp.sum(gradient * gradient)
    squares = jnp.full((8, 128), squares, WIDE)
    for bit in (CORE_BIT, Y_BIT, X_BIT, TEAM, 2 * TEAM):
        squares = squares + flip(squares, bit)
    grad_norm = jnp.sqrt(squares[0, 0])
    factor = CLIP_NORM / jnp.maximum(grad_norm, CLIP_NORM)
    masters = (
        widen_master,
        triple_master,
        mixing_master,
        expand_master,
        shrink_master,
        narrow_master,
        gains_master,
    )
    firsts_old = (
        widen_first,
        triple_first,
        mixing_first,
        expand_first,
        shrink_first,
        narrow_first,
        gains_first,
    )
    seconds_old = (
        widen_second,
        triple_second,
        mixing_second,
        expand_second,
        shrink_second,
        narrow_second,
        gains_second,
    )
    rates = (
        2.0 * D_BYTE ** (-0.5),
        2.0 * D ** (-0.5),
        0.4,
        2.0 * D ** (-0.5),
        2.0 * FF ** (-0.5),
        2.0 * D ** (-0.5),
        0.6,
    )
    decays = (DECAY_RATE, DECAY_RATE, DECAY_RATE, DECAY_RATE, DECAY_RATE, DECAY_RATE, 0.0)
    results = [new_block[None], grad_block[None], grad_norm]
    for index in range(7):
        results.extend(
            adam_update(
                masters[index],
                firsts_old[index],
                seconds_old[index],
                reduced[index],
                factor,
                rates[index],
                decays[index],
            )
        )
    return tuple(results)


def plane_solution(mesh):
    fine = Mesh(mesh.devices.reshape(PLANES, 2, 2, 2), AXES)
    byte_spec = P(("y", "c"), ("z", "x"))
    rows_spec = P(AXES, None)
    gains_spec = P(None, AXES)
    return jax.shard_map(
        per_member,
        mesh=fine,
        in_specs=(byte_spec,) * 4 + (rows_spec,) * 18 + (gains_spec,) * 3,
        out_specs=(byte_spec,) * 2 + (P(),) + (rows_spec,) * 18 + (gains_spec,) * 3,
        check_vma=False,
    )


def solution(mesh):
    if plane_fits(mesh):
        return plane_solution(mesh)
    placed = (
        P("dp", "seq", None),
        P("dp", "seq"),
        P("dp", "seq"),
        P("dp", "seq", None),
        P(("seq", "dp"), None),
        P(("seq", "dp"), None),
        P(("seq", "dp"), None),
        P(("seq", "dp"), None),
        P(("seq", "dp"), None),
        P(("seq", "dp"), None),
        P(("seq", "dp"), None),
        P(("seq", "dp"), None),
        P(("seq", "dp"), None),
        P(("seq", "dp"), None),
        P(("seq", "dp"), None),
        P(("seq", "dp"), None),
        P(("seq", "dp"), None),
        P(("seq", "dp"), None),
        P(("seq", "dp"), None),
        P(("seq", "dp"), None),
        P(("seq", "dp"), None),
        P(("seq", "dp"), None),
        P(None, ("seq", "dp")),
        P(None, ("seq", "dp")),
        P(None, ("seq", "dp")),
    )
    return jax.shard_map(
        per_device,
        mesh=mesh,
        in_specs=placed,
        out_specs=(
            P("dp", "seq", None),
            P("dp", "seq", None),
            P(),
            P(("seq", "dp"), None),
            P(("seq", "dp"), None),
            P(("seq", "dp"), None),
            P(("seq", "dp"), None),
            P(("seq", "dp"), None),
            P(("seq", "dp"), None),
            P(("seq", "dp"), None),
            P(("seq", "dp"), None),
            P(("seq", "dp"), None),
            P(("seq", "dp"), None),
            P(("seq", "dp"), None),
            P(("seq", "dp"), None),
            P(("seq", "dp"), None),
            P(("seq", "dp"), None),
            P(("seq", "dp"), None),
            P(("seq", "dp"), None),
            P(("seq", "dp"), None),
            P(("seq", "dp"), None),
            P(None, ("seq", "dp")),
            P(None, ("seq", "dp")),
            P(None, ("seq", "dp")),
        ),
        check_vma=False,
    )
```

```python
import jax
import jax.numpy as jnp
from jax import lax
from jax.experimental import pallas as pl
from jax.experimental.pallas import tpu as pltpu
from jax.sharding import Mesh, PartitionSpec as P

D_BYTE = 768
D = 1536
HEADS = 24
HEAD_DIM = 64
FF = 6144
STEP = 10


NORM_EPS = 1e-05
SCORE_SCALE = 0.125
MASK_FILL = -1e30
BETA_ONE = 0.9
BETA_TWO = 0.95
ADAM_EPS = 1e-08
DECAY_RATE = 0.1
CLIP_NORM = 1.0


def prefix(part, axis, combine, identity):
    place = lax.axis_index(axis)
    gathered = lax.all_gather(part, axis)
    state = jnp.zeros_like(part) + jnp.asarray(identity, part.dtype)

    def one(hop, state):
        return combine(state, lax.dynamic_index_in_dim(gathered, hop, 0, False))

    return lax.fori_loop(0, place, one, state)


def normalize(values, gain):
    inverse = lax.rsqrt(jnp.mean(values * values, axis=-1, keepdims=True) + NORM_EPS)
    return values * inverse * gain


def add_counts(earlier, later):
    return earlier + later


def block_rows(amount):
    for option in (1024, 768, 512, 384, 256):
        if amount >= option and amount % option == 0:
            return option
    return amount


def spread_positions(first_row, amount, patch_dev, devices):
    whole_rows = first_row + jnp.arange(amount, dtype=jnp.int32)
    return whole_rows % patch_dev * devices + whole_rows // patch_dev


def make_attend(queries, patch_docs, patch_pos, patch_dev, devices):

    def attend(running, shards, offset):
        piece_keys, piece_values, piece_docs = shards
        amount = piece_keys.shape[0]
        span_rows = block_rows(amount)
        number = amount // span_rows
        key_blocks = piece_keys.reshape(number, span_rows, HEADS, HEAD_DIM)
        value_blocks = piece_values.reshape(number, span_rows, HEADS, HEAD_DIM)
        doc_blocks = piece_docs.reshape(number, span_rows)
        firsts = span_rows * jnp.arange(number, dtype=jnp.int32)

        def advance(status, section):
            block_keys, block_values, block_docs, block_first = section
            running_top, running_sum, running_out = status
            scores = (
                jnp.einsum("phd,khd->hpk", queries, block_keys, preferred_element_type=jnp.float32)
                * SCORE_SCALE
            )
            key_pos = spread_positions(block_first, span_rows, patch_dev, devices)
            allowed = (patch_docs[:, None] == block_docs[None, :]) & (
                key_pos[None, :] <= patch_pos[:, None]
            )
            masked = jnp.where(allowed[None], scores, MASK_FILL)
            new_top = jnp.maximum(running_top, jnp.max(masked, axis=-1))
            weights = jnp.where(allowed[None], jnp.exp(masked - new_top[..., None]), 0.0)
            rescale = jnp.exp(running_top - new_top)
            running_sum = running_sum * rescale + jnp.sum(weights, axis=-1)
            running_out = running_out * rescale[..., None] + jnp.einsum(
                "hpk,khd->hpd",
                weights.astype(jnp.bfloat16),
                block_values,
                preferred_element_type=jnp.float32,
            )
            return ((new_top, running_sum, running_out), None)

        running, _ = lax.scan(advance, running, (key_blocks, value_blocks, doc_blocks, firsts))
        return running

    return attend


def outer_sum(left, right):
    return jnp.einsum("pi,pj->ij", left, right, preferred_element_type=jnp.float32)


def back_product(grads, weight):
    return jnp.einsum("pj,ij->pi", grads, weight, preferred_element_type=jnp.float32)


def adam_update(master, first_old, second_old, gradient, clip_factor, learn_rate, weight_decay):
    clipped = gradient * clip_factor
    moment = BETA_ONE * first_old + (1.0 - BETA_ONE) * clipped
    square = BETA_TWO * second_old + (1.0 - BETA_TWO) * clipped * clipped
    corrected = (
        moment / (1.0 - BETA_ONE**STEP) / (jnp.sqrt(square / (1.0 - BETA_TWO**STEP)) + ADAM_EPS)
    )
    weight = master - learn_rate * (corrected + weight_decay * master)
    return (weight, moment, square)


def per_device(
    byte_rows,
    starts,
    doc_ids,
    out_cotangent,
    widen_master,
    widen_first,
    widen_second,
    triple_master,
    triple_first,
    triple_second,
    mixing_master,
    mixing_first,
    mixing_second,
    expand_master,
    expand_first,
    expand_second,
    shrink_master,
    shrink_first,
    shrink_second,
    narrow_master,
    narrow_first,
    narrow_second,
    gains_master,
    gains_first,
    gains_second,
):
    widen_full, triple_full, mixing_full, expand_full, shrink_full, narrow_full, gains_full = (
        lax.all_gather(widen_master.astype(jnp.bfloat16), ("seq", "dp"), axis=0, tiled=True),
        lax.all_gather(triple_master.astype(jnp.bfloat16), ("seq", "dp"), axis=0, tiled=True),
        lax.all_gather(mixing_master.astype(jnp.bfloat16), ("seq", "dp"), axis=0, tiled=True),
        lax.all_gather(expand_master.astype(jnp.bfloat16), ("seq", "dp"), axis=0, tiled=True),
        lax.all_gather(shrink_master.astype(jnp.bfloat16), ("seq", "dp"), axis=0, tiled=True),
        lax.all_gather(narrow_master.astype(jnp.bfloat16), ("seq", "dp"), axis=0, tiled=True),
        lax.all_gather(gains_master.astype(jnp.bfloat16), ("seq", "dp"), axis=1, tiled=True),
    )
    gain_one = gains_full[0].astype(jnp.float32)
    gain_two = gains_full[1].astype(jnp.float32)
    devices = lax.axis_size("seq")
    seq_place = lax.axis_index("seq")
    byte_block = byte_rows[0]
    start_flags = starts[0]
    doc_local = doc_ids[0]
    cotangent_rows = out_cotangent[0]
    byte_width = byte_block.shape[1]
    patch_dev = 3 * byte_block.shape[0] // 16
    capacity = patch_dev + patch_dev // 2
    slot_count = (capacity + devices - 2) // devices + 1
    buffer_rows = devices * slot_count
    amount = jnp.sum(start_flags)
    offset = prefix(amount, "seq", add_counts, jnp.int32(0))
    ranking = jnp.cumsum(start_flags) - start_flags
    patch_index = offset + ranking
    owners = patch_index % devices
    local_row = patch_index // devices
    slot_index = local_row - offset // devices
    target_slot = jnp.where(start_flags == 1, owners * slot_count + slot_index, buffer_rows)
    send_rows = (
        jnp.zeros((buffer_rows, byte_width), jnp.bfloat16)
        .at[target_slot]
        .set(byte_block, mode="drop")
    )
    send_meta = (
        jnp.full((buffer_rows, 2), patch_dev, jnp.int32)
        .at[target_slot]
        .set(jnp.stack([local_row, doc_local], axis=-1), mode="drop")
    )
    send_grad = (
        jnp.zeros((buffer_rows, byte_width), jnp.bfloat16)
        .at[target_slot]
        .set(cotangent_rows, mode="drop")
    )
    arrived_rows, arrived_meta = (
        lax.all_to_all(send_rows, "seq", split_axis=0, concat_axis=0, tiled=True),
        lax.all_to_all(send_meta, "seq", split_axis=0, concat_axis=0, tiled=True),
    )
    target = arrived_meta[:, 0]
    valid_slot = target < patch_dev
    patch_rows = (
        jnp.zeros((patch_dev, byte_width), jnp.bfloat16).at[target].set(arrived_rows, mode="drop")
    )
    patch_docs = jnp.zeros((patch_dev,), jnp.int32).at[target].set(arrived_meta[:, 1], mode="drop")
    patch_pos = seq_place + devices * jnp.arange(patch_dev, dtype=jnp.int32)
    widened = jnp.dot(patch_rows, widen_full, preferred_element_type=jnp.float32)
    model_width = widened.shape[1]
    first_low = normalize(widened, gain_one).astype(jnp.bfloat16)
    projected = jnp.dot(first_low, triple_full, preferred_element_type=jnp.float32).astype(
        jnp.bfloat16
    )
    queries = projected[:, :model_width].reshape(patch_dev, HEADS, HEAD_DIM)
    key_rows = projected[:, model_width : 2 * model_width]
    value_rows = projected[:, 2 * model_width :]
    initial = (
        jnp.full((HEADS, patch_dev), MASK_FILL, jnp.float32),
        jnp.zeros((HEADS, patch_dev), jnp.float32),
        jnp.zeros((HEADS, patch_dev, HEAD_DIM), jnp.float32),
    )
    attend = make_attend(queries, patch_docs, patch_pos, patch_dev, devices)
    running = attend(
        initial,
        (
            lax.all_gather(key_rows, "seq", axis=0, tiled=True),
            lax.all_gather(value_rows, "seq", axis=0, tiled=True),
            lax.all_gather(patch_docs, "seq", axis=0, tiled=True),
        ),
        jnp.int32(0),
    )
    running_top, running_sum, running_out = running
    attended = running_out / running_sum[..., None]
    log_total = running_top + jnp.log(running_sum)
    attended_low = (
        jnp.transpose(attended, (1, 0, 2)).reshape(patch_dev, model_width).astype(jnp.bfloat16)
    )
    resid_one = widened + jnp.dot(attended_low, mixing_full, preferred_element_type=jnp.float32)
    second_low = normalize(resid_one, gain_two).astype(jnp.bfloat16)
    expanded = jnp.dot(second_low, expand_full, preferred_element_type=jnp.float32)
    active_low = jax.nn.gelu(expanded).astype(jnp.bfloat16)
    resid_two = resid_one + jnp.dot(active_low, shrink_full, preferred_element_type=jnp.float32)
    resid_low = resid_two.astype(jnp.bfloat16)
    narrow_low = jnp.dot(resid_low, narrow_full, preferred_element_type=jnp.float32).astype(
        jnp.bfloat16
    )
    returned = jnp.where(valid_slot[:, None], jnp.take(narrow_low, target, axis=0, mode="clip"), 0)
    back_rows = lax.all_to_all(returned, "seq", split_axis=0, concat_axis=0, tiled=True)
    added = jnp.take(back_rows, target_slot, axis=0, mode="clip").astype(jnp.float32)
    new_block = byte_block.astype(jnp.float32) + jnp.where(start_flags[:, None] == 1, added, 0.0)
    arrived_grad = lax.all_to_all(send_grad, "seq", split_axis=0, concat_axis=0, tiled=True)
    narrow_back = (
        jnp.zeros((patch_dev, byte_width), jnp.bfloat16).at[target].set(arrived_grad, mode="drop")
    )
    narrow_grad = outer_sum(resid_low, narrow_back)
    upper_back = back_product(narrow_back, narrow_full)
    shrink_back = upper_back.astype(jnp.bfloat16)
    shrink_grad = outer_sum(active_low, shrink_back)
    active_back = back_product(shrink_back, shrink_full)
    _, gelu_pull = jax.vjp(jax.nn.gelu, expanded)
    expand_back = gelu_pull(active_back)[0].astype(jnp.bfloat16)
    expand_grad = outer_sum(second_low, expand_back)
    second_back = back_product(expand_back, expand_full)
    _, second_pull = jax.vjp(normalize, resid_one, gain_two)
    second_part, second_gain = second_pull(second_back)
    lower_back = upper_back + second_part
    mixed_back = lower_back.astype(jnp.bfloat16)
    mixing_grad = outer_sum(attended_low, mixed_back)
    attend_back = (
        back_product(mixed_back, mixing_full)
        .astype(jnp.bfloat16)
        .reshape(patch_dev, HEADS, HEAD_DIM)
    )
    delta_rows = jnp.einsum("phd,hpd->hp", attend_back.astype(jnp.float32), attended)
    all_keys, all_values, all_docs = (
        lax.all_gather(key_rows, "seq", axis=0, tiled=True),
        lax.all_gather(value_rows, "seq", axis=0, tiled=True),
        lax.all_gather(patch_docs, "seq", axis=0, tiled=True),
    )
    total_keys = all_keys.shape[0]
    span_rows = block_rows(total_keys)
    number = total_keys // span_rows
    key_blocks = all_keys.reshape(number, span_rows, HEADS, HEAD_DIM)
    value_blocks = all_values.reshape(number, span_rows, HEADS, HEAD_DIM)
    doc_blocks = all_docs.reshape(number, span_rows)
    firsts = span_rows * jnp.arange(number, dtype=jnp.int32)
    query_start = jnp.zeros((patch_dev, HEADS, HEAD_DIM), jnp.float32)

    def backstep(query_back, section):
        block_keys, block_values, block_docs, block_first = section
        scores = (
            jnp.einsum("phd,khd->hpk", queries, block_keys, preferred_element_type=jnp.float32)
            * SCORE_SCALE
        )
        key_pos = spread_positions(block_first, span_rows, patch_dev, devices)
        allowed = (patch_docs[:, None] == block_docs[None, :]) & (
            key_pos[None, :] <= patch_pos[:, None]
        )
        probs = jnp.where(allowed[None], jnp.exp(scores - log_total[..., None]), 0.0)
        prob_back = jnp.einsum(
            "phd,khd->hpk", attend_back, block_values, preferred_element_type=jnp.float32
        )
        score_back = (probs * (prob_back - delta_rows[..., None])).astype(jnp.bfloat16)
        query_back = (
            query_back
            + jnp.einsum("hpk,khd->phd", score_back, block_keys, preferred_element_type=jnp.float32)
            * SCORE_SCALE
        )
        keys_part = (
            jnp.einsum("hpk,phd->khd", score_back, queries, preferred_element_type=jnp.float32)
            * SCORE_SCALE
        )
        values_part = jnp.einsum(
            "hpk,phd->khd",
            probs.astype(jnp.bfloat16),
            attend_back,
            preferred_element_type=jnp.float32,
        )
        return (
            query_back,
            (
                keys_part.reshape(span_rows, model_width),
                values_part.reshape(span_rows, model_width),
            ),
        )

    query_back, (keys_back, values_back) = lax.scan(
        backstep, query_start, (key_blocks, value_blocks, doc_blocks, firsts)
    )
    keys_own, values_own = (
        lax.psum_scatter(
            keys_back.reshape(total_keys, model_width).astype(jnp.bfloat16),
            "seq",
            scatter_dimension=0,
            tiled=True,
        ).astype(jnp.float32),
        lax.psum_scatter(
            values_back.reshape(total_keys, model_width).astype(jnp.bfloat16),
            "seq",
            scatter_dimension=0,
            tiled=True,
        ).astype(jnp.float32),
    )
    triple_back = jnp.concatenate(
        [query_back.reshape(patch_dev, model_width), keys_own, values_own], axis=1
    ).astype(jnp.bfloat16)
    triple_grad = outer_sum(first_low, triple_back)
    first_back = back_product(triple_back, triple_full)
    _, first_pull = jax.vjp(normalize, widened, gain_one)
    first_part, first_gain = first_pull(first_back)
    base_low = (lower_back + first_part).astype(jnp.bfloat16)
    widen_grad = outer_sum(patch_rows, base_low)
    patch_back = back_product(base_low, widen_full).astype(jnp.bfloat16)
    grad_slots = jnp.where(
        valid_slot[:, None], jnp.take(patch_back, target, axis=0, mode="clip"), 0
    )
    grad_rows = lax.all_to_all(grad_slots, "seq", split_axis=0, concat_axis=0, tiled=True)
    coming = jnp.take(grad_rows, target_slot, axis=0, mode="clip").astype(jnp.float32)
    grad_block = cotangent_rows.astype(jnp.float32) + jnp.where(
        start_flags[:, None] == 1, coming, 0.0
    )
    gains_grad = jnp.stack([first_gain, second_gain], axis=0)
    reduced = (
        lax.psum_scatter(widen_grad, ("seq", "dp"), scatter_dimension=0, tiled=True),
        lax.psum_scatter(triple_grad, ("seq", "dp"), scatter_dimension=0, tiled=True),
        lax.psum_scatter(mixing_grad, ("seq", "dp"), scatter_dimension=0, tiled=True),
        lax.psum_scatter(expand_grad, ("seq", "dp"), scatter_dimension=0, tiled=True),
        lax.psum_scatter(shrink_grad, ("seq", "dp"), scatter_dimension=0, tiled=True),
        lax.psum_scatter(narrow_grad, ("seq", "dp"), scatter_dimension=0, tiled=True),
        lax.psum_scatter(gains_grad, ("seq", "dp"), scatter_dimension=1, tiled=True),
    )
    local_squares = jnp.float32(0.0)
    for member in reduced:
        local_squares = local_squares + jnp.sum(member * member)
    norm_squared = lax.psum(local_squares, ("seq", "dp"))
    grad_norm = jnp.sqrt(norm_squared)
    factor = CLIP_NORM / jnp.maximum(grad_norm, CLIP_NORM)
    masters = (
        widen_master,
        triple_master,
        mixing_master,
        expand_master,
        shrink_master,
        narrow_master,
        gains_master,
    )
    firsts_old = (
        widen_first,
        triple_first,
        mixing_first,
        expand_first,
        shrink_first,
        narrow_first,
        gains_first,
    )
    seconds_old = (
        widen_second,
        triple_second,
        mixing_second,
        expand_second,
        shrink_second,
        narrow_second,
        gains_second,
    )
    rates = (
        2.0 * D_BYTE ** (-0.5),
        2.0 * D ** (-0.5),
        0.4,
        2.0 * D ** (-0.5),
        2.0 * FF ** (-0.5),
        2.0 * D ** (-0.5),
        0.6,
    )
    decays = (DECAY_RATE, DECAY_RATE, DECAY_RATE, DECAY_RATE, DECAY_RATE, DECAY_RATE, 0.0)
    updates = [
        adam_update(
            masters[index],
            firsts_old[index],
            seconds_old[index],
            reduced[index],
            factor,
            rates[index],
            decays[index],
        )
        for index in range(7)
    ]
    return (
        new_block.astype(jnp.bfloat16)[None],
        grad_block.astype(jnp.bfloat16)[None],
        grad_norm,
        updates[0][0],
        updates[0][1],
        updates[0][2],
        updates[1][0],
        updates[1][1],
        updates[1][2],
        updates[2][0],
        updates[2][1],
        updates[2][2],
        updates[3][0],
        updates[3][1],
        updates[3][2],
        updates[4][0],
        updates[4][1],
        updates[4][2],
        updates[5][0],
        updates[5][1],
        updates[5][2],
        updates[6][0],
        updates[6][1],
        updates[6][2],
    )


PLANES = 4
TEAM = 8
CORE_BIT, Y_BIT, X_BIT = 1, 2, 4
AXES = ("z", "x", "y", "c")
TEAM_AXES = ("x", "y", "c")
LOW = jnp.bfloat16
WIDE = jnp.float32
VMEM_LIMIT = 56 * 1024 * 1024
LOG2_E = 1.4426950408889634
GELU_A = 0.7978845608028654
GELU_B = 0.044715


def plane_fits(mesh):
    return mesh.shape["seq"] == 2 * PLANES and mesh.shape["dp"] == PLANES


def flip(value, bit):
    pairs = [(place, place ^ bit) for place in range(PLANES * TEAM)]
    return lax.ppermute(value, AXES, pairs)


def shift_plane(value, hop):
    pairs = [
        (plane * TEAM + t, (plane + hop) % PLANES * TEAM + t)
        for plane in range(PLANES)
        for t in range(TEAM)
    ]
    return lax.ppermute(value, AXES, pairs)


SEQUENCE_OF_PLANE = (2, 0, 1, 3)


def source_of(plane, t):
    return (plane + t // 2 % 2 + 2 * (t % 2) + 2 * PLANES) % PLANES * 2 + t // 4


def byte_pairs():
    return [
        (source_of(plane, t) * PLANES + SEQUENCE_OF_PLANE[plane], plane * TEAM + t)
        for plane in range(PLANES)
        for t in range(TEAM)
    ]


def to_plane(value):
    return lax.ppermute(value, AXES, byte_pairs())


def from_plane(value):
    return lax.ppermute(value, AXES, [(there, here) for here, there in byte_pairs()])


def team_gather(block, cut=None, before_relay=lambda own: ()):
    cut = block.shape[0] // 2 if cut is None else cut
    from_x = flip(block, X_BIT)
    from_y = flip(block, Y_BIT)
    from_core = flip(block, CORE_BIT)
    from_x, from_y = after((from_x, from_y), *before_relay(from_core))
    to_x, to_y = from_y[:cut], from_x[cut:]
    upper = flip(to_x, X_BIT)
    lower = flip(to_y, Y_BIT)
    y_core = flip(from_y, CORE_BIT)
    x_core = flip(from_x, CORE_BIT)
    return [
        block,
        from_core,
        from_y,
        y_core,
        from_x,
        x_core,
        upper,
        lower,
        flip(upper, CORE_BIT),
        flip(lower, CORE_BIT),
    ], (to_x, to_y)


PIECES = 10


def piece(refs, m):
    if m < 6:
        return refs[m][...]
    return jnp.concatenate([refs[2 * m - 6][...], refs[2 * m - 5][...]], axis=0)


def team_scatter(far_send, far_keep, x_send, x_keep, y_send, y_keep, own_send, own_keep):
    def pair(send, keep):
        return keep.astype(WIDE) + flip(send, CORE_BIT).astype(WIDE)

    far = pair(far_send, far_keep).astype(LOW)
    cut = far.shape[0] // 2
    upper = flip(far[:cut], X_BIT).astype(WIDE)
    lower = flip(far[cut:], Y_BIT).astype(WIDE)
    to_x, to_y = pair(x_send, x_keep), pair(y_send, y_keep)
    to_x = jnp.concatenate([to_x[:cut], to_x[cut:] + lower], axis=0).astype(LOW)
    to_y = jnp.concatenate([to_y[:cut] + upper, to_y[cut:]], axis=0).astype(LOW)
    terms = (own_keep, flip(own_send, CORE_BIT), flip(to_x, X_BIT), flip(to_y, Y_BIT))
    return terms, (to_x, to_y)


def put_terms(outs, m, value):
    outs[7 - m][...] = value.astype(LOW)


def term_shapes(rows, width):
    return (jax.ShapeDtypeStruct((rows, width), LOW),) * TEAM


def add_terms(refs, lanes=slice(None)):
    total = refs[0][:, lanes].astype(WIDE)
    for ref in refs[1:]:
        total = total + ref[:, lanes].astype(WIDE)
    return total


def after(value, *earlier):
    return lax.optimization_barrier((value,) + earlier)[0]


def plane_gather_small(block):
    return [block] + [shift_plane(block, hop) for hop in (1, 2, 3)]


def plane_scatter_small(stack):
    back = lax.all_to_all(stack.astype(LOW), "z", split_axis=0, concat_axis=0, tiled=True)
    return jnp.sum(back.astype(WIDE), axis=0)


def team_exchange(value):
    return lax.all_to_all(value, TEAM_AXES, split_axis=0, concat_axis=0, tiled=True)


def pick(value, place, axis):
    return lax.dynamic_index_in_dim(value, place, axis, False)


def in_vmem():
    return pl.BlockSpec(memory_space=pltpu.VMEM)


def in_smem():
    return pl.BlockSpec(memory_space=pltpu.SMEM)


def params():
    return pltpu.CompilerParams(vmem_limit_bytes=VMEM_LIMIT)


def estimate(microseconds):
    return pl.CostEstimate(
        flops=int(microseconds * 8e+08), bytes_accessed=int(microseconds * 2e+06), transcendentals=0
    )


def nn(left, right):
    return lax.dot_general(left, right, (((1,), (0,)), ((), ())), preferred_element_type=WIDE)


def nt(left, right):
    return lax.dot_general(left, right, (((1,), (1,)), ((), ())), preferred_element_type=WIDE)


def tn(left, right):
    return lax.dot_general(left, right, (((0,), (0,)), ((), ())), preferred_element_type=WIDE)


def slot_matrix(flags, slots):
    amount = flags.shape[1]
    row = lax.broadcasted_iota(jnp.int32, (amount, amount), 0)
    column = lax.broadcasted_iota(jnp.int32, (amount, amount), 1)
    before = jnp.where(row < column, 1.0, 0.0).astype(LOW)
    rank = nn(jnp.broadcast_to(flags, (8, amount)).astype(LOW), before)[:1]
    rank = jnp.where(flags > 0.5, rank, -1.0)
    slot = lax.broadcasted_iota(jnp.int32, (slots, amount), 0).astype(WIDE)
    return jnp.where(slot == rank, 1.0, 0.0).astype(LOW)


def pack_kernel(starts_ref, docs_ref, rows_ref, cotangent_ref, rows_out, chosen_out):
    capacity = chosen_out.shape[0]
    width = rows_out.shape[1]
    flags = starts_ref[...].astype(WIDE)
    chosen = slot_matrix(flags, 384)
    amount = jnp.sum(flags)
    docs = nt(jnp.broadcast_to(docs_ref[...].astype(WIDE), (16, flags.shape[1])).astype(LOW), chosen)
    docs = jnp.concatenate([docs, jnp.zeros((16, width - 384), WIDE)], axis=1)
    row = lax.broadcasted_iota(jnp.int32, (16, width), 0)
    high = jnp.floor(amount * 0.5)
    meta = jnp.where(row == 0, docs, jnp.where(row == 1, high, amount - 2.0 * high))
    chosen = chosen[:capacity]
    chosen_out[...] = chosen
    rows_out[:16] = meta.astype(LOW)
    rows_out[16 : 16 + capacity] = nn(chosen, rows_ref[...]).astype(LOW)
    rows_out[16 + capacity :] = nn(chosen, cotangent_ref[...]).astype(LOW)


def pack(starts, docs, rows, cotangent_rows, capacity):
    amount, width = rows.shape
    return pl.pallas_call(
        pack_kernel,
        out_shape=(
            jax.ShapeDtypeStruct((2 * capacity + 16, width), LOW),
            jax.ShapeDtypeStruct((capacity, amount), LOW),
        ),
        in_specs=[in_vmem()] * 4,
        out_specs=(in_vmem(), in_vmem()),
        compiler_params=params(),
        cost_estimate=estimate(5),
        name="pack",
    )(starts, docs, rows, cotangent_rows)


def unpack_kernel(chosen_ref, rows_ref, cotangent_ref, back_ref, rows_out, cotangent_out):
    width = rows_ref.shape[1]
    added = tn(chosen_ref[...], back_ref[...])
    rows_out[...] = (rows_ref[...].astype(WIDE) + added[:, :width]).astype(LOW)
    cotangent_out[...] = (cotangent_ref[...].astype(WIDE) + added[:, width:]).astype(LOW)


def unpack(chosen, rows, cotangent_rows, back):
    return pl.pallas_call(
        unpack_kernel,
        out_shape=(jax.ShapeDtypeStruct(rows.shape, LOW),) * 2,
        in_specs=[in_vmem()] * 4,
        out_specs=(in_vmem(),) * 2,
        compiler_params=params(),
        cost_estimate=estimate(5),
        name="unpack",
    )(chosen, rows, cotangent_rows, back)


def window_matrix(first, amount, capacity):
    target = lax.broadcasted_iota(jnp.int32, (capacity + 16, capacity), 0)
    source = lax.broadcasted_iota(jnp.int32, (capacity + 16, capacity), 1)
    moved = (target == source + first % 16) & (source < amount)
    return jnp.where(moved, 1.0, 0.0).astype(LOW)


def widen_kernel(place_ref, *refs):
    pieces = refs[:PIECES]
    widen_out, gains_out, narrow_out = refs[PIECES : PIECES + 3]
    widen_wide, gains = refs[PIECES + 3 :]
    plane, t = place_ref[0], place_ref[1]
    shards = PLANES * TEAM
    shard = widen_out.shape[0] // shards
    model = widen_out.shape[1]
    width = model // 2
    gain_shard = model // shards
    for m in range(TEAM):
        low = piece(pieces, m)
        here = low.astype(WIDE)
        for hop in range(PLANES):
            place = (plane - hop + PLANES) % PLANES * TEAM + (t ^ m)
            at = pl.ds(pl.multiple_of(place * shard, 8), shard)
            base = hop * (64 + gain_shard)
            narrow_at = pl.ds(pl.multiple_of(place * gain_shard, 16), gain_shard)
            narrow_out[narrow_at] = low[base + 64 : base + 64 + gain_shard]
            widen_wide[at, :width] = here[base : base + shard]
            widen_wide[at, width:] = here[base + 32 : base + 32 + shard]
            gains[0, pl.ds(place, 1)] = here[base + shard : base + shard + 1, :128]
            gains[1, pl.ds(place, 1)] = here[base + shard + 1 : base + shard + 2, :128]
    widen_out[...] = widen_wide[...].astype(LOW)
    column = lax.broadcasted_iota(jnp.int32, (shards, model), 1)
    owner = lax.broadcasted_iota(jnp.int32, (shards, model), 0)
    owned = (column >= owner * gain_shard) & (column < (owner + 1) * gain_shard)
    inside = jnp.sum(jnp.where(owned, column - owner * gain_shard, 0).astype(WIDE), axis=0, keepdims=True)
    row = lax.broadcasted_iota(jnp.int32, (128, model), 0).astype(WIDE)
    owned = jnp.where(owned, 1.0, 0.0).astype(LOW)
    for k in range(2):
        spread = tn(gains[k].astype(LOW), owned)
        line = jnp.sum(jnp.where(row == inside, spread, 0.0), axis=0, keepdims=True)
        gains_out[k * 8 : k * 8 + 8] = jnp.broadcast_to(line, (8, model))


def widen_whole(place, pieces, shard, model):
    return pl.pallas_call(
        widen_kernel,
        out_shape=(
            jax.ShapeDtypeStruct((shard * PLANES * TEAM, model), LOW),
            jax.ShapeDtypeStruct((16, model), WIDE),
            jax.ShapeDtypeStruct((model, pieces[0].shape[1]), LOW),
        ),
        in_specs=[in_smem()] + [in_vmem()] * PIECES,
        out_specs=(in_vmem(),) * 3,
        scratch_shapes=[
            pltpu.VMEM((shard * PLANES * TEAM, model), WIDE),
            pltpu.VMEM((2, PLANES * TEAM, 128), WIDE),
        ],
        compiler_params=params(),
        cost_estimate=estimate(5),
        name="widen_whole",
    )(place, *pieces)


def enter_kernel(capacity, place_ref, gains_ref, widen_ref, *refs):
    pieces = refs[:PIECES]
    low_out, own_wide, own_rows, doc_column, doc_row, spans = refs[PIECES : PIECES + 6]
    rows, docs = refs[PIECES + 6 :]
    plane, t = place_ref[0], place_ref[1]
    member_rows = own_rows.shape[0]
    total = low_out.shape[0]

    metas = [pieces[m][:16] for m in range(6)] + [pieces[6][:16], pieces[8][:16]]
    blocks = [piece(pieces, m)[16 : 16 + capacity] for m in range(TEAM)]
    amounts, sources = [], []
    for m in range(TEAM):
        meta = metas[m].astype(WIDE)
        row = lax.broadcasted_iota(jnp.int32, meta.shape, 0)
        lane = lax.broadcasted_iota(jnp.int32, meta.shape, 1)
        picked = jnp.where(lane == 0, jnp.where(row == 1, 2.0 * meta, jnp.where(row == 2, meta, 0.0)), 0.0)
        amounts.append(jnp.sum(picked).astype(jnp.int32))
        sources.append(source_of(plane, t ^ m))
    firsts = []
    for m in range(TEAM):
        first = jnp.int32(0)
        for other in range(TEAM):
            if other != m:
                first = first + jnp.where(sources[other] < sources[m], amounts[other], 0)
        firsts.append(first)
        spans[m] = first
        spans[TEAM + m] = amounts[m]

    rows[...] = jnp.zeros_like(rows)
    docs[...] = jnp.zeros_like(docs)
    for m in range(TEAM):
        moving = window_matrix(firsts[m], amounts[m], capacity)
        at = pl.ds(pl.multiple_of(firsts[m] // 16 * 16, 16), capacity + 16)
        rows[at] = rows[at] + nn(moving, blocks[m]).astype(LOW)
        names = metas[m][:1, :384]
        names = jnp.broadcast_to(names, (128, 384))[:, :capacity]
        docs[at] = docs[at] + nt(moving, names)

    doc_column[...] = docs[:total]
    select = jnp.where(lax.broadcasted_iota(jnp.int32, (8, 128), 1) == 0, 1.0, 0.0).astype(LOW)
    doc_row[...] = nt(select, docs[:total].astype(LOW))
    own_rows[...] = rows[pl.ds(pl.multiple_of(t * member_rows, 16), member_rows)]

    def one(k, carry):
        at = pl.ds(pl.multiple_of(k * 2 * member_rows, 16), 2 * member_rows)
        wide = nn(rows[at], widen_ref[...])
        inverse = lax.rsqrt(jnp.mean(wide * wide, axis=-1, keepdims=True) + NORM_EPS)
        low_out[at] = (wide * inverse * gains_ref[:1]).astype(LOW)
        return carry

    lax.fori_loop(0, TEAM // 2, one, 0)
    own_wide[...] = nn(own_rows[...], widen_ref[...])


def enter(place, gains, widen_full, pieces, capacity, member_rows):
    width, model = widen_full.shape
    total = member_rows * TEAM
    padded = total + capacity + 16
    return pl.pallas_call(
        lambda *refs: enter_kernel(capacity, *refs),
        out_shape=(
            jax.ShapeDtypeStruct((total, model), LOW),
            jax.ShapeDtypeStruct((member_rows, model), WIDE),
            jax.ShapeDtypeStruct((member_rows, width), LOW),
            jax.ShapeDtypeStruct((total, 128), WIDE),
            jax.ShapeDtypeStruct((8, total), WIDE),
            jax.ShapeDtypeStruct((2 * TEAM,), jnp.int32),
        ),
        in_specs=[in_smem(), in_vmem(), in_vmem()] + [in_vmem()] * PIECES,
        out_specs=(in_vmem(),) * 5 + (in_smem(),),
        scratch_shapes=[
            pltpu.VMEM((padded, width), LOW),
            pltpu.VMEM((padded, 128), WIDE),
        ],
        compiler_params=params(),
        cost_estimate=estimate(14),
        name="enter",
    )(place, gains, widen_full, *pieces)


def cotangent_kernel(capacity, place_ref, spans_ref, narrow_ref, *refs):
    pieces = refs[:PIECES]
    low_out, own_wide, all_rows = refs[PIECES : PIECES + 3]
    (rows,) = refs[PIECES + 3 :]
    t = place_ref[1]
    member_rows = own_wide.shape[0]
    rows[...] = jnp.zeros_like(rows)
    for m in range(TEAM):
        first = spans_ref[m]
        moving = window_matrix(first, spans_ref[TEAM + m], capacity)
        at = pl.ds(pl.multiple_of(first // 16 * 16, 16), capacity + 16)
        rows[at] = rows[at] + nn(moving, piece(pieces, m)[16 + capacity :]).astype(LOW)
    all_rows[...] = rows[: all_rows.shape[0]]

    def one(k, carry):
        first = pl.multiple_of((t ^ (2 * k)) * member_rows, 16)
        second = pl.multiple_of((t ^ (2 * k + 1)) * member_rows, 16)
        here = jnp.concatenate(
            [rows[pl.ds(first, member_rows)], rows[pl.ds(second, member_rows)]], axis=0
        )
        at = pl.ds(pl.multiple_of(k * 2 * member_rows, 16), 2 * member_rows)
        low_out[at] = nt(here, narrow_ref[...]).astype(LOW)
        return carry

    lax.fori_loop(0, TEAM // 2, one, 0)
    own_wide[...] = nt(
        rows[pl.ds(pl.multiple_of(t * member_rows, 16), member_rows)], narrow_ref[...]
    )


def cotangent(place, spans, narrow_full, pieces, capacity, member_rows):
    model, width = narrow_full.shape
    total = member_rows * TEAM
    return pl.pallas_call(
        lambda *refs: cotangent_kernel(capacity, *refs),
        out_shape=(
            jax.ShapeDtypeStruct((total, model), LOW),
            jax.ShapeDtypeStruct((member_rows, model), WIDE),
            jax.ShapeDtypeStruct((total, width), LOW),
        ),
        in_specs=[in_smem(), in_smem()] + [in_vmem()] * (1 + PIECES),
        out_specs=(in_vmem(),) * 3,
        scratch_shapes=[pltpu.VMEM((total + capacity + 16, width), LOW)],
        compiler_params=params(),
        cost_estimate=estimate(13),
        name="cotangent",
    )(place, spans, narrow_full, *pieces)


def leave_kernel(place_ref, spans_ref, *refs):
    pieces, out_ref, total = refs[:PIECES], refs[PIECES], refs[PIECES + 1]
    t = place_ref[1]
    first = spans_ref[0]
    capacity = out_ref.shape[0]
    total[...] = jnp.zeros_like(total)
    for m in range(TEAM):
        rows = pieces[0].shape[0]
        offset = (t ^ m) * rows - first

        @pl.when((offset < capacity) & (offset + rows > 0))
        def _(m=m, offset=offset, rows=rows):
            target = lax.broadcasted_iota(jnp.int32, (capacity, rows), 0)
            source = lax.broadcasted_iota(jnp.int32, (capacity, rows), 1) + offset
            total[...] += nn(jnp.where(target == source, 1.0, 0.0).astype(LOW), piece(pieces, m))

    out_ref[...] = total[...].astype(LOW)


def leave(place, spans, pieces, capacity):
    width = pieces[0].shape[1]
    return pl.pallas_call(
        leave_kernel,
        out_shape=jax.ShapeDtypeStruct((capacity, width), LOW),
        in_specs=[in_smem(), in_smem()] + [in_vmem()] * PIECES,
        out_specs=in_vmem(),
        scratch_shapes=[pltpu.VMEM((capacity, width), WIDE)],
        compiler_params=params(),
        cost_estimate=estimate(2),
        name="leave",
    )(place, spans, *pieces)


def norm_kernel(wide_ref, gains_ref, *refs):
    resid_out, low_out = refs[4:]
    resid = wide_ref[...] + add_terms(refs[:4])
    resid_out[...] = resid
    inverse = lax.rsqrt(jnp.mean(resid * resid, axis=-1, keepdims=True) + NORM_EPS)
    low_out[...] = (resid * inverse * gains_ref[8:9]).astype(LOW)


def add_and_norm(wide, gains, terms):
    return pl.pallas_call(
        norm_kernel,
        out_shape=(
            jax.ShapeDtypeStruct(wide.shape, WIDE),
            jax.ShapeDtypeStruct(wide.shape, LOW),
        ),
        in_specs=[in_vmem()] * 6,
        out_specs=(in_vmem(),) * 2,
        compiler_params=params(),
        cost_estimate=estimate(2),
        name="add_and_norm",
    )(wide, gains, *terms)


def norm_back(resid, gain, incoming):
    inverse = lax.rsqrt(jnp.mean(resid * resid, axis=-1, keepdims=True) + NORM_EPS)
    scaled = incoming * gain
    along = jnp.mean(scaled * resid, axis=-1, keepdims=True)
    back = inverse * scaled - resid * (inverse * inverse * inverse * along)
    return back, jnp.sum(incoming * resid * inverse, axis=0, keepdims=True)


def second_back_kernel(resid_ref, gains_ref, upper_ref, *refs):
    lower_out, low_out, gain_out = refs[4:]
    back, gain_back = norm_back(
        resid_ref[...], gains_ref[8:9], add_terms(refs[:4], slice(resid_ref.shape[1]))
    )
    lower = upper_ref[...] + back
    lower_out[...] = lower
    low_out[...] = lower.astype(LOW)
    gain_out[...] = jnp.broadcast_to(gain_back, gain_out.shape)


def second_norm_back(resid, gains, upper, terms):
    rows, model = resid.shape
    return pl.pallas_call(
        second_back_kernel,
        out_shape=(
            jax.ShapeDtypeStruct((rows, model), WIDE),
            jax.ShapeDtypeStruct((rows, model), LOW),
            jax.ShapeDtypeStruct((8, model), WIDE),
        ),
        in_specs=[in_vmem()] * 7,
        out_specs=(in_vmem(),) * 3,
        compiler_params=params(),
        cost_estimate=estimate(2),
        name="second_norm_back",
    )(resid, gains, upper, *terms)


def first_back_kernel(
    place_ref, wide_ref, gains_ref, lower_ref, rows_ref, widen_ref, second_gain_ref, narrow_ref, *refs
):
    patch_out = refs[4]
    outs = refs[5:13]
    grad = refs[13]
    t = place_ref[1]
    back, first_gain = norm_back(wide_ref[...], gains_ref[:1], add_terms(refs[:4]))
    low = (lower_ref[...] + back).astype(LOW)
    grad[...] = tn(rows_ref[...], low)
    shard = grad.shape[0] // (PLANES * TEAM)
    row = lax.broadcasted_iota(jnp.int32, (16, grad.shape[1]), 0)
    gain_rows = jnp.where(row == 0, first_gain, jnp.where(row == 1, second_gain_ref[:1], 0.0))
    for m in (7, 6, 5, 3, 4, 2, 1, 0):
        parts = [
            grad[pl.ds(pl.multiple_of((plane * TEAM + (t ^ m)) * shard, 8), shard)]
            for plane in range(PLANES)
        ]
        put_terms(outs, m, jnp.concatenate(parts + [gain_rows], axis=0))
    width = narrow_ref.shape[1]
    patch_out[:, :width] = narrow_ref[...]
    patch_out[:, width:] = nt(low, widen_ref[...]).astype(LOW)


def first_norm_back(place, wide, gains, lower, rows, widen_full, second_gain, narrow_low, terms):
    model = wide.shape[1]
    width = widen_full.shape[0]
    return pl.pallas_call(
        first_back_kernel,
        out_shape=(jax.ShapeDtypeStruct((rows.shape[0], 2 * width), LOW),)
        + term_shapes(width // TEAM + 16, model),
        in_specs=[in_smem()] + [in_vmem()] * 11,
        out_specs=(in_vmem(),) * 9,
        scratch_shapes=[pltpu.VMEM((width, model), WIDE)],
        compiler_params=params(),
        cost_estimate=estimate(5),
        name="first_norm_back",
    )(place, wide, gains, lower, rows, widen_full, second_gain, narrow_low, *terms)


def exit_kernel(resid_ref, narrow_ref, *refs):
    low_out, narrow_out = refs[4:]
    model = resid_ref.shape[1]
    wide = resid_ref[...] + add_terms(refs[:4], slice(model, 2 * model))
    low = wide.astype(LOW)
    shard = low_out.shape[2] // PLANES
    for m in range(TEAM):
        parts = [
            wide[:, (plane * TEAM + m) * shard : (plane * TEAM + m + 1) * shard]
            for plane in range(PLANES)
        ]
        low_out[m] = jnp.concatenate(parts, axis=1).astype(LOW)
    narrow_out[...] = nn(low, narrow_ref[...]).astype(LOW)


def exit_block(resid, narrow_full, terms):
    rows, model = resid.shape
    return pl.pallas_call(
        exit_kernel,
        out_shape=(
            jax.ShapeDtypeStruct((TEAM, rows, model // TEAM), LOW),
            jax.ShapeDtypeStruct((rows, narrow_full.shape[1]), LOW),
        ),
        in_specs=[in_vmem()] * 6,
        out_specs=(in_vmem(),) * 2,
        compiler_params=params(),
        cost_estimate=estimate(4),
        name="exit_block",
    )(resid, narrow_full, *terms)


def forward_terms_kernel(left_ref, right_ref, *outs):
    rows = left_ref.shape[0] // TEAM
    for k in (3, 2, 1, 0):
        product = nn(left_ref[2 * k * rows : (2 * k + 2) * rows], right_ref[...])
        put_terms(outs, 2 * k + 1, product[rows:])
        put_terms(outs, 2 * k, product[:rows])


def forward_terms(left, right):
    return pl.pallas_call(
        forward_terms_kernel,
        out_shape=term_shapes(left.shape[0] // TEAM, right.shape[1]),
        in_specs=[in_vmem()] * 2,
        out_specs=(in_vmem(),) * 8,
        compiler_params=params(),
        cost_estimate=estimate(6),
        name="forward_terms",
    )(left, right)


def feed_kernel(expand_ref, shrink_ref, back_ref, *refs):
    pieces = refs[:PIECES]
    second_out, active_out, expand_out = refs[PIECES : PIECES + 3]
    outs = refs[PIECES + 3 :]
    rows = back_ref.shape[0] // TEAM
    for k in (3, 2, 1, 0):
        at = slice(2 * k * rows, (2 * k + 2) * rows)
        low = jnp.concatenate([piece(pieces, 2 * k), piece(pieces, 2 * k + 1)], axis=0)
        second_out[at] = low
        value = nn(low, expand_ref[...])
        square = value * value
        bend = jnp.tanh(GELU_A * (value + GELU_B * square * value))
        active_out[at] = (0.5 * value * (1.0 + bend)).astype(LOW)
        slope = 0.5 * (1.0 + bend) + 0.5 * value * (1.0 - bend * bend) * (
            GELU_A * (1.0 + 3.0 * GELU_B * square)
        )
        back = (slope * nt(back_ref[at], shrink_ref[...])).astype(LOW)
        expand_out[at] = back
        product = jnp.concatenate(
            [nt(back, expand_ref[...]).astype(LOW), nn(active_out[at], shrink_ref[...]).astype(LOW)],
            axis=1,
        )
        put_terms(outs, 2 * k + 1, product[rows:])
        put_terms(outs, 2 * k, product[:rows])


def feed(expand_own, shrink_own, shrink_back, pieces):
    total, model = shrink_back.shape
    hidden = expand_own.shape[1]
    return pl.pallas_call(
        feed_kernel,
        out_shape=(
            jax.ShapeDtypeStruct((total, model), LOW),
            jax.ShapeDtypeStruct((total, hidden), LOW),
            jax.ShapeDtypeStruct((total, hidden), LOW),
        )
        + term_shapes(total // TEAM, 2 * model),
        in_specs=[in_vmem()] * (3 + PIECES),
        out_specs=(in_vmem(),) * 11,
        compiler_params=params(),
        cost_estimate=estimate(18),
        name="feed",
    )(expand_own, shrink_own, shrink_back, *pieces)


def attend_kernel(
    own,
    tile,
    place_ref,
    first_ref,
    triple_ref,
    doc_column,
    doc_row,
    projected_ref,
    flat_out,
    low_out,
    total_out,
    queries,
    keys,
    values,
    attended,
):
    t = place_ref[1]
    rows = first_ref.shape[0]
    member_rows = rows // TEAM
    width = own * HEAD_DIM

    def project(k, carry):
        at = pl.ds(pl.multiple_of(k * 2 * member_rows, 16), 2 * member_rows)
        projected_ref[at] = nn(first_ref[at], triple_ref[...]).astype(LOW)
        return carry

    lax.fori_loop(0, TEAM // 2, project, 0)
    for h in range(own):
        lanes = slice(h * HEAD_DIM, (h + 1) * HEAD_DIM)
        queries[h] = projected_ref[:, :width][:, lanes]
        keys[h] = projected_ref[:, width : 2 * width][:, lanes]
        values[h] = jnp.transpose(
            projected_ref[:, 2 * width :][:, lanes].astype(WIDE)
        ).astype(LOW)
    total_out[...] = jnp.zeros_like(total_out)
    scale = SCORE_SCALE * LOG2_E
    causal = lax.broadcasted_iota(jnp.int32, (tile, tile), 0) <= lax.broadcasted_iota(
        jnp.int32, (tile, tile), 1
    )

    def one_query(j, carry):
        at_query = pl.ds(pl.multiple_of(j * tile, tile), tile)
        query_docs = doc_row[:1, at_query]

        def one_key(i, status, diagonal):
            at_key = pl.ds(pl.multiple_of(i * tile, tile), tile)
            allowed = doc_column[at_key, :1] == query_docs
            if diagonal:
                allowed = allowed & causal
            result = []
            for h in range(own):
                scores = nt(keys[h, at_key], queries[h, at_query]) * scale
                masked = jnp.where(allowed, scores, MASK_FILL)
                best = jnp.max(masked, axis=0, keepdims=True)
                if diagonal:
                    top = best
                    weights = jnp.exp2(masked - top)
                    summed = jnp.sum(weights, axis=0, keepdims=True)
                    out = nn(values[h, :, at_key], weights.astype(LOW))
                else:
                    old_top, old_sum, old_out = status[h]
                    top = jnp.maximum(old_top, best)
                    weights = jnp.exp2(masked - top)
                    rescale = jnp.exp2(old_top - top)
                    summed = old_sum * rescale + jnp.sum(weights, axis=0, keepdims=True)
                    out = old_out * rescale + nn(values[h, :, at_key], weights.astype(LOW))
                result.append((top, summed, out))
            return tuple(result)

        status = one_key(j, None, True)
        status = lax.fori_loop(0, j, lambda i, now: one_key(i, now, False), status)
        for h in range(own):
            top, summed, out = status[h]
            done = out / summed
            flat_out[h * HEAD_DIM : (h + 1) * HEAD_DIM, at_query] = done
            total_out[h : h + 1, at_query] = top + jnp.log2(summed)
        return carry

    lax.fori_loop(0, rows // tile, one_query, 0)
    attended[...] = jnp.transpose(flat_out[...]).astype(LOW)
    for k in (3, 2, 1, 0):
        pair = jnp.concatenate(
            [
                attended[pl.ds(pl.multiple_of((t ^ m) * member_rows, 16), member_rows)]
                for m in (2 * k, 2 * k + 1)
            ],
            axis=0,
        )
        low_out[2 * k * member_rows : (2 * k + 2) * member_rows] = pair


def attend_team(place, first_low, triple_own, doc_column, doc_row, own):
    rows, model = first_low.shape
    width = own * HEAD_DIM
    tile = rows // 2
    return pl.pallas_call(
        lambda *refs: attend_kernel(own, tile, *refs),
        out_shape=(
            jax.ShapeDtypeStruct((rows, 3 * width), LOW),
            jax.ShapeDtypeStruct((width, rows), WIDE),
            jax.ShapeDtypeStruct((rows, width), LOW),
            jax.ShapeDtypeStruct((8, rows), WIDE),
        ),
        in_specs=[in_smem()] + [in_vmem()] * 4,
        out_specs=(in_vmem(),) * 4,
        scratch_shapes=[
            pltpu.VMEM((own, rows, HEAD_DIM), LOW),
            pltpu.VMEM((own, rows, HEAD_DIM), LOW),
            pltpu.VMEM((own, HEAD_DIM, rows), LOW),
            pltpu.VMEM((rows, width), LOW),
        ],
        compiler_params=params(),
        cost_estimate=estimate(20),
        name="attend",
    )(place, first_low, triple_own, doc_column, doc_row)


def attend_back_setup(own, projected_ref, flat_ref, back_ref, scratch):
    queries, keys, values, backs, keys_flat, backs_flat, deltas = scratch
    width = own * HEAD_DIM
    for h in range(own):
        lanes = slice(h * HEAD_DIM, (h + 1) * HEAD_DIM)
        key = projected_ref[:, width : 2 * width][:, lanes]
        back = back_ref[:, lanes]
        back_flat = jnp.transpose(back.astype(WIDE))
        queries[h] = projected_ref[:, :width][:, lanes]
        keys[h] = key
        values[h] = projected_ref[:, 2 * width :][:, lanes]
        backs[h] = back
        keys_flat[h] = jnp.transpose(key.astype(WIDE)).astype(LOW)
        backs_flat[h] = back_flat.astype(LOW)
        deltas[h : h + 1] = jnp.sum(back_flat * flat_ref[lanes], axis=0, keepdims=True)


def attend_back_tile(own, tile, i, total_ref, doc_column, doc_row, scratch, query_back):
    queries, keys, values, backs, keys_flat, backs_flat, deltas = scratch
    rows = queries.shape[1]
    scale = SCORE_SCALE * LOG2_E
    causal = lax.broadcasted_iota(jnp.int32, (tile, tile), 0) <= lax.broadcasted_iota(
        jnp.int32, (tile, tile), 1
    )
    at_key = slice(i * tile, (i + 1) * tile)
    status = [None] * own
    for j in range(i, rows // tile):
        at_query = slice(j * tile, (j + 1) * tile)
        allowed = doc_column[at_key, :1] == doc_row[:1, at_query]
        if i == j:
            allowed = allowed & causal
        for h in range(own):
            scores = nt(keys[h, at_key], queries[h, at_query]) * scale
            probs = jnp.where(allowed, jnp.exp2(scores - total_ref[h : h + 1, at_query]), 0.0)
            prob_back = nn(values[h, at_key], backs_flat[h, :, at_query])
            score_back = (probs * (prob_back - deltas[h : h + 1, at_query])).astype(LOW)
            value_part = nn(probs.astype(LOW), backs[h, at_query])
            key_part = nn(score_back, queries[h, at_query])
            query_part = nn(keys_flat[h, :, at_key], score_back)
            if i == 0:
                query_back[h, :, at_query] = query_part
            else:
                query_back[h, :, at_query] += query_part
            if status[h] is None:
                status[h] = (key_part, value_part)
            else:
                status[h] = (status[h][0] + key_part, status[h][1] + value_part)
    return jnp.concatenate(
        [status[h][0] * SCORE_SCALE for h in range(own)] + [status[h][1] for h in range(own)],
        axis=1,
    ).astype(LOW)


def attend_back_first_kernel(
    own,
    tile,
    place_ref,
    projected_ref,
    flat_ref,
    total_ref,
    doc_column,
    doc_row,
    back_ref,
    tile_out,
    query_back,
    *scratch,
):
    attend_back_setup(own, projected_ref, flat_ref, back_ref, scratch)
    for i in range(tile_out.shape[0] // tile):
        tile_out[i * tile : (i + 1) * tile] = attend_back_tile(
            own, tile, i, total_ref, doc_column, doc_row, scratch, query_back
        )


def attend_back_rest_kernel(
    own,
    tile,
    place_ref,
    projected_ref,
    flat_ref,
    total_ref,
    doc_column,
    doc_row,
    back_ref,
    tile_ref,
    earlier_ref,
    triple_ref,
    out_ref,
    *refs,
):
    outs, query_back, scratch = refs[:8], refs[8], refs[9:]
    t = place_ref[1]
    rows = projected_ref.shape[0]
    member_rows = rows // TEAM
    width = own * HEAD_DIM
    attend_back_setup(own, projected_ref, flat_ref, back_ref, scratch)
    query_back[...] = earlier_ref[...]
    done = tile_ref.shape[0]
    out_ref[:done, width:] = tile_ref[...]
    for i in range(done // tile, rows // tile):
        out_ref[i * tile : (i + 1) * tile, width:] = attend_back_tile(
            own, tile, i, total_ref, doc_column, doc_row, scratch, query_back
        )
    flat = jnp.concatenate([query_back[h] for h in range(own)], axis=0) * SCORE_SCALE
    out_ref[:, :width] = jnp.transpose(flat).astype(LOW)
    for k in (3, 2, 1, 0):
        pair = jnp.concatenate(
            [
                out_ref[pl.ds(pl.multiple_of((t ^ m) * member_rows, 16), member_rows)]
                for m in (2 * k, 2 * k + 1)
            ],
            axis=0,
        )
        product = nt(pair, triple_ref[...])
        put_terms(outs, 2 * k + 1, product[member_rows:])
        put_terms(outs, 2 * k, product[:member_rows])


def attend_back_scratch(own, rows):
    tall = pltpu.VMEM((own, rows, HEAD_DIM), LOW)
    long = pltpu.VMEM((own, HEAD_DIM, rows), LOW)
    return [tall, tall, tall, tall, long, long, pltpu.VMEM((8, rows), WIDE)]


def attend_back_first(place, projected, flat, totals, doc_column, doc_row, back, own):
    rows = projected.shape[0]
    tile = rows // 3
    return pl.pallas_call(
        lambda *refs: attend_back_first_kernel(own, tile, *refs),
        out_shape=(
            jax.ShapeDtypeStruct((2 * tile, 2 * own * HEAD_DIM), LOW),
            jax.ShapeDtypeStruct((own, HEAD_DIM, rows), WIDE),
        ),
        in_specs=[in_smem()] + [in_vmem()] * 6,
        out_specs=(in_vmem(),) * 2,
        scratch_shapes=attend_back_scratch(own, rows),
        compiler_params=params(),
        cost_estimate=estimate(12),
        name="attend_back_first",
    )(place, projected, flat, totals, doc_column, doc_row, back)


def attend_back_rest(
    place, projected, flat, totals, doc_column, doc_row, back, first_tile, query_back, triple_own, own
):
    rows = projected.shape[0]
    tile = rows // 3
    return pl.pallas_call(
        lambda *refs: attend_back_rest_kernel(own, tile, *refs),
        out_shape=(jax.ShapeDtypeStruct(projected.shape, LOW),)
        + term_shapes(rows // TEAM, triple_own.shape[0]),
        in_specs=[in_smem()] + [in_vmem()] * 9,
        out_specs=(in_vmem(),) * 9,
        scratch_shapes=[pltpu.VMEM((own, HEAD_DIM, rows), WIDE)] + attend_back_scratch(own, rows),
        compiler_params=params(),
        cost_estimate=estimate(18),
        name="attend_back_rest",
    )(
        place,
        projected,
        flat,
        totals,
        doc_column,
        doc_row,
        back,
        first_tile,
        query_back,
        triple_own,
    )


def mixing_send_kernel(place_ref, *refs):
    stack_ref, out_ref = refs
    out_ref[...] = jnp.zeros_like(out_ref)
    x = place_ref[1] // 4
    for source in range(PLANES):
        out_ref[2 * source + x] = stack_ref[source]


def mixing_exchange(place, stack, core):
    rows, width = stack.shape[1:]
    sent = pl.pallas_call(
        mixing_send_kernel,
        out_shape=jax.ShapeDtypeStruct((TEAM, rows, width), LOW),
        in_specs=[in_smem(), in_vmem()],
        out_specs=in_vmem(),
        compiler_params=params(),
        cost_estimate=estimate(2),
        name="mixing_send",
    )(place, stack)
    return lax.dynamic_slice_in_dim(
        team_exchange(sent), core * PLANES, PLANES, 0
    ).reshape(PLANES * rows, width)


def mixing_return(sent, x):
    back = team_exchange(sent)
    return pick(back.reshape((PLANES, 2) + back.shape[1:]), x, 1)


def mix_back_kernel(place_ref, mixing_ref, attended_ref, *refs):
    pieces = refs[:PIECES]
    back_ref, mixing_out, mixed = refs[PIECES:]
    t = place_ref[1]
    member_rows = back_ref.shape[0] // TEAM
    for k in range(TEAM // 2):
        pair = jnp.concatenate([piece(pieces, 2 * k), piece(pieces, 2 * k + 1)], axis=0)
        mixed[2 * k * member_rows : (2 * k + 2) * member_rows] = pair
        back = nt(pair, mixing_ref[...]).astype(LOW)
        for m in (2 * k, 2 * k + 1):
            at = pl.ds(pl.multiple_of((t ^ m) * member_rows, 16), member_rows)
            back_ref[at] = back[(m - 2 * k) * member_rows : (m - 2 * k + 1) * member_rows]
    gradient = tn(attended_ref[...], mixed[...]).astype(LOW)
    mixing_out[...] = jnp.zeros_like(mixing_out)
    rows = gradient.shape[0] // PLANES
    for k in range(PLANES):
        mixing_out[t % 2 * PLANES + k] = gradient[k * rows : (k + 1) * rows]


def mix_back(place, mixing_own, attended, pieces):
    rows, width = attended.shape
    model = mixing_own.shape[1]
    return pl.pallas_call(
        mix_back_kernel,
        out_shape=(
            jax.ShapeDtypeStruct((rows, width), LOW),
            jax.ShapeDtypeStruct((TEAM, width // PLANES, model), LOW),
        ),
        in_specs=[in_smem()] + [in_vmem()] * (2 + PIECES),
        out_specs=(in_vmem(),) * 2,
        scratch_shapes=[pltpu.VMEM((rows, model), LOW)],
        compiler_params=params(),
        cost_estimate=estimate(5),
        name="mix_back",
    )(place, mixing_own, attended, *pieces)


def columns_kernel_of(piece_width, in_ref, out_ref, square_ref):
    total = jnp.zeros((1, 1), WIDE)
    for group in range(in_ref.shape[2] // piece_width):
        for pair in range(TEAM // 2):
            lanes = slice(group * piece_width, (group + 1) * piece_width)
            value = jnp.concatenate(
                [in_ref[2 * pair][:, lanes].astype(WIDE), in_ref[2 * pair + 1][:, lanes].astype(WIDE)],
                axis=1,
            )
            first = (group * TEAM + 2 * pair) * piece_width
            out_ref[:, first : first + 2 * piece_width] = value
            total = total + jnp.sum(value * value, axis=(0, 1), keepdims=True)
    square_ref[...] = jnp.broadcast_to(total, square_ref.shape)


def to_columns(value, piece_width):
    members, rows, width = value.shape
    out, square = pl.pallas_call(
        lambda *refs: columns_kernel_of(piece_width, *refs),
        out_shape=(
            jax.ShapeDtypeStruct((rows, members * width), WIDE),
            jax.ShapeDtypeStruct((8, 128), WIDE),
        ),
        in_specs=[in_vmem()],
        out_specs=(in_vmem(),) * 2,
        compiler_params=params(),
        cost_estimate=estimate(2),
        name="to_columns",
    )(value)
    return out, square[0, 0]


def adam_kernel(rates, factor_ref, *refs):
    number = len(rates)
    factor = factor_ref[0]
    for index in range(number):
        gradient, master, first, second = (refs[k * number + index][...] for k in range(4))
        weight, moment, square = adam_update(
            master, first, second, gradient, factor, rates[index], DECAY_RATE
        )
        refs[4 * number + 3 * index][...] = weight
        refs[4 * number + 3 * index + 1][...] = moment
        refs[4 * number + 3 * index + 2][...] = square


def adam_all(factor, gradients, masters, firsts, seconds, rates):
    steps = 6

    def block(array):
        rows, columns = array.shape
        return pl.BlockSpec((rows, columns // steps), lambda step: (0, step))

    blocks = [block(master) for master in masters]
    return pl.pallas_call(
        lambda *refs: adam_kernel(rates, *refs),
        grid=(steps,),
        out_shape=[
            jax.ShapeDtypeStruct(master.shape, WIDE) for master in masters for _ in range(3)
        ],
        in_specs=[in_smem()] + blocks * 4,
        out_specs=[one for one in blocks for _ in range(3)],
        compiler_params=params(),
        cost_estimate=estimate(10),
        name="adam_all",
    )(factor, *gradients, *masters, *firsts, *seconds)


def per_member(
    byte_rows,
    starts,
    doc_ids,
    out_cotangent,
    widen_master,
    widen_first,
    widen_second,
    triple_master,
    triple_first,
    triple_second,
    mixing_master,
    mixing_first,
    mixing_second,
    expand_master,
    expand_first,
    expand_second,
    shrink_master,
    shrink_first,
    shrink_second,
    narrow_master,
    narrow_first,
    narrow_second,
    gains_master,
    gains_first,
    gains_second,
):
    plane = lax.axis_index("z")
    x, y, core = lax.axis_index("x"), lax.axis_index("y"), lax.axis_index("c")
    t = 4 * x + 2 * y + core
    place = jnp.stack([plane, t]).astype(jnp.int32)
    byte_block, cotangent_rows = byte_rows[0], out_cotangent[0]
    bytes_dev, byte_width = byte_block.shape
    model = triple_master.shape[1] // 3
    hidden = expand_master.shape[1]
    shard = triple_master.shape[0]
    widen_shard = widen_master.shape[0]
    member_rows = 3 * bytes_dev // 16
    capacity = member_rows + member_rows // 2
    total = TEAM * member_rows
    own = HEADS // TEAM
    own_width = model // TEAM
    own_hidden = hidden // TEAM
    piece_hidden = own_hidden // PLANES

    widen_low = widen_master.astype(LOW)
    gains_low = gains_master.astype(LOW)
    gain_rows = jnp.pad(gains_low, ((0, 32 - widen_shard - 2), (0, byte_width - shard)))
    small = jnp.concatenate(
        [
            widen_low[:, :byte_width],
            gain_rows,
            widen_low[:, byte_width:],
            jnp.zeros((32 - widen_shard, byte_width), LOW),
            narrow_master.astype(LOW),
        ],
        axis=0,
    )
    small = plane_gather_small(small)
    row_buffer, chosen = pack(
        after(starts, small[1]), doc_ids, byte_block, cotangent_rows, capacity
    )
    packed = row_buffer
    row_buffer = to_plane(row_buffer)
    small, small_marks = team_gather(jnp.concatenate(small, axis=0))
    widen_full, gains_full, narrow_full = widen_whole(place, small, widen_shard, model)
    triple_own = triple_master.astype(LOW).reshape(shard, 3, TEAM, own_width)
    triple_own = jnp.transpose(triple_own, (2, 0, 1, 3)).reshape(TEAM, shard, 3 * own_width)
    triple_own = team_exchange(triple_own)
    mixing_rows = shard * model // (3 * own_width)
    triple_sent = jnp.concatenate(
        [
            after(triple_own, row_buffer, small[2], small[4]).reshape(TEAM * shard, 3 * own_width),
            mixing_master.astype(LOW).reshape(mixing_rows, 3 * own_width),
        ],
        axis=0,
    )
    gathered = lax.all_gather(triple_sent, "z", axis=0)
    triple_own = gathered[:, : TEAM * shard].reshape(model, 3 * own_width)
    mixing_stack = gathered[:, TEAM * shard :].reshape(PLANES, shard, model)
    expand_own = after(expand_master, triple_sent).astype(LOW)
    expand_own = expand_own.reshape(shard, PLANES, TEAM, piece_hidden)
    expand_own = jnp.transpose(expand_own, (2, 0, 1, 3)).reshape(TEAM, shard, own_hidden)
    expand_own = team_exchange(expand_own).reshape(TEAM * shard, own_hidden)
    shrink_low = shrink_master.astype(LOW)
    fed = lax.all_gather(
        jnp.concatenate(
            [expand_own, shrink_low[:, :own_hidden], shrink_low[:, own_hidden:]], axis=0
        ),
        "z",
        axis=0,
    )
    expand_own = fed[:, : TEAM * shard].reshape(model, own_hidden)
    shrink_own = jnp.concatenate(
        [
            fed[:, TEAM * shard : TEAM * shard + piece_hidden],
            fed[:, TEAM * shard + piece_hidden :],
        ],
        axis=2,
    ).reshape(own_hidden, model)
    entering, enter_marks = team_gather(after(row_buffer, *small_marks))
    first_low, widened, patch_rows, doc_column, doc_row, spans = enter(
        place,
        gains_full,
        widen_full,
        entering,
        capacity,
        member_rows,
    )
    shrink_back, upper_back, narrow_back = cotangent(
        after(place, spans), spans, narrow_full, entering, capacity, member_rows
    )
    mixing_own = mixing_exchange(place, mixing_stack, core)

    projected, flat, attended_low, totals = attend_team(
        after(place, shrink_back), first_low, triple_own, doc_column, doc_row, own
    )
    terms, marks = team_scatter(*forward_terms(attended_low, mixing_own))
    resid_one, second_own = add_and_norm(widened, gains_full, terms)

    second_pieces, _ = team_gather(second_own)
    second_low, active_low, expand_back, *terms = feed(
        expand_own, shrink_own, shrink_back, second_pieces
    )
    terms, marks = team_scatter(*terms)
    shrink_grad = tn(after(active_low, *marks), shrink_back).astype(LOW)
    shrink_sum = lax.psum_scatter(shrink_grad, "z", scatter_dimension=0, tiled=True)
    lower_back, mixed_own, second_gain = second_norm_back(
        after(resid_one, shrink_grad), gains_full, upper_back, terms
    )
    exit_out = []

    def leave_forward(own):
        exit_out.extend(exit_block(after(resid_one, own), narrow_full, terms))
        return exit_out[:1]

    mixed, mixed_marks = team_gather(mixed_own, None, leave_forward)
    resid_low, narrow_low = exit_out
    resid_low = team_exchange(resid_low).reshape(total, own_width)
    expand_grad = tn(after(second_low, *mixed_marks), expand_back).astype(LOW)
    expand_sum = lax.psum_scatter(expand_grad, "z", scatter_dimension=0, tiled=True)

    attend_back, mixing_grad = mix_back(
        after(place, expand_grad), mixing_own, attended_low, mixed
    )
    narrow_grad = tn(resid_low, after(narrow_back, attend_back)).astype(LOW)
    attention = (projected, flat, totals, doc_column, doc_row, attend_back)
    first_tile, query_back = attend_back_first(
        after(place, shrink_sum, narrow_grad), *attention, own
    )
    mixing_stack = mixing_return(after(mixing_grad, first_tile), x)
    triple_back, *terms = attend_back_rest(
        place, *attention, first_tile, query_back, triple_own, own
    )
    both = plane_scatter_small(
        jnp.concatenate(
            [after(mixing_stack, triple_back), narrow_grad.reshape(PLANES, shard, byte_width)],
            axis=2,
        )
    )
    mixing_sum, narrow_sum = both[:, :model], both[:, model:]
    first_terms, marks = team_scatter(*terms)
    triple_grad = tn(after(first_low, expand_sum, *marks), triple_back).astype(LOW)
    triple_sum = lax.psum_scatter(triple_grad, "z", scatter_dimension=0, tiled=True)

    back_rows, *terms = first_norm_back(
        after(place, triple_grad, mixing_sum),
        widened,
        gains_full,
        lower_back,
        patch_rows,
        widen_full,
        second_gain,
        narrow_low,
        first_terms,
    )
    terms, marks = team_scatter(*terms)
    widen_ready = sum(term.astype(WIDE) for term in terms)
    gains_ready = widen_ready[PLANES * widen_shard :][:8]
    widen_sum = plane_scatter_small(
        jnp.concatenate(
            [
                widen_ready[: PLANES * widen_shard].reshape(PLANES, widen_shard, model),
                jnp.broadcast_to(gains_ready, (PLANES, 8, model)),
            ],
            axis=1,
        )
    )
    gains_sum = lax.dynamic_slice(
        widen_sum[widen_shard : widen_shard + 2], (0, (plane * TEAM + t) * shard), (2, shard)
    )
    widen_sum = widen_sum[:widen_shard]
    back_rows, _ = team_gather(after(back_rows, terms[2]))
    back_buffer = from_plane(leave(place, spans, back_rows, capacity))
    new_block, grad_block = unpack(chosen, byte_block, cotangent_rows, back_buffer)

    triple_sum = team_exchange(triple_sum.reshape(TEAM, shard, 3 * own_width))
    triple_sum, triple_square = to_columns(triple_sum, own_width)
    expand_sum = team_exchange(expand_sum.reshape(TEAM, shard, own_hidden))
    expand_sum, expand_square = to_columns(expand_sum, piece_hidden)
    shrink_sum = shrink_sum.astype(WIDE)

    reduced = (widen_sum, triple_sum, mixing_sum, expand_sum, shrink_sum, narrow_sum, gains_sum)
    squares = triple_square + expand_square
    for gradient in (widen_sum, mixing_sum, shrink_sum, narrow_sum, gains_sum):
        squares = squares + jnp.sum(gradient * gradient)
    squares = jnp.full((8, 128), squares, WIDE)
    for bit in (CORE_BIT, Y_BIT, X_BIT, TEAM, 2 * TEAM):
        squares = squares + flip(squares, bit)
    grad_norm = jnp.sqrt(squares[0, 0])
    factor = CLIP_NORM / jnp.maximum(grad_norm, CLIP_NORM)
    rates = (
        2.0 * D_BYTE ** (-0.5),
        2.0 * D ** (-0.5),
        0.4,
        2.0 * D ** (-0.5),
        2.0 * FF ** (-0.5),
        2.0 * D ** (-0.5),
    )
    updated = adam_all(
        factor.reshape(1),
        reduced[:6],
        (widen_master, triple_master, mixing_master, expand_master, shrink_master, narrow_master),
        (widen_first, triple_first, mixing_first, expand_first, shrink_first, narrow_first),
        (widen_second, triple_second, mixing_second, expand_second, shrink_second, narrow_second),
        rates,
    )
    gains = adam_update(gains_master, gains_first, gains_second, gains_sum, factor, 0.6, 0.0)
    return (new_block[None], grad_block[None], grad_norm, *updated, *gains)


def plane_solution(mesh):
    fine = Mesh(mesh.devices.reshape(PLANES, 2, 2, 2), AXES)
    byte_spec = P(("y", "c"), ("z", "x"))
    rows_spec = P(AXES, None)
    gains_spec = P(None, AXES)
    return jax.shard_map(
        per_member,
        mesh=fine,
        in_specs=(byte_spec,) * 4 + (rows_spec,) * 18 + (gains_spec,) * 3,
        out_specs=(byte_spec,) * 2 + (P(),) + (rows_spec,) * 18 + (gains_spec,) * 3,
        check_vma=False,
    )


def solution(mesh):
    if plane_fits(mesh):
        return plane_solution(mesh)
    placed = (
        P("dp", "seq", None),
        P("dp", "seq"),
        P("dp", "seq"),
        P("dp", "seq", None),
        P(("seq", "dp"), None),
        P(("seq", "dp"), None),
        P(("seq", "dp"), None),
        P(("seq", "dp"), None),
        P(("seq", "dp"), None),
        P(("seq", "dp"), None),
        P(("seq", "dp"), None),
        P(("seq", "dp"), None),
        P(("seq", "dp"), None),
        P(("seq", "dp"), None),
        P(("seq", "dp"), None),
        P(("seq", "dp"), None),
        P(("seq", "dp"), None),
        P(("seq", "dp"), None),
        P(("seq", "dp"), None),
        P(("seq", "dp"), None),
        P(("seq", "dp"), None),
        P(("seq", "dp"), None),
        P(None, ("seq", "dp")),
        P(None, ("seq", "dp")),
        P(None, ("seq", "dp")),
    )
    return jax.shard_map(
        per_device,
        mesh=mesh,
        in_specs=placed,
        out_specs=(
            P("dp", "seq", None),
            P("dp", "seq", None),
            P(),
            P(("seq", "dp"), None),
            P(("seq", "dp"), None),
            P(("seq", "dp"), None),
            P(("seq", "dp"), None),
            P(("seq", "dp"), None),
            P(("seq", "dp"), None),
            P(("seq", "dp"), None),
            P(("seq", "dp"), None),
            P(("seq", "dp"), None),
            P(("seq", "dp"), None),
            P(("seq", "dp"), None),
            P(("seq", "dp"), None),
            P(("seq", "dp"), None),
            P(("seq", "dp"), None),
            P(("seq", "dp"), None),
            P(("seq", "dp"), None),
            P(("seq", "dp"), None),
            P(("seq", "dp"), None),
            P(None, ("seq", "dp")),
            P(None, ("seq", "dp")),
            P(None, ("seq", "dp")),
        ),
        check_vma=False,
    )
```

```python
import jax
import jax.numpy as jnp
from jax import lax
from jax.experimental import pallas as pl
from jax.experimental.pallas import tpu as pltpu
from jax.sharding import Mesh, PartitionSpec as P

D_BYTE = 768
D = 1536
HEADS = 24
HEAD_DIM = 64
FF = 6144
STEP = 10


NORM_EPS = 1e-05
SCORE_SCALE = 0.125
MASK_FILL = -1e30
BETA_ONE = 0.9
BETA_TWO = 0.95
ADAM_EPS = 1e-08
DECAY_RATE = 0.1
CLIP_NORM = 1.0


def prefix(part, axis, combine, identity):
    place = lax.axis_index(axis)
    gathered = lax.all_gather(part, axis)
    state = jnp.zeros_like(part) + jnp.asarray(identity, part.dtype)

    def one(hop, state):
        return combine(state, lax.dynamic_index_in_dim(gathered, hop, 0, False))

    return lax.fori_loop(0, place, one, state)


def normalize(values, gain):
    inverse = lax.rsqrt(jnp.mean(values * values, axis=-1, keepdims=True) + NORM_EPS)
    return values * inverse * gain


def add_counts(earlier, later):
    return earlier + later


def block_rows(amount):
    for option in (1024, 768, 512, 384, 256):
        if amount >= option and amount % option == 0:
            return option
    return amount


def spread_positions(first_row, amount, patch_dev, devices):
    whole_rows = first_row + jnp.arange(amount, dtype=jnp.int32)
    return whole_rows % patch_dev * devices + whole_rows // patch_dev


def make_attend(queries, patch_docs, patch_pos, patch_dev, devices):

    def attend(running, shards, offset):
        piece_keys, piece_values, piece_docs = shards
        amount = piece_keys.shape[0]
        span_rows = block_rows(amount)
        number = amount // span_rows
        key_blocks = piece_keys.reshape(number, span_rows, HEADS, HEAD_DIM)
        value_blocks = piece_values.reshape(number, span_rows, HEADS, HEAD_DIM)
        doc_blocks = piece_docs.reshape(number, span_rows)
        firsts = span_rows * jnp.arange(number, dtype=jnp.int32)

        def advance(status, section):
            block_keys, block_values, block_docs, block_first = section
            running_top, running_sum, running_out = status
            scores = (
                jnp.einsum("phd,khd->hpk", queries, block_keys, preferred_element_type=jnp.float32)
                * SCORE_SCALE
            )
            key_pos = spread_positions(block_first, span_rows, patch_dev, devices)
            allowed = (patch_docs[:, None] == block_docs[None, :]) & (
                key_pos[None, :] <= patch_pos[:, None]
            )
            masked = jnp.where(allowed[None], scores, MASK_FILL)
            new_top = jnp.maximum(running_top, jnp.max(masked, axis=-1))
            weights = jnp.where(allowed[None], jnp.exp(masked - new_top[..., None]), 0.0)
            rescale = jnp.exp(running_top - new_top)
            running_sum = running_sum * rescale + jnp.sum(weights, axis=-1)
            running_out = running_out * rescale[..., None] + jnp.einsum(
                "hpk,khd->hpd",
                weights.astype(jnp.bfloat16),
                block_values,
                preferred_element_type=jnp.float32,
            )
            return ((new_top, running_sum, running_out), None)

        running, _ = lax.scan(advance, running, (key_blocks, value_blocks, doc_blocks, firsts))
        return running

    return attend


def outer_sum(left, right):
    return jnp.einsum("pi,pj->ij", left, right, preferred_element_type=jnp.float32)


def back_product(grads, weight):
    return jnp.einsum("pj,ij->pi", grads, weight, preferred_element_type=jnp.float32)


def adam_update(master, first_old, second_old, gradient, clip_factor, learn_rate, weight_decay):
    clipped = gradient * clip_factor
    moment = BETA_ONE * first_old + (1.0 - BETA_ONE) * clipped
    square = BETA_TWO * second_old + (1.0 - BETA_TWO) * clipped * clipped
    corrected = (
        moment / (1.0 - BETA_ONE**STEP) / (jnp.sqrt(square / (1.0 - BETA_TWO**STEP)) + ADAM_EPS)
    )
    weight = master - learn_rate * (corrected + weight_decay * master)
    return (weight, moment, square)


def per_device(
    byte_rows,
    starts,
    doc_ids,
    out_cotangent,
    widen_master,
    widen_first,
    widen_second,
    triple_master,
    triple_first,
    triple_second,
    mixing_master,
    mixing_first,
    mixing_second,
    expand_master,
    expand_first,
    expand_second,
    shrink_master,
    shrink_first,
    shrink_second,
    narrow_master,
    narrow_first,
    narrow_second,
    gains_master,
    gains_first,
    gains_second,
):
    widen_full, triple_full, mixing_full, expand_full, shrink_full, narrow_full, gains_full = (
        lax.all_gather(widen_master.astype(jnp.bfloat16), ("seq", "dp"), axis=0, tiled=True),
        lax.all_gather(triple_master.astype(jnp.bfloat16), ("seq", "dp"), axis=0, tiled=True),
        lax.all_gather(mixing_master.astype(jnp.bfloat16), ("seq", "dp"), axis=0, tiled=True),
        lax.all_gather(expand_master.astype(jnp.bfloat16), ("seq", "dp"), axis=0, tiled=True),
        lax.all_gather(shrink_master.astype(jnp.bfloat16), ("seq", "dp"), axis=0, tiled=True),
        lax.all_gather(narrow_master.astype(jnp.bfloat16), ("seq", "dp"), axis=0, tiled=True),
        lax.all_gather(gains_master.astype(jnp.bfloat16), ("seq", "dp"), axis=1, tiled=True),
    )
    gain_one = gains_full[0].astype(jnp.float32)
    gain_two = gains_full[1].astype(jnp.float32)
    devices = lax.axis_size("seq")
    seq_place = lax.axis_index("seq")
    byte_block = byte_rows[0]
    start_flags = starts[0]
    doc_local = doc_ids[0]
    cotangent_rows = out_cotangent[0]
    byte_width = byte_block.shape[1]
    patch_dev = 3 * byte_block.shape[0] // 16
    capacity = patch_dev + patch_dev // 2
    slot_count = (capacity + devices - 2) // devices + 1
    buffer_rows = devices * slot_count
    amount = jnp.sum(start_flags)
    offset = prefix(amount, "seq", add_counts, jnp.int32(0))
    ranking = jnp.cumsum(start_flags) - start_flags
    patch_index = offset + ranking
    owners = patch_index % devices
    local_row = patch_index // devices
    slot_index = local_row - offset // devices
    target_slot = jnp.where(start_flags == 1, owners * slot_count + slot_index, buffer_rows)
    send_rows = (
        jnp.zeros((buffer_rows, byte_width), jnp.bfloat16)
        .at[target_slot]
        .set(byte_block, mode="drop")
    )
    send_meta = (
        jnp.full((buffer_rows, 2), patch_dev, jnp.int32)
        .at[target_slot]
        .set(jnp.stack([local_row, doc_local], axis=-1), mode="drop")
    )
    send_grad = (
        jnp.zeros((buffer_rows, byte_width), jnp.bfloat16)
        .at[target_slot]
        .set(cotangent_rows, mode="drop")
    )
    arrived_rows, arrived_meta = (
        lax.all_to_all(send_rows, "seq", split_axis=0, concat_axis=0, tiled=True),
        lax.all_to_all(send_meta, "seq", split_axis=0, concat_axis=0, tiled=True),
    )
    target = arrived_meta[:, 0]
    valid_slot = target < patch_dev
    patch_rows = (
        jnp.zeros((patch_dev, byte_width), jnp.bfloat16).at[target].set(arrived_rows, mode="drop")
    )
    patch_docs = jnp.zeros((patch_dev,), jnp.int32).at[target].set(arrived_meta[:, 1], mode="drop")
    patch_pos = seq_place + devices * jnp.arange(patch_dev, dtype=jnp.int32)
    widened = jnp.dot(patch_rows, widen_full, preferred_element_type=jnp.float32)
    model_width = widened.shape[1]
    first_low = normalize(widened, gain_one).astype(jnp.bfloat16)
    projected = jnp.dot(first_low, triple_full, preferred_element_type=jnp.float32).astype(
        jnp.bfloat16
    )
    queries = projected[:, :model_width].reshape(patch_dev, HEADS, HEAD_DIM)
    key_rows = projected[:, model_width : 2 * model_width]
    value_rows = projected[:, 2 * model_width :]
    initial = (
        jnp.full((HEADS, patch_dev), MASK_FILL, jnp.float32),
        jnp.zeros((HEADS, patch_dev), jnp.float32),
        jnp.zeros((HEADS, patch_dev, HEAD_DIM), jnp.float32),
    )
    attend = make_attend(queries, patch_docs, patch_pos, patch_dev, devices)
    running = attend(
        initial,
        (
            lax.all_gather(key_rows, "seq", axis=0, tiled=True),
            lax.all_gather(value_rows, "seq", axis=0, tiled=True),
            lax.all_gather(patch_docs, "seq", axis=0, tiled=True),
        ),
        jnp.int32(0),
    )
    running_top, running_sum, running_out = running
    attended = running_out / running_sum[..., None]
    log_total = running_top + jnp.log(running_sum)
    attended_low = (
        jnp.transpose(attended, (1, 0, 2)).reshape(patch_dev, model_width).astype(jnp.bfloat16)
    )
    resid_one = widened + jnp.dot(attended_low, mixing_full, preferred_element_type=jnp.float32)
    second_low = normalize(resid_one, gain_two).astype(jnp.bfloat16)
    expanded = jnp.dot(second_low, expand_full, preferred_element_type=jnp.float32)
    active_low = jax.nn.gelu(expanded).astype(jnp.bfloat16)
    resid_two = resid_one + jnp.dot(active_low, shrink_full, preferred_element_type=jnp.float32)
    resid_low = resid_two.astype(jnp.bfloat16)
    narrow_low = jnp.dot(resid_low, narrow_full, preferred_element_type=jnp.float32).astype(
        jnp.bfloat16
    )
    returned = jnp.where(valid_slot[:, None], jnp.take(narrow_low, target, axis=0, mode="clip"), 0)
    back_rows = lax.all_to_all(returned, "seq", split_axis=0, concat_axis=0, tiled=True)
    added = jnp.take(back_rows, target_slot, axis=0, mode="clip").astype(jnp.float32)
    new_block = byte_block.astype(jnp.float32) + jnp.where(start_flags[:, None] == 1, added, 0.0)
    arrived_grad = lax.all_to_all(send_grad, "seq", split_axis=0, concat_axis=0, tiled=True)
    narrow_back = (
        jnp.zeros((patch_dev, byte_width), jnp.bfloat16).at[target].set(arrived_grad, mode="drop")
    )
    narrow_grad = outer_sum(resid_low, narrow_back)
    upper_back = back_product(narrow_back, narrow_full)
    shrink_back = upper_back.astype(jnp.bfloat16)
    shrink_grad = outer_sum(active_low, shrink_back)
    active_back = back_product(shrink_back, shrink_full)
    _, gelu_pull = jax.vjp(jax.nn.gelu, expanded)
    expand_back = gelu_pull(active_back)[0].astype(jnp.bfloat16)
    expand_grad = outer_sum(second_low, expand_back)
    second_back = back_product(expand_back, expand_full)
    _, second_pull = jax.vjp(normalize, resid_one, gain_two)
    second_part, second_gain = second_pull(second_back)
    lower_back = upper_back + second_part
    mixed_back = lower_back.astype(jnp.bfloat16)
    mixing_grad = outer_sum(attended_low, mixed_back)
    attend_back = (
        back_product(mixed_back, mixing_full)
        .astype(jnp.bfloat16)
        .reshape(patch_dev, HEADS, HEAD_DIM)
    )
    delta_rows = jnp.einsum("phd,hpd->hp", attend_back.astype(jnp.float32), attended)
    all_keys, all_values, all_docs = (
        lax.all_gather(key_rows, "seq", axis=0, tiled=True),
        lax.all_gather(value_rows, "seq", axis=0, tiled=True),
        lax.all_gather(patch_docs, "seq", axis=0, tiled=True),
    )
    total_keys = all_keys.shape[0]
    span_rows = block_rows(total_keys)
    number = total_keys // span_rows
    key_blocks = all_keys.reshape(number, span_rows, HEADS, HEAD_DIM)
    value_blocks = all_values.reshape(number, span_rows, HEADS, HEAD_DIM)
    doc_blocks = all_docs.reshape(number, span_rows)
    firsts = span_rows * jnp.arange(number, dtype=jnp.int32)
    query_start = jnp.zeros((patch_dev, HEADS, HEAD_DIM), jnp.float32)

    def backstep(query_back, section):
        block_keys, block_values, block_docs, block_first = section
        scores = (
            jnp.einsum("phd,khd->hpk", queries, block_keys, preferred_element_type=jnp.float32)
            * SCORE_SCALE
        )
        key_pos = spread_positions(block_first, span_rows, patch_dev, devices)
        allowed = (patch_docs[:, None] == block_docs[None, :]) & (
            key_pos[None, :] <= patch_pos[:, None]
        )
        probs = jnp.where(allowed[None], jnp.exp(scores - log_total[..., None]), 0.0)
        prob_back = jnp.einsum(
            "phd,khd->hpk", attend_back, block_values, preferred_element_type=jnp.float32
        )
        score_back = (probs * (prob_back - delta_rows[..., None])).astype(jnp.bfloat16)
        query_back = (
            query_back
            + jnp.einsum("hpk,khd->phd", score_back, block_keys, preferred_element_type=jnp.float32)
            * SCORE_SCALE
        )
        keys_part = (
            jnp.einsum("hpk,phd->khd", score_back, queries, preferred_element_type=jnp.float32)
            * SCORE_SCALE
        )
        values_part = jnp.einsum(
            "hpk,phd->khd",
            probs.astype(jnp.bfloat16),
            attend_back,
            preferred_element_type=jnp.float32,
        )
        return (
            query_back,
            (
                keys_part.reshape(span_rows, model_width),
                values_part.reshape(span_rows, model_width),
            ),
        )

    query_back, (keys_back, values_back) = lax.scan(
        backstep, query_start, (key_blocks, value_blocks, doc_blocks, firsts)
    )
    keys_own, values_own = (
        lax.psum_scatter(
            keys_back.reshape(total_keys, model_width).astype(jnp.bfloat16),
            "seq",
            scatter_dimension=0,
            tiled=True,
        ).astype(jnp.float32),
        lax.psum_scatter(
            values_back.reshape(total_keys, model_width).astype(jnp.bfloat16),
            "seq",
            scatter_dimension=0,
            tiled=True,
        ).astype(jnp.float32),
    )
    triple_back = jnp.concatenate(
        [query_back.reshape(patch_dev, model_width), keys_own, values_own], axis=1
    ).astype(jnp.bfloat16)
    triple_grad = outer_sum(first_low, triple_back)
    first_back = back_product(triple_back, triple_full)
    _, first_pull = jax.vjp(normalize, widened, gain_one)
    first_part, first_gain = first_pull(first_back)
    base_low = (lower_back + first_part).astype(jnp.bfloat16)
    widen_grad = outer_sum(patch_rows, base_low)
    patch_back = back_product(base_low, widen_full).astype(jnp.bfloat16)
    grad_slots = jnp.where(
        valid_slot[:, None], jnp.take(patch_back, target, axis=0, mode="clip"), 0
    )
    grad_rows = lax.all_to_all(grad_slots, "seq", split_axis=0, concat_axis=0, tiled=True)
    coming = jnp.take(grad_rows, target_slot, axis=0, mode="clip").astype(jnp.float32)
    grad_block = cotangent_rows.astype(jnp.float32) + jnp.where(
        start_flags[:, None] == 1, coming, 0.0
    )
    gains_grad = jnp.stack([first_gain, second_gain], axis=0)
    reduced = (
        lax.psum_scatter(widen_grad, ("seq", "dp"), scatter_dimension=0, tiled=True),
        lax.psum_scatter(triple_grad, ("seq", "dp"), scatter_dimension=0, tiled=True),
        lax.psum_scatter(mixing_grad, ("seq", "dp"), scatter_dimension=0, tiled=True),
        lax.psum_scatter(expand_grad, ("seq", "dp"), scatter_dimension=0, tiled=True),
        lax.psum_scatter(shrink_grad, ("seq", "dp"), scatter_dimension=0, tiled=True),
        lax.psum_scatter(narrow_grad, ("seq", "dp"), scatter_dimension=0, tiled=True),
        lax.psum_scatter(gains_grad, ("seq", "dp"), scatter_dimension=1, tiled=True),
    )
    local_squares = jnp.float32(0.0)
    for member in reduced:
        local_squares = local_squares + jnp.sum(member * member)
    norm_squared = lax.psum(local_squares, ("seq", "dp"))
    grad_norm = jnp.sqrt(norm_squared)
    factor = CLIP_NORM / jnp.maximum(grad_norm, CLIP_NORM)
    masters = (
        widen_master,
        triple_master,
        mixing_master,
        expand_master,
        shrink_master,
        narrow_master,
        gains_master,
    )
    firsts_old = (
        widen_first,
        triple_first,
        mixing_first,
        expand_first,
        shrink_first,
        narrow_first,
        gains_first,
    )
    seconds_old = (
        widen_second,
        triple_second,
        mixing_second,
        expand_second,
        shrink_second,
        narrow_second,
        gains_second,
    )
    rates = (
        2.0 * D_BYTE ** (-0.5),
        2.0 * D ** (-0.5),
        0.4,
        2.0 * D ** (-0.5),
        2.0 * FF ** (-0.5),
        2.0 * D ** (-0.5),
        0.6,
    )
    decays = (DECAY_RATE, DECAY_RATE, DECAY_RATE, DECAY_RATE, DECAY_RATE, DECAY_RATE, 0.0)
    updates = [
        adam_update(
            masters[index],
            firsts_old[index],
            seconds_old[index],
            reduced[index],
            factor,
            rates[index],
            decays[index],
        )
        for index in range(7)
    ]
    return (
        new_block.astype(jnp.bfloat16)[None],
        grad_block.astype(jnp.bfloat16)[None],
        grad_norm,
        updates[0][0],
        updates[0][1],
        updates[0][2],
        updates[1][0],
        updates[1][1],
        updates[1][2],
        updates[2][0],
        updates[2][1],
        updates[2][2],
        updates[3][0],
        updates[3][1],
        updates[3][2],
        updates[4][0],
        updates[4][1],
        updates[4][2],
        updates[5][0],
        updates[5][1],
        updates[5][2],
        updates[6][0],
        updates[6][1],
        updates[6][2],
    )


PLANES = 4
TEAM = 8
CORE_BIT, Y_BIT, X_BIT = 1, 2, 4
AXES = ("z", "x", "y", "c")
TEAM_AXES = ("x", "y", "c")
LOW = jnp.bfloat16
WIDE = jnp.float32
VMEM_LIMIT = 56 * 1024 * 1024
LOG2_E = 1.4426950408889634
GELU_A = 0.7978845608028654
GELU_B = 0.044715


def plane_fits(mesh):
    return mesh.shape["seq"] == 2 * PLANES and mesh.shape["dp"] == PLANES


def flip(value, bit):
    pairs = [(place, place ^ bit) for place in range(PLANES * TEAM)]
    return lax.ppermute(value, AXES, pairs)


def shift_plane(value, hop):
    pairs = [
        (plane * TEAM + t, (plane + hop) % PLANES * TEAM + t)
        for plane in range(PLANES)
        for t in range(TEAM)
    ]
    return lax.ppermute(value, AXES, pairs)


SEQUENCE_OF_PLANE = (2, 0, 1, 3)


def source_of(plane, t):
    return (plane + t // 2 % 2 + 2 * (t % 2) + 2 * PLANES) % PLANES * 2 + t // 4


def byte_pairs():
    return [
        (source_of(plane, t) * PLANES + SEQUENCE_OF_PLANE[plane], plane * TEAM + t)
        for plane in range(PLANES)
        for t in range(TEAM)
    ]


def to_plane(value):
    return lax.ppermute(value, AXES, byte_pairs())


def from_plane(value):
    return lax.ppermute(value, AXES, [(there, here) for here, there in byte_pairs()])


def team_gather(block, cut=None, before_relay=lambda own: ()):
    cut = block.shape[0] // 2 if cut is None else cut
    from_x = flip(block, X_BIT)
    from_y = flip(block, Y_BIT)
    from_core = flip(block, CORE_BIT)
    from_x, from_y = after((from_x, from_y), *before_relay(from_core))
    to_x, to_y = from_y[:cut], from_x[cut:]
    upper = flip(to_x, X_BIT)
    lower = flip(to_y, Y_BIT)
    y_core = flip(from_y, CORE_BIT)
    x_core = flip(from_x, CORE_BIT)
    return [
        block,
        from_core,
        from_y,
        y_core,
        from_x,
        x_core,
        upper,
        lower,
        flip(upper, CORE_BIT),
        flip(lower, CORE_BIT),
    ], (to_x, to_y)


PIECES = 10


def piece(refs, m):
    if m < 6:
        return refs[m][...]
    return jnp.concatenate([refs[2 * m - 6][...], refs[2 * m - 5][...]], axis=0)


def team_scatter(far_send, far_keep, x_send, x_keep, y_send, y_keep, own_send, own_keep):
    def pair(send, keep):
        return keep.astype(WIDE) + flip(send, CORE_BIT).astype(WIDE)

    far = pair(far_send, far_keep).astype(LOW)
    cut = far.shape[0] // 2
    upper = flip(far[:cut], X_BIT).astype(WIDE)
    lower = flip(far[cut:], Y_BIT).astype(WIDE)
    to_x, to_y = pair(x_send, x_keep), pair(y_send, y_keep)
    to_x = jnp.concatenate([to_x[:cut], to_x[cut:] + lower], axis=0).astype(LOW)
    to_y = jnp.concatenate([to_y[:cut] + upper, to_y[cut:]], axis=0).astype(LOW)
    terms = (own_keep, flip(own_send, CORE_BIT), flip(to_x, X_BIT), flip(to_y, Y_BIT))
    return terms, (to_x, to_y)


def put_terms(outs, m, value):
    outs[7 - m][...] = value.astype(LOW)


def term_shapes(rows, width):
    return (jax.ShapeDtypeStruct((rows, width), LOW),) * TEAM


def add_terms(refs, lanes=slice(None)):
    total = refs[0][:, lanes].astype(WIDE)
    for ref in refs[1:]:
        total = total + ref[:, lanes].astype(WIDE)
    return total


def after(value, *earlier):
    return lax.optimization_barrier((value,) + earlier)[0]


def plane_gather_small(block):
    return [block] + [shift_plane(block, hop) for hop in (1, 2, 3)]


def plane_scatter_small(stack):
    back = lax.all_to_all(stack.astype(LOW), "z", split_axis=0, concat_axis=0, tiled=True)
    return jnp.sum(back.astype(WIDE), axis=0)


def team_exchange(value):
    return lax.all_to_all(value, TEAM_AXES, split_axis=0, concat_axis=0, tiled=True)


def pick(value, place, axis):
    return lax.dynamic_index_in_dim(value, place, axis, False)


def in_vmem():
    return pl.BlockSpec(memory_space=pltpu.VMEM)


def in_smem():
    return pl.BlockSpec(memory_space=pltpu.SMEM)


def params():
    return pltpu.CompilerParams(vmem_limit_bytes=VMEM_LIMIT)


def estimate(microseconds):
    return pl.CostEstimate(
        flops=int(microseconds * 8e8), bytes_accessed=int(microseconds * 2e6), transcendentals=0
    )


def nn(left, right):
    return lax.dot_general(left, right, (((1,), (0,)), ((), ())), preferred_element_type=WIDE)


def nt(left, right):
    return lax.dot_general(left, right, (((1,), (1,)), ((), ())), preferred_element_type=WIDE)


def tn(left, right):
    return lax.dot_general(left, right, (((0,), (0,)), ((), ())), preferred_element_type=WIDE)


def slot_matrix(flags, slots):
    amount = flags.shape[1]
    row = lax.broadcasted_iota(jnp.int32, (amount, amount), 0)
    column = lax.broadcasted_iota(jnp.int32, (amount, amount), 1)
    before = jnp.where(row < column, 1.0, 0.0).astype(LOW)
    rank = nn(jnp.broadcast_to(flags, (8, amount)).astype(LOW), before)[:1]
    rank = jnp.where(flags > 0.5, rank, -1.0)
    slot = lax.broadcasted_iota(jnp.int32, (slots, amount), 0).astype(WIDE)
    return jnp.where(slot == rank, 1.0, 0.0).astype(LOW)


def pack_kernel(starts_ref, docs_ref, rows_ref, cotangent_ref, rows_out, chosen_out):
    capacity = chosen_out.shape[0]
    width = rows_out.shape[1]
    flags = starts_ref[...].astype(WIDE)
    chosen = slot_matrix(flags, 384)
    amount = jnp.sum(flags)
    docs = nt(jnp.broadcast_to(docs_ref[...].astype(WIDE), (16, flags.shape[1])).astype(LOW), chosen)
    docs = jnp.concatenate([docs, jnp.zeros((16, width - 384), WIDE)], axis=1)
    row = lax.broadcasted_iota(jnp.int32, (16, width), 0)
    high = jnp.floor(amount * 0.5)
    meta = jnp.where(row == 0, docs, jnp.where(row == 1, high, amount - 2.0 * high))
    chosen = chosen[:capacity]
    chosen_out[...] = chosen
    rows_out[:16] = meta.astype(LOW)
    rows_out[16 : 16 + capacity] = nn(chosen, rows_ref[...]).astype(LOW)
    rows_out[16 + capacity :] = nn(chosen, cotangent_ref[...]).astype(LOW)


def pack(starts, docs, rows, cotangent_rows, capacity):
    amount, width = rows.shape
    return pl.pallas_call(
        pack_kernel,
        out_shape=(
            jax.ShapeDtypeStruct((2 * capacity + 16, width), LOW),
            jax.ShapeDtypeStruct((capacity, amount), LOW),
        ),
        in_specs=[in_vmem()] * 4,
        out_specs=(in_vmem(), in_vmem()),
        compiler_params=params(),
        cost_estimate=estimate(5),
        name="pack",
    )(starts, docs, rows, cotangent_rows)


def unpack_kernel(chosen_ref, rows_ref, cotangent_ref, back_ref, rows_out, cotangent_out):
    width = rows_ref.shape[1]
    added = tn(chosen_ref[...], back_ref[...])
    rows_out[...] = (rows_ref[...].astype(WIDE) + added[:, :width]).astype(LOW)
    cotangent_out[...] = (cotangent_ref[...].astype(WIDE) + added[:, width:]).astype(LOW)


def unpack(chosen, rows, cotangent_rows, back):
    return pl.pallas_call(
        unpack_kernel,
        out_shape=(jax.ShapeDtypeStruct(rows.shape, LOW),) * 2,
        in_specs=[in_vmem()] * 4,
        out_specs=(in_vmem(),) * 2,
        compiler_params=params(),
        cost_estimate=estimate(5),
        name="unpack",
    )(chosen, rows, cotangent_rows, back)


def window_matrix(first, amount, capacity):
    target = lax.broadcasted_iota(jnp.int32, (capacity + 16, capacity), 0)
    source = lax.broadcasted_iota(jnp.int32, (capacity + 16, capacity), 1)
    moved = (target == source + first % 16) & (source < amount)
    return jnp.where(moved, 1.0, 0.0).astype(LOW)


def widen_kernel(place_ref, *refs):
    pieces = refs[:PIECES]
    widen_out, gains_out, narrow_out = refs[PIECES : PIECES + 3]
    widen_wide, gains = refs[PIECES + 3 :]
    plane, t = place_ref[0], place_ref[1]
    shards = PLANES * TEAM
    shard = widen_out.shape[0] // shards
    model = widen_out.shape[1]
    width = model // 2
    gain_shard = model // shards
    for m in range(TEAM):
        low = piece(pieces, m)
        here = low.astype(WIDE)
        for hop in range(PLANES):
            place = (plane - hop + PLANES) % PLANES * TEAM + (t ^ m)
            at = pl.ds(pl.multiple_of(place * shard, 8), shard)
            base = hop * (64 + gain_shard)
            narrow_at = pl.ds(pl.multiple_of(place * gain_shard, 16), gain_shard)
            narrow_out[narrow_at] = low[base + 64 : base + 64 + gain_shard]
            widen_wide[at, :width] = here[base : base + shard]
            widen_wide[at, width:] = here[base + 32 : base + 32 + shard]
            gains[0, pl.ds(place, 1)] = here[base + shard : base + shard + 1, :128]
            gains[1, pl.ds(place, 1)] = here[base + shard + 1 : base + shard + 2, :128]
    widen_out[...] = widen_wide[...].astype(LOW)
    column = lax.broadcasted_iota(jnp.int32, (shards, model), 1)
    owner = lax.broadcasted_iota(jnp.int32, (shards, model), 0)
    owned = (column >= owner * gain_shard) & (column < (owner + 1) * gain_shard)
    inside = jnp.sum(jnp.where(owned, column - owner * gain_shard, 0).astype(WIDE), axis=0, keepdims=True)
    row = lax.broadcasted_iota(jnp.int32, (128, model), 0).astype(WIDE)
    owned = jnp.where(owned, 1.0, 0.0).astype(LOW)
    for k in range(2):
        spread = tn(gains[k].astype(LOW), owned)
        line = jnp.sum(jnp.where(row == inside, spread, 0.0), axis=0, keepdims=True)
        gains_out[k * 8 : k * 8 + 8] = jnp.broadcast_to(line, (8, model))


def widen_whole(place, pieces, shard, model):
    return pl.pallas_call(
        widen_kernel,
        out_shape=(
            jax.ShapeDtypeStruct((shard * PLANES * TEAM, model), LOW),
            jax.ShapeDtypeStruct((16, model), WIDE),
            jax.ShapeDtypeStruct((model, pieces[0].shape[1]), LOW),
        ),
        in_specs=[in_smem()] + [in_vmem()] * PIECES,
        out_specs=(in_vmem(),) * 3,
        scratch_shapes=[
            pltpu.VMEM((shard * PLANES * TEAM, model), WIDE),
            pltpu.VMEM((2, PLANES * TEAM, 128), WIDE),
        ],
        compiler_params=params(),
        cost_estimate=estimate(5),
        name="widen_whole",
    )(place, *pieces)


def enter_kernel(capacity, place_ref, gains_ref, widen_ref, *refs):
    pieces = refs[:PIECES]
    low_out, own_wide, own_rows, doc_column, doc_row, spans = refs[PIECES : PIECES + 6]
    rows, docs = refs[PIECES + 6 :]
    plane, t = place_ref[0], place_ref[1]
    member_rows = own_rows.shape[0]
    total = low_out.shape[0]

    metas = [pieces[m][:16] for m in range(6)] + [pieces[6][:16], pieces[8][:16]]
    blocks = [piece(pieces, m)[16 : 16 + capacity] for m in range(TEAM)]
    amounts, sources = [], []
    for m in range(TEAM):
        meta = metas[m].astype(WIDE)
        row = lax.broadcasted_iota(jnp.int32, meta.shape, 0)
        lane = lax.broadcasted_iota(jnp.int32, meta.shape, 1)
        picked = jnp.where(lane == 0, jnp.where(row == 1, 2.0 * meta, jnp.where(row == 2, meta, 0.0)), 0.0)
        amounts.append(jnp.sum(picked).astype(jnp.int32))
        sources.append(source_of(plane, t ^ m))
    firsts = []
    for m in range(TEAM):
        first = jnp.int32(0)
        for other in range(TEAM):
            if other != m:
                first = first + jnp.where(sources[other] < sources[m], amounts[other], 0)
        firsts.append(first)
        spans[m] = first
        spans[TEAM + m] = amounts[m]

    rows[...] = jnp.zeros_like(rows)
    docs[...] = jnp.zeros_like(docs)
    for m in range(TEAM):
        moving = window_matrix(firsts[m], amounts[m], capacity)
        at = pl.ds(pl.multiple_of(firsts[m] // 16 * 16, 16), capacity + 16)
        rows[at] = rows[at] + nn(moving, blocks[m]).astype(LOW)
        names = metas[m][:1, :384]
        names = jnp.broadcast_to(names, (128, 384))[:, :capacity]
        docs[at] = docs[at] + nt(moving, names)

    doc_column[...] = docs[:total]
    select = jnp.where(lax.broadcasted_iota(jnp.int32, (8, 128), 1) == 0, 1.0, 0.0).astype(LOW)
    doc_row[...] = nt(select, docs[:total].astype(LOW))
    own_rows[...] = rows[pl.ds(pl.multiple_of(t * member_rows, 16), member_rows)]

    def one(k, carry):
        at = pl.ds(pl.multiple_of(k * 2 * member_rows, 16), 2 * member_rows)
        wide = nn(rows[at], widen_ref[...])
        inverse = lax.rsqrt(jnp.mean(wide * wide, axis=-1, keepdims=True) + NORM_EPS)
        low_out[at] = (wide * inverse * gains_ref[:1]).astype(LOW)
        return carry

    lax.fori_loop(0, TEAM // 2, one, 0)
    own_wide[...] = nn(own_rows[...], widen_ref[...])


def enter(place, gains, widen_full, pieces, capacity, member_rows):
    width, model = widen_full.shape
    total = member_rows * TEAM
    padded = total + capacity + 16
    return pl.pallas_call(
        lambda *refs: enter_kernel(capacity, *refs),
        out_shape=(
            jax.ShapeDtypeStruct((total, model), LOW),
            jax.ShapeDtypeStruct((member_rows, model), WIDE),
            jax.ShapeDtypeStruct((member_rows, width), LOW),
            jax.ShapeDtypeStruct((total, 128), WIDE),
            jax.ShapeDtypeStruct((8, total), WIDE),
            jax.ShapeDtypeStruct((2 * TEAM,), jnp.int32),
        ),
        in_specs=[in_smem(), in_vmem(), in_vmem()] + [in_vmem()] * PIECES,
        out_specs=(in_vmem(),) * 5 + (in_smem(),),
        scratch_shapes=[
            pltpu.VMEM((padded, width), LOW),
            pltpu.VMEM((padded, 128), WIDE),
        ],
        compiler_params=params(),
        cost_estimate=estimate(14),
        name="enter",
    )(place, gains, widen_full, *pieces)


def cotangent_kernel(capacity, place_ref, spans_ref, narrow_ref, *refs):
    pieces = refs[:PIECES]
    low_out, own_wide, all_rows = refs[PIECES : PIECES + 3]
    (rows,) = refs[PIECES + 3 :]
    t = place_ref[1]
    member_rows = own_wide.shape[0]
    rows[...] = jnp.zeros_like(rows)
    for m in range(TEAM):
        first = spans_ref[m]
        moving = window_matrix(first, spans_ref[TEAM + m], capacity)
        at = pl.ds(pl.multiple_of(first // 16 * 16, 16), capacity + 16)
        rows[at] = rows[at] + nn(moving, piece(pieces, m)[16 + capacity :]).astype(LOW)
    all_rows[...] = rows[: all_rows.shape[0]]

    def one(k, carry):
        first = pl.multiple_of((t ^ (2 * k)) * member_rows, 16)
        second = pl.multiple_of((t ^ (2 * k + 1)) * member_rows, 16)
        here = jnp.concatenate(
            [rows[pl.ds(first, member_rows)], rows[pl.ds(second, member_rows)]], axis=0
        )
        at = pl.ds(pl.multiple_of(k * 2 * member_rows, 16), 2 * member_rows)
        low_out[at] = nt(here, narrow_ref[...]).astype(LOW)
        return carry

    lax.fori_loop(0, TEAM // 2, one, 0)
    own_wide[...] = nt(
        rows[pl.ds(pl.multiple_of(t * member_rows, 16), member_rows)], narrow_ref[...]
    )


def cotangent(place, spans, narrow_full, pieces, capacity, member_rows):
    model, width = narrow_full.shape
    total = member_rows * TEAM
    return pl.pallas_call(
        lambda *refs: cotangent_kernel(capacity, *refs),
        out_shape=(
            jax.ShapeDtypeStruct((total, model), LOW),
            jax.ShapeDtypeStruct((member_rows, model), WIDE),
            jax.ShapeDtypeStruct((total, width), LOW),
        ),
        in_specs=[in_smem(), in_smem()] + [in_vmem()] * (1 + PIECES),
        out_specs=(in_vmem(),) * 3,
        scratch_shapes=[pltpu.VMEM((total + capacity + 16, width), LOW)],
        compiler_params=params(),
        cost_estimate=estimate(13),
        name="cotangent",
    )(place, spans, narrow_full, *pieces)


def leave_kernel(place_ref, spans_ref, *refs):
    pieces, out_ref, total = refs[:PIECES], refs[PIECES], refs[PIECES + 1]
    t = place_ref[1]
    first = spans_ref[0]
    capacity = out_ref.shape[0]
    total[...] = jnp.zeros_like(total)
    for m in range(TEAM):
        rows = pieces[0].shape[0]
        offset = (t ^ m) * rows - first

        @pl.when((offset < capacity) & (offset + rows > 0))
        def _(m=m, offset=offset, rows=rows):
            target = lax.broadcasted_iota(jnp.int32, (capacity, rows), 0)
            source = lax.broadcasted_iota(jnp.int32, (capacity, rows), 1) + offset
            total[...] += nn(jnp.where(target == source, 1.0, 0.0).astype(LOW), piece(pieces, m))

    out_ref[...] = total[...].astype(LOW)


def leave(place, spans, pieces, capacity):
    width = pieces[0].shape[1]
    return pl.pallas_call(
        leave_kernel,
        out_shape=jax.ShapeDtypeStruct((capacity, width), LOW),
        in_specs=[in_smem(), in_smem()] + [in_vmem()] * PIECES,
        out_specs=in_vmem(),
        scratch_shapes=[pltpu.VMEM((capacity, width), WIDE)],
        compiler_params=params(),
        cost_estimate=estimate(2),
        name="leave",
    )(place, spans, *pieces)


def norm_kernel(wide_ref, gains_ref, *refs):
    resid_out, low_out = refs[4:]
    resid = wide_ref[...] + add_terms(refs[:4])
    resid_out[...] = resid
    inverse = lax.rsqrt(jnp.mean(resid * resid, axis=-1, keepdims=True) + NORM_EPS)
    low_out[...] = (resid * inverse * gains_ref[8:9]).astype(LOW)


def add_and_norm(wide, gains, terms):
    return pl.pallas_call(
        norm_kernel,
        out_shape=(
            jax.ShapeDtypeStruct(wide.shape, WIDE),
            jax.ShapeDtypeStruct(wide.shape, LOW),
        ),
        in_specs=[in_vmem()] * 6,
        out_specs=(in_vmem(),) * 2,
        compiler_params=params(),
        cost_estimate=estimate(2),
        name="add_and_norm",
    )(wide, gains, *terms)


def norm_back(resid, gain, incoming):
    inverse = lax.rsqrt(jnp.mean(resid * resid, axis=-1, keepdims=True) + NORM_EPS)
    scaled = incoming * gain
    along = jnp.mean(scaled * resid, axis=-1, keepdims=True)
    back = inverse * scaled - resid * (inverse * inverse * inverse * along)
    return back, jnp.sum(incoming * resid * inverse, axis=0, keepdims=True)


def second_back_kernel(resid_ref, gains_ref, upper_ref, *refs):
    lower_out, low_out, gain_out = refs[4:]
    back, gain_back = norm_back(
        resid_ref[...], gains_ref[8:9], add_terms(refs[:4], slice(resid_ref.shape[1]))
    )
    lower = upper_ref[...] + back
    lower_out[...] = lower
    low_out[...] = lower.astype(LOW)
    gain_out[...] = jnp.broadcast_to(gain_back, gain_out.shape)


def second_norm_back(resid, gains, upper, terms):
    rows, model = resid.shape
    return pl.pallas_call(
        second_back_kernel,
        out_shape=(
            jax.ShapeDtypeStruct((rows, model), WIDE),
            jax.ShapeDtypeStruct((rows, model), LOW),
            jax.ShapeDtypeStruct((8, model), WIDE),
        ),
        in_specs=[in_vmem()] * 7,
        out_specs=(in_vmem(),) * 3,
        compiler_params=params(),
        cost_estimate=estimate(2),
        name="second_norm_back",
    )(resid, gains, upper, *terms)


def first_back_kernel(
    place_ref, wide_ref, gains_ref, lower_ref, rows_ref, widen_ref, second_gain_ref, narrow_ref, *refs
):
    patch_out = refs[4]
    outs = refs[5:13]
    grad = refs[13]
    t = place_ref[1]
    back, first_gain = norm_back(wide_ref[...], gains_ref[:1], add_terms(refs[:4]))
    low = (lower_ref[...] + back).astype(LOW)
    grad[...] = tn(rows_ref[...], low)
    shard = grad.shape[0] // (PLANES * TEAM)
    row = lax.broadcasted_iota(jnp.int32, (16, grad.shape[1]), 0)
    gain_rows = jnp.where(row == 0, first_gain, jnp.where(row == 1, second_gain_ref[:1], 0.0))
    for m in (7, 6, 5, 3, 4, 2, 1, 0):
        parts = [
            grad[pl.ds(pl.multiple_of((plane * TEAM + (t ^ m)) * shard, 8), shard)]
            for plane in range(PLANES)
        ]
        put_terms(outs, m, jnp.concatenate(parts + [gain_rows], axis=0))
    width = narrow_ref.shape[1]
    patch_out[:, :width] = narrow_ref[...]
    patch_out[:, width:] = nt(low, widen_ref[...]).astype(LOW)


def first_norm_back(place, wide, gains, lower, rows, widen_full, second_gain, narrow_low, terms):
    model = wide.shape[1]
    width = widen_full.shape[0]
    return pl.pallas_call(
        first_back_kernel,
        out_shape=(jax.ShapeDtypeStruct((rows.shape[0], 2 * width), LOW),)
        + term_shapes(width // TEAM + 16, model),
        in_specs=[in_smem()] + [in_vmem()] * 11,
        out_specs=(in_vmem(),) * 9,
        scratch_shapes=[pltpu.VMEM((width, model), WIDE)],
        compiler_params=params(),
        cost_estimate=estimate(5),
        name="first_norm_back",
    )(place, wide, gains, lower, rows, widen_full, second_gain, narrow_low, *terms)


def exit_kernel(resid_ref, narrow_ref, *refs):
    low_out, narrow_out = refs[4:]
    model = resid_ref.shape[1]
    wide = resid_ref[...] + add_terms(refs[:4], slice(model, 2 * model))
    low = wide.astype(LOW)
    shard = low_out.shape[2] // PLANES
    for m in range(TEAM):
        parts = [
            wide[:, (plane * TEAM + m) * shard : (plane * TEAM + m + 1) * shard]
            for plane in range(PLANES)
        ]
        low_out[m] = jnp.concatenate(parts, axis=1).astype(LOW)
    narrow_out[...] = nn(low, narrow_ref[...]).astype(LOW)


def exit_block(resid, narrow_full, terms):
    rows, model = resid.shape
    return pl.pallas_call(
        exit_kernel,
        out_shape=(
            jax.ShapeDtypeStruct((TEAM, rows, model // TEAM), LOW),
            jax.ShapeDtypeStruct((rows, narrow_full.shape[1]), LOW),
        ),
        in_specs=[in_vmem()] * 6,
        out_specs=(in_vmem(),) * 2,
        compiler_params=params(),
        cost_estimate=estimate(4),
        name="exit_block",
    )(resid, narrow_full, *terms)


def forward_terms_kernel(left_ref, right_ref, *outs):
    rows = left_ref.shape[0] // TEAM
    for k in (3, 2, 1, 0):
        product = nn(left_ref[2 * k * rows : (2 * k + 2) * rows], right_ref[...])
        put_terms(outs, 2 * k + 1, product[rows:])
        put_terms(outs, 2 * k, product[:rows])


def forward_terms(left, right):
    return pl.pallas_call(
        forward_terms_kernel,
        out_shape=term_shapes(left.shape[0] // TEAM, right.shape[1]),
        in_specs=[in_vmem()] * 2,
        out_specs=(in_vmem(),) * 8,
        compiler_params=params(),
        cost_estimate=estimate(6),
        name="forward_terms",
    )(left, right)


def feed_kernel(expand_ref, shrink_ref, back_ref, *refs):
    pieces = refs[:PIECES]
    second_out, active_out, expand_out = refs[PIECES : PIECES + 3]
    outs = refs[PIECES + 3 :]
    rows = back_ref.shape[0] // TEAM
    for k in (3, 2, 1, 0):
        at = slice(2 * k * rows, (2 * k + 2) * rows)
        low = jnp.concatenate([piece(pieces, 2 * k), piece(pieces, 2 * k + 1)], axis=0)
        second_out[at] = low
        value = nn(low, expand_ref[...])
        square = value * value
        bend = jnp.tanh(GELU_A * (value + GELU_B * square * value))
        active_out[at] = (0.5 * value * (1.0 + bend)).astype(LOW)
        slope = 0.5 * (1.0 + bend) + 0.5 * value * (1.0 - bend * bend) * (
            GELU_A * (1.0 + 3.0 * GELU_B * square)
        )
        back = (slope * nt(back_ref[at], shrink_ref[...])).astype(LOW)
        expand_out[at] = back
        product = jnp.concatenate(
            [nt(back, expand_ref[...]).astype(LOW), nn(active_out[at], shrink_ref[...]).astype(LOW)],
            axis=1,
        )
        put_terms(outs, 2 * k + 1, product[rows:])
        put_terms(outs, 2 * k, product[:rows])


def feed(expand_own, shrink_own, shrink_back, pieces):
    total, model = shrink_back.shape
    hidden = expand_own.shape[1]
    return pl.pallas_call(
        feed_kernel,
        out_shape=(
            jax.ShapeDtypeStruct((total, model), LOW),
            jax.ShapeDtypeStruct((total, hidden), LOW),
            jax.ShapeDtypeStruct((total, hidden), LOW),
        )
        + term_shapes(total // TEAM, 2 * model),
        in_specs=[in_vmem()] * (3 + PIECES),
        out_specs=(in_vmem(),) * 11,
        compiler_params=params(),
        cost_estimate=estimate(18),
        name="feed",
    )(expand_own, shrink_own, shrink_back, *pieces)


def attend_kernel(
    own,
    tile,
    place_ref,
    first_ref,
    triple_ref,
    doc_column,
    doc_row,
    projected_ref,
    flat_out,
    low_out,
    total_out,
    queries,
    keys,
    values,
    attended,
):
    t = place_ref[1]
    rows = first_ref.shape[0]
    member_rows = rows // TEAM
    width = own * HEAD_DIM

    def project(k, carry):
        at = pl.ds(pl.multiple_of(k * 2 * member_rows, 16), 2 * member_rows)
        projected_ref[at] = nn(first_ref[at], triple_ref[...]).astype(LOW)
        return carry

    lax.fori_loop(0, TEAM // 2, project, 0)
    for h in range(own):
        lanes = slice(h * HEAD_DIM, (h + 1) * HEAD_DIM)
        queries[h] = projected_ref[:, :width][:, lanes]
        keys[h] = projected_ref[:, width : 2 * width][:, lanes]
        values[h] = jnp.transpose(
            projected_ref[:, 2 * width :][:, lanes].astype(WIDE)
        ).astype(LOW)
    total_out[...] = jnp.zeros_like(total_out)
    scale = SCORE_SCALE * LOG2_E
    causal = lax.broadcasted_iota(jnp.int32, (tile, tile), 0) <= lax.broadcasted_iota(
        jnp.int32, (tile, tile), 1
    )

    def one_query(j, carry):
        at_query = pl.ds(pl.multiple_of(j * tile, tile), tile)
        query_docs = doc_row[:1, at_query]

        def one_key(i, status, diagonal):
            at_key = pl.ds(pl.multiple_of(i * tile, tile), tile)
            allowed = doc_column[at_key, :1] == query_docs
            if diagonal:
                allowed = allowed & causal
            result = []
            for h in range(own):
                scores = nt(keys[h, at_key], queries[h, at_query]) * scale
                masked = jnp.where(allowed, scores, MASK_FILL)
                best = jnp.max(masked, axis=0, keepdims=True)
                if diagonal:
                    top = best
                    weights = jnp.exp2(masked - top)
                    summed = jnp.sum(weights, axis=0, keepdims=True)
                    out = nn(values[h, :, at_key], weights.astype(LOW))
                else:
                    old_top, old_sum, old_out = status[h]
                    top = jnp.maximum(old_top, best)
                    weights = jnp.exp2(masked - top)
                    rescale = jnp.exp2(old_top - top)
                    summed = old_sum * rescale + jnp.sum(weights, axis=0, keepdims=True)
                    out = old_out * rescale + nn(values[h, :, at_key], weights.astype(LOW))
                result.append((top, summed, out))
            return tuple(result)

        status = one_key(j, None, True)
        status = lax.fori_loop(0, j, lambda i, now: one_key(i, now, False), status)
        for h in range(own):
            top, summed, out = status[h]
            done = out / summed
            flat_out[h * HEAD_DIM : (h + 1) * HEAD_DIM, at_query] = done
            total_out[h : h + 1, at_query] = top + jnp.log2(summed)
        return carry

    lax.fori_loop(0, rows // tile, one_query, 0)
    attended[...] = jnp.transpose(flat_out[...]).astype(LOW)
    for k in (3, 2, 1, 0):
        pair = jnp.concatenate(
            [
                attended[pl.ds(pl.multiple_of((t ^ m) * member_rows, 16), member_rows)]
                for m in (2 * k, 2 * k + 1)
            ],
            axis=0,
        )
        low_out[2 * k * member_rows : (2 * k + 2) * member_rows] = pair


def attend_team(place, first_low, triple_own, doc_column, doc_row, own):
    rows, model = first_low.shape
    width = own * HEAD_DIM
    tile = rows // 2
    return pl.pallas_call(
        lambda *refs: attend_kernel(own, tile, *refs),
        out_shape=(
            jax.ShapeDtypeStruct((rows, 3 * width), LOW),
            jax.ShapeDtypeStruct((width, rows), WIDE),
            jax.ShapeDtypeStruct((rows, width), LOW),
            jax.ShapeDtypeStruct((8, rows), WIDE),
        ),
        in_specs=[in_smem()] + [in_vmem()] * 4,
        out_specs=(in_vmem(),) * 4,
        scratch_shapes=[
            pltpu.VMEM((own, rows, HEAD_DIM), LOW),
            pltpu.VMEM((own, rows, HEAD_DIM), LOW),
            pltpu.VMEM((own, HEAD_DIM, rows), LOW),
            pltpu.VMEM((rows, width), LOW),
        ],
        compiler_params=params(),
        cost_estimate=estimate(20),
        name="attend",
    )(place, first_low, triple_own, doc_column, doc_row)


def attend_back_setup(own, projected_ref, flat_ref, back_ref, scratch):
    queries, keys, values, backs, keys_flat, backs_flat, deltas = scratch
    width = own * HEAD_DIM
    for h in range(own):
        lanes = slice(h * HEAD_DIM, (h + 1) * HEAD_DIM)
        key = projected_ref[:, width : 2 * width][:, lanes]
        back = back_ref[:, lanes]
        back_flat = jnp.transpose(back.astype(WIDE))
        queries[h] = projected_ref[:, :width][:, lanes]
        keys[h] = key
        values[h] = projected_ref[:, 2 * width :][:, lanes]
        backs[h] = back
        keys_flat[h] = jnp.transpose(key.astype(WIDE)).astype(LOW)
        backs_flat[h] = back_flat.astype(LOW)
        deltas[h : h + 1] = jnp.sum(back_flat * flat_ref[lanes], axis=0, keepdims=True)


def attend_back_tile(own, tile, i, total_ref, doc_column, doc_row, scratch, query_back):
    queries, keys, values, backs, keys_flat, backs_flat, deltas = scratch
    rows = queries.shape[1]
    scale = SCORE_SCALE * LOG2_E
    causal = lax.broadcasted_iota(jnp.int32, (tile, tile), 0) <= lax.broadcasted_iota(
        jnp.int32, (tile, tile), 1
    )
    at_key = slice(i * tile, (i + 1) * tile)
    status = [None] * own
    for j in range(i, rows // tile):
        at_query = slice(j * tile, (j + 1) * tile)
        allowed = doc_column[at_key, :1] == doc_row[:1, at_query]
        if i == j:
            allowed = allowed & causal
        for h in range(own):
            scores = nt(keys[h, at_key], queries[h, at_query]) * scale
            probs = jnp.where(allowed, jnp.exp2(scores - total_ref[h : h + 1, at_query]), 0.0)
            prob_back = nn(values[h, at_key], backs_flat[h, :, at_query])
            score_back = (probs * (prob_back - deltas[h : h + 1, at_query])).astype(LOW)
            value_part = nn(probs.astype(LOW), backs[h, at_query])
            key_part = nn(score_back, queries[h, at_query])
            query_part = nn(keys_flat[h, :, at_key], score_back)
            if i == 0:
                query_back[h, :, at_query] = query_part
            else:
                query_back[h, :, at_query] += query_part
            if status[h] is None:
                status[h] = (key_part, value_part)
            else:
                status[h] = (status[h][0] + key_part, status[h][1] + value_part)
    return jnp.concatenate(
        [status[h][0] * SCORE_SCALE for h in range(own)] + [status[h][1] for h in range(own)],
        axis=1,
    ).astype(LOW)


def attend_back_first_kernel(
    own,
    tile,
    place_ref,
    projected_ref,
    flat_ref,
    total_ref,
    doc_column,
    doc_row,
    back_ref,
    tile_out,
    query_back,
    *scratch,
):
    attend_back_setup(own, projected_ref, flat_ref, back_ref, scratch)
    for i in range(tile_out.shape[0] // tile):
        tile_out[i * tile : (i + 1) * tile] = attend_back_tile(
            own, tile, i, total_ref, doc_column, doc_row, scratch, query_back
        )


def attend_back_rest_kernel(
    own,
    tile,
    place_ref,
    projected_ref,
    flat_ref,
    total_ref,
    doc_column,
    doc_row,
    back_ref,
    tile_ref,
    earlier_ref,
    triple_ref,
    out_ref,
    *refs,
):
    outs, query_back, scratch = refs[:8], refs[8], refs[9:]
    t = place_ref[1]
    rows = projected_ref.shape[0]
    member_rows = rows // TEAM
    width = own * HEAD_DIM
    attend_back_setup(own, projected_ref, flat_ref, back_ref, scratch)
    query_back[...] = earlier_ref[...]
    done = tile_ref.shape[0]
    out_ref[:done, width:] = tile_ref[...]
    for i in range(done // tile, rows // tile):
        out_ref[i * tile : (i + 1) * tile, width:] = attend_back_tile(
            own, tile, i, total_ref, doc_column, doc_row, scratch, query_back
        )
    flat = jnp.concatenate([query_back[h] for h in range(own)], axis=0) * SCORE_SCALE
    out_ref[:, :width] = jnp.transpose(flat).astype(LOW)
    for k in (3, 2, 1, 0):
        pair = jnp.concatenate(
            [
                out_ref[pl.ds(pl.multiple_of((t ^ m) * member_rows, 16), member_rows)]
                for m in (2 * k, 2 * k + 1)
            ],
            axis=0,
        )
        product = nt(pair, triple_ref[...])
        put_terms(outs, 2 * k + 1, product[member_rows:])
        put_terms(outs, 2 * k, product[:member_rows])


def attend_back_scratch(own, rows):
    tall = pltpu.VMEM((own, rows, HEAD_DIM), LOW)
    long = pltpu.VMEM((own, HEAD_DIM, rows), LOW)
    return [tall, tall, tall, tall, long, long, pltpu.VMEM((8, rows), WIDE)]


def attend_back_first(place, projected, flat, totals, doc_column, doc_row, back, own):
    rows = projected.shape[0]
    tile = rows // 3
    return pl.pallas_call(
        lambda *refs: attend_back_first_kernel(own, tile, *refs),
        out_shape=(
            jax.ShapeDtypeStruct((2 * tile, 2 * own * HEAD_DIM), LOW),
            jax.ShapeDtypeStruct((own, HEAD_DIM, rows), WIDE),
        ),
        in_specs=[in_smem()] + [in_vmem()] * 6,
        out_specs=(in_vmem(),) * 2,
        scratch_shapes=attend_back_scratch(own, rows),
        compiler_params=params(),
        cost_estimate=estimate(12),
        name="attend_back_first",
    )(place, projected, flat, totals, doc_column, doc_row, back)


def attend_back_rest(
    place, projected, flat, totals, doc_column, doc_row, back, first_tile, query_back, triple_own, own
):
    rows = projected.shape[0]
    tile = rows // 3
    return pl.pallas_call(
        lambda *refs: attend_back_rest_kernel(own, tile, *refs),
        out_shape=(jax.ShapeDtypeStruct(projected.shape, LOW),)
        + term_shapes(rows // TEAM, triple_own.shape[0]),
        in_specs=[in_smem()] + [in_vmem()] * 9,
        out_specs=(in_vmem(),) * 9,
        scratch_shapes=[pltpu.VMEM((own, HEAD_DIM, rows), WIDE)] + attend_back_scratch(own, rows),
        compiler_params=params(),
        cost_estimate=estimate(18),
        name="attend_back_rest",
    )(
        place,
        projected,
        flat,
        totals,
        doc_column,
        doc_row,
        back,
        first_tile,
        query_back,
        triple_own,
    )


def mixing_send_kernel(place_ref, *refs):
    stack_ref, out_ref = refs
    out_ref[...] = jnp.zeros_like(out_ref)
    x = place_ref[1] // 4
    for source in range(PLANES):
        out_ref[2 * source + x] = stack_ref[source]


def mixing_send(place, stack):
    rows, width = stack.shape[1:]
    return pl.pallas_call(
        mixing_send_kernel,
        out_shape=jax.ShapeDtypeStruct((TEAM, rows, width), LOW),
        in_specs=[in_smem(), in_vmem()],
        out_specs=in_vmem(),
        compiler_params=params(),
        cost_estimate=estimate(2),
        name="mixing_send",
    )(place, stack)


def mixing_exchange(sent, core):
    rows, width = sent.shape[1:]
    return lax.dynamic_slice_in_dim(
        team_exchange(sent), core * PLANES, PLANES, 0
    ).reshape(PLANES * rows, width)


def mixing_return(sent, x):
    back = team_exchange(sent)
    return pick(back.reshape((PLANES, 2) + back.shape[1:]), x, 1)


def mix_back_kernel(place_ref, mixing_ref, attended_ref, *refs):
    pieces = refs[:PIECES]
    back_ref, mixing_out, mixed = refs[PIECES:]
    t = place_ref[1]
    member_rows = back_ref.shape[0] // TEAM
    for k in range(TEAM // 2):
        pair = jnp.concatenate([piece(pieces, 2 * k), piece(pieces, 2 * k + 1)], axis=0)
        mixed[2 * k * member_rows : (2 * k + 2) * member_rows] = pair
        back = nt(pair, mixing_ref[...]).astype(LOW)
        for m in (2 * k, 2 * k + 1):
            at = pl.ds(pl.multiple_of((t ^ m) * member_rows, 16), member_rows)
            back_ref[at] = back[(m - 2 * k) * member_rows : (m - 2 * k + 1) * member_rows]
    gradient = tn(attended_ref[...], mixed[...]).astype(LOW)
    mixing_out[...] = jnp.zeros_like(mixing_out)
    rows = gradient.shape[0] // PLANES
    for k in range(PLANES):
        mixing_out[t % 2 * PLANES + k] = gradient[k * rows : (k + 1) * rows]


def mix_back(place, mixing_own, attended, pieces):
    rows, width = attended.shape
    model = mixing_own.shape[1]
    return pl.pallas_call(
        mix_back_kernel,
        out_shape=(
            jax.ShapeDtypeStruct((rows, width), LOW),
            jax.ShapeDtypeStruct((TEAM, width // PLANES, model), LOW),
        ),
        in_specs=[in_smem()] + [in_vmem()] * (2 + PIECES),
        out_specs=(in_vmem(),) * 2,
        scratch_shapes=[pltpu.VMEM((rows, model), LOW)],
        compiler_params=params(),
        cost_estimate=estimate(5),
        name="mix_back",
    )(place, mixing_own, attended, *pieces)


def columns_kernel_of(piece_width, in_ref, out_ref, square_ref):
    total = jnp.zeros((1, 1), WIDE)
    for group in range(in_ref.shape[2] // piece_width):
        for pair in range(TEAM // 2):
            lanes = slice(group * piece_width, (group + 1) * piece_width)
            value = jnp.concatenate(
                [in_ref[2 * pair][:, lanes].astype(WIDE), in_ref[2 * pair + 1][:, lanes].astype(WIDE)],
                axis=1,
            )
            first = (group * TEAM + 2 * pair) * piece_width
            out_ref[:, first : first + 2 * piece_width] = value
            total = total + jnp.sum(value * value, axis=(0, 1), keepdims=True)
    square_ref[...] = jnp.broadcast_to(total, square_ref.shape)


def to_columns(value, piece_width):
    members, rows, width = value.shape
    out, square = pl.pallas_call(
        lambda *refs: columns_kernel_of(piece_width, *refs),
        out_shape=(
            jax.ShapeDtypeStruct((rows, members * width), WIDE),
            jax.ShapeDtypeStruct((8, 128), WIDE),
        ),
        in_specs=[in_vmem()],
        out_specs=(in_vmem(),) * 2,
        compiler_params=params(),
        cost_estimate=estimate(2),
        name="to_columns",
    )(value)
    return out, square[0, 0]


def adam_kernel(rates, factor_ref, *refs):
    number = len(rates)
    factor = factor_ref[0]
    for index in range(number):
        gradient, master, first, second = (refs[k * number + index][...] for k in range(4))
        weight, moment, square = adam_update(
            master, first, second, gradient, factor, rates[index], DECAY_RATE
        )
        refs[4 * number + 3 * index][...] = weight
        refs[4 * number + 3 * index + 1][...] = moment
        refs[4 * number + 3 * index + 2][...] = square


def adam_all(factor, gradients, masters, firsts, seconds, rates):
    steps = 6

    def block(array):
        rows, columns = array.shape
        return pl.BlockSpec((rows, columns // steps), lambda step: (0, step))

    blocks = [block(master) for master in masters]
    return pl.pallas_call(
        lambda *refs: adam_kernel(rates, *refs),
        grid=(steps,),
        out_shape=[
            jax.ShapeDtypeStruct(master.shape, WIDE) for master in masters for _ in range(3)
        ],
        in_specs=[in_smem()] + blocks * 4,
        out_specs=[one for one in blocks for _ in range(3)],
        compiler_params=params(),
        cost_estimate=estimate(10),
        name="adam_all",
    )(factor, *gradients, *masters, *firsts, *seconds)


def per_member(
    byte_rows,
    starts,
    doc_ids,
    out_cotangent,
    widen_master,
    widen_first,
    widen_second,
    triple_master,
    triple_first,
    triple_second,
    mixing_master,
    mixing_first,
    mixing_second,
    expand_master,
    expand_first,
    expand_second,
    shrink_master,
    shrink_first,
    shrink_second,
    narrow_master,
    narrow_first,
    narrow_second,
    gains_master,
    gains_first,
    gains_second,
):
    plane = lax.axis_index("z")
    x, y, core = lax.axis_index("x"), lax.axis_index("y"), lax.axis_index("c")
    t = 4 * x + 2 * y + core
    place = jnp.stack([plane, t]).astype(jnp.int32)
    byte_block, cotangent_rows = byte_rows[0], out_cotangent[0]
    bytes_dev, byte_width = byte_block.shape
    model = triple_master.shape[1] // 3
    hidden = expand_master.shape[1]
    shard = triple_master.shape[0]
    widen_shard = widen_master.shape[0]
    member_rows = 3 * bytes_dev // 16
    capacity = member_rows + member_rows // 2
    total = TEAM * member_rows
    own = HEADS // TEAM
    own_width = model // TEAM
    own_hidden = hidden // TEAM
    piece_hidden = own_hidden // PLANES

    widen_low = widen_master.astype(LOW)
    gains_low = gains_master.astype(LOW)
    gain_rows = jnp.pad(gains_low, ((0, 32 - widen_shard - 2), (0, byte_width - shard)))
    small = jnp.concatenate(
        [
            widen_low[:, :byte_width],
            gain_rows,
            widen_low[:, byte_width:],
            jnp.zeros((32 - widen_shard, byte_width), LOW),
            narrow_master.astype(LOW),
        ],
        axis=0,
    )
    small = plane_gather_small(small)
    row_buffer, chosen = pack(
        after(starts, small[1]), doc_ids, byte_block, cotangent_rows, capacity
    )
    packed = row_buffer
    row_buffer = to_plane(row_buffer)
    small, small_marks = team_gather(jnp.concatenate(small, axis=0))
    widen_full, gains_full, narrow_full = widen_whole(place, small, widen_shard, model)
    triple_own = triple_master.astype(LOW).reshape(shard, 3, TEAM, own_width)
    triple_own = jnp.transpose(triple_own, (2, 0, 1, 3)).reshape(TEAM, shard, 3 * own_width)
    triple_own = team_exchange(triple_own)
    mixing_rows = shard * model // (3 * own_width)
    triple_sent = jnp.concatenate(
        [
            after(triple_own, row_buffer, small[2], small[4]).reshape(TEAM * shard, 3 * own_width),
            mixing_master.astype(LOW).reshape(mixing_rows, 3 * own_width),
        ],
        axis=0,
    )
    gathered = lax.all_gather(triple_sent, "z", axis=0)
    triple_own = gathered[:, : TEAM * shard].reshape(model, 3 * own_width)
    mixing_stack = gathered[:, TEAM * shard :].reshape(PLANES, shard, model)
    expand_own = after(expand_master, triple_sent).astype(LOW)
    expand_own = expand_own.reshape(shard, PLANES, TEAM, piece_hidden)
    expand_own = jnp.transpose(expand_own, (2, 0, 1, 3)).reshape(TEAM, shard, own_hidden)
    expand_own = team_exchange(expand_own).reshape(TEAM * shard, own_hidden)
    shrink_low = shrink_master.astype(LOW)
    fed = lax.all_gather(
        jnp.concatenate(
            [expand_own, shrink_low[:, :own_hidden], shrink_low[:, own_hidden:]], axis=0
        ),
        "z",
        axis=0,
    )
    expand_own = fed[:, : TEAM * shard].reshape(model, own_hidden)
    shrink_own = jnp.concatenate(
        [
            fed[:, TEAM * shard : TEAM * shard + piece_hidden],
            fed[:, TEAM * shard + piece_hidden :],
        ],
        axis=2,
    ).reshape(own_hidden, model)
    entering, enter_marks = team_gather(after(row_buffer, *small_marks))
    first_low, widened, patch_rows, doc_column, doc_row, spans = enter(
        place,
        gains_full,
        widen_full,
        entering,
        capacity,
        member_rows,
    )
    mixing_sent = mixing_send(place, mixing_stack)
    mixing_own = mixing_exchange(mixing_sent, core)

    projected, flat, attended_low, totals = attend_team(
        after(place, mixing_sent), first_low, triple_own, doc_column, doc_row, own
    )
    terms, marks = team_scatter(*forward_terms(attended_low, mixing_own))
    shrink_back, upper_back, narrow_back = cotangent(
        after(place, *marks), spans, narrow_full, entering, capacity, member_rows
    )
    resid_one, second_own = add_and_norm(after(widened, shrink_back), gains_full, terms)

    second_pieces, _ = team_gather(second_own)
    second_low, active_low, expand_back, *terms = feed(
        expand_own, shrink_own, shrink_back, second_pieces
    )
    terms, marks = team_scatter(*terms)
    shrink_grad = tn(after(active_low, *marks), shrink_back).astype(LOW)
    shrink_sum = lax.psum_scatter(shrink_grad, "z", scatter_dimension=0, tiled=True)
    lower_back, mixed_own, second_gain = second_norm_back(
        after(resid_one, shrink_grad), gains_full, upper_back, terms
    )
    exit_out = []

    def leave_forward(own):
        exit_out.extend(exit_block(after(resid_one, own), narrow_full, terms))
        return exit_out[:1]

    mixed, mixed_marks = team_gather(mixed_own, None, leave_forward)
    resid_low, narrow_low = exit_out
    resid_low = team_exchange(resid_low).reshape(total, own_width)
    expand_grad = tn(after(second_low, *mixed_marks), expand_back).astype(LOW)
    expand_sum = lax.psum_scatter(expand_grad, "z", scatter_dimension=0, tiled=True)

    attend_back, mixing_grad = mix_back(
        after(place, expand_grad), mixing_own, attended_low, mixed
    )
    narrow_grad = tn(resid_low, after(narrow_back, attend_back)).astype(LOW)
    attention = (projected, flat, totals, doc_column, doc_row, attend_back)
    first_tile, query_back = attend_back_first(
        after(place, shrink_sum, narrow_grad), *attention, own
    )
    mixing_stack = mixing_return(mixing_grad, x)
    both = plane_scatter_small(
        jnp.concatenate(
            [mixing_stack, after(narrow_grad, first_tile).reshape(PLANES, shard, byte_width)],
            axis=2,
        )
    )
    mixing_sum, narrow_sum = both[:, :model], both[:, model:]
    triple_back, *terms = attend_back_rest(
        after(place, mixing_stack), *attention, first_tile, query_back, triple_own, own
    )
    first_terms, marks = team_scatter(*terms)
    triple_grad = tn(after(first_low, expand_sum, *marks), triple_back).astype(LOW)
    triple_sum = lax.psum_scatter(triple_grad, "z", scatter_dimension=0, tiled=True)
    expand_sum = team_exchange(expand_sum.reshape(TEAM, shard, own_hidden))

    back_rows, *terms = first_norm_back(
        after(place, triple_grad, mixing_sum, expand_sum),
        widened,
        gains_full,
        lower_back,
        patch_rows,
        widen_full,
        second_gain,
        narrow_low,
        first_terms,
    )
    terms, marks = team_scatter(*terms)
    widen_ready = sum(term.astype(WIDE) for term in terms)
    gains_ready = widen_ready[PLANES * widen_shard :][:8]
    widen_sum = plane_scatter_small(
        jnp.concatenate(
            [
                widen_ready[: PLANES * widen_shard].reshape(PLANES, widen_shard, model),
                jnp.broadcast_to(gains_ready, (PLANES, 8, model)),
            ],
            axis=1,
        )
    )
    gains_sum = lax.dynamic_slice(
        widen_sum[widen_shard : widen_shard + 2], (0, (plane * TEAM + t) * shard), (2, shard)
    )
    widen_sum = widen_sum[:widen_shard]
    back_rows, _ = team_gather(after(back_rows, terms[2]))
    back_buffer = from_plane(leave(place, spans, back_rows, capacity))
    new_block, grad_block = unpack(chosen, byte_block, cotangent_rows, back_buffer)

    triple_sum = team_exchange(triple_sum.reshape(TEAM, shard, 3 * own_width))
    triple_sum, triple_square = to_columns(triple_sum, own_width)
    expand_sum, expand_square = to_columns(expand_sum, piece_hidden)
    shrink_sum = shrink_sum.astype(WIDE)

    reduced = (widen_sum, triple_sum, mixing_sum, expand_sum, shrink_sum, narrow_sum, gains_sum)
    squares = triple_square + expand_square
    for gradient in (widen_sum, mixing_sum, shrink_sum, narrow_sum, gains_sum):
        squares = squares + jnp.sum(gradient * gradient)
    squares = jnp.full((8, 128), squares, WIDE)
    for bit in (CORE_BIT, Y_BIT, X_BIT, TEAM, 2 * TEAM):
        squares = squares + flip(squares, bit)
    grad_norm = jnp.sqrt(squares[0, 0])
    factor = CLIP_NORM / jnp.maximum(grad_norm, CLIP_NORM)
    rates = (
        2.0 * D_BYTE ** (-0.5),
        2.0 * D ** (-0.5),
        0.4,
        2.0 * D ** (-0.5),
        2.0 * FF ** (-0.5),
        2.0 * D ** (-0.5),
    )
    updated = adam_all(
        factor.reshape(1),
        reduced[:6],
        (widen_master, triple_master, mixing_master, expand_master, shrink_master, narrow_master),
        (widen_first, triple_first, mixing_first, expand_first, shrink_first, narrow_first),
        (widen_second, triple_second, mixing_second, expand_second, shrink_second, narrow_second),
        rates,
    )
    gains = adam_update(gains_master, gains_first, gains_second, gains_sum, factor, 0.6, 0.0)
    return (new_block[None], grad_block[None], grad_norm, *updated, *gains)


def plane_solution(mesh):
    fine = Mesh(mesh.devices.reshape(PLANES, 2, 2, 2), AXES)
    byte_spec = P(("y", "c"), ("z", "x"))
    rows_spec = P(AXES, None)
    gains_spec = P(None, AXES)
    return jax.shard_map(
        per_member,
        mesh=fine,
        in_specs=(byte_spec,) * 4 + (rows_spec,) * 18 + (gains_spec,) * 3,
        out_specs=(byte_spec,) * 2 + (P(),) + (rows_spec,) * 18 + (gains_spec,) * 3,
        check_vma=False,
    )


def solution(mesh):
    if plane_fits(mesh):
        return plane_solution(mesh)
    placed = (
        P("dp", "seq", None),
        P("dp", "seq"),
        P("dp", "seq"),
        P("dp", "seq", None),
        P(("seq", "dp"), None),
        P(("seq", "dp"), None),
        P(("seq", "dp"), None),
        P(("seq", "dp"), None),
        P(("seq", "dp"), None),
        P(("seq", "dp"), None),
        P(("seq", "dp"), None),
        P(("seq", "dp"), None),
        P(("seq", "dp"), None),
        P(("seq", "dp"), None),
        P(("seq", "dp"), None),
        P(("seq", "dp"), None),
        P(("seq", "dp"), None),
        P(("seq", "dp"), None),
        P(("seq", "dp"), None),
        P(("seq", "dp"), None),
        P(("seq", "dp"), None),
        P(("seq", "dp"), None),
        P(None, ("seq", "dp")),
        P(None, ("seq", "dp")),
        P(None, ("seq", "dp")),
    )
    return jax.shard_map(
        per_device,
        mesh=mesh,
        in_specs=placed,
        out_specs=(
            P("dp", "seq", None),
            P("dp", "seq", None),
            P(),
            P(("seq", "dp"), None),
            P(("seq", "dp"), None),
            P(("seq", "dp"), None),
            P(("seq", "dp"), None),
            P(("seq", "dp"), None),
            P(("seq", "dp"), None),
            P(("seq", "dp"), None),
            P(("seq", "dp"), None),
            P(("seq", "dp"), None),
            P(("seq", "dp"), None),
            P(("seq", "dp"), None),
            P(("seq", "dp"), None),
            P(("seq", "dp"), None),
            P(("seq", "dp"), None),
            P(("seq", "dp"), None),
            P(("seq", "dp"), None),
            P(("seq", "dp"), None),
            P(("seq", "dp"), None),
            P(None, ("seq", "dp")),
            P(None, ("seq", "dp")),
            P(None, ("seq", "dp")),
        ),
        check_vma=False,
    )
```

```python
import jax
import jax.numpy as jnp
from jax import lax
from jax.experimental import pallas as pl
from jax.experimental.pallas import tpu as pltpu
from jax.sharding import Mesh, PartitionSpec as P

D_BYTE = 768
D = 1536
HEADS = 24
HEAD_DIM = 64
FF = 6144
STEP = 10


NORM_EPS = 1e-05
SCORE_SCALE = 0.125
MASK_FILL = -1e30
BETA_ONE = 0.9
BETA_TWO = 0.95
ADAM_EPS = 1e-08
DECAY_RATE = 0.1
CLIP_NORM = 1.0


def prefix(part, axis, combine, identity):
    place = lax.axis_index(axis)
    gathered = lax.all_gather(part, axis)
    state = jnp.zeros_like(part) + jnp.asarray(identity, part.dtype)

    def one(hop, state):
        return combine(state, lax.dynamic_index_in_dim(gathered, hop, 0, False))

    return lax.fori_loop(0, place, one, state)


def normalize(values, gain):
    inverse = lax.rsqrt(jnp.mean(values * values, axis=-1, keepdims=True) + NORM_EPS)
    return values * inverse * gain


def add_counts(earlier, later):
    return earlier + later


def block_rows(amount):
    for option in (1024, 768, 512, 384, 256):
        if amount >= option and amount % option == 0:
            return option
    return amount


def spread_positions(first_row, amount, patch_dev, devices):
    whole_rows = first_row + jnp.arange(amount, dtype=jnp.int32)
    return whole_rows % patch_dev * devices + whole_rows // patch_dev


def make_attend(queries, patch_docs, patch_pos, patch_dev, devices):

    def attend(running, shards, offset):
        piece_keys, piece_values, piece_docs = shards
        amount = piece_keys.shape[0]
        span_rows = block_rows(amount)
        number = amount // span_rows
        key_blocks = piece_keys.reshape(number, span_rows, HEADS, HEAD_DIM)
        value_blocks = piece_values.reshape(number, span_rows, HEADS, HEAD_DIM)
        doc_blocks = piece_docs.reshape(number, span_rows)
        firsts = span_rows * jnp.arange(number, dtype=jnp.int32)

        def advance(status, section):
            block_keys, block_values, block_docs, block_first = section
            running_top, running_sum, running_out = status
            scores = (
                jnp.einsum("phd,khd->hpk", queries, block_keys, preferred_element_type=jnp.float32)
                * SCORE_SCALE
            )
            key_pos = spread_positions(block_first, span_rows, patch_dev, devices)
            allowed = (patch_docs[:, None] == block_docs[None, :]) & (
                key_pos[None, :] <= patch_pos[:, None]
            )
            masked = jnp.where(allowed[None], scores, MASK_FILL)
            new_top = jnp.maximum(running_top, jnp.max(masked, axis=-1))
            weights = jnp.where(allowed[None], jnp.exp(masked - new_top[..., None]), 0.0)
            rescale = jnp.exp(running_top - new_top)
            running_sum = running_sum * rescale + jnp.sum(weights, axis=-1)
            running_out = running_out * rescale[..., None] + jnp.einsum(
                "hpk,khd->hpd",
                weights.astype(jnp.bfloat16),
                block_values,
                preferred_element_type=jnp.float32,
            )
            return ((new_top, running_sum, running_out), None)

        running, _ = lax.scan(advance, running, (key_blocks, value_blocks, doc_blocks, firsts))
        return running

    return attend


def outer_sum(left, right):
    return jnp.einsum("pi,pj->ij", left, right, preferred_element_type=jnp.float32)


def back_product(grads, weight):
    return jnp.einsum("pj,ij->pi", grads, weight, preferred_element_type=jnp.float32)


def adam_update(master, first_old, second_old, gradient, clip_factor, learn_rate, weight_decay):
    clipped = gradient * clip_factor
    moment = BETA_ONE * first_old + (1.0 - BETA_ONE) * clipped
    square = BETA_TWO * second_old + (1.0 - BETA_TWO) * clipped * clipped
    corrected = (
        moment / (1.0 - BETA_ONE**STEP) / (jnp.sqrt(square / (1.0 - BETA_TWO**STEP)) + ADAM_EPS)
    )
    weight = master - learn_rate * (corrected + weight_decay * master)
    return (weight, moment, square)


def per_device(
    byte_rows,
    starts,
    doc_ids,
    out_cotangent,
    widen_master,
    widen_first,
    widen_second,
    triple_master,
    triple_first,
    triple_second,
    mixing_master,
    mixing_first,
    mixing_second,
    expand_master,
    expand_first,
    expand_second,
    shrink_master,
    shrink_first,
    shrink_second,
    narrow_master,
    narrow_first,
    narrow_second,
    gains_master,
    gains_first,
    gains_second,
):
    widen_full, triple_full, mixing_full, expand_full, shrink_full, narrow_full, gains_full = (
        lax.all_gather(widen_master.astype(jnp.bfloat16), ("seq", "dp"), axis=0, tiled=True),
        lax.all_gather(triple_master.astype(jnp.bfloat16), ("seq", "dp"), axis=0, tiled=True),
        lax.all_gather(mixing_master.astype(jnp.bfloat16), ("seq", "dp"), axis=0, tiled=True),
        lax.all_gather(expand_master.astype(jnp.bfloat16), ("seq", "dp"), axis=0, tiled=True),
        lax.all_gather(shrink_master.astype(jnp.bfloat16), ("seq", "dp"), axis=0, tiled=True),
        lax.all_gather(narrow_master.astype(jnp.bfloat16), ("seq", "dp"), axis=0, tiled=True),
        lax.all_gather(gains_master.astype(jnp.bfloat16), ("seq", "dp"), axis=1, tiled=True),
    )
    gain_one = gains_full[0].astype(jnp.float32)
    gain_two = gains_full[1].astype(jnp.float32)
    devices = lax.axis_size("seq")
    seq_place = lax.axis_index("seq")
    byte_block = byte_rows[0]
    start_flags = starts[0]
    doc_local = doc_ids[0]
    cotangent_rows = out_cotangent[0]
    byte_width = byte_block.shape[1]
    patch_dev = 3 * byte_block.shape[0] // 16
    capacity = patch_dev + patch_dev // 2
    slot_count = (capacity + devices - 2) // devices + 1
    buffer_rows = devices * slot_count
    amount = jnp.sum(start_flags)
    offset = prefix(amount, "seq", add_counts, jnp.int32(0))
    ranking = jnp.cumsum(start_flags) - start_flags
    patch_index = offset + ranking
    owners = patch_index % devices
    local_row = patch_index // devices
    slot_index = local_row - offset // devices
    target_slot = jnp.where(start_flags == 1, owners * slot_count + slot_index, buffer_rows)
    send_rows = (
        jnp.zeros((buffer_rows, byte_width), jnp.bfloat16)
        .at[target_slot]
        .set(byte_block, mode="drop")
    )
    send_meta = (
        jnp.full((buffer_rows, 2), patch_dev, jnp.int32)
        .at[target_slot]
        .set(jnp.stack([local_row, doc_local], axis=-1), mode="drop")
    )
    send_grad = (
        jnp.zeros((buffer_rows, byte_width), jnp.bfloat16)
        .at[target_slot]
        .set(cotangent_rows, mode="drop")
    )
    arrived_rows, arrived_meta = (
        lax.all_to_all(send_rows, "seq", split_axis=0, concat_axis=0, tiled=True),
        lax.all_to_all(send_meta, "seq", split_axis=0, concat_axis=0, tiled=True),
    )
    target = arrived_meta[:, 0]
    valid_slot = target < patch_dev
    patch_rows = (
        jnp.zeros((patch_dev, byte_width), jnp.bfloat16).at[target].set(arrived_rows, mode="drop")
    )
    patch_docs = jnp.zeros((patch_dev,), jnp.int32).at[target].set(arrived_meta[:, 1], mode="drop")
    patch_pos = seq_place + devices * jnp.arange(patch_dev, dtype=jnp.int32)
    widened = jnp.dot(patch_rows, widen_full, preferred_element_type=jnp.float32)
    model_width = widened.shape[1]
    first_low = normalize(widened, gain_one).astype(jnp.bfloat16)
    projected = jnp.dot(first_low, triple_full, preferred_element_type=jnp.float32).astype(
        jnp.bfloat16
    )
    queries = projected[:, :model_width].reshape(patch_dev, HEADS, HEAD_DIM)
    key_rows = projected[:, model_width : 2 * model_width]
    value_rows = projected[:, 2 * model_width :]
    initial = (
        jnp.full((HEADS, patch_dev), MASK_FILL, jnp.float32),
        jnp.zeros((HEADS, patch_dev), jnp.float32),
        jnp.zeros((HEADS, patch_dev, HEAD_DIM), jnp.float32),
    )
    attend = make_attend(queries, patch_docs, patch_pos, patch_dev, devices)
    running = attend(
        initial,
        (
            lax.all_gather(key_rows, "seq", axis=0, tiled=True),
            lax.all_gather(value_rows, "seq", axis=0, tiled=True),
            lax.all_gather(patch_docs, "seq", axis=0, tiled=True),
        ),
        jnp.int32(0),
    )
    running_top, running_sum, running_out = running
    attended = running_out / running_sum[..., None]
    log_total = running_top + jnp.log(running_sum)
    attended_low = (
        jnp.transpose(attended, (1, 0, 2)).reshape(patch_dev, model_width).astype(jnp.bfloat16)
    )
    resid_one = widened + jnp.dot(attended_low, mixing_full, preferred_element_type=jnp.float32)
    second_low = normalize(resid_one, gain_two).astype(jnp.bfloat16)
    expanded = jnp.dot(second_low, expand_full, preferred_element_type=jnp.float32)
    active_low = jax.nn.gelu(expanded).astype(jnp.bfloat16)
    resid_two = resid_one + jnp.dot(active_low, shrink_full, preferred_element_type=jnp.float32)
    resid_low = resid_two.astype(jnp.bfloat16)
    narrow_low = jnp.dot(resid_low, narrow_full, preferred_element_type=jnp.float32).astype(
        jnp.bfloat16
    )
    returned = jnp.where(valid_slot[:, None], jnp.take(narrow_low, target, axis=0, mode="clip"), 0)
    back_rows = lax.all_to_all(returned, "seq", split_axis=0, concat_axis=0, tiled=True)
    added = jnp.take(back_rows, target_slot, axis=0, mode="clip").astype(jnp.float32)
    new_block = byte_block.astype(jnp.float32) + jnp.where(start_flags[:, None] == 1, added, 0.0)
    arrived_grad = lax.all_to_all(send_grad, "seq", split_axis=0, concat_axis=0, tiled=True)
    narrow_back = (
        jnp.zeros((patch_dev, byte_width), jnp.bfloat16).at[target].set(arrived_grad, mode="drop")
    )
    narrow_grad = outer_sum(resid_low, narrow_back)
    upper_back = back_product(narrow_back, narrow_full)
    shrink_back = upper_back.astype(jnp.bfloat16)
    shrink_grad = outer_sum(active_low, shrink_back)
    active_back = back_product(shrink_back, shrink_full)
    _, gelu_pull = jax.vjp(jax.nn.gelu, expanded)
    expand_back = gelu_pull(active_back)[0].astype(jnp.bfloat16)
    expand_grad = outer_sum(second_low, expand_back)
    second_back = back_product(expand_back, expand_full)
    _, second_pull = jax.vjp(normalize, resid_one, gain_two)
    second_part, second_gain = second_pull(second_back)
    lower_back = upper_back + second_part
    mixed_back = lower_back.astype(jnp.bfloat16)
    mixing_grad = outer_sum(attended_low, mixed_back)
    attend_back = (
        back_product(mixed_back, mixing_full)
        .astype(jnp.bfloat16)
        .reshape(patch_dev, HEADS, HEAD_DIM)
    )
    delta_rows = jnp.einsum("phd,hpd->hp", attend_back.astype(jnp.float32), attended)
    all_keys, all_values, all_docs = (
        lax.all_gather(key_rows, "seq", axis=0, tiled=True),
        lax.all_gather(value_rows, "seq", axis=0, tiled=True),
        lax.all_gather(patch_docs, "seq", axis=0, tiled=True),
    )
    total_keys = all_keys.shape[0]
    span_rows = block_rows(total_keys)
    number = total_keys // span_rows
    key_blocks = all_keys.reshape(number, span_rows, HEADS, HEAD_DIM)
    value_blocks = all_values.reshape(number, span_rows, HEADS, HEAD_DIM)
    doc_blocks = all_docs.reshape(number, span_rows)
    firsts = span_rows * jnp.arange(number, dtype=jnp.int32)
    query_start = jnp.zeros((patch_dev, HEADS, HEAD_DIM), jnp.float32)

    def backstep(query_back, section):
        block_keys, block_values, block_docs, block_first = section
        scores = (
            jnp.einsum("phd,khd->hpk", queries, block_keys, preferred_element_type=jnp.float32)
            * SCORE_SCALE
        )
        key_pos = spread_positions(block_first, span_rows, patch_dev, devices)
        allowed = (patch_docs[:, None] == block_docs[None, :]) & (
            key_pos[None, :] <= patch_pos[:, None]
        )
        probs = jnp.where(allowed[None], jnp.exp(scores - log_total[..., None]), 0.0)
        prob_back = jnp.einsum(
            "phd,khd->hpk", attend_back, block_values, preferred_element_type=jnp.float32
        )
        score_back = (probs * (prob_back - delta_rows[..., None])).astype(jnp.bfloat16)
        query_back = (
            query_back
            + jnp.einsum("hpk,khd->phd", score_back, block_keys, preferred_element_type=jnp.float32)
            * SCORE_SCALE
        )
        keys_part = (
            jnp.einsum("hpk,phd->khd", score_back, queries, preferred_element_type=jnp.float32)
            * SCORE_SCALE
        )
        values_part = jnp.einsum(
            "hpk,phd->khd",
            probs.astype(jnp.bfloat16),
            attend_back,
            preferred_element_type=jnp.float32,
        )
        return (
            query_back,
            (
                keys_part.reshape(span_rows, model_width),
                values_part.reshape(span_rows, model_width),
            ),
        )

    query_back, (keys_back, values_back) = lax.scan(
        backstep, query_start, (key_blocks, value_blocks, doc_blocks, firsts)
    )
    keys_own, values_own = (
        lax.psum_scatter(
            keys_back.reshape(total_keys, model_width).astype(jnp.bfloat16),
            "seq",
            scatter_dimension=0,
            tiled=True,
        ).astype(jnp.float32),
        lax.psum_scatter(
            values_back.reshape(total_keys, model_width).astype(jnp.bfloat16),
            "seq",
            scatter_dimension=0,
            tiled=True,
        ).astype(jnp.float32),
    )
    triple_back = jnp.concatenate(
        [query_back.reshape(patch_dev, model_width), keys_own, values_own], axis=1
    ).astype(jnp.bfloat16)
    triple_grad = outer_sum(first_low, triple_back)
    first_back = back_product(triple_back, triple_full)
    _, first_pull = jax.vjp(normalize, widened, gain_one)
    first_part, first_gain = first_pull(first_back)
    base_low = (lower_back + first_part).astype(jnp.bfloat16)
    widen_grad = outer_sum(patch_rows, base_low)
    patch_back = back_product(base_low, widen_full).astype(jnp.bfloat16)
    grad_slots = jnp.where(
        valid_slot[:, None], jnp.take(patch_back, target, axis=0, mode="clip"), 0
    )
    grad_rows = lax.all_to_all(grad_slots, "seq", split_axis=0, concat_axis=0, tiled=True)
    coming = jnp.take(grad_rows, target_slot, axis=0, mode="clip").astype(jnp.float32)
    grad_block = cotangent_rows.astype(jnp.float32) + jnp.where(
        start_flags[:, None] == 1, coming, 0.0
    )
    gains_grad = jnp.stack([first_gain, second_gain], axis=0)
    reduced = (
        lax.psum_scatter(widen_grad, ("seq", "dp"), scatter_dimension=0, tiled=True),
        lax.psum_scatter(triple_grad, ("seq", "dp"), scatter_dimension=0, tiled=True),
        lax.psum_scatter(mixing_grad, ("seq", "dp"), scatter_dimension=0, tiled=True),
        lax.psum_scatter(expand_grad, ("seq", "dp"), scatter_dimension=0, tiled=True),
        lax.psum_scatter(shrink_grad, ("seq", "dp"), scatter_dimension=0, tiled=True),
        lax.psum_scatter(narrow_grad, ("seq", "dp"), scatter_dimension=0, tiled=True),
        lax.psum_scatter(gains_grad, ("seq", "dp"), scatter_dimension=1, tiled=True),
    )
    local_squares = jnp.float32(0.0)
    for member in reduced:
        local_squares = local_squares + jnp.sum(member * member)
    norm_squared = lax.psum(local_squares, ("seq", "dp"))
    grad_norm = jnp.sqrt(norm_squared)
    factor = CLIP_NORM / jnp.maximum(grad_norm, CLIP_NORM)
    masters = (
        widen_master,
        triple_master,
        mixing_master,
        expand_master,
        shrink_master,
        narrow_master,
        gains_master,
    )
    firsts_old = (
        widen_first,
        triple_first,
        mixing_first,
        expand_first,
        shrink_first,
        narrow_first,
        gains_first,
    )
    seconds_old = (
        widen_second,
        triple_second,
        mixing_second,
        expand_second,
        shrink_second,
        narrow_second,
        gains_second,
    )
    rates = (
        2.0 * D_BYTE ** (-0.5),
        2.0 * D ** (-0.5),
        0.4,
        2.0 * D ** (-0.5),
        2.0 * FF ** (-0.5),
        2.0 * D ** (-0.5),
        0.6,
    )
    decays = (DECAY_RATE, DECAY_RATE, DECAY_RATE, DECAY_RATE, DECAY_RATE, DECAY_RATE, 0.0)
    updates = [
        adam_update(
            masters[index],
            firsts_old[index],
            seconds_old[index],
            reduced[index],
            factor,
            rates[index],
            decays[index],
        )
        for index in range(7)
    ]
    return (
        new_block.astype(jnp.bfloat16)[None],
        grad_block.astype(jnp.bfloat16)[None],
        grad_norm,
        updates[0][0],
        updates[0][1],
        updates[0][2],
        updates[1][0],
        updates[1][1],
        updates[1][2],
        updates[2][0],
        updates[2][1],
        updates[2][2],
        updates[3][0],
        updates[3][1],
        updates[3][2],
        updates[4][0],
        updates[4][1],
        updates[4][2],
        updates[5][0],
        updates[5][1],
        updates[5][2],
        updates[6][0],
        updates[6][1],
        updates[6][2],
    )


PLANES = 4
TEAM = 8
CORE_BIT, Y_BIT, X_BIT = 1, 2, 4
AXES = ("z", "x", "y", "c")
TEAM_AXES = ("x", "y", "c")
LOW = jnp.bfloat16
WIDE = jnp.float32
VMEM_LIMIT = 56 * 1024 * 1024
LOG2_E = 1.4426950408889634
GELU_A = 0.7978845608028654
GELU_B = 0.044715


def plane_fits(mesh):
    return mesh.shape["seq"] == 2 * PLANES and mesh.shape["dp"] == PLANES


def flip(value, bit):
    pairs = [(place, place ^ bit) for place in range(PLANES * TEAM)]
    return lax.ppermute(value, AXES, pairs)


def shift_plane(value, hop):
    pairs = [
        (plane * TEAM + t, (plane + hop) % PLANES * TEAM + t)
        for plane in range(PLANES)
        for t in range(TEAM)
    ]
    return lax.ppermute(value, AXES, pairs)


SEQUENCE_OF_PLANE = (2, 0, 1, 3)


def source_of(plane, t):
    return (plane + t // 2 % 2 + 2 * (t % 2) + 2 * PLANES) % PLANES * 2 + t // 4


def byte_pairs():
    return [
        (source_of(plane, t) * PLANES + SEQUENCE_OF_PLANE[plane], plane * TEAM + t)
        for plane in range(PLANES)
        for t in range(TEAM)
    ]


def to_plane(value):
    return lax.ppermute(value, AXES, byte_pairs())


def from_plane(value):
    return lax.ppermute(value, AXES, [(there, here) for here, there in byte_pairs()])


def team_gather(block, cut=None, before_relay=lambda own: ()):
    cut = block.shape[0] // 2 if cut is None else cut
    from_x = flip(block, X_BIT)
    from_y = flip(block, Y_BIT)
    from_core = flip(block, CORE_BIT)
    from_x, from_y = after((from_x, from_y), *before_relay(from_core))
    to_x, to_y = from_y[:cut], from_x[cut:]
    upper = flip(to_x, X_BIT)
    lower = flip(to_y, Y_BIT)
    y_core = flip(from_y, CORE_BIT)
    x_core = flip(from_x, CORE_BIT)
    return [
        block,
        from_core,
        from_y,
        y_core,
        from_x,
        x_core,
        upper,
        lower,
        flip(upper, CORE_BIT),
        flip(lower, CORE_BIT),
    ], (to_x, to_y)


PIECES = 10


def piece(refs, m):
    if m < 6:
        return refs[m][...]
    return jnp.concatenate([refs[2 * m - 6][...], refs[2 * m - 5][...]], axis=0)


def team_scatter(far_send, far_keep, x_send, x_keep, y_send, y_keep, own_send, own_keep):
    def pair(send, keep):
        return keep.astype(WIDE) + flip(send, CORE_BIT).astype(WIDE)

    far = pair(far_send, far_keep).astype(LOW)
    cut = far.shape[0] // 2
    upper = flip(far[:cut], X_BIT).astype(WIDE)
    lower = flip(far[cut:], Y_BIT).astype(WIDE)
    to_x, to_y = pair(x_send, x_keep), pair(y_send, y_keep)
    to_x = jnp.concatenate([to_x[:cut], to_x[cut:] + lower], axis=0).astype(LOW)
    to_y = jnp.concatenate([to_y[:cut] + upper, to_y[cut:]], axis=0).astype(LOW)
    terms = (own_keep, flip(own_send, CORE_BIT), flip(to_x, X_BIT), flip(to_y, Y_BIT))
    return terms, (to_x, to_y)


def put_terms(outs, m, value):
    outs[7 - m][...] = value.astype(LOW)


def term_shapes(rows, width):
    return (jax.ShapeDtypeStruct((rows, width), LOW),) * TEAM


def add_terms(refs, lanes=slice(None)):
    total = refs[0][:, lanes].astype(WIDE)
    for ref in refs[1:]:
        total = total + ref[:, lanes].astype(WIDE)
    return total


def after(value, *earlier):
    return lax.optimization_barrier((value,) + earlier)[0]


def plane_gather_small(block):
    return [block] + [shift_plane(block, hop) for hop in (1, 2, 3)]


def plane_scatter_small(stack):
    back = lax.all_to_all(stack.astype(LOW), "z", split_axis=0, concat_axis=0, tiled=True)
    return jnp.sum(back.astype(WIDE), axis=0)


def team_exchange(value):
    return lax.all_to_all(value, TEAM_AXES, split_axis=0, concat_axis=0, tiled=True)


def pick(value, place, axis):
    return lax.dynamic_index_in_dim(value, place, axis, False)


def in_vmem():
    return pl.BlockSpec(memory_space=pltpu.VMEM)


def in_smem():
    return pl.BlockSpec(memory_space=pltpu.SMEM)


def params():
    return pltpu.CompilerParams(vmem_limit_bytes=VMEM_LIMIT)


def estimate(microseconds):
    return pl.CostEstimate(
        flops=int(microseconds * 8e8), bytes_accessed=int(microseconds * 2e6), transcendentals=0
    )


def nn(left, right):
    return lax.dot_general(left, right, (((1,), (0,)), ((), ())), preferred_element_type=WIDE)


def nt(left, right):
    return lax.dot_general(left, right, (((1,), (1,)), ((), ())), preferred_element_type=WIDE)


def tn(left, right):
    return lax.dot_general(left, right, (((0,), (0,)), ((), ())), preferred_element_type=WIDE)


def slot_matrix(flags, slots):
    amount = flags.shape[1]
    row = lax.broadcasted_iota(jnp.int32, (amount, amount), 0)
    column = lax.broadcasted_iota(jnp.int32, (amount, amount), 1)
    before = jnp.where(row < column, 1.0, 0.0).astype(LOW)
    rank = nn(jnp.broadcast_to(flags, (8, amount)).astype(LOW), before)[:1]
    rank = jnp.where(flags > 0.5, rank, -1.0)
    slot = lax.broadcasted_iota(jnp.int32, (slots, amount), 0).astype(WIDE)
    return jnp.where(slot == rank, 1.0, 0.0).astype(LOW)


def pack_kernel(starts_ref, docs_ref, rows_ref, cotangent_ref, rows_out, chosen_out):
    capacity = chosen_out.shape[0]
    width = rows_out.shape[1]
    flags = starts_ref[...].astype(WIDE)
    chosen = slot_matrix(flags, 384)
    amount = jnp.sum(flags)
    docs = nt(jnp.broadcast_to(docs_ref[...].astype(WIDE), (16, flags.shape[1])).astype(LOW), chosen)
    docs = jnp.concatenate([docs, jnp.zeros((16, width - 384), WIDE)], axis=1)
    row = lax.broadcasted_iota(jnp.int32, (16, width), 0)
    high = jnp.floor(amount * 0.5)
    meta = jnp.where(row == 0, docs, jnp.where(row == 1, high, amount - 2.0 * high))
    chosen = chosen[:capacity]
    chosen_out[...] = chosen
    rows_out[:16] = meta.astype(LOW)
    rows_out[16 : 16 + capacity] = nn(chosen, rows_ref[...]).astype(LOW)
    rows_out[16 + capacity :] = nn(chosen, cotangent_ref[...]).astype(LOW)


def pack(starts, docs, rows, cotangent_rows, capacity):
    amount, width = rows.shape
    return pl.pallas_call(
        pack_kernel,
        out_shape=(
            jax.ShapeDtypeStruct((2 * capacity + 16, width), LOW),
            jax.ShapeDtypeStruct((capacity, amount), LOW),
        ),
        in_specs=[in_vmem()] * 4,
        out_specs=(in_vmem(), in_vmem()),
        compiler_params=params(),
        cost_estimate=estimate(5),
        name="pack",
    )(starts, docs, rows, cotangent_rows)


def unpack_kernel(chosen_ref, rows_ref, cotangent_ref, back_ref, rows_out, cotangent_out):
    width = rows_ref.shape[1]
    added = tn(chosen_ref[...], back_ref[...])
    rows_out[...] = (rows_ref[...].astype(WIDE) + added[:, :width]).astype(LOW)
    cotangent_out[...] = (cotangent_ref[...].astype(WIDE) + added[:, width:]).astype(LOW)


def unpack(chosen, rows, cotangent_rows, back):
    return pl.pallas_call(
        unpack_kernel,
        out_shape=(jax.ShapeDtypeStruct(rows.shape, LOW),) * 2,
        in_specs=[in_vmem()] * 4,
        out_specs=(in_vmem(),) * 2,
        compiler_params=params(),
        cost_estimate=estimate(5),
        name="unpack",
    )(chosen, rows, cotangent_rows, back)


def window_matrix(first, amount, capacity):
    target = lax.broadcasted_iota(jnp.int32, (capacity + 16, capacity), 0)
    source = lax.broadcasted_iota(jnp.int32, (capacity + 16, capacity), 1)
    moved = (target == source + first % 16) & (source < amount)
    return jnp.where(moved, 1.0, 0.0).astype(LOW)


def widen_kernel(place_ref, *refs):
    pieces = refs[:PIECES]
    widen_out, gains_out, narrow_out = refs[PIECES : PIECES + 3]
    widen_wide, gains = refs[PIECES + 3 :]
    plane, t = place_ref[0], place_ref[1]
    shards = PLANES * TEAM
    shard = widen_out.shape[0] // shards
    model = widen_out.shape[1]
    width = model // 2
    gain_shard = model // shards
    for m in range(TEAM):
        low = piece(pieces, m)
        here = low.astype(WIDE)
        for hop in range(PLANES):
            place = (plane - hop + PLANES) % PLANES * TEAM + (t ^ m)
            at = pl.ds(pl.multiple_of(place * shard, 8), shard)
            base = hop * (64 + gain_shard)
            narrow_at = pl.ds(pl.multiple_of(place * gain_shard, 16), gain_shard)
            narrow_out[narrow_at] = low[base + 64 : base + 64 + gain_shard]
            widen_wide[at, :width] = here[base : base + shard]
            widen_wide[at, width:] = here[base + 32 : base + 32 + shard]
            gains[0, pl.ds(place, 1)] = here[base + shard : base + shard + 1, :128]
            gains[1, pl.ds(place, 1)] = here[base + shard + 1 : base + shard + 2, :128]
    widen_out[...] = widen_wide[...].astype(LOW)
    column = lax.broadcasted_iota(jnp.int32, (shards, model), 1)
    owner = lax.broadcasted_iota(jnp.int32, (shards, model), 0)
    owned = (column >= owner * gain_shard) & (column < (owner + 1) * gain_shard)
    inside = jnp.sum(jnp.where(owned, column - owner * gain_shard, 0).astype(WIDE), axis=0, keepdims=True)
    row = lax.broadcasted_iota(jnp.int32, (128, model), 0).astype(WIDE)
    owned = jnp.where(owned, 1.0, 0.0).astype(LOW)
    for k in range(2):
        spread = tn(gains[k].astype(LOW), owned)
        line = jnp.sum(jnp.where(row == inside, spread, 0.0), axis=0, keepdims=True)
        gains_out[k * 8 : k * 8 + 8] = jnp.broadcast_to(line, (8, model))


def widen_whole(place, pieces, shard, model):
    return pl.pallas_call(
        widen_kernel,
        out_shape=(
            jax.ShapeDtypeStruct((shard * PLANES * TEAM, model), LOW),
            jax.ShapeDtypeStruct((16, model), WIDE),
            jax.ShapeDtypeStruct((model, pieces[0].shape[1]), LOW),
        ),
        in_specs=[in_smem()] + [in_vmem()] * PIECES,
        out_specs=(in_vmem(),) * 3,
        scratch_shapes=[
            pltpu.VMEM((shard * PLANES * TEAM, model), WIDE),
            pltpu.VMEM((2, PLANES * TEAM, 128), WIDE),
        ],
        compiler_params=params(),
        cost_estimate=estimate(5),
        name="widen_whole",
    )(place, *pieces)


def enter_kernel(capacity, place_ref, gains_ref, widen_ref, *refs):
    pieces = refs[:PIECES]
    low_out, own_wide, own_rows, doc_column, doc_row, spans = refs[PIECES : PIECES + 6]
    rows, docs = refs[PIECES + 6 :]
    plane, t = place_ref[0], place_ref[1]
    member_rows = own_rows.shape[0]
    total = low_out.shape[0]

    metas = [pieces[m][:16] for m in range(6)] + [pieces[6][:16], pieces[8][:16]]
    blocks = [piece(pieces, m)[16 : 16 + capacity] for m in range(TEAM)]
    amounts, sources = [], []
    for m in range(TEAM):
        meta = metas[m].astype(WIDE)
        row = lax.broadcasted_iota(jnp.int32, meta.shape, 0)
        lane = lax.broadcasted_iota(jnp.int32, meta.shape, 1)
        picked = jnp.where(lane == 0, jnp.where(row == 1, 2.0 * meta, jnp.where(row == 2, meta, 0.0)), 0.0)
        amounts.append(jnp.sum(picked).astype(jnp.int32))
        sources.append(source_of(plane, t ^ m))
    firsts = []
    for m in range(TEAM):
        first = jnp.int32(0)
        for other in range(TEAM):
            if other != m:
                first = first + jnp.where(sources[other] < sources[m], amounts[other], 0)
        firsts.append(first)
        spans[m] = first
        spans[TEAM + m] = amounts[m]

    rows[...] = jnp.zeros_like(rows)
    docs[...] = jnp.zeros_like(docs)
    for m in range(TEAM):
        moving = window_matrix(firsts[m], amounts[m], capacity)
        at = pl.ds(pl.multiple_of(firsts[m] // 16 * 16, 16), capacity + 16)
        rows[at] = rows[at] + nn(moving, blocks[m]).astype(LOW)
        names = metas[m][:1, :384]
        names = jnp.broadcast_to(names, (128, 384))[:, :capacity]
        docs[at] = docs[at] + nt(moving, names)

    doc_column[...] = docs[:total]
    select = jnp.where(lax.broadcasted_iota(jnp.int32, (8, 128), 1) == 0, 1.0, 0.0).astype(LOW)
    doc_row[...] = nt(select, docs[:total].astype(LOW))
    own_rows[...] = rows[pl.ds(pl.multiple_of(t * member_rows, 16), member_rows)]

    def one(k, carry):
        at = pl.ds(pl.multiple_of(k * 2 * member_rows, 16), 2 * member_rows)
        wide = nn(rows[at], widen_ref[...])
        inverse = lax.rsqrt(jnp.mean(wide * wide, axis=-1, keepdims=True) + NORM_EPS)
        low_out[at] = (wide * inverse * gains_ref[:1]).astype(LOW)
        return carry

    lax.fori_loop(0, TEAM // 2, one, 0)
    own_wide[...] = nn(own_rows[...], widen_ref[...])


def enter(place, gains, widen_full, pieces, capacity, member_rows):
    width, model = widen_full.shape
    total = member_rows * TEAM
    padded = total + capacity + 16
    return pl.pallas_call(
        lambda *refs: enter_kernel(capacity, *refs),
        out_shape=(
            jax.ShapeDtypeStruct((total, model), LOW),
            jax.ShapeDtypeStruct((member_rows, model), WIDE),
            jax.ShapeDtypeStruct((member_rows, width), LOW),
            jax.ShapeDtypeStruct((total, 128), WIDE),
            jax.ShapeDtypeStruct((8, total), WIDE),
            jax.ShapeDtypeStruct((2 * TEAM,), jnp.int32),
        ),
        in_specs=[in_smem(), in_vmem(), in_vmem()] + [in_vmem()] * PIECES,
        out_specs=(in_vmem(),) * 5 + (in_smem(),),
        scratch_shapes=[
            pltpu.VMEM((padded, width), LOW),
            pltpu.VMEM((padded, 128), WIDE),
        ],
        compiler_params=params(),
        cost_estimate=estimate(14),
        name="enter",
    )(place, gains, widen_full, *pieces)


def cotangent_kernel(capacity, place_ref, spans_ref, narrow_ref, *refs):
    pieces = refs[:PIECES]
    low_out, own_wide, all_rows = refs[PIECES : PIECES + 3]
    (rows,) = refs[PIECES + 3 :]
    t = place_ref[1]
    member_rows = own_wide.shape[0]
    rows[...] = jnp.zeros_like(rows)
    for m in range(TEAM):
        first = spans_ref[m]
        moving = window_matrix(first, spans_ref[TEAM + m], capacity)
        at = pl.ds(pl.multiple_of(first // 16 * 16, 16), capacity + 16)
        rows[at] = rows[at] + nn(moving, piece(pieces, m)[16 + capacity :]).astype(LOW)
    all_rows[...] = rows[: all_rows.shape[0]]

    def one(k, carry):
        first = pl.multiple_of((t ^ (2 * k)) * member_rows, 16)
        second = pl.multiple_of((t ^ (2 * k + 1)) * member_rows, 16)
        here = jnp.concatenate(
            [rows[pl.ds(first, member_rows)], rows[pl.ds(second, member_rows)]], axis=0
        )
        at = pl.ds(pl.multiple_of(k * 2 * member_rows, 16), 2 * member_rows)
        low_out[at] = nt(here, narrow_ref[...]).astype(LOW)
        return carry

    lax.fori_loop(0, TEAM // 2, one, 0)
    own_wide[...] = nt(
        rows[pl.ds(pl.multiple_of(t * member_rows, 16), member_rows)], narrow_ref[...]
    )


def cotangent(place, spans, narrow_full, pieces, capacity, member_rows):
    model, width = narrow_full.shape
    total = member_rows * TEAM
    return pl.pallas_call(
        lambda *refs: cotangent_kernel(capacity, *refs),
        out_shape=(
            jax.ShapeDtypeStruct((total, model), LOW),
            jax.ShapeDtypeStruct((member_rows, model), WIDE),
            jax.ShapeDtypeStruct((total, width), LOW),
        ),
        in_specs=[in_smem(), in_smem()] + [in_vmem()] * (1 + PIECES),
        out_specs=(in_vmem(),) * 3,
        scratch_shapes=[pltpu.VMEM((total + capacity + 16, width), LOW)],
        compiler_params=params(),
        cost_estimate=estimate(13),
        name="cotangent",
    )(place, spans, narrow_full, *pieces)


def leave_kernel(place_ref, spans_ref, *refs):
    pieces, out_ref, total = refs[:PIECES], refs[PIECES], refs[PIECES + 1]
    t = place_ref[1]
    first = spans_ref[0]
    capacity = out_ref.shape[0]
    total[...] = jnp.zeros_like(total)
    for m in range(TEAM):
        rows = pieces[0].shape[0]
        offset = (t ^ m) * rows - first

        @pl.when((offset < capacity) & (offset + rows > 0))
        def _(m=m, offset=offset, rows=rows):
            target = lax.broadcasted_iota(jnp.int32, (capacity, rows), 0)
            source = lax.broadcasted_iota(jnp.int32, (capacity, rows), 1) + offset
            total[...] += nn(jnp.where(target == source, 1.0, 0.0).astype(LOW), piece(pieces, m))

    out_ref[...] = total[...].astype(LOW)


def leave(place, spans, pieces, capacity):
    width = pieces[0].shape[1]
    return pl.pallas_call(
        leave_kernel,
        out_shape=jax.ShapeDtypeStruct((capacity, width), LOW),
        in_specs=[in_smem(), in_smem()] + [in_vmem()] * PIECES,
        out_specs=in_vmem(),
        scratch_shapes=[pltpu.VMEM((capacity, width), WIDE)],
        compiler_params=params(),
        cost_estimate=estimate(2),
        name="leave",
    )(place, spans, *pieces)


def norm_kernel(wide_ref, gains_ref, *refs):
    resid_out, low_out = refs[4:]
    resid = wide_ref[...] + add_terms(refs[:4])
    resid_out[...] = resid
    inverse = lax.rsqrt(jnp.mean(resid * resid, axis=-1, keepdims=True) + NORM_EPS)
    low_out[...] = (resid * inverse * gains_ref[8:9]).astype(LOW)


def add_and_norm(wide, gains, terms):
    return pl.pallas_call(
        norm_kernel,
        out_shape=(
            jax.ShapeDtypeStruct(wide.shape, WIDE),
            jax.ShapeDtypeStruct(wide.shape, LOW),
        ),
        in_specs=[in_vmem()] * 6,
        out_specs=(in_vmem(),) * 2,
        compiler_params=params(),
        cost_estimate=estimate(2),
        name="add_and_norm",
    )(wide, gains, *terms)


def norm_back(resid, gain, incoming):
    inverse = lax.rsqrt(jnp.mean(resid * resid, axis=-1, keepdims=True) + NORM_EPS)
    scaled = incoming * gain
    along = jnp.mean(scaled * resid, axis=-1, keepdims=True)
    back = inverse * scaled - resid * (inverse * inverse * inverse * along)
    return back, jnp.sum(incoming * resid * inverse, axis=0, keepdims=True)


def second_back_kernel(resid_ref, gains_ref, upper_ref, *refs):
    lower_out, low_out, gain_out = refs[4:]
    back, gain_back = norm_back(
        resid_ref[...], gains_ref[8:9], add_terms(refs[:4], slice(resid_ref.shape[1]))
    )
    lower = upper_ref[...] + back
    lower_out[...] = lower
    low_out[...] = lower.astype(LOW)
    gain_out[...] = jnp.broadcast_to(gain_back, gain_out.shape)


def second_norm_back(resid, gains, upper, terms):
    rows, model = resid.shape
    return pl.pallas_call(
        second_back_kernel,
        out_shape=(
            jax.ShapeDtypeStruct((rows, model), WIDE),
            jax.ShapeDtypeStruct((rows, model), LOW),
            jax.ShapeDtypeStruct((8, model), WIDE),
        ),
        in_specs=[in_vmem()] * 7,
        out_specs=(in_vmem(),) * 3,
        compiler_params=params(),
        cost_estimate=estimate(2),
        name="second_norm_back",
    )(resid, gains, upper, *terms)


def first_back_kernel(
    place_ref, wide_ref, gains_ref, lower_ref, rows_ref, widen_ref, second_gain_ref, narrow_ref, *refs
):
    patch_out = refs[4]
    outs = refs[5:13]
    grad = refs[13]
    t = place_ref[1]
    back, first_gain = norm_back(wide_ref[...], gains_ref[:1], add_terms(refs[:4]))
    low = (lower_ref[...] + back).astype(LOW)
    grad[...] = tn(rows_ref[...], low)
    shard = grad.shape[0] // (PLANES * TEAM)
    row = lax.broadcasted_iota(jnp.int32, (16, grad.shape[1]), 0)
    gain_rows = jnp.where(row == 0, first_gain, jnp.where(row == 1, second_gain_ref[:1], 0.0))
    for m in (7, 6, 5, 3, 4, 2, 1, 0):
        parts = [
            grad[pl.ds(pl.multiple_of((plane * TEAM + (t ^ m)) * shard, 8), shard)]
            for plane in range(PLANES)
        ]
        put_terms(outs, m, jnp.concatenate(parts + [gain_rows], axis=0))
    width = narrow_ref.shape[1]
    patch_out[:, :width] = narrow_ref[...]
    patch_out[:, width:] = nt(low, widen_ref[...]).astype(LOW)


def first_norm_back(place, wide, gains, lower, rows, widen_full, second_gain, narrow_low, terms):
    model = wide.shape[1]
    width = widen_full.shape[0]
    return pl.pallas_call(
        first_back_kernel,
        out_shape=(jax.ShapeDtypeStruct((rows.shape[0], 2 * width), LOW),)
        + term_shapes(width // TEAM + 16, model),
        in_specs=[in_smem()] + [in_vmem()] * 11,
        out_specs=(in_vmem(),) * 9,
        scratch_shapes=[pltpu.VMEM((width, model), WIDE)],
        compiler_params=params(),
        cost_estimate=estimate(5),
        name="first_norm_back",
    )(place, wide, gains, lower, rows, widen_full, second_gain, narrow_low, *terms)


def exit_kernel(resid_ref, narrow_ref, *refs):
    low_out, narrow_out = refs[4:]
    model = resid_ref.shape[1]
    wide = resid_ref[...] + add_terms(refs[:4], slice(model, 2 * model))
    low = wide.astype(LOW)
    shard = low_out.shape[2] // PLANES
    for m in range(TEAM):
        parts = [
            wide[:, (plane * TEAM + m) * shard : (plane * TEAM + m + 1) * shard]
            for plane in range(PLANES)
        ]
        low_out[m] = jnp.concatenate(parts, axis=1).astype(LOW)
    narrow_out[...] = nn(low, narrow_ref[...]).astype(LOW)


def exit_block(resid, narrow_full, terms):
    rows, model = resid.shape
    return pl.pallas_call(
        exit_kernel,
        out_shape=(
            jax.ShapeDtypeStruct((TEAM, rows, model // TEAM), LOW),
            jax.ShapeDtypeStruct((rows, narrow_full.shape[1]), LOW),
        ),
        in_specs=[in_vmem()] * 6,
        out_specs=(in_vmem(),) * 2,
        compiler_params=params(),
        cost_estimate=estimate(4),
        name="exit_block",
    )(resid, narrow_full, *terms)


def forward_terms_kernel(left_ref, right_ref, *outs):
    rows = left_ref.shape[0] // TEAM
    for k in (3, 2, 1, 0):
        product = nn(left_ref[2 * k * rows : (2 * k + 2) * rows], right_ref[...])
        put_terms(outs, 2 * k + 1, product[rows:])
        put_terms(outs, 2 * k, product[:rows])


def forward_terms(left, right):
    return pl.pallas_call(
        forward_terms_kernel,
        out_shape=term_shapes(left.shape[0] // TEAM, right.shape[1]),
        in_specs=[in_vmem()] * 2,
        out_specs=(in_vmem(),) * 8,
        compiler_params=params(),
        cost_estimate=estimate(6),
        name="forward_terms",
    )(left, right)


def feed_kernel(expand_ref, shrink_ref, back_ref, *refs):
    pieces = refs[:PIECES]
    second_out, active_out, expand_out = refs[PIECES : PIECES + 3]
    outs = refs[PIECES + 3 :]
    rows = back_ref.shape[0] // TEAM
    for k in (3, 2, 1, 0):
        at = slice(2 * k * rows, (2 * k + 2) * rows)
        low = jnp.concatenate([piece(pieces, 2 * k), piece(pieces, 2 * k + 1)], axis=0)
        second_out[at] = low
        value = nn(low, expand_ref[...])
        square = value * value
        bend = jnp.tanh(GELU_A * (value + GELU_B * square * value))
        active_out[at] = (0.5 * value * (1.0 + bend)).astype(LOW)
        slope = 0.5 * (1.0 + bend) + 0.5 * value * (1.0 - bend * bend) * (
            GELU_A * (1.0 + 3.0 * GELU_B * square)
        )
        back = (slope * nt(back_ref[at], shrink_ref[...])).astype(LOW)
        expand_out[at] = back
        product = jnp.concatenate(
            [nt(back, expand_ref[...]).astype(LOW), nn(active_out[at], shrink_ref[...]).astype(LOW)],
            axis=1,
        )
        put_terms(outs, 2 * k + 1, product[rows:])
        put_terms(outs, 2 * k, product[:rows])


def feed(expand_own, shrink_own, shrink_back, pieces):
    total, model = shrink_back.shape
    hidden = expand_own.shape[1]
    return pl.pallas_call(
        feed_kernel,
        out_shape=(
            jax.ShapeDtypeStruct((total, model), LOW),
            jax.ShapeDtypeStruct((total, hidden), LOW),
            jax.ShapeDtypeStruct((total, hidden), LOW),
        )
        + term_shapes(total // TEAM, 2 * model),
        in_specs=[in_vmem()] * (3 + PIECES),
        out_specs=(in_vmem(),) * 11,
        compiler_params=params(),
        cost_estimate=estimate(18),
        name="feed",
    )(expand_own, shrink_own, shrink_back, *pieces)


def attend_kernel(
    own,
    tile,
    place_ref,
    first_ref,
    triple_ref,
    doc_column,
    doc_row,
    projected_ref,
    flat_out,
    low_out,
    total_out,
    queries,
    keys,
    values,
    attended,
):
    t = place_ref[1]
    rows = first_ref.shape[0]
    member_rows = rows // TEAM
    width = own * HEAD_DIM

    def project(k, carry):
        at = pl.ds(pl.multiple_of(k * 2 * member_rows, 16), 2 * member_rows)
        projected_ref[at] = nn(first_ref[at], triple_ref[...]).astype(LOW)
        return carry

    lax.fori_loop(0, TEAM // 2, project, 0)
    for h in range(own):
        lanes = slice(h * HEAD_DIM, (h + 1) * HEAD_DIM)
        queries[h] = projected_ref[:, :width][:, lanes]
        keys[h] = projected_ref[:, width : 2 * width][:, lanes]
        values[h] = jnp.transpose(
            projected_ref[:, 2 * width :][:, lanes].astype(WIDE)
        ).astype(LOW)
    total_out[...] = jnp.zeros_like(total_out)
    scale = SCORE_SCALE * LOG2_E
    causal = lax.broadcasted_iota(jnp.int32, (tile, tile), 0) <= lax.broadcasted_iota(
        jnp.int32, (tile, tile), 1
    )

    def one_query(j, carry):
        at_query = pl.ds(pl.multiple_of(j * tile, tile), tile)
        query_docs = doc_row[:1, at_query]

        def one_key(i, status, diagonal):
            at_key = pl.ds(pl.multiple_of(i * tile, tile), tile)
            allowed = doc_column[at_key, :1] == query_docs
            if diagonal:
                allowed = allowed & causal
            result = []
            for h in range(own):
                scores = nt(keys[h, at_key], queries[h, at_query]) * scale
                masked = jnp.where(allowed, scores, MASK_FILL)
                best = jnp.max(masked, axis=0, keepdims=True)
                if diagonal:
                    top = best
                    weights = jnp.exp2(masked - top)
                    summed = jnp.sum(weights, axis=0, keepdims=True)
                    out = nn(values[h, :, at_key], weights.astype(LOW))
                else:
                    old_top, old_sum, old_out = status[h]
                    top = jnp.maximum(old_top, best)
                    weights = jnp.exp2(masked - top)
                    rescale = jnp.exp2(old_top - top)
                    summed = old_sum * rescale + jnp.sum(weights, axis=0, keepdims=True)
                    out = old_out * rescale + nn(values[h, :, at_key], weights.astype(LOW))
                result.append((top, summed, out))
            return tuple(result)

        status = one_key(j, None, True)
        status = lax.fori_loop(0, j, lambda i, now: one_key(i, now, False), status)
        for h in range(own):
            top, summed, out = status[h]
            done = out / summed
            flat_out[h * HEAD_DIM : (h + 1) * HEAD_DIM, at_query] = done
            total_out[h : h + 1, at_query] = top + jnp.log2(summed)
        return carry

    lax.fori_loop(0, rows // tile, one_query, 0)
    attended[...] = jnp.transpose(flat_out[...]).astype(LOW)
    for k in (3, 2, 1, 0):
        pair = jnp.concatenate(
            [
                attended[pl.ds(pl.multiple_of((t ^ m) * member_rows, 16), member_rows)]
                for m in (2 * k, 2 * k + 1)
            ],
            axis=0,
        )
        low_out[2 * k * member_rows : (2 * k + 2) * member_rows] = pair


def attend_team(place, first_low, triple_own, doc_column, doc_row, own):
    rows, model = first_low.shape
    width = own * HEAD_DIM
    tile = rows // 2
    return pl.pallas_call(
        lambda *refs: attend_kernel(own, tile, *refs),
        out_shape=(
            jax.ShapeDtypeStruct((rows, 3 * width), LOW),
            jax.ShapeDtypeStruct((width, rows), WIDE),
            jax.ShapeDtypeStruct((rows, width), LOW),
            jax.ShapeDtypeStruct((8, rows), WIDE),
        ),
        in_specs=[in_smem()] + [in_vmem()] * 4,
        out_specs=(in_vmem(),) * 4,
        scratch_shapes=[
            pltpu.VMEM((own, rows, HEAD_DIM), LOW),
            pltpu.VMEM((own, rows, HEAD_DIM), LOW),
            pltpu.VMEM((own, HEAD_DIM, rows), LOW),
            pltpu.VMEM((rows, width), LOW),
        ],
        compiler_params=params(),
        cost_estimate=estimate(20),
        name="attend",
    )(place, first_low, triple_own, doc_column, doc_row)


def attend_back_setup(own, projected_ref, flat_ref, back_ref, scratch):
    queries, keys, values, backs, keys_flat, backs_flat, deltas = scratch
    width = own * HEAD_DIM
    for h in range(own):
        lanes = slice(h * HEAD_DIM, (h + 1) * HEAD_DIM)
        key = projected_ref[:, width : 2 * width][:, lanes]
        back = back_ref[:, lanes]
        back_flat = jnp.transpose(back.astype(WIDE))
        queries[h] = projected_ref[:, :width][:, lanes]
        keys[h] = key
        values[h] = projected_ref[:, 2 * width :][:, lanes]
        backs[h] = back
        keys_flat[h] = jnp.transpose(key.astype(WIDE)).astype(LOW)
        backs_flat[h] = back_flat.astype(LOW)
        deltas[h : h + 1] = jnp.sum(back_flat * flat_ref[lanes], axis=0, keepdims=True)


def attend_back_tile(own, tile, i, total_ref, doc_column, doc_row, scratch, query_back):
    queries, keys, values, backs, keys_flat, backs_flat, deltas = scratch
    rows = queries.shape[1]
    scale = SCORE_SCALE * LOG2_E
    causal = lax.broadcasted_iota(jnp.int32, (tile, tile), 0) <= lax.broadcasted_iota(
        jnp.int32, (tile, tile), 1
    )
    at_key = slice(i * tile, (i + 1) * tile)
    status = [None] * own
    for j in range(i, rows // tile):
        at_query = slice(j * tile, (j + 1) * tile)
        allowed = doc_column[at_key, :1] == doc_row[:1, at_query]
        if i == j:
            allowed = allowed & causal
        for h in range(own):
            scores = nt(keys[h, at_key], queries[h, at_query]) * scale
            probs = jnp.where(allowed, jnp.exp2(scores - total_ref[h : h + 1, at_query]), 0.0)
            prob_back = nn(values[h, at_key], backs_flat[h, :, at_query])
            score_back = (probs * (prob_back - deltas[h : h + 1, at_query])).astype(LOW)
            value_part = nn(probs.astype(LOW), backs[h, at_query])
            key_part = nn(score_back, queries[h, at_query])
            query_part = nn(keys_flat[h, :, at_key], score_back)
            if i == 0:
                query_back[h, :, at_query] = query_part
            else:
                query_back[h, :, at_query] += query_part
            if status[h] is None:
                status[h] = (key_part, value_part)
            else:
                status[h] = (status[h][0] + key_part, status[h][1] + value_part)
    return jnp.concatenate(
        [status[h][0] * SCORE_SCALE for h in range(own)] + [status[h][1] for h in range(own)],
        axis=1,
    ).astype(LOW)


def attend_back_first_kernel(
    own,
    tile,
    place_ref,
    projected_ref,
    flat_ref,
    total_ref,
    doc_column,
    doc_row,
    back_ref,
    tile_out,
    query_back,
    *scratch,
):
    attend_back_setup(own, projected_ref, flat_ref, back_ref, scratch)
    for i in range(tile_out.shape[0] // tile):
        tile_out[i * tile : (i + 1) * tile] = attend_back_tile(
            own, tile, i, total_ref, doc_column, doc_row, scratch, query_back
        )


def attend_back_rest_kernel(
    own,
    tile,
    place_ref,
    projected_ref,
    flat_ref,
    total_ref,
    doc_column,
    doc_row,
    back_ref,
    tile_ref,
    earlier_ref,
    triple_ref,
    out_ref,
    *refs,
):
    outs, query_back, scratch = refs[:8], refs[8], refs[9:]
    t = place_ref[1]
    rows = projected_ref.shape[0]
    member_rows = rows // TEAM
    width = own * HEAD_DIM
    attend_back_setup(own, projected_ref, flat_ref, back_ref, scratch)
    query_back[...] = earlier_ref[...]
    done = tile_ref.shape[0]
    out_ref[:done, width:] = tile_ref[...]
    for i in range(done // tile, rows // tile):
        out_ref[i * tile : (i + 1) * tile, width:] = attend_back_tile(
            own, tile, i, total_ref, doc_column, doc_row, scratch, query_back
        )
    flat = jnp.concatenate([query_back[h] for h in range(own)], axis=0) * SCORE_SCALE
    out_ref[:, :width] = jnp.transpose(flat).astype(LOW)
    for k in (3, 2, 1, 0):
        pair = jnp.concatenate(
            [
                out_ref[pl.ds(pl.multiple_of((t ^ m) * member_rows, 16), member_rows)]
                for m in (2 * k, 2 * k + 1)
            ],
            axis=0,
        )
        product = nt(pair, triple_ref[...])
        put_terms(outs, 2 * k + 1, product[member_rows:])
        put_terms(outs, 2 * k, product[:member_rows])


def attend_back_scratch(own, rows):
    tall = pltpu.VMEM((own, rows, HEAD_DIM), LOW)
    long = pltpu.VMEM((own, HEAD_DIM, rows), LOW)
    return [tall, tall, tall, tall, long, long, pltpu.VMEM((8, rows), WIDE)]


def attend_back_first(place, projected, flat, totals, doc_column, doc_row, back, own):
    rows = projected.shape[0]
    tile = rows // 3
    return pl.pallas_call(
        lambda *refs: attend_back_first_kernel(own, tile, *refs),
        out_shape=(
            jax.ShapeDtypeStruct((2 * tile, 2 * own * HEAD_DIM), LOW),
            jax.ShapeDtypeStruct((own, HEAD_DIM, rows), WIDE),
        ),
        in_specs=[in_smem()] + [in_vmem()] * 6,
        out_specs=(in_vmem(),) * 2,
        scratch_shapes=attend_back_scratch(own, rows),
        compiler_params=params(),
        cost_estimate=estimate(12),
        name="attend_back_first",
    )(place, projected, flat, totals, doc_column, doc_row, back)


def attend_back_rest(
    place, projected, flat, totals, doc_column, doc_row, back, first_tile, query_back, triple_own, own
):
    rows = projected.shape[0]
    tile = rows // 3
    return pl.pallas_call(
        lambda *refs: attend_back_rest_kernel(own, tile, *refs),
        out_shape=(jax.ShapeDtypeStruct(projected.shape, LOW),)
        + term_shapes(rows // TEAM, triple_own.shape[0]),
        in_specs=[in_smem()] + [in_vmem()] * 9,
        out_specs=(in_vmem(),) * 9,
        scratch_shapes=[pltpu.VMEM((own, HEAD_DIM, rows), WIDE)] + attend_back_scratch(own, rows),
        compiler_params=params(),
        cost_estimate=estimate(18),
        name="attend_back_rest",
    )(
        place,
        projected,
        flat,
        totals,
        doc_column,
        doc_row,
        back,
        first_tile,
        query_back,
        triple_own,
    )


def mixing_send_kernel(place_ref, *refs):
    stack_ref, out_ref = refs
    out_ref[...] = jnp.zeros_like(out_ref)
    x = place_ref[1] // 4
    for source in range(PLANES):
        out_ref[2 * source + x] = stack_ref[source]


def mixing_send(place, stack):
    rows, width = stack.shape[1:]
    return pl.pallas_call(
        mixing_send_kernel,
        out_shape=jax.ShapeDtypeStruct((TEAM, rows, width), LOW),
        in_specs=[in_smem(), in_vmem()],
        out_specs=in_vmem(),
        compiler_params=params(),
        cost_estimate=estimate(2),
        name="mixing_send",
    )(place, stack)


def mixing_exchange(sent, core):
    rows, width = sent.shape[1:]
    return lax.dynamic_slice_in_dim(
        team_exchange(sent), core * PLANES, PLANES, 0
    ).reshape(PLANES * rows, width)


def mixing_return(sent, x):
    back = team_exchange(sent)
    return pick(back.reshape((PLANES, 2) + back.shape[1:]), x, 1)


def mix_back_kernel(place_ref, mixing_ref, attended_ref, *refs):
    pieces = refs[:PIECES]
    back_ref, mixing_out, mixed = refs[PIECES:]
    t = place_ref[1]
    member_rows = back_ref.shape[0] // TEAM
    for k in range(TEAM // 2):
        pair = jnp.concatenate([piece(pieces, 2 * k), piece(pieces, 2 * k + 1)], axis=0)
        mixed[2 * k * member_rows : (2 * k + 2) * member_rows] = pair
        back = nt(pair, mixing_ref[...]).astype(LOW)
        for m in (2 * k, 2 * k + 1):
            at = pl.ds(pl.multiple_of((t ^ m) * member_rows, 16), member_rows)
            back_ref[at] = back[(m - 2 * k) * member_rows : (m - 2 * k + 1) * member_rows]
    gradient = tn(attended_ref[...], mixed[...]).astype(LOW)
    mixing_out[...] = jnp.zeros_like(mixing_out)
    rows = gradient.shape[0] // PLANES
    for k in range(PLANES):
        mixing_out[t % 2 * PLANES + k] = gradient[k * rows : (k + 1) * rows]


def mix_back(place, mixing_own, attended, pieces):
    rows, width = attended.shape
    model = mixing_own.shape[1]
    return pl.pallas_call(
        mix_back_kernel,
        out_shape=(
            jax.ShapeDtypeStruct((rows, width), LOW),
            jax.ShapeDtypeStruct((TEAM, width // PLANES, model), LOW),
        ),
        in_specs=[in_smem()] + [in_vmem()] * (2 + PIECES),
        out_specs=(in_vmem(),) * 2,
        scratch_shapes=[pltpu.VMEM((rows, model), LOW)],
        compiler_params=params(),
        cost_estimate=estimate(5),
        name="mix_back",
    )(place, mixing_own, attended, *pieces)


def columns_kernel_of(piece_width, in_ref, out_ref, square_ref):
    total = jnp.zeros((1, 1), WIDE)
    for group in range(in_ref.shape[2] // piece_width):
        for pair in range(TEAM // 2):
            lanes = slice(group * piece_width, (group + 1) * piece_width)
            value = jnp.concatenate(
                [in_ref[2 * pair][:, lanes].astype(WIDE), in_ref[2 * pair + 1][:, lanes].astype(WIDE)],
                axis=1,
            )
            first = (group * TEAM + 2 * pair) * piece_width
            out_ref[:, first : first + 2 * piece_width] = value
            total = total + jnp.sum(value * value, axis=(0, 1), keepdims=True)
    square_ref[...] = jnp.broadcast_to(total, square_ref.shape)


def to_columns(value, piece_width):
    members, rows, width = value.shape
    out, square = pl.pallas_call(
        lambda *refs: columns_kernel_of(piece_width, *refs),
        out_shape=(
            jax.ShapeDtypeStruct((rows, members * width), WIDE),
            jax.ShapeDtypeStruct((8, 128), WIDE),
        ),
        in_specs=[in_vmem()],
        out_specs=(in_vmem(),) * 2,
        compiler_params=params(),
        cost_estimate=estimate(2),
        name="to_columns",
    )(value)
    return out, square[0, 0]


def adam_kernel(rates, factor_ref, *refs):
    number = len(rates)
    factor = factor_ref[0]
    for index in range(number):
        gradient, master, first, second = (refs[k * number + index][...] for k in range(4))
        weight, moment, square = adam_update(
            master, first, second, gradient, factor, rates[index], DECAY_RATE
        )
        refs[4 * number + 3 * index][...] = weight
        refs[4 * number + 3 * index + 1][...] = moment
        refs[4 * number + 3 * index + 2][...] = square


def adam_all(factor, gradients, masters, firsts, seconds, rates):
    steps = 6

    def block(array):
        rows, columns = array.shape
        return pl.BlockSpec((rows, columns // steps), lambda step: (0, step))

    blocks = [block(master) for master in masters]
    return pl.pallas_call(
        lambda *refs: adam_kernel(rates, *refs),
        grid=(steps,),
        out_shape=[
            jax.ShapeDtypeStruct(master.shape, WIDE) for master in masters for _ in range(3)
        ],
        in_specs=[in_smem()] + blocks * 4,
        out_specs=[one for one in blocks for _ in range(3)],
        compiler_params=params(),
        cost_estimate=estimate(10),
        name="adam_all",
    )(factor, *gradients, *masters, *firsts, *seconds)


def per_member(
    byte_rows,
    starts,
    doc_ids,
    out_cotangent,
    widen_master,
    widen_first,
    widen_second,
    triple_master,
    triple_first,
    triple_second,
    mixing_master,
    mixing_first,
    mixing_second,
    expand_master,
    expand_first,
    expand_second,
    shrink_master,
    shrink_first,
    shrink_second,
    narrow_master,
    narrow_first,
    narrow_second,
    gains_master,
    gains_first,
    gains_second,
):
    plane = lax.axis_index("z")
    x, y, core = lax.axis_index("x"), lax.axis_index("y"), lax.axis_index("c")
    t = 4 * x + 2 * y + core
    place = jnp.stack([plane, t]).astype(jnp.int32)
    byte_block, cotangent_rows = byte_rows[0], out_cotangent[0]
    bytes_dev, byte_width = byte_block.shape
    model = triple_master.shape[1] // 3
    hidden = expand_master.shape[1]
    shard = triple_master.shape[0]
    widen_shard = widen_master.shape[0]
    member_rows = 3 * bytes_dev // 16
    capacity = member_rows + member_rows // 2
    total = TEAM * member_rows
    own = HEADS // TEAM
    own_width = model // TEAM
    own_hidden = hidden // TEAM
    piece_hidden = own_hidden // PLANES

    widen_low = widen_master.astype(LOW)
    gains_low = gains_master.astype(LOW)
    gain_rows = jnp.pad(gains_low, ((0, 32 - widen_shard - 2), (0, byte_width - shard)))
    small = jnp.concatenate(
        [
            widen_low[:, :byte_width],
            gain_rows,
            widen_low[:, byte_width:],
            jnp.zeros((32 - widen_shard, byte_width), LOW),
            narrow_master.astype(LOW),
        ],
        axis=0,
    )
    small = plane_gather_small(small)
    row_buffer, chosen = pack(
        after(starts, small[1]), doc_ids, byte_block, cotangent_rows, capacity
    )
    packed = row_buffer
    row_buffer = to_plane(row_buffer)
    small, small_marks = team_gather(jnp.concatenate(small, axis=0))
    widen_full, gains_full, narrow_full = widen_whole(place, small, widen_shard, model)
    triple_own = triple_master.astype(LOW).reshape(shard, 3, TEAM, own_width)
    triple_own = jnp.transpose(triple_own, (2, 0, 1, 3)).reshape(TEAM, shard, 3 * own_width)
    triple_own = team_exchange(triple_own)
    mixing_rows = shard * model // (3 * own_width)
    triple_sent = jnp.concatenate(
        [
            after(triple_own, row_buffer, small[2], small[4]).reshape(TEAM * shard, 3 * own_width),
            mixing_master.astype(LOW).reshape(mixing_rows, 3 * own_width),
        ],
        axis=0,
    )
    gathered = lax.all_gather(triple_sent, "z", axis=0)
    triple_own = gathered[:, : TEAM * shard].reshape(model, 3 * own_width)
    mixing_stack = gathered[:, TEAM * shard :].reshape(PLANES, shard, model)
    expand_own = after(expand_master, triple_sent).astype(LOW)
    expand_own = expand_own.reshape(shard, PLANES, TEAM, piece_hidden)
    expand_own = jnp.transpose(expand_own, (2, 0, 1, 3)).reshape(TEAM, shard, own_hidden)
    expand_own = team_exchange(expand_own).reshape(TEAM * shard, own_hidden)
    shrink_low = shrink_master.astype(LOW)
    fed = lax.all_gather(
        jnp.concatenate(
            [expand_own, shrink_low[:, :own_hidden], shrink_low[:, own_hidden:]], axis=0
        ),
        "z",
        axis=0,
    )
    expand_own = fed[:, : TEAM * shard].reshape(model, own_hidden)
    shrink_own = jnp.concatenate(
        [
            fed[:, TEAM * shard : TEAM * shard + piece_hidden],
            fed[:, TEAM * shard + piece_hidden :],
        ],
        axis=2,
    ).reshape(own_hidden, model)
    entering, enter_marks = team_gather(after(row_buffer, *small_marks))
    first_low, widened, patch_rows, doc_column, doc_row, spans = enter(
        place,
        gains_full,
        widen_full,
        entering,
        capacity,
        member_rows,
    )
    mixing_sent = mixing_send(place, mixing_stack)
    mixing_own = mixing_exchange(mixing_sent, core)

    projected, flat, attended_low, totals = attend_team(
        after(place, mixing_sent), first_low, triple_own, doc_column, doc_row, own
    )
    terms, marks = team_scatter(*forward_terms(attended_low, mixing_own))
    shrink_back, upper_back, narrow_back = cotangent(
        after(place, *marks), spans, narrow_full, entering, capacity, member_rows
    )
    resid_one, second_own = add_and_norm(after(widened, shrink_back), gains_full, terms)

    second_pieces, _ = team_gather(second_own)
    second_low, active_low, expand_back, *terms = feed(
        expand_own, shrink_own, shrink_back, second_pieces
    )
    terms, marks = team_scatter(*terms)
    shrink_grad = tn(after(active_low, *marks), shrink_back).astype(LOW)
    shrink_sum = lax.psum_scatter(shrink_grad, "z", scatter_dimension=0, tiled=True)
    lower_back, mixed_own, second_gain = second_norm_back(
        after(resid_one, shrink_grad), gains_full, upper_back, terms
    )
    exit_out = []

    def leave_forward(own):
        exit_out.extend(exit_block(after(resid_one, own), narrow_full, terms))
        return exit_out[:1]

    mixed, mixed_marks = team_gather(mixed_own, None, leave_forward)
    resid_low, narrow_low = exit_out
    resid_low = team_exchange(resid_low).reshape(total, own_width)
    expand_grad = tn(after(second_low, *mixed_marks), expand_back).astype(LOW)
    expand_sum = lax.psum_scatter(expand_grad, "z", scatter_dimension=0, tiled=True)

    attend_back, mixing_grad = mix_back(
        after(place, expand_grad), mixing_own, attended_low, mixed
    )
    narrow_grad = tn(resid_low, after(narrow_back, attend_back)).astype(LOW)
    attention = (projected, flat, totals, doc_column, doc_row, attend_back)
    first_tile, query_back = attend_back_first(
        after(place, shrink_sum, narrow_grad), *attention, own
    )
    mixing_stack = mixing_return(mixing_grad, x)
    triple_back, *terms = attend_back_rest(
        after(place, mixing_stack), *attention, first_tile, query_back, triple_own, own
    )
    first_terms, marks = team_scatter(*terms)
    triple_grad = tn(after(first_low, expand_sum, *marks), triple_back).astype(LOW)
    triple_sum = lax.psum_scatter(triple_grad, "z", scatter_dimension=0, tiled=True)
    expand_sum = team_exchange(expand_sum.reshape(TEAM, shard, own_hidden))

    both = plane_scatter_small(
        jnp.concatenate(
            [
                after(mixing_stack, first_terms[2], first_terms[3]),
                narrow_grad.reshape(PLANES, shard, byte_width),
            ],
            axis=2,
        )
    )
    mixing_sum, narrow_sum = both[:, :model], both[:, model:]

    back_rows, *terms = first_norm_back(
        after(place, triple_grad, expand_sum),
        widened,
        gains_full,
        lower_back,
        patch_rows,
        widen_full,
        second_gain,
        narrow_low,
        first_terms,
    )
    terms, marks = team_scatter(*terms)
    widen_ready = sum(term.astype(WIDE) for term in terms)
    gains_ready = widen_ready[PLANES * widen_shard :][:8]
    widen_sum = plane_scatter_small(
        jnp.concatenate(
            [
                after(widen_ready, mixing_sum)[: PLANES * widen_shard].reshape(
                    PLANES, widen_shard, model
                ),
                jnp.broadcast_to(gains_ready, (PLANES, 8, model)),
            ],
            axis=1,
        )
    )
    gains_sum = lax.dynamic_slice(
        widen_sum[widen_shard : widen_shard + 2], (0, (plane * TEAM + t) * shard), (2, shard)
    )
    widen_sum = widen_sum[:widen_shard]
    back_rows, _ = team_gather(after(back_rows, terms[2]), None, lambda own: (widen_sum,))
    back_buffer = from_plane(leave(place, spans, back_rows, capacity))
    new_block, grad_block = unpack(chosen, byte_block, cotangent_rows, back_buffer)

    triple_sum = team_exchange(triple_sum.reshape(TEAM, shard, 3 * own_width))
    triple_sum, triple_square = to_columns(triple_sum, own_width)
    expand_sum, expand_square = to_columns(expand_sum, piece_hidden)
    shrink_sum = shrink_sum.astype(WIDE)

    reduced = (widen_sum, triple_sum, mixing_sum, expand_sum, shrink_sum, narrow_sum, gains_sum)
    squares = triple_square + expand_square
    for gradient in (widen_sum, mixing_sum, shrink_sum, narrow_sum, gains_sum):
        squares = squares + jnp.sum(gradient * gradient)
    squares = jnp.full((8, 128), squares, WIDE)
    for bit in (CORE_BIT, Y_BIT, X_BIT, TEAM, 2 * TEAM):
        squares = squares + flip(squares, bit)
    grad_norm = jnp.sqrt(squares[0, 0])
    factor = CLIP_NORM / jnp.maximum(grad_norm, CLIP_NORM)
    rates = (
        2.0 * D_BYTE ** (-0.5),
        2.0 * D ** (-0.5),
        0.4,
        2.0 * D ** (-0.5),
        2.0 * FF ** (-0.5),
        2.0 * D ** (-0.5),
    )
    updated = adam_all(
        factor.reshape(1),
        reduced[:6],
        (widen_master, triple_master, mixing_master, expand_master, shrink_master, narrow_master),
        (widen_first, triple_first, mixing_first, expand_first, shrink_first, narrow_first),
        (widen_second, triple_second, mixing_second, expand_second, shrink_second, narrow_second),
        rates,
    )
    gains = adam_update(gains_master, gains_first, gains_second, gains_sum, factor, 0.6, 0.0)
    return (new_block[None], grad_block[None], grad_norm, *updated, *gains)


def plane_solution(mesh):
    fine = Mesh(mesh.devices.reshape(PLANES, 2, 2, 2), AXES)
    byte_spec = P(("y", "c"), ("z", "x"))
    rows_spec = P(AXES, None)
    gains_spec = P(None, AXES)
    return jax.shard_map(
        per_member,
        mesh=fine,
        in_specs=(byte_spec,) * 4 + (rows_spec,) * 18 + (gains_spec,) * 3,
        out_specs=(byte_spec,) * 2 + (P(),) + (rows_spec,) * 18 + (gains_spec,) * 3,
        check_vma=False,
    )


def solution(mesh):
    if plane_fits(mesh):
        return plane_solution(mesh)
    placed = (
        P("dp", "seq", None),
        P("dp", "seq"),
        P("dp", "seq"),
        P("dp", "seq", None),
        P(("seq", "dp"), None),
        P(("seq", "dp"), None),
        P(("seq", "dp"), None),
        P(("seq", "dp"), None),
        P(("seq", "dp"), None),
        P(("seq", "dp"), None),
        P(("seq", "dp"), None),
        P(("seq", "dp"), None),
        P(("seq", "dp"), None),
        P(("seq", "dp"), None),
        P(("seq", "dp"), None),
        P(("seq", "dp"), None),
        P(("seq", "dp"), None),
        P(("seq", "dp"), None),
        P(("seq", "dp"), None),
        P(("seq", "dp"), None),
        P(("seq", "dp"), None),
        P(("seq", "dp"), None),
        P(None, ("seq", "dp")),
        P(None, ("seq", "dp")),
        P(None, ("seq", "dp")),
    )
    return jax.shard_map(
        per_device,
        mesh=mesh,
        in_specs=placed,
        out_specs=(
            P("dp", "seq", None),
            P("dp", "seq", None),
            P(),
            P(("seq", "dp"), None),
            P(("seq", "dp"), None),
            P(("seq", "dp"), None),
            P(("seq", "dp"), None),
            P(("seq", "dp"), None),
            P(("seq", "dp"), None),
            P(("seq", "dp"), None),
            P(("seq", "dp"), None),
            P(("seq", "dp"), None),
            P(("seq", "dp"), None),
            P(("seq", "dp"), None),
            P(("seq", "dp"), None),
            P(("seq", "dp"), None),
            P(("seq", "dp"), None),
            P(("seq", "dp"), None),
            P(("seq", "dp"), None),
            P(("seq", "dp"), None),
            P(("seq", "dp"), None),
            P(None, ("seq", "dp")),
            P(None, ("seq", "dp")),
            P(None, ("seq", "dp")),
        ),
        check_vma=False,
    )
```

```python
import jax
import jax.numpy as jnp
from jax import lax
from jax.experimental import pallas as pl
from jax.experimental.pallas import tpu as pltpu
from jax.sharding import Mesh, PartitionSpec as P

D_BYTE = 768
D = 1536
HEADS = 24
HEAD_DIM = 64
FF = 6144
STEP = 10


NORM_EPS = 1e-05
SCORE_SCALE = 0.125
MASK_FILL = -1e30
BETA_ONE = 0.9
BETA_TWO = 0.95
ADAM_EPS = 1e-08
DECAY_RATE = 0.1
CLIP_NORM = 1.0


def prefix(part, axis, combine, identity):
    place = lax.axis_index(axis)
    gathered = lax.all_gather(part, axis)
    state = jnp.zeros_like(part) + jnp.asarray(identity, part.dtype)

    def one(hop, state):
        return combine(state, lax.dynamic_index_in_dim(gathered, hop, 0, False))

    return lax.fori_loop(0, place, one, state)


def normalize(values, gain):
    inverse = lax.rsqrt(jnp.mean(values * values, axis=-1, keepdims=True) + NORM_EPS)
    return values * inverse * gain


def add_counts(earlier, later):
    return earlier + later


def block_rows(amount):
    for option in (1024, 768, 512, 384, 256):
        if amount >= option and amount % option == 0:
            return option
    return amount


def spread_positions(first_row, amount, patch_dev, devices):
    whole_rows = first_row + jnp.arange(amount, dtype=jnp.int32)
    return whole_rows % patch_dev * devices + whole_rows // patch_dev


def make_attend(queries, patch_docs, patch_pos, patch_dev, devices):

    def attend(running, shards, offset):
        piece_keys, piece_values, piece_docs = shards
        amount = piece_keys.shape[0]
        span_rows = block_rows(amount)
        number = amount // span_rows
        key_blocks = piece_keys.reshape(number, span_rows, HEADS, HEAD_DIM)
        value_blocks = piece_values.reshape(number, span_rows, HEADS, HEAD_DIM)
        doc_blocks = piece_docs.reshape(number, span_rows)
        firsts = span_rows * jnp.arange(number, dtype=jnp.int32)

        def advance(status, section):
            block_keys, block_values, block_docs, block_first = section
            running_top, running_sum, running_out = status
            scores = (
                jnp.einsum("phd,khd->hpk", queries, block_keys, preferred_element_type=jnp.float32)
                * SCORE_SCALE
            )
            key_pos = spread_positions(block_first, span_rows, patch_dev, devices)
            allowed = (patch_docs[:, None] == block_docs[None, :]) & (
                key_pos[None, :] <= patch_pos[:, None]
            )
            masked = jnp.where(allowed[None], scores, MASK_FILL)
            new_top = jnp.maximum(running_top, jnp.max(masked, axis=-1))
            weights = jnp.where(allowed[None], jnp.exp(masked - new_top[..., None]), 0.0)
            rescale = jnp.exp(running_top - new_top)
            running_sum = running_sum * rescale + jnp.sum(weights, axis=-1)
            running_out = running_out * rescale[..., None] + jnp.einsum(
                "hpk,khd->hpd",
                weights.astype(jnp.bfloat16),
                block_values,
                preferred_element_type=jnp.float32,
            )
            return ((new_top, running_sum, running_out), None)

        running, _ = lax.scan(advance, running, (key_blocks, value_blocks, doc_blocks, firsts))
        return running

    return attend


def outer_sum(left, right):
    return jnp.einsum("pi,pj->ij", left, right, preferred_element_type=jnp.float32)


def back_product(grads, weight):
    return jnp.einsum("pj,ij->pi", grads, weight, preferred_element_type=jnp.float32)


def adam_update(master, first_old, second_old, gradient, clip_factor, learn_rate, weight_decay):
    clipped = gradient * clip_factor
    moment = BETA_ONE * first_old + (1.0 - BETA_ONE) * clipped
    square = BETA_TWO * second_old + (1.0 - BETA_TWO) * clipped * clipped
    corrected = (
        moment / (1.0 - BETA_ONE**STEP) / (jnp.sqrt(square / (1.0 - BETA_TWO**STEP)) + ADAM_EPS)
    )
    weight = master - learn_rate * (corrected + weight_decay * master)
    return (weight, moment, square)


def per_device(
    byte_rows,
    starts,
    doc_ids,
    out_cotangent,
    widen_master,
    widen_first,
    widen_second,
    triple_master,
    triple_first,
    triple_second,
    mixing_master,
    mixing_first,
    mixing_second,
    expand_master,
    expand_first,
    expand_second,
    shrink_master,
    shrink_first,
    shrink_second,
    narrow_master,
    narrow_first,
    narrow_second,
    gains_master,
    gains_first,
    gains_second,
):
    widen_full, triple_full, mixing_full, expand_full, shrink_full, narrow_full, gains_full = (
        lax.all_gather(widen_master.astype(jnp.bfloat16), ("seq", "dp"), axis=0, tiled=True),
        lax.all_gather(triple_master.astype(jnp.bfloat16), ("seq", "dp"), axis=0, tiled=True),
        lax.all_gather(mixing_master.astype(jnp.bfloat16), ("seq", "dp"), axis=0, tiled=True),
        lax.all_gather(expand_master.astype(jnp.bfloat16), ("seq", "dp"), axis=0, tiled=True),
        lax.all_gather(shrink_master.astype(jnp.bfloat16), ("seq", "dp"), axis=0, tiled=True),
        lax.all_gather(narrow_master.astype(jnp.bfloat16), ("seq", "dp"), axis=0, tiled=True),
        lax.all_gather(gains_master.astype(jnp.bfloat16), ("seq", "dp"), axis=1, tiled=True),
    )
    gain_one = gains_full[0].astype(jnp.float32)
    gain_two = gains_full[1].astype(jnp.float32)
    devices = lax.axis_size("seq")
    seq_place = lax.axis_index("seq")
    byte_block = byte_rows[0]
    start_flags = starts[0]
    doc_local = doc_ids[0]
    cotangent_rows = out_cotangent[0]
    byte_width = byte_block.shape[1]
    patch_dev = 3 * byte_block.shape[0] // 16
    capacity = patch_dev + patch_dev // 2
    slot_count = (capacity + devices - 2) // devices + 1
    buffer_rows = devices * slot_count
    amount = jnp.sum(start_flags)
    offset = prefix(amount, "seq", add_counts, jnp.int32(0))
    ranking = jnp.cumsum(start_flags) - start_flags
    patch_index = offset + ranking
    owners = patch_index % devices
    local_row = patch_index // devices
    slot_index = local_row - offset // devices
    target_slot = jnp.where(start_flags == 1, owners * slot_count + slot_index, buffer_rows)
    send_rows = (
        jnp.zeros((buffer_rows, byte_width), jnp.bfloat16)
        .at[target_slot]
        .set(byte_block, mode="drop")
    )
    send_meta = (
        jnp.full((buffer_rows, 2), patch_dev, jnp.int32)
        .at[target_slot]
        .set(jnp.stack([local_row, doc_local], axis=-1), mode="drop")
    )
    send_grad = (
        jnp.zeros((buffer_rows, byte_width), jnp.bfloat16)
        .at[target_slot]
        .set(cotangent_rows, mode="drop")
    )
    arrived_rows, arrived_meta = (
        lax.all_to_all(send_rows, "seq", split_axis=0, concat_axis=0, tiled=True),
        lax.all_to_all(send_meta, "seq", split_axis=0, concat_axis=0, tiled=True),
    )
    target = arrived_meta[:, 0]
    valid_slot = target < patch_dev
    patch_rows = (
        jnp.zeros((patch_dev, byte_width), jnp.bfloat16).at[target].set(arrived_rows, mode="drop")
    )
    patch_docs = jnp.zeros((patch_dev,), jnp.int32).at[target].set(arrived_meta[:, 1], mode="drop")
    patch_pos = seq_place + devices * jnp.arange(patch_dev, dtype=jnp.int32)
    widened = jnp.dot(patch_rows, widen_full, preferred_element_type=jnp.float32)
    model_width = widened.shape[1]
    first_low = normalize(widened, gain_one).astype(jnp.bfloat16)
    projected = jnp.dot(first_low, triple_full, preferred_element_type=jnp.float32).astype(
        jnp.bfloat16
    )
    queries = projected[:, :model_width].reshape(patch_dev, HEADS, HEAD_DIM)
    key_rows = projected[:, model_width : 2 * model_width]
    value_rows = projected[:, 2 * model_width :]
    initial = (
        jnp.full((HEADS, patch_dev), MASK_FILL, jnp.float32),
        jnp.zeros((HEADS, patch_dev), jnp.float32),
        jnp.zeros((HEADS, patch_dev, HEAD_DIM), jnp.float32),
    )
    attend = make_attend(queries, patch_docs, patch_pos, patch_dev, devices)
    running = attend(
        initial,
        (
            lax.all_gather(key_rows, "seq", axis=0, tiled=True),
            lax.all_gather(value_rows, "seq", axis=0, tiled=True),
            lax.all_gather(patch_docs, "seq", axis=0, tiled=True),
        ),
        jnp.int32(0),
    )
    running_top, running_sum, running_out = running
    attended = running_out / running_sum[..., None]
    log_total = running_top + jnp.log(running_sum)
    attended_low = (
        jnp.transpose(attended, (1, 0, 2)).reshape(patch_dev, model_width).astype(jnp.bfloat16)
    )
    resid_one = widened + jnp.dot(attended_low, mixing_full, preferred_element_type=jnp.float32)
    second_low = normalize(resid_one, gain_two).astype(jnp.bfloat16)
    expanded = jnp.dot(second_low, expand_full, preferred_element_type=jnp.float32)
    active_low = jax.nn.gelu(expanded).astype(jnp.bfloat16)
    resid_two = resid_one + jnp.dot(active_low, shrink_full, preferred_element_type=jnp.float32)
    resid_low = resid_two.astype(jnp.bfloat16)
    narrow_low = jnp.dot(resid_low, narrow_full, preferred_element_type=jnp.float32).astype(
        jnp.bfloat16
    )
    returned = jnp.where(valid_slot[:, None], jnp.take(narrow_low, target, axis=0, mode="clip"), 0)
    back_rows = lax.all_to_all(returned, "seq", split_axis=0, concat_axis=0, tiled=True)
    added = jnp.take(back_rows, target_slot, axis=0, mode="clip").astype(jnp.float32)
    new_block = byte_block.astype(jnp.float32) + jnp.where(start_flags[:, None] == 1, added, 0.0)
    arrived_grad = lax.all_to_all(send_grad, "seq", split_axis=0, concat_axis=0, tiled=True)
    narrow_back = (
        jnp.zeros((patch_dev, byte_width), jnp.bfloat16).at[target].set(arrived_grad, mode="drop")
    )
    narrow_grad = outer_sum(resid_low, narrow_back)
    upper_back = back_product(narrow_back, narrow_full)
    shrink_back = upper_back.astype(jnp.bfloat16)
    shrink_grad = outer_sum(active_low, shrink_back)
    active_back = back_product(shrink_back, shrink_full)
    _, gelu_pull = jax.vjp(jax.nn.gelu, expanded)
    expand_back = gelu_pull(active_back)[0].astype(jnp.bfloat16)
    expand_grad = outer_sum(second_low, expand_back)
    second_back = back_product(expand_back, expand_full)
    _, second_pull = jax.vjp(normalize, resid_one, gain_two)
    second_part, second_gain = second_pull(second_back)
    lower_back = upper_back + second_part
    mixed_back = lower_back.astype(jnp.bfloat16)
    mixing_grad = outer_sum(attended_low, mixed_back)
    attend_back = (
        back_product(mixed_back, mixing_full)
        .astype(jnp.bfloat16)
        .reshape(patch_dev, HEADS, HEAD_DIM)
    )
    delta_rows = jnp.einsum("phd,hpd->hp", attend_back.astype(jnp.float32), attended)
    all_keys, all_values, all_docs = (
        lax.all_gather(key_rows, "seq", axis=0, tiled=True),
        lax.all_gather(value_rows, "seq", axis=0, tiled=True),
        lax.all_gather(patch_docs, "seq", axis=0, tiled=True),
    )
    total_keys = all_keys.shape[0]
    span_rows = block_rows(total_keys)
    number = total_keys // span_rows
    key_blocks = all_keys.reshape(number, span_rows, HEADS, HEAD_DIM)
    value_blocks = all_values.reshape(number, span_rows, HEADS, HEAD_DIM)
    doc_blocks = all_docs.reshape(number, span_rows)
    firsts = span_rows * jnp.arange(number, dtype=jnp.int32)
    query_start = jnp.zeros((patch_dev, HEADS, HEAD_DIM), jnp.float32)

    def backstep(query_back, section):
        block_keys, block_values, block_docs, block_first = section
        scores = (
            jnp.einsum("phd,khd->hpk", queries, block_keys, preferred_element_type=jnp.float32)
            * SCORE_SCALE
        )
        key_pos = spread_positions(block_first, span_rows, patch_dev, devices)
        allowed = (patch_docs[:, None] == block_docs[None, :]) & (
            key_pos[None, :] <= patch_pos[:, None]
        )
        probs = jnp.where(allowed[None], jnp.exp(scores - log_total[..., None]), 0.0)
        prob_back = jnp.einsum(
            "phd,khd->hpk", attend_back, block_values, preferred_element_type=jnp.float32
        )
        score_back = (probs * (prob_back - delta_rows[..., None])).astype(jnp.bfloat16)
        query_back = (
            query_back
            + jnp.einsum("hpk,khd->phd", score_back, block_keys, preferred_element_type=jnp.float32)
            * SCORE_SCALE
        )
        keys_part = (
            jnp.einsum("hpk,phd->khd", score_back, queries, preferred_element_type=jnp.float32)
            * SCORE_SCALE
        )
        values_part = jnp.einsum(
            "hpk,phd->khd",
            probs.astype(jnp.bfloat16),
            attend_back,
            preferred_element_type=jnp.float32,
        )
        return (
            query_back,
            (
                keys_part.reshape(span_rows, model_width),
                values_part.reshape(span_rows, model_width),
            ),
        )

    query_back, (keys_back, values_back) = lax.scan(
        backstep, query_start, (key_blocks, value_blocks, doc_blocks, firsts)
    )
    keys_own, values_own = (
        lax.psum_scatter(
            keys_back.reshape(total_keys, model_width).astype(jnp.bfloat16),
            "seq",
            scatter_dimension=0,
            tiled=True,
        ).astype(jnp.float32),
        lax.psum_scatter(
            values_back.reshape(total_keys, model_width).astype(jnp.bfloat16),
            "seq",
            scatter_dimension=0,
            tiled=True,
        ).astype(jnp.float32),
    )
    triple_back = jnp.concatenate(
        [query_back.reshape(patch_dev, model_width), keys_own, values_own], axis=1
    ).astype(jnp.bfloat16)
    triple_grad = outer_sum(first_low, triple_back)
    first_back = back_product(triple_back, triple_full)
    _, first_pull = jax.vjp(normalize, widened, gain_one)
    first_part, first_gain = first_pull(first_back)
    base_low = (lower_back + first_part).astype(jnp.bfloat16)
    widen_grad = outer_sum(patch_rows, base_low)
    patch_back = back_product(base_low, widen_full).astype(jnp.bfloat16)
    grad_slots = jnp.where(
        valid_slot[:, None], jnp.take(patch_back, target, axis=0, mode="clip"), 0
    )
    grad_rows = lax.all_to_all(grad_slots, "seq", split_axis=0, concat_axis=0, tiled=True)
    coming = jnp.take(grad_rows, target_slot, axis=0, mode="clip").astype(jnp.float32)
    grad_block = cotangent_rows.astype(jnp.float32) + jnp.where(
        start_flags[:, None] == 1, coming, 0.0
    )
    gains_grad = jnp.stack([first_gain, second_gain], axis=0)
    reduced = (
        lax.psum_scatter(widen_grad, ("seq", "dp"), scatter_dimension=0, tiled=True),
        lax.psum_scatter(triple_grad, ("seq", "dp"), scatter_dimension=0, tiled=True),
        lax.psum_scatter(mixing_grad, ("seq", "dp"), scatter_dimension=0, tiled=True),
        lax.psum_scatter(expand_grad, ("seq", "dp"), scatter_dimension=0, tiled=True),
        lax.psum_scatter(shrink_grad, ("seq", "dp"), scatter_dimension=0, tiled=True),
        lax.psum_scatter(narrow_grad, ("seq", "dp"), scatter_dimension=0, tiled=True),
        lax.psum_scatter(gains_grad, ("seq", "dp"), scatter_dimension=1, tiled=True),
    )
    local_squares = jnp.float32(0.0)
    for member in reduced:
        local_squares = local_squares + jnp.sum(member * member)
    norm_squared = lax.psum(local_squares, ("seq", "dp"))
    grad_norm = jnp.sqrt(norm_squared)
    factor = CLIP_NORM / jnp.maximum(grad_norm, CLIP_NORM)
    masters = (
        widen_master,
        triple_master,
        mixing_master,
        expand_master,
        shrink_master,
        narrow_master,
        gains_master,
    )
    firsts_old = (
        widen_first,
        triple_first,
        mixing_first,
        expand_first,
        shrink_first,
        narrow_first,
        gains_first,
    )
    seconds_old = (
        widen_second,
        triple_second,
        mixing_second,
        expand_second,
        shrink_second,
        narrow_second,
        gains_second,
    )
    rates = (
        2.0 * D_BYTE ** (-0.5),
        2.0 * D ** (-0.5),
        0.4,
        2.0 * D ** (-0.5),
        2.0 * FF ** (-0.5),
        2.0 * D ** (-0.5),
        0.6,
    )
    decays = (DECAY_RATE, DECAY_RATE, DECAY_RATE, DECAY_RATE, DECAY_RATE, DECAY_RATE, 0.0)
    updates = [
        adam_update(
            masters[index],
            firsts_old[index],
            seconds_old[index],
            reduced[index],
            factor,
            rates[index],
            decays[index],
        )
        for index in range(7)
    ]
    return (
        new_block.astype(jnp.bfloat16)[None],
        grad_block.astype(jnp.bfloat16)[None],
        grad_norm,
        updates[0][0],
        updates[0][1],
        updates[0][2],
        updates[1][0],
        updates[1][1],
        updates[1][2],
        updates[2][0],
        updates[2][1],
        updates[2][2],
        updates[3][0],
        updates[3][1],
        updates[3][2],
        updates[4][0],
        updates[4][1],
        updates[4][2],
        updates[5][0],
        updates[5][1],
        updates[5][2],
        updates[6][0],
        updates[6][1],
        updates[6][2],
    )


PLANES = 4
TEAM = 8
CORE_BIT, Y_BIT, X_BIT = 1, 2, 4
AXES = ("z", "x", "y", "c")
TEAM_AXES = ("x", "y", "c")
LOW = jnp.bfloat16
WIDE = jnp.float32
VMEM_LIMIT = 56 * 1024 * 1024
LOG2_E = 1.4426950408889634
GELU_A = 0.7978845608028654
GELU_B = 0.044715


def plane_fits(mesh):
    return mesh.shape["seq"] == 2 * PLANES and mesh.shape["dp"] == PLANES


def flip(value, bit):
    pairs = [(place, place ^ bit) for place in range(PLANES * TEAM)]
    return lax.ppermute(value, AXES, pairs)


def shift_plane(value, hop):
    pairs = [
        (plane * TEAM + t, (plane + hop) % PLANES * TEAM + t)
        for plane in range(PLANES)
        for t in range(TEAM)
    ]
    return lax.ppermute(value, AXES, pairs)


SEQUENCE_OF_PLANE = (2, 0, 1, 3)


def source_of(plane, t):
    return (plane + t // 2 % 2 + 2 * (t % 2) + 2 * PLANES) % PLANES * 2 + t // 4


def byte_pairs():
    return [
        (source_of(plane, t) * PLANES + SEQUENCE_OF_PLANE[plane], plane * TEAM + t)
        for plane in range(PLANES)
        for t in range(TEAM)
    ]


def to_plane(value):
    return lax.ppermute(value, AXES, byte_pairs())


def from_plane(value):
    return lax.ppermute(value, AXES, [(there, here) for here, there in byte_pairs()])


def team_gather(block, cut=None, before_relay=lambda own: ()):
    cut = block.shape[0] // 2 if cut is None else cut
    from_x = flip(block, X_BIT)
    from_y = flip(block, Y_BIT)
    from_core = flip(block, CORE_BIT)
    from_x, from_y = after((from_x, from_y), *before_relay(from_core))
    to_x, to_y = from_y[:cut], from_x[cut:]
    upper = flip(to_x, X_BIT)
    lower = flip(to_y, Y_BIT)
    y_core = flip(from_y, CORE_BIT)
    x_core = flip(from_x, CORE_BIT)
    return [
        block,
        from_core,
        from_y,
        y_core,
        from_x,
        x_core,
        upper,
        lower,
        flip(upper, CORE_BIT),
        flip(lower, CORE_BIT),
    ], (to_x, to_y)


PIECES = 10


def piece(refs, m):
    if m < 6:
        return refs[m][...]
    return jnp.concatenate([refs[2 * m - 6][...], refs[2 * m - 5][...]], axis=0)


def team_scatter(far_send, far_keep, x_send, x_keep, y_send, y_keep, own_send, own_keep):
    def pair(send, keep):
        return keep.astype(WIDE) + flip(send, CORE_BIT).astype(WIDE)

    far = pair(far_send, far_keep).astype(LOW)
    cut = far.shape[0] // 2
    upper = flip(far[:cut], X_BIT).astype(WIDE)
    lower = flip(far[cut:], Y_BIT).astype(WIDE)
    to_x, to_y = pair(x_send, x_keep), pair(y_send, y_keep)
    to_x = jnp.concatenate([to_x[:cut], to_x[cut:] + lower], axis=0).astype(LOW)
    to_y = jnp.concatenate([to_y[:cut] + upper, to_y[cut:]], axis=0).astype(LOW)
    terms = (own_keep, flip(own_send, CORE_BIT), flip(to_x, X_BIT), flip(to_y, Y_BIT))
    return terms, (to_x, to_y)


def put_terms(outs, m, value):
    outs[7 - m][...] = value.astype(LOW)


def term_shapes(rows, width):
    return (jax.ShapeDtypeStruct((rows, width), LOW),) * TEAM


def add_terms(refs, lanes=slice(None)):
    total = refs[0][:, lanes].astype(WIDE)
    for ref in refs[1:]:
        total = total + ref[:, lanes].astype(WIDE)
    return total


def after(value, *earlier):
    return lax.optimization_barrier((value,) + earlier)[0]


def plane_gather_small(block):
    return [block] + [shift_plane(block, hop) for hop in (1, 2, 3)]


def plane_scatter_small(stack):
    back = lax.all_to_all(stack.astype(LOW), "z", split_axis=0, concat_axis=0, tiled=True)
    return jnp.sum(back.astype(WIDE), axis=0)


def team_exchange(value):
    return lax.all_to_all(value, TEAM_AXES, split_axis=0, concat_axis=0, tiled=True)


def pick(value, place, axis):
    return lax.dynamic_index_in_dim(value, place, axis, False)


def in_vmem():
    return pl.BlockSpec(memory_space=pltpu.VMEM)


def in_smem():
    return pl.BlockSpec(memory_space=pltpu.SMEM)


def params():
    return pltpu.CompilerParams(vmem_limit_bytes=VMEM_LIMIT)


def estimate(microseconds):
    return pl.CostEstimate(
        flops=int(microseconds * 8e8), bytes_accessed=int(microseconds * 2e6), transcendentals=0
    )


def nn(left, right):
    return lax.dot_general(left, right, (((1,), (0,)), ((), ())), preferred_element_type=WIDE)


def nt(left, right):
    return lax.dot_general(left, right, (((1,), (1,)), ((), ())), preferred_element_type=WIDE)


def tn(left, right):
    return lax.dot_general(left, right, (((0,), (0,)), ((), ())), preferred_element_type=WIDE)


def slot_matrix(flags, slots):
    amount = flags.shape[1]
    row = lax.broadcasted_iota(jnp.int32, (amount, amount), 0)
    column = lax.broadcasted_iota(jnp.int32, (amount, amount), 1)
    before = jnp.where(row < column, 1.0, 0.0).astype(LOW)
    rank = nn(jnp.broadcast_to(flags, (8, amount)).astype(LOW), before)[:1]
    rank = jnp.where(flags > 0.5, rank, -1.0)
    slot = lax.broadcasted_iota(jnp.int32, (slots, amount), 0).astype(WIDE)
    return jnp.where(slot == rank, 1.0, 0.0).astype(LOW)


def pack_kernel(starts_ref, docs_ref, rows_ref, cotangent_ref, rows_out, chosen_out):
    capacity = chosen_out.shape[0]
    width = rows_out.shape[1]
    flags = starts_ref[...].astype(WIDE)
    chosen = slot_matrix(flags, 384)
    amount = jnp.sum(flags)
    docs = nt(jnp.broadcast_to(docs_ref[...].astype(WIDE), (16, flags.shape[1])).astype(LOW), chosen)
    docs = jnp.concatenate([docs, jnp.zeros((16, width - 384), WIDE)], axis=1)
    row = lax.broadcasted_iota(jnp.int32, (16, width), 0)
    high = jnp.floor(amount * 0.5)
    meta = jnp.where(row == 0, docs, jnp.where(row == 1, high, amount - 2.0 * high))
    chosen = chosen[:capacity]
    chosen_out[...] = chosen
    rows_out[:16] = meta.astype(LOW)
    rows_out[16 : 16 + capacity] = nn(chosen, rows_ref[...]).astype(LOW)
    rows_out[16 + capacity :] = nn(chosen, cotangent_ref[...]).astype(LOW)


def pack(starts, docs, rows, cotangent_rows, capacity):
    amount, width = rows.shape
    return pl.pallas_call(
        pack_kernel,
        out_shape=(
            jax.ShapeDtypeStruct((2 * capacity + 16, width), LOW),
            jax.ShapeDtypeStruct((capacity, amount), LOW),
        ),
        in_specs=[in_vmem()] * 4,
        out_specs=(in_vmem(), in_vmem()),
        compiler_params=params(),
        cost_estimate=estimate(5),
        name="pack",
    )(starts, docs, rows, cotangent_rows)


def unpack_kernel(chosen_ref, rows_ref, cotangent_ref, back_ref, rows_out, cotangent_out):
    width = rows_ref.shape[1]
    added = tn(chosen_ref[...], back_ref[...])
    rows_out[...] = (rows_ref[...].astype(WIDE) + added[:, :width]).astype(LOW)
    cotangent_out[...] = (cotangent_ref[...].astype(WIDE) + added[:, width:]).astype(LOW)


def unpack(chosen, rows, cotangent_rows, back):
    return pl.pallas_call(
        unpack_kernel,
        out_shape=(jax.ShapeDtypeStruct(rows.shape, LOW),) * 2,
        in_specs=[in_vmem()] * 4,
        out_specs=(in_vmem(),) * 2,
        compiler_params=params(),
        cost_estimate=estimate(5),
        name="unpack",
    )(chosen, rows, cotangent_rows, back)


def window_matrix(first, amount, capacity):
    target = lax.broadcasted_iota(jnp.int32, (capacity + 16, capacity), 0)
    source = lax.broadcasted_iota(jnp.int32, (capacity + 16, capacity), 1)
    moved = (target == source + first % 16) & (source < amount)
    return jnp.where(moved, 1.0, 0.0).astype(LOW)


def widen_kernel(place_ref, *refs):
    pieces = refs[:PIECES]
    widen_out, gains_out, narrow_out = refs[PIECES : PIECES + 3]
    widen_wide, gains = refs[PIECES + 3 :]
    plane, t = place_ref[0], place_ref[1]
    shards = PLANES * TEAM
    shard = widen_out.shape[0] // shards
    model = widen_out.shape[1]
    width = model // 2
    gain_shard = model // shards
    for m in range(TEAM):
        low = piece(pieces, m)
        here = low.astype(WIDE)
        for hop in range(PLANES):
            place = (plane - hop + PLANES) % PLANES * TEAM + (t ^ m)
            at = pl.ds(pl.multiple_of(place * shard, 8), shard)
            base = hop * (64 + gain_shard)
            narrow_at = pl.ds(pl.multiple_of(place * gain_shard, 16), gain_shard)
            narrow_out[narrow_at] = low[base + 64 : base + 64 + gain_shard]
            widen_wide[at, :width] = here[base : base + shard]
            widen_wide[at, width:] = here[base + 32 : base + 32 + shard]
            gains[0, pl.ds(place, 1)] = here[base + shard : base + shard + 1, :128]
            gains[1, pl.ds(place, 1)] = here[base + shard + 1 : base + shard + 2, :128]
    widen_out[...] = widen_wide[...].astype(LOW)
    column = lax.broadcasted_iota(jnp.int32, (shards, model), 1)
    owner = lax.broadcasted_iota(jnp.int32, (shards, model), 0)
    owned = (column >= owner * gain_shard) & (column < (owner + 1) * gain_shard)
    inside = jnp.sum(jnp.where(owned, column - owner * gain_shard, 0).astype(WIDE), axis=0, keepdims=True)
    row = lax.broadcasted_iota(jnp.int32, (128, model), 0).astype(WIDE)
    owned = jnp.where(owned, 1.0, 0.0).astype(LOW)
    for k in range(2):
        spread = tn(gains[k].astype(LOW), owned)
        line = jnp.sum(jnp.where(row == inside, spread, 0.0), axis=0, keepdims=True)
        gains_out[k * 8 : k * 8 + 8] = jnp.broadcast_to(line, (8, model))


def widen_whole(place, pieces, shard, model):
    return pl.pallas_call(
        widen_kernel,
        out_shape=(
            jax.ShapeDtypeStruct((shard * PLANES * TEAM, model), LOW),
            jax.ShapeDtypeStruct((16, model), WIDE),
            jax.ShapeDtypeStruct((model, pieces[0].shape[1]), LOW),
        ),
        in_specs=[in_smem()] + [in_vmem()] * PIECES,
        out_specs=(in_vmem(),) * 3,
        scratch_shapes=[
            pltpu.VMEM((shard * PLANES * TEAM, model), WIDE),
            pltpu.VMEM((2, PLANES * TEAM, 128), WIDE),
        ],
        compiler_params=params(),
        cost_estimate=estimate(5),
        name="widen_whole",
    )(place, *pieces)


def enter_kernel(capacity, place_ref, gains_ref, widen_ref, *refs):
    pieces = refs[:PIECES]
    low_out, own_wide, own_rows, doc_column, doc_row, spans = refs[PIECES : PIECES + 6]
    rows, docs = refs[PIECES + 6 :]
    plane, t = place_ref[0], place_ref[1]
    member_rows = own_rows.shape[0]
    total = low_out.shape[0]

    metas = [pieces[m][:16] for m in range(6)] + [pieces[6][:16], pieces[8][:16]]
    blocks = [piece(pieces, m)[16 : 16 + capacity] for m in range(TEAM)]
    amounts, sources = [], []
    for m in range(TEAM):
        meta = metas[m].astype(WIDE)
        row = lax.broadcasted_iota(jnp.int32, meta.shape, 0)
        lane = lax.broadcasted_iota(jnp.int32, meta.shape, 1)
        picked = jnp.where(lane == 0, jnp.where(row == 1, 2.0 * meta, jnp.where(row == 2, meta, 0.0)), 0.0)
        amounts.append(jnp.sum(picked).astype(jnp.int32))
        sources.append(source_of(plane, t ^ m))
    firsts = []
    for m in range(TEAM):
        first = jnp.int32(0)
        for other in range(TEAM):
            if other != m:
                first = first + jnp.where(sources[other] < sources[m], amounts[other], 0)
        firsts.append(first)
        spans[m] = first
        spans[TEAM + m] = amounts[m]

    rows[...] = jnp.zeros_like(rows)
    docs[...] = jnp.zeros_like(docs)
    for m in range(TEAM):
        moving = window_matrix(firsts[m], amounts[m], capacity)
        at = pl.ds(pl.multiple_of(firsts[m] // 16 * 16, 16), capacity + 16)
        rows[at] = rows[at] + nn(moving, blocks[m]).astype(LOW)
        names = metas[m][:1, :384]
        names = jnp.broadcast_to(names, (128, 384))[:, :capacity]
        docs[at] = docs[at] + nt(moving, names)

    doc_column[...] = docs[:total]
    select = jnp.where(lax.broadcasted_iota(jnp.int32, (8, 128), 1) == 0, 1.0, 0.0).astype(LOW)
    doc_row[...] = nt(select, docs[:total].astype(LOW))
    own_rows[...] = rows[pl.ds(pl.multiple_of(t * member_rows, 16), member_rows)]

    def one(k, carry):
        at = pl.ds(pl.multiple_of(k * 2 * member_rows, 16), 2 * member_rows)
        wide = nn(rows[at], widen_ref[...])
        inverse = lax.rsqrt(jnp.mean(wide * wide, axis=-1, keepdims=True) + NORM_EPS)
        low_out[at] = (wide * inverse * gains_ref[:1]).astype(LOW)
        return carry

    lax.fori_loop(0, TEAM // 2, one, 0)
    own_wide[...] = nn(own_rows[...], widen_ref[...])


def enter(place, gains, widen_full, pieces, capacity, member_rows):
    width, model = widen_full.shape
    total = member_rows * TEAM
    padded = total + capacity + 16
    return pl.pallas_call(
        lambda *refs: enter_kernel(capacity, *refs),
        out_shape=(
            jax.ShapeDtypeStruct((total, model), LOW),
            jax.ShapeDtypeStruct((member_rows, model), WIDE),
            jax.ShapeDtypeStruct((member_rows, width), LOW),
            jax.ShapeDtypeStruct((total, 128), WIDE),
            jax.ShapeDtypeStruct((8, total), WIDE),
            jax.ShapeDtypeStruct((2 * TEAM,), jnp.int32),
        ),
        in_specs=[in_smem(), in_vmem(), in_vmem()] + [in_vmem()] * PIECES,
        out_specs=(in_vmem(),) * 5 + (in_smem(),),
        scratch_shapes=[
            pltpu.VMEM((padded, width), LOW),
            pltpu.VMEM((padded, 128), WIDE),
        ],
        compiler_params=params(),
        cost_estimate=estimate(14),
        name="enter",
    )(place, gains, widen_full, *pieces)


def cotangent_kernel(capacity, place_ref, spans_ref, narrow_ref, *refs):
    pieces = refs[:PIECES]
    low_out, own_wide, all_rows = refs[PIECES : PIECES + 3]
    (rows,) = refs[PIECES + 3 :]
    t = place_ref[1]
    member_rows = own_wide.shape[0]
    rows[...] = jnp.zeros_like(rows)
    for m in range(TEAM):
        first = spans_ref[m]
        moving = window_matrix(first, spans_ref[TEAM + m], capacity)
        at = pl.ds(pl.multiple_of(first // 16 * 16, 16), capacity + 16)
        rows[at] = rows[at] + nn(moving, piece(pieces, m)[16 + capacity :]).astype(LOW)
    all_rows[...] = rows[: all_rows.shape[0]]

    def one(k, carry):
        first = pl.multiple_of((t ^ (2 * k)) * member_rows, 16)
        second = pl.multiple_of((t ^ (2 * k + 1)) * member_rows, 16)
        here = jnp.concatenate(
            [rows[pl.ds(first, member_rows)], rows[pl.ds(second, member_rows)]], axis=0
        )
        at = pl.ds(pl.multiple_of(k * 2 * member_rows, 16), 2 * member_rows)
        low_out[at] = nt(here, narrow_ref[...]).astype(LOW)
        return carry

    lax.fori_loop(0, TEAM // 2, one, 0)
    own_wide[...] = nt(
        rows[pl.ds(pl.multiple_of(t * member_rows, 16), member_rows)], narrow_ref[...]
    )


def cotangent(place, spans, narrow_full, pieces, capacity, member_rows):
    model, width = narrow_full.shape
    total = member_rows * TEAM
    return pl.pallas_call(
        lambda *refs: cotangent_kernel(capacity, *refs),
        out_shape=(
            jax.ShapeDtypeStruct((total, model), LOW),
            jax.ShapeDtypeStruct((member_rows, model), WIDE),
            jax.ShapeDtypeStruct((total, width), LOW),
        ),
        in_specs=[in_smem(), in_smem()] + [in_vmem()] * (1 + PIECES),
        out_specs=(in_vmem(),) * 3,
        scratch_shapes=[pltpu.VMEM((total + capacity + 16, width), LOW)],
        compiler_params=params(),
        cost_estimate=estimate(13),
        name="cotangent",
    )(place, spans, narrow_full, *pieces)


def leave_kernel(place_ref, spans_ref, *refs):
    pieces, out_ref, total = refs[:PIECES], refs[PIECES], refs[PIECES + 1]
    t = place_ref[1]
    first = spans_ref[0]
    capacity = out_ref.shape[0]
    total[...] = jnp.zeros_like(total)
    for m in range(TEAM):
        rows = pieces[0].shape[0]
        offset = (t ^ m) * rows - first

        @pl.when((offset < capacity) & (offset + rows > 0))
        def _(m=m, offset=offset, rows=rows):
            target = lax.broadcasted_iota(jnp.int32, (capacity, rows), 0)
            source = lax.broadcasted_iota(jnp.int32, (capacity, rows), 1) + offset
            total[...] += nn(jnp.where(target == source, 1.0, 0.0).astype(LOW), piece(pieces, m))

    out_ref[...] = total[...].astype(LOW)


def leave(place, spans, pieces, capacity):
    width = pieces[0].shape[1]
    return pl.pallas_call(
        leave_kernel,
        out_shape=jax.ShapeDtypeStruct((capacity, width), LOW),
        in_specs=[in_smem(), in_smem()] + [in_vmem()] * PIECES,
        out_specs=in_vmem(),
        scratch_shapes=[pltpu.VMEM((capacity, width), WIDE)],
        compiler_params=params(),
        cost_estimate=estimate(2),
        name="leave",
    )(place, spans, *pieces)


def norm_kernel(wide_ref, gains_ref, *refs):
    resid_out, low_out = refs[4:]
    resid = wide_ref[...] + add_terms(refs[:4])
    resid_out[...] = resid
    inverse = lax.rsqrt(jnp.mean(resid * resid, axis=-1, keepdims=True) + NORM_EPS)
    low_out[...] = (resid * inverse * gains_ref[8:9]).astype(LOW)


def add_and_norm(wide, gains, terms):
    return pl.pallas_call(
        norm_kernel,
        out_shape=(
            jax.ShapeDtypeStruct(wide.shape, WIDE),
            jax.ShapeDtypeStruct(wide.shape, LOW),
        ),
        in_specs=[in_vmem()] * 6,
        out_specs=(in_vmem(),) * 2,
        compiler_params=params(),
        cost_estimate=estimate(2),
        name="add_and_norm",
    )(wide, gains, *terms)


def norm_back(resid, gain, incoming):
    inverse = lax.rsqrt(jnp.mean(resid * resid, axis=-1, keepdims=True) + NORM_EPS)
    scaled = incoming * gain
    along = jnp.mean(scaled * resid, axis=-1, keepdims=True)
    back = inverse * scaled - resid * (inverse * inverse * inverse * along)
    return back, jnp.sum(incoming * resid * inverse, axis=0, keepdims=True)


def second_back_kernel(resid_ref, gains_ref, upper_ref, *refs):
    lower_out, low_out, gain_out = refs[4:]
    back, gain_back = norm_back(
        resid_ref[...], gains_ref[8:9], add_terms(refs[:4], slice(resid_ref.shape[1]))
    )
    lower = upper_ref[...] + back
    lower_out[...] = lower
    low_out[...] = lower.astype(LOW)
    gain_out[...] = jnp.broadcast_to(gain_back, gain_out.shape)


def second_norm_back(resid, gains, upper, terms):
    rows, model = resid.shape
    return pl.pallas_call(
        second_back_kernel,
        out_shape=(
            jax.ShapeDtypeStruct((rows, model), WIDE),
            jax.ShapeDtypeStruct((rows, model), LOW),
            jax.ShapeDtypeStruct((8, model), WIDE),
        ),
        in_specs=[in_vmem()] * 7,
        out_specs=(in_vmem(),) * 3,
        compiler_params=params(),
        cost_estimate=estimate(2),
        name="second_norm_back",
    )(resid, gains, upper, *terms)


def first_back_kernel(
    place_ref, wide_ref, gains_ref, lower_ref, rows_ref, widen_ref, second_gain_ref, narrow_ref, *refs
):
    patch_out = refs[4]
    outs = refs[5:13]
    grad = refs[13]
    t = place_ref[1]
    back, first_gain = norm_back(wide_ref[...], gains_ref[:1], add_terms(refs[:4]))
    low = (lower_ref[...] + back).astype(LOW)
    grad[...] = tn(rows_ref[...], low)
    shard = grad.shape[0] // (PLANES * TEAM)
    row = lax.broadcasted_iota(jnp.int32, (16, grad.shape[1]), 0)
    gain_rows = jnp.where(row == 0, first_gain, jnp.where(row == 1, second_gain_ref[:1], 0.0))
    for m in (7, 6, 5, 3, 4, 2, 1, 0):
        parts = [
            grad[pl.ds(pl.multiple_of((plane * TEAM + (t ^ m)) * shard, 8), shard)]
            for plane in range(PLANES)
        ]
        put_terms(outs, m, jnp.concatenate(parts + [gain_rows], axis=0))
    width = narrow_ref.shape[1]
    patch_out[:, :width] = narrow_ref[...]
    patch_out[:, width:] = nt(low, widen_ref[...]).astype(LOW)


def first_norm_back(place, wide, gains, lower, rows, widen_full, second_gain, narrow_low, terms):
    model = wide.shape[1]
    width = widen_full.shape[0]
    return pl.pallas_call(
        first_back_kernel,
        out_shape=(jax.ShapeDtypeStruct((rows.shape[0], 2 * width), LOW),)
        + term_shapes(width // TEAM + 16, model),
        in_specs=[in_smem()] + [in_vmem()] * 11,
        out_specs=(in_vmem(),) * 9,
        scratch_shapes=[pltpu.VMEM((width, model), WIDE)],
        compiler_params=params(),
        cost_estimate=estimate(5),
        name="first_norm_back",
    )(place, wide, gains, lower, rows, widen_full, second_gain, narrow_low, *terms)


def exit_kernel(resid_ref, narrow_ref, *refs):
    low_out, narrow_out = refs[4:]
    model = resid_ref.shape[1]
    wide = resid_ref[...] + add_terms(refs[:4], slice(model, 2 * model))
    low = wide.astype(LOW)
    shard = low_out.shape[2] // PLANES
    for m in range(TEAM):
        parts = [
            wide[:, (plane * TEAM + m) * shard : (plane * TEAM + m + 1) * shard]
            for plane in range(PLANES)
        ]
        low_out[m] = jnp.concatenate(parts, axis=1).astype(LOW)
    narrow_out[...] = nn(low, narrow_ref[...]).astype(LOW)


def exit_block(resid, narrow_full, terms):
    rows, model = resid.shape
    return pl.pallas_call(
        exit_kernel,
        out_shape=(
            jax.ShapeDtypeStruct((TEAM, rows, model // TEAM), LOW),
            jax.ShapeDtypeStruct((rows, narrow_full.shape[1]), LOW),
        ),
        in_specs=[in_vmem()] * 6,
        out_specs=(in_vmem(),) * 2,
        compiler_params=params(),
        cost_estimate=estimate(4),
        name="exit_block",
    )(resid, narrow_full, *terms)


def forward_terms_kernel(left_ref, right_ref, *outs):
    rows = left_ref.shape[0] // TEAM
    for k in (3, 2, 1, 0):
        product = nn(left_ref[2 * k * rows : (2 * k + 2) * rows], right_ref[...])
        put_terms(outs, 2 * k + 1, product[rows:])
        put_terms(outs, 2 * k, product[:rows])


def forward_terms(left, right):
    return pl.pallas_call(
        forward_terms_kernel,
        out_shape=term_shapes(left.shape[0] // TEAM, right.shape[1]),
        in_specs=[in_vmem()] * 2,
        out_specs=(in_vmem(),) * 8,
        compiler_params=params(),
        cost_estimate=estimate(6),
        name="forward_terms",
    )(left, right)


def feed_kernel(expand_ref, shrink_ref, back_ref, *refs):
    pieces = refs[:PIECES]
    second_out, active_out, expand_out = refs[PIECES : PIECES + 3]
    outs = refs[PIECES + 3 :]
    rows = back_ref.shape[0] // TEAM
    for k in (3, 2, 1, 0):
        at = slice(2 * k * rows, (2 * k + 2) * rows)
        low = jnp.concatenate([piece(pieces, 2 * k), piece(pieces, 2 * k + 1)], axis=0)
        second_out[at] = low
        value = nn(low, expand_ref[...])
        square = value * value
        bend = jnp.tanh(GELU_A * (value + GELU_B * square * value))
        active_out[at] = (0.5 * value * (1.0 + bend)).astype(LOW)
        slope = 0.5 * (1.0 + bend) + 0.5 * value * (1.0 - bend * bend) * (
            GELU_A * (1.0 + 3.0 * GELU_B * square)
        )
        back = (slope * nt(back_ref[at], shrink_ref[...])).astype(LOW)
        expand_out[at] = back
        product = jnp.concatenate(
            [nt(back, expand_ref[...]).astype(LOW), nn(active_out[at], shrink_ref[...]).astype(LOW)],
            axis=1,
        )
        put_terms(outs, 2 * k + 1, product[rows:])
        put_terms(outs, 2 * k, product[:rows])


def feed(expand_own, shrink_own, shrink_back, pieces):
    total, model = shrink_back.shape
    hidden = expand_own.shape[1]
    return pl.pallas_call(
        feed_kernel,
        out_shape=(
            jax.ShapeDtypeStruct((total, model), LOW),
            jax.ShapeDtypeStruct((total, hidden), LOW),
            jax.ShapeDtypeStruct((total, hidden), LOW),
        )
        + term_shapes(total // TEAM, 2 * model),
        in_specs=[in_vmem()] * (3 + PIECES),
        out_specs=(in_vmem(),) * 11,
        compiler_params=params(),
        cost_estimate=estimate(18),
        name="feed",
    )(expand_own, shrink_own, shrink_back, *pieces)


def attend_kernel(
    own,
    tile,
    place_ref,
    first_ref,
    triple_ref,
    doc_column,
    doc_row,
    projected_ref,
    flat_out,
    low_out,
    total_out,
    queries,
    keys,
    values,
    attended,
):
    t = place_ref[1]
    rows = first_ref.shape[0]
    member_rows = rows // TEAM
    width = own * HEAD_DIM

    def project(k, carry):
        at = pl.ds(pl.multiple_of(k * 2 * member_rows, 16), 2 * member_rows)
        projected_ref[at] = nn(first_ref[at], triple_ref[...]).astype(LOW)
        return carry

    lax.fori_loop(0, TEAM // 2, project, 0)
    for h in range(own):
        lanes = slice(h * HEAD_DIM, (h + 1) * HEAD_DIM)
        queries[h] = projected_ref[:, :width][:, lanes]
        keys[h] = projected_ref[:, width : 2 * width][:, lanes]
        values[h] = jnp.transpose(
            projected_ref[:, 2 * width :][:, lanes].astype(WIDE)
        ).astype(LOW)
    total_out[...] = jnp.zeros_like(total_out)
    scale = SCORE_SCALE * LOG2_E
    causal = lax.broadcasted_iota(jnp.int32, (tile, tile), 0) <= lax.broadcasted_iota(
        jnp.int32, (tile, tile), 1
    )

    def one_query(j, carry):
        at_query = pl.ds(pl.multiple_of(j * tile, tile), tile)
        query_docs = doc_row[:1, at_query]

        def one_key(i, status, diagonal):
            at_key = pl.ds(pl.multiple_of(i * tile, tile), tile)
            allowed = doc_column[at_key, :1] == query_docs
            if diagonal:
                allowed = allowed & causal
            result = []
            for h in range(own):
                scores = nt(keys[h, at_key], queries[h, at_query]) * scale
                masked = jnp.where(allowed, scores, MASK_FILL)
                best = jnp.max(masked, axis=0, keepdims=True)
                if diagonal:
                    top = best
                    weights = jnp.exp2(masked - top)
                    summed = jnp.sum(weights, axis=0, keepdims=True)
                    out = nn(values[h, :, at_key], weights.astype(LOW))
                else:
                    old_top, old_sum, old_out = status[h]
                    top = jnp.maximum(old_top, best)
                    weights = jnp.exp2(masked - top)
                    rescale = jnp.exp2(old_top - top)
                    summed = old_sum * rescale + jnp.sum(weights, axis=0, keepdims=True)
                    out = old_out * rescale + nn(values[h, :, at_key], weights.astype(LOW))
                result.append((top, summed, out))
            return tuple(result)

        status = one_key(j, None, True)
        status = lax.fori_loop(0, j, lambda i, now: one_key(i, now, False), status)
        for h in range(own):
            top, summed, out = status[h]
            done = out / summed
            flat_out[h * HEAD_DIM : (h + 1) * HEAD_DIM, at_query] = done
            total_out[h : h + 1, at_query] = top + jnp.log2(summed)
        return carry

    lax.fori_loop(0, rows // tile, one_query, 0)
    attended[...] = jnp.transpose(flat_out[...]).astype(LOW)
    for k in (3, 2, 1, 0):
        pair = jnp.concatenate(
            [
                attended[pl.ds(pl.multiple_of((t ^ m) * member_rows, 16), member_rows)]
                for m in (2 * k, 2 * k + 1)
            ],
            axis=0,
        )
        low_out[2 * k * member_rows : (2 * k + 2) * member_rows] = pair


def attend_team(place, first_low, triple_own, doc_column, doc_row, own):
    rows, model = first_low.shape
    width = own * HEAD_DIM
    tile = rows // 2
    return pl.pallas_call(
        lambda *refs: attend_kernel(own, tile, *refs),
        out_shape=(
            jax.ShapeDtypeStruct((rows, 3 * width), LOW),
            jax.ShapeDtypeStruct((width, rows), WIDE),
            jax.ShapeDtypeStruct((rows, width), LOW),
            jax.ShapeDtypeStruct((8, rows), WIDE),
        ),
        in_specs=[in_smem()] + [in_vmem()] * 4,
        out_specs=(in_vmem(),) * 4,
        scratch_shapes=[
            pltpu.VMEM((own, rows, HEAD_DIM), LOW),
            pltpu.VMEM((own, rows, HEAD_DIM), LOW),
            pltpu.VMEM((own, HEAD_DIM, rows), LOW),
            pltpu.VMEM((rows, width), LOW),
        ],
        compiler_params=params(),
        cost_estimate=estimate(20),
        name="attend",
    )(place, first_low, triple_own, doc_column, doc_row)


def attend_back_setup(own, projected_ref, flat_ref, back_ref, scratch):
    queries, keys, values, backs, keys_flat, backs_flat, deltas = scratch
    width = own * HEAD_DIM
    for h in range(own):
        lanes = slice(h * HEAD_DIM, (h + 1) * HEAD_DIM)
        key = projected_ref[:, width : 2 * width][:, lanes]
        back = back_ref[:, lanes]
        back_flat = jnp.transpose(back.astype(WIDE))
        queries[h] = projected_ref[:, :width][:, lanes]
        keys[h] = key
        values[h] = projected_ref[:, 2 * width :][:, lanes]
        backs[h] = back
        keys_flat[h] = jnp.transpose(key.astype(WIDE)).astype(LOW)
        backs_flat[h] = back_flat.astype(LOW)
        deltas[h : h + 1] = jnp.sum(back_flat * flat_ref[lanes], axis=0, keepdims=True)


def attend_back_tile(own, tile, i, total_ref, doc_column, doc_row, scratch, query_back):
    queries, keys, values, backs, keys_flat, backs_flat, deltas = scratch
    rows = queries.shape[1]
    scale = SCORE_SCALE * LOG2_E
    causal = lax.broadcasted_iota(jnp.int32, (tile, tile), 0) <= lax.broadcasted_iota(
        jnp.int32, (tile, tile), 1
    )
    at_key = slice(i * tile, (i + 1) * tile)
    status = [None] * own
    for j in range(i, rows // tile):
        at_query = slice(j * tile, (j + 1) * tile)
        allowed = doc_column[at_key, :1] == doc_row[:1, at_query]
        if i == j:
            allowed = allowed & causal
        for h in range(own):
            scores = nt(keys[h, at_key], queries[h, at_query]) * scale
            probs = jnp.where(allowed, jnp.exp2(scores - total_ref[h : h + 1, at_query]), 0.0)
            prob_back = nn(values[h, at_key], backs_flat[h, :, at_query])
            score_back = (probs * (prob_back - deltas[h : h + 1, at_query])).astype(LOW)
            value_part = nn(probs.astype(LOW), backs[h, at_query])
            key_part = nn(score_back, queries[h, at_query])
            query_part = nn(keys_flat[h, :, at_key], score_back)
            if i == 0:
                query_back[h, :, at_query] = query_part
            else:
                query_back[h, :, at_query] += query_part
            if status[h] is None:
                status[h] = (key_part, value_part)
            else:
                status[h] = (status[h][0] + key_part, status[h][1] + value_part)
    return jnp.concatenate(
        [status[h][0] * SCORE_SCALE for h in range(own)] + [status[h][1] for h in range(own)],
        axis=1,
    ).astype(LOW)


def attend_back_first_kernel(
    own,
    tile,
    place_ref,
    projected_ref,
    flat_ref,
    total_ref,
    doc_column,
    doc_row,
    back_ref,
    tile_out,
    query_back,
    *scratch,
):
    attend_back_setup(own, projected_ref, flat_ref, back_ref, scratch)
    for i in range(tile_out.shape[0] // tile):
        tile_out[i * tile : (i + 1) * tile] = attend_back_tile(
            own, tile, i, total_ref, doc_column, doc_row, scratch, query_back
        )


def attend_back_rest_kernel(
    own,
    tile,
    place_ref,
    projected_ref,
    flat_ref,
    total_ref,
    doc_column,
    doc_row,
    back_ref,
    tile_ref,
    earlier_ref,
    triple_ref,
    out_ref,
    *refs,
):
    outs, query_back, scratch = refs[:8], refs[8], refs[9:]
    t = place_ref[1]
    rows = projected_ref.shape[0]
    member_rows = rows // TEAM
    width = own * HEAD_DIM
    attend_back_setup(own, projected_ref, flat_ref, back_ref, scratch)
    query_back[...] = earlier_ref[...]
    done = tile_ref.shape[0]
    out_ref[:done, width:] = tile_ref[...]
    for i in range(done // tile, rows // tile):
        out_ref[i * tile : (i + 1) * tile, width:] = attend_back_tile(
            own, tile, i, total_ref, doc_column, doc_row, scratch, query_back
        )
    flat = jnp.concatenate([query_back[h] for h in range(own)], axis=0) * SCORE_SCALE
    out_ref[:, :width] = jnp.transpose(flat).astype(LOW)
    for k in (3, 2, 1, 0):
        pair = jnp.concatenate(
            [
                out_ref[pl.ds(pl.multiple_of((t ^ m) * member_rows, 16), member_rows)]
                for m in (2 * k, 2 * k + 1)
            ],
            axis=0,
        )
        product = nt(pair, triple_ref[...])
        put_terms(outs, 2 * k + 1, product[member_rows:])
        put_terms(outs, 2 * k, product[:member_rows])


def attend_back_scratch(own, rows):
    tall = pltpu.VMEM((own, rows, HEAD_DIM), LOW)
    long = pltpu.VMEM((own, HEAD_DIM, rows), LOW)
    return [tall, tall, tall, tall, long, long, pltpu.VMEM((8, rows), WIDE)]


def attend_back_first(place, projected, flat, totals, doc_column, doc_row, back, own):
    rows = projected.shape[0]
    tile = rows // 3
    return pl.pallas_call(
        lambda *refs: attend_back_first_kernel(own, tile, *refs),
        out_shape=(
            jax.ShapeDtypeStruct((2 * tile, 2 * own * HEAD_DIM), LOW),
            jax.ShapeDtypeStruct((own, HEAD_DIM, rows), WIDE),
        ),
        in_specs=[in_smem()] + [in_vmem()] * 6,
        out_specs=(in_vmem(),) * 2,
        scratch_shapes=attend_back_scratch(own, rows),
        compiler_params=params(),
        cost_estimate=estimate(12),
        name="attend_back_first",
    )(place, projected, flat, totals, doc_column, doc_row, back)


def attend_back_rest(
    place, projected, flat, totals, doc_column, doc_row, back, first_tile, query_back, triple_own, own
):
    rows = projected.shape[0]
    tile = rows // 3
    return pl.pallas_call(
        lambda *refs: attend_back_rest_kernel(own, tile, *refs),
        out_shape=(jax.ShapeDtypeStruct(projected.shape, LOW),)
        + term_shapes(rows // TEAM, triple_own.shape[0]),
        in_specs=[in_smem()] + [in_vmem()] * 9,
        out_specs=(in_vmem(),) * 9,
        scratch_shapes=[pltpu.VMEM((own, HEAD_DIM, rows), WIDE)] + attend_back_scratch(own, rows),
        compiler_params=params(),
        cost_estimate=estimate(18),
        name="attend_back_rest",
    )(
        place,
        projected,
        flat,
        totals,
        doc_column,
        doc_row,
        back,
        first_tile,
        query_back,
        triple_own,
    )


def mixing_send_kernel(place_ref, *refs):
    stack_ref, out_ref = refs
    out_ref[...] = jnp.zeros_like(out_ref)
    x = place_ref[1] // 4
    for source in range(PLANES):
        out_ref[2 * source + x] = stack_ref[source]


def mixing_send(place, stack):
    rows, width = stack.shape[1:]
    return pl.pallas_call(
        mixing_send_kernel,
        out_shape=jax.ShapeDtypeStruct((TEAM, rows, width), LOW),
        in_specs=[in_smem(), in_vmem()],
        out_specs=in_vmem(),
        compiler_params=params(),
        cost_estimate=estimate(2),
        name="mixing_send",
    )(place, stack)


def mixing_exchange(sent, core):
    rows, width = sent.shape[1:]
    return lax.dynamic_slice_in_dim(
        team_exchange(sent), core * PLANES, PLANES, 0
    ).reshape(PLANES * rows, width)


def mixing_return(sent, x):
    back = team_exchange(sent)
    return pick(back.reshape((PLANES, 2) + back.shape[1:]), x, 1)


def mix_back_kernel(place_ref, mixing_ref, attended_ref, *refs):
    pieces = refs[:PIECES]
    back_ref, mixing_out, mixed = refs[PIECES:]
    t = place_ref[1]
    member_rows = back_ref.shape[0] // TEAM
    for k in range(TEAM // 2):
        pair = jnp.concatenate([piece(pieces, 2 * k), piece(pieces, 2 * k + 1)], axis=0)
        mixed[2 * k * member_rows : (2 * k + 2) * member_rows] = pair
        back = nt(pair, mixing_ref[...]).astype(LOW)
        for m in (2 * k, 2 * k + 1):
            at = pl.ds(pl.multiple_of((t ^ m) * member_rows, 16), member_rows)
            back_ref[at] = back[(m - 2 * k) * member_rows : (m - 2 * k + 1) * member_rows]
    gradient = tn(attended_ref[...], mixed[...]).astype(LOW)
    mixing_out[...] = jnp.zeros_like(mixing_out)
    rows = gradient.shape[0] // PLANES
    for k in range(PLANES):
        mixing_out[t % 2 * PLANES + k] = gradient[k * rows : (k + 1) * rows]


def mix_back(place, mixing_own, attended, pieces):
    rows, width = attended.shape
    model = mixing_own.shape[1]
    return pl.pallas_call(
        mix_back_kernel,
        out_shape=(
            jax.ShapeDtypeStruct((rows, width), LOW),
            jax.ShapeDtypeStruct((TEAM, width // PLANES, model), LOW),
        ),
        in_specs=[in_smem()] + [in_vmem()] * (2 + PIECES),
        out_specs=(in_vmem(),) * 2,
        scratch_shapes=[pltpu.VMEM((rows, model), LOW)],
        compiler_params=params(),
        cost_estimate=estimate(5),
        name="mix_back",
    )(place, mixing_own, attended, *pieces)


def columns_kernel_of(piece_width, in_ref, out_ref, square_ref):
    total = jnp.zeros((1, 1), WIDE)
    for group in range(in_ref.shape[2] // piece_width):
        for pair in range(TEAM // 2):
            lanes = slice(group * piece_width, (group + 1) * piece_width)
            value = jnp.concatenate(
                [in_ref[2 * pair][:, lanes].astype(WIDE), in_ref[2 * pair + 1][:, lanes].astype(WIDE)],
                axis=1,
            )
            first = (group * TEAM + 2 * pair) * piece_width
            out_ref[:, first : first + 2 * piece_width] = value
            total = total + jnp.sum(value * value, axis=(0, 1), keepdims=True)
    square_ref[...] = jnp.broadcast_to(total, square_ref.shape)


def to_columns(value, piece_width):
    members, rows, width = value.shape
    out, square = pl.pallas_call(
        lambda *refs: columns_kernel_of(piece_width, *refs),
        out_shape=(
            jax.ShapeDtypeStruct((rows, members * width), WIDE),
            jax.ShapeDtypeStruct((8, 128), WIDE),
        ),
        in_specs=[in_vmem()],
        out_specs=(in_vmem(),) * 2,
        compiler_params=params(),
        cost_estimate=estimate(2),
        name="to_columns",
    )(value)
    return out, square[0, 0]


def adam_kernel(rates, factor_ref, *refs):
    number = len(rates)
    factor = factor_ref[0]
    for index in range(number):
        gradient, master, first, second = (refs[k * number + index][...] for k in range(4))
        weight, moment, square = adam_update(
            master, first, second, gradient, factor, rates[index], DECAY_RATE
        )
        refs[4 * number + 3 * index][...] = weight
        refs[4 * number + 3 * index + 1][...] = moment
        refs[4 * number + 3 * index + 2][...] = square


def adam_all(factor, gradients, masters, firsts, seconds, rates):
    steps = 6

    def block(array):
        rows, columns = array.shape
        return pl.BlockSpec((rows, columns // steps), lambda step: (0, step))

    blocks = [block(master) for master in masters]
    return pl.pallas_call(
        lambda *refs: adam_kernel(rates, *refs),
        grid=(steps,),
        out_shape=[
            jax.ShapeDtypeStruct(master.shape, WIDE) for master in masters for _ in range(3)
        ],
        in_specs=[in_smem()] + blocks * 4,
        out_specs=[one for one in blocks for _ in range(3)],
        compiler_params=params(),
        cost_estimate=estimate(10),
        name="adam_all",
    )(factor, *gradients, *masters, *firsts, *seconds)


def per_member(
    byte_rows,
    starts,
    doc_ids,
    out_cotangent,
    widen_master,
    widen_first,
    widen_second,
    triple_master,
    triple_first,
    triple_second,
    mixing_master,
    mixing_first,
    mixing_second,
    expand_master,
    expand_first,
    expand_second,
    shrink_master,
    shrink_first,
    shrink_second,
    narrow_master,
    narrow_first,
    narrow_second,
    gains_master,
    gains_first,
    gains_second,
):
    plane = lax.axis_index("z")
    x, y, core = lax.axis_index("x"), lax.axis_index("y"), lax.axis_index("c")
    t = 4 * x + 2 * y + core
    place = jnp.stack([plane, t]).astype(jnp.int32)
    byte_block, cotangent_rows = byte_rows[0], out_cotangent[0]
    bytes_dev, byte_width = byte_block.shape
    model = triple_master.shape[1] // 3
    hidden = expand_master.shape[1]
    shard = triple_master.shape[0]
    widen_shard = widen_master.shape[0]
    member_rows = 3 * bytes_dev // 16
    capacity = member_rows + member_rows // 2
    total = TEAM * member_rows
    own = HEADS // TEAM
    own_width = model // TEAM
    own_hidden = hidden // TEAM
    piece_hidden = own_hidden // PLANES

    widen_low = widen_master.astype(LOW)
    gains_low = gains_master.astype(LOW)
    gain_rows = jnp.pad(gains_low, ((0, 32 - widen_shard - 2), (0, byte_width - shard)))
    small = jnp.concatenate(
        [
            widen_low[:, :byte_width],
            gain_rows,
            widen_low[:, byte_width:],
            jnp.zeros((32 - widen_shard, byte_width), LOW),
            narrow_master.astype(LOW),
        ],
        axis=0,
    )
    small = plane_gather_small(small)
    row_buffer, chosen = pack(
        after(starts, small[1]), doc_ids, byte_block, cotangent_rows, capacity
    )
    packed = row_buffer
    row_buffer = to_plane(row_buffer)
    small, small_marks = team_gather(jnp.concatenate(small, axis=0))
    widen_full, gains_full, narrow_full = widen_whole(place, small, widen_shard, model)
    triple_own = triple_master.astype(LOW).reshape(shard, 3, TEAM, own_width)
    triple_own = jnp.transpose(triple_own, (2, 0, 1, 3)).reshape(TEAM, shard, 3 * own_width)
    triple_own = team_exchange(triple_own)
    mixing_rows = shard * model // (3 * own_width)
    triple_sent = jnp.concatenate(
        [
            after(triple_own, row_buffer, small[2], small[4]).reshape(TEAM * shard, 3 * own_width),
            mixing_master.astype(LOW).reshape(mixing_rows, 3 * own_width),
        ],
        axis=0,
    )
    gathered = lax.all_gather(triple_sent, "z", axis=0)
    triple_own = gathered[:, : TEAM * shard].reshape(model, 3 * own_width)
    mixing_stack = gathered[:, TEAM * shard :].reshape(PLANES, shard, model)
    expand_own = after(expand_master, triple_sent).astype(LOW)
    expand_own = expand_own.reshape(shard, PLANES, TEAM, piece_hidden)
    expand_own = jnp.transpose(expand_own, (2, 0, 1, 3)).reshape(TEAM, shard, own_hidden)
    expand_own = team_exchange(expand_own).reshape(TEAM * shard, own_hidden)
    shrink_low = shrink_master.astype(LOW)
    fed = lax.all_gather(
        jnp.concatenate(
            [expand_own, shrink_low[:, :own_hidden], shrink_low[:, own_hidden:]], axis=0
        ),
        "z",
        axis=0,
    )
    expand_own = fed[:, : TEAM * shard].reshape(model, own_hidden)
    shrink_own = jnp.concatenate(
        [
            fed[:, TEAM * shard : TEAM * shard + piece_hidden],
            fed[:, TEAM * shard + piece_hidden :],
        ],
        axis=2,
    ).reshape(own_hidden, model)
    entering, enter_marks = team_gather(after(row_buffer, *small_marks))
    first_low, widened, patch_rows, doc_column, doc_row, spans = enter(
        place,
        gains_full,
        widen_full,
        entering,
        capacity,
        member_rows,
    )
    mixing_sent = mixing_send(place, mixing_stack)
    mixing_own = mixing_exchange(mixing_sent, core)

    projected, flat, attended_low, totals = attend_team(
        after(place, mixing_sent), first_low, triple_own, doc_column, doc_row, own
    )
    terms, marks = team_scatter(*forward_terms(attended_low, mixing_own))
    shrink_back, upper_back, narrow_back = cotangent(
        after(place, *marks), spans, narrow_full, entering, capacity, member_rows
    )
    resid_one, second_own = add_and_norm(after(widened, shrink_back), gains_full, terms)

    second_pieces, _ = team_gather(second_own)
    second_low, active_low, expand_back, *terms = feed(
        expand_own, shrink_own, shrink_back, second_pieces
    )
    terms, marks = team_scatter(*terms)
    shrink_grad = tn(after(active_low, *marks), shrink_back).astype(LOW)
    shrink_sum = lax.psum_scatter(shrink_grad, "z", scatter_dimension=0, tiled=True)
    lower_back, mixed_own, second_gain = second_norm_back(
        after(resid_one, shrink_grad), gains_full, upper_back, terms
    )
    exit_out = []

    def leave_forward(own):
        exit_out.extend(exit_block(after(resid_one, own), narrow_full, terms))
        return exit_out[:1]

    mixed, mixed_marks = team_gather(mixed_own, None, leave_forward)
    resid_low, narrow_low = exit_out
    resid_low = team_exchange(resid_low).reshape(total, own_width)
    expand_grad = tn(after(second_low, *mixed_marks), expand_back).astype(LOW)
    expand_sum = lax.psum_scatter(expand_grad, "z", scatter_dimension=0, tiled=True)

    attend_back, mixing_grad = mix_back(
        after(place, expand_grad), mixing_own, attended_low, mixed
    )
    narrow_grad = tn(resid_low, after(narrow_back, attend_back)).astype(LOW)
    attention = (projected, flat, totals, doc_column, doc_row, attend_back)
    first_tile, query_back = attend_back_first(
        after(place, shrink_sum, narrow_grad), *attention, own
    )
    mixing_stack = mixing_return(mixing_grad, x)
    both = plane_scatter_small(
        jnp.concatenate(
            [mixing_stack, after(narrow_grad, first_tile).reshape(PLANES, shard, byte_width)],
            axis=2,
        )
    )
    mixing_sum, narrow_sum = both[:, :model], both[:, model:]
    triple_back, *terms = attend_back_rest(
        after(place, mixing_stack), *attention, first_tile, query_back, triple_own, own
    )
    first_terms, marks = team_scatter(*terms)
    triple_grad = tn(after(first_low, expand_sum, *marks), triple_back).astype(LOW)
    triple_sum = lax.psum_scatter(triple_grad, "z", scatter_dimension=0, tiled=True)
    expand_sum = team_exchange(expand_sum.reshape(TEAM, shard, own_hidden))

    back_rows, *terms = first_norm_back(
        after(place, triple_grad, mixing_sum, expand_sum),
        widened,
        gains_full,
        lower_back,
        patch_rows,
        widen_full,
        second_gain,
        narrow_low,
        first_terms,
    )
    terms, marks = team_scatter(*terms)
    widen_ready = sum(term.astype(WIDE) for term in terms)
    gains_ready = widen_ready[PLANES * widen_shard :][:8]
    widen_sum = plane_scatter_small(
        jnp.concatenate(
            [
                widen_ready[: PLANES * widen_shard].reshape(PLANES, widen_shard, model),
                jnp.broadcast_to(gains_ready, (PLANES, 8, model)),
            ],
            axis=1,
        )
    )
    gains_sum = lax.dynamic_slice(
        widen_sum[widen_shard : widen_shard + 2], (0, (plane * TEAM + t) * shard), (2, shard)
    )
    widen_sum = widen_sum[:widen_shard]
    back_rows, _ = team_gather(after(back_rows, terms[2]), None, lambda own: (widen_sum,))
    back_buffer = from_plane(leave(place, spans, back_rows, capacity))
    new_block, grad_block = unpack(chosen, byte_block, cotangent_rows, back_buffer)

    triple_sum = team_exchange(triple_sum.reshape(TEAM, shard, 3 * own_width))
    triple_sum, triple_square = to_columns(triple_sum, own_width)
    expand_sum, expand_square = to_columns(expand_sum, piece_hidden)
    shrink_sum = shrink_sum.astype(WIDE)

    reduced = (widen_sum, triple_sum, mixing_sum, expand_sum, shrink_sum, narrow_sum, gains_sum)
    squares = triple_square + expand_square
    for gradient in (widen_sum, mixing_sum, shrink_sum, narrow_sum, gains_sum):
        squares = squares + jnp.sum(gradient * gradient)
    squares = jnp.full((8, 128), squares, WIDE)
    for bit in (CORE_BIT, Y_BIT, X_BIT, TEAM, 2 * TEAM):
        squares = squares + flip(squares, bit)
    grad_norm = jnp.sqrt(squares[0, 0])
    factor = CLIP_NORM / jnp.maximum(grad_norm, CLIP_NORM)
    rates = (
        2.0 * D_BYTE ** (-0.5),
        2.0 * D ** (-0.5),
        0.4,
        2.0 * D ** (-0.5),
        2.0 * FF ** (-0.5),
        2.0 * D ** (-0.5),
    )
    updated = adam_all(
        factor.reshape(1),
        reduced[:6],
        (widen_master, triple_master, mixing_master, expand_master, shrink_master, narrow_master),
        (widen_first, triple_first, mixing_first, expand_first, shrink_first, narrow_first),
        (widen_second, triple_second, mixing_second, expand_second, shrink_second, narrow_second),
        rates,
    )
    gains = adam_update(gains_master, gains_first, gains_second, gains_sum, factor, 0.6, 0.0)
    return (new_block[None], grad_block[None], grad_norm, *updated, *gains)


def plane_solution(mesh):
    fine = Mesh(mesh.devices.reshape(PLANES, 2, 2, 2), AXES)
    byte_spec = P(("y", "c"), ("z", "x"))
    rows_spec = P(AXES, None)
    gains_spec = P(None, AXES)
    return jax.shard_map(
        per_member,
        mesh=fine,
        in_specs=(byte_spec,) * 4 + (rows_spec,) * 18 + (gains_spec,) * 3,
        out_specs=(byte_spec,) * 2 + (P(),) + (rows_spec,) * 18 + (gains_spec,) * 3,
        check_vma=False,
    )


def solution(mesh):
    if plane_fits(mesh):
        return plane_solution(mesh)
    placed = (
        P("dp", "seq", None),
        P("dp", "seq"),
        P("dp", "seq"),
        P("dp", "seq", None),
        P(("seq", "dp"), None),
        P(("seq", "dp"), None),
        P(("seq", "dp"), None),
        P(("seq", "dp"), None),
        P(("seq", "dp"), None),
        P(("seq", "dp"), None),
        P(("seq", "dp"), None),
        P(("seq", "dp"), None),
        P(("seq", "dp"), None),
        P(("seq", "dp"), None),
        P(("seq", "dp"), None),
        P(("seq", "dp"), None),
        P(("seq", "dp"), None),
        P(("seq", "dp"), None),
        P(("seq", "dp"), None),
        P(("seq", "dp"), None),
        P(("seq", "dp"), None),
        P(("seq", "dp"), None),
        P(None, ("seq", "dp")),
        P(None, ("seq", "dp")),
        P(None, ("seq", "dp")),
    )
    return jax.shard_map(
        per_device,
        mesh=mesh,
        in_specs=placed,
        out_specs=(
            P("dp", "seq", None),
            P("dp", "seq", None),
            P(),
            P(("seq", "dp"), None),
            P(("seq", "dp"), None),
            P(("seq", "dp"), None),
            P(("seq", "dp"), None),
            P(("seq", "dp"), None),
            P(("seq", "dp"), None),
            P(("seq", "dp"), None),
            P(("seq", "dp"), None),
            P(("seq", "dp"), None),
            P(("seq", "dp"), None),
            P(("seq", "dp"), None),
            P(("seq", "dp"), None),
            P(("seq", "dp"), None),
            P(("seq", "dp"), None),
            P(("seq", "dp"), None),
            P(("seq", "dp"), None),
            P(("seq", "dp"), None),
            P(("seq", "dp"), None),
            P(None, ("seq", "dp")),
            P(None, ("seq", "dp")),
            P(None, ("seq", "dp")),
        ),
        check_vma=False,
    )
```

```python
import jax
import jax.numpy as jnp
from jax import lax
from jax.experimental import pallas as pl
from jax.experimental.pallas import tpu as pltpu
from jax.sharding import Mesh, PartitionSpec as P

D_BYTE = 768
D = 1536
HEADS = 24
HEAD_DIM = 64
FF = 6144
STEP = 10


NORM_EPS = 1e-05
SCORE_SCALE = 0.125
MASK_FILL = -1e30
BETA_ONE = 0.9
BETA_TWO = 0.95
ADAM_EPS = 1e-08
DECAY_RATE = 0.1
CLIP_NORM = 1.0


def prefix(part, axis, combine, identity):
    place = lax.axis_index(axis)
    gathered = lax.all_gather(part, axis)
    state = jnp.zeros_like(part) + jnp.asarray(identity, part.dtype)

    def one(hop, state):
        return combine(state, lax.dynamic_index_in_dim(gathered, hop, 0, False))

    return lax.fori_loop(0, place, one, state)


def normalize(values, gain):
    inverse = lax.rsqrt(jnp.mean(values * values, axis=-1, keepdims=True) + NORM_EPS)
    return values * inverse * gain


def add_counts(earlier, later):
    return earlier + later


def block_rows(amount):
    for option in (1024, 768, 512, 384, 256):
        if amount >= option and amount % option == 0:
            return option
    return amount


def spread_positions(first_row, amount, patch_dev, devices):
    whole_rows = first_row + jnp.arange(amount, dtype=jnp.int32)
    return whole_rows % patch_dev * devices + whole_rows // patch_dev


def make_attend(queries, patch_docs, patch_pos, patch_dev, devices):

    def attend(running, shards, offset):
        piece_keys, piece_values, piece_docs = shards
        amount = piece_keys.shape[0]
        span_rows = block_rows(amount)
        number = amount // span_rows
        key_blocks = piece_keys.reshape(number, span_rows, HEADS, HEAD_DIM)
        value_blocks = piece_values.reshape(number, span_rows, HEADS, HEAD_DIM)
        doc_blocks = piece_docs.reshape(number, span_rows)
        firsts = span_rows * jnp.arange(number, dtype=jnp.int32)

        def advance(status, section):
            block_keys, block_values, block_docs, block_first = section
            running_top, running_sum, running_out = status
            scores = (
                jnp.einsum("phd,khd->hpk", queries, block_keys, preferred_element_type=jnp.float32)
                * SCORE_SCALE
            )
            key_pos = spread_positions(block_first, span_rows, patch_dev, devices)
            allowed = (patch_docs[:, None] == block_docs[None, :]) & (
                key_pos[None, :] <= patch_pos[:, None]
            )
            masked = jnp.where(allowed[None], scores, MASK_FILL)
            new_top = jnp.maximum(running_top, jnp.max(masked, axis=-1))
            weights = jnp.where(allowed[None], jnp.exp(masked - new_top[..., None]), 0.0)
            rescale = jnp.exp(running_top - new_top)
            running_sum = running_sum * rescale + jnp.sum(weights, axis=-1)
            running_out = running_out * rescale[..., None] + jnp.einsum(
                "hpk,khd->hpd",
                weights.astype(jnp.bfloat16),
                block_values,
                preferred_element_type=jnp.float32,
            )
            return ((new_top, running_sum, running_out), None)

        running, _ = lax.scan(advance, running, (key_blocks, value_blocks, doc_blocks, firsts))
        return running

    return attend


def outer_sum(left, right):
    return jnp.einsum("pi,pj->ij", left, right, preferred_element_type=jnp.float32)


def back_product(grads, weight):
    return jnp.einsum("pj,ij->pi", grads, weight, preferred_element_type=jnp.float32)


def adam_update(master, first_old, second_old, gradient, clip_factor, learn_rate, weight_decay):
    clipped = gradient * clip_factor
    moment = BETA_ONE * first_old + (1.0 - BETA_ONE) * clipped
    square = BETA_TWO * second_old + (1.0 - BETA_TWO) * clipped * clipped
    corrected = (
        moment / (1.0 - BETA_ONE**STEP) / (jnp.sqrt(square / (1.0 - BETA_TWO**STEP)) + ADAM_EPS)
    )
    weight = master - learn_rate * (corrected + weight_decay * master)
    return (weight, moment, square)


def per_device(
    byte_rows,
    starts,
    doc_ids,
    out_cotangent,
    widen_master,
    widen_first,
    widen_second,
    triple_master,
    triple_first,
    triple_second,
    mixing_master,
    mixing_first,
    mixing_second,
    expand_master,
    expand_first,
    expand_second,
    shrink_master,
    shrink_first,
    shrink_second,
    narrow_master,
    narrow_first,
    narrow_second,
    gains_master,
    gains_first,
    gains_second,
):
    widen_full, triple_full, mixing_full, expand_full, shrink_full, narrow_full, gains_full = (
        lax.all_gather(widen_master.astype(jnp.bfloat16), ("seq", "dp"), axis=0, tiled=True),
        lax.all_gather(triple_master.astype(jnp.bfloat16), ("seq", "dp"), axis=0, tiled=True),
        lax.all_gather(mixing_master.astype(jnp.bfloat16), ("seq", "dp"), axis=0, tiled=True),
        lax.all_gather(expand_master.astype(jnp.bfloat16), ("seq", "dp"), axis=0, tiled=True),
        lax.all_gather(shrink_master.astype(jnp.bfloat16), ("seq", "dp"), axis=0, tiled=True),
        lax.all_gather(narrow_master.astype(jnp.bfloat16), ("seq", "dp"), axis=0, tiled=True),
        lax.all_gather(gains_master.astype(jnp.bfloat16), ("seq", "dp"), axis=1, tiled=True),
    )
    gain_one = gains_full[0].astype(jnp.float32)
    gain_two = gains_full[1].astype(jnp.float32)
    devices = lax.axis_size("seq")
    seq_place = lax.axis_index("seq")
    byte_block = byte_rows[0]
    start_flags = starts[0]
    doc_local = doc_ids[0]
    cotangent_rows = out_cotangent[0]
    byte_width = byte_block.shape[1]
    patch_dev = 3 * byte_block.shape[0] // 16
    capacity = patch_dev + patch_dev // 2
    slot_count = (capacity + devices - 2) // devices + 1
    buffer_rows = devices * slot_count
    amount = jnp.sum(start_flags)
    offset = prefix(amount, "seq", add_counts, jnp.int32(0))
    ranking = jnp.cumsum(start_flags) - start_flags
    patch_index = offset + ranking
    owners = patch_index % devices
    local_row = patch_index // devices
    slot_index = local_row - offset // devices
    target_slot = jnp.where(start_flags == 1, owners * slot_count + slot_index, buffer_rows)
    send_rows = (
        jnp.zeros((buffer_rows, byte_width), jnp.bfloat16)
        .at[target_slot]
        .set(byte_block, mode="drop")
    )
    send_meta = (
        jnp.full((buffer_rows, 2), patch_dev, jnp.int32)
        .at[target_slot]
        .set(jnp.stack([local_row, doc_local], axis=-1), mode="drop")
    )
    send_grad = (
        jnp.zeros((buffer_rows, byte_width), jnp.bfloat16)
        .at[target_slot]
        .set(cotangent_rows, mode="drop")
    )
    arrived_rows, arrived_meta = (
        lax.all_to_all(send_rows, "seq", split_axis=0, concat_axis=0, tiled=True),
        lax.all_to_all(send_meta, "seq", split_axis=0, concat_axis=0, tiled=True),
    )
    target = arrived_meta[:, 0]
    valid_slot = target < patch_dev
    patch_rows = (
        jnp.zeros((patch_dev, byte_width), jnp.bfloat16).at[target].set(arrived_rows, mode="drop")
    )
    patch_docs = jnp.zeros((patch_dev,), jnp.int32).at[target].set(arrived_meta[:, 1], mode="drop")
    patch_pos = seq_place + devices * jnp.arange(patch_dev, dtype=jnp.int32)
    widened = jnp.dot(patch_rows, widen_full, preferred_element_type=jnp.float32)
    model_width = widened.shape[1]
    first_low = normalize(widened, gain_one).astype(jnp.bfloat16)
    projected = jnp.dot(first_low, triple_full, preferred_element_type=jnp.float32).astype(
        jnp.bfloat16
    )
    queries = projected[:, :model_width].reshape(patch_dev, HEADS, HEAD_DIM)
    key_rows = projected[:, model_width : 2 * model_width]
    value_rows = projected[:, 2 * model_width :]
    initial = (
        jnp.full((HEADS, patch_dev), MASK_FILL, jnp.float32),
        jnp.zeros((HEADS, patch_dev), jnp.float32),
        jnp.zeros((HEADS, patch_dev, HEAD_DIM), jnp.float32),
    )
    attend = make_attend(queries, patch_docs, patch_pos, patch_dev, devices)
    running = attend(
        initial,
        (
            lax.all_gather(key_rows, "seq", axis=0, tiled=True),
            lax.all_gather(value_rows, "seq", axis=0, tiled=True),
            lax.all_gather(patch_docs, "seq", axis=0, tiled=True),
        ),
        jnp.int32(0),
    )
    running_top, running_sum, running_out = running
    attended = running_out / running_sum[..., None]
    log_total = running_top + jnp.log(running_sum)
    attended_low = (
        jnp.transpose(attended, (1, 0, 2)).reshape(patch_dev, model_width).astype(jnp.bfloat16)
    )
    resid_one = widened + jnp.dot(attended_low, mixing_full, preferred_element_type=jnp.float32)
    second_low = normalize(resid_one, gain_two).astype(jnp.bfloat16)
    expanded = jnp.dot(second_low, expand_full, preferred_element_type=jnp.float32)
    active_low = jax.nn.gelu(expanded).astype(jnp.bfloat16)
    resid_two = resid_one + jnp.dot(active_low, shrink_full, preferred_element_type=jnp.float32)
    resid_low = resid_two.astype(jnp.bfloat16)
    narrow_low = jnp.dot(resid_low, narrow_full, preferred_element_type=jnp.float32).astype(
        jnp.bfloat16
    )
    returned = jnp.where(valid_slot[:, None], jnp.take(narrow_low, target, axis=0, mode="clip"), 0)
    back_rows = lax.all_to_all(returned, "seq", split_axis=0, concat_axis=0, tiled=True)
    added = jnp.take(back_rows, target_slot, axis=0, mode="clip").astype(jnp.float32)
    new_block = byte_block.astype(jnp.float32) + jnp.where(start_flags[:, None] == 1, added, 0.0)
    arrived_grad = lax.all_to_all(send_grad, "seq", split_axis=0, concat_axis=0, tiled=True)
    narrow_back = (
        jnp.zeros((patch_dev, byte_width), jnp.bfloat16).at[target].set(arrived_grad, mode="drop")
    )
    narrow_grad = outer_sum(resid_low, narrow_back)
    upper_back = back_product(narrow_back, narrow_full)
    shrink_back = upper_back.astype(jnp.bfloat16)
    shrink_grad = outer_sum(active_low, shrink_back)
    active_back = back_product(shrink_back, shrink_full)
    _, gelu_pull = jax.vjp(jax.nn.gelu, expanded)
    expand_back = gelu_pull(active_back)[0].astype(jnp.bfloat16)
    expand_grad = outer_sum(second_low, expand_back)
    second_back = back_product(expand_back, expand_full)
    _, second_pull = jax.vjp(normalize, resid_one, gain_two)
    second_part, second_gain = second_pull(second_back)
    lower_back = upper_back + second_part
    mixed_back = lower_back.astype(jnp.bfloat16)
    mixing_grad = outer_sum(attended_low, mixed_back)
    attend_back = (
        back_product(mixed_back, mixing_full)
        .astype(jnp.bfloat16)
        .reshape(patch_dev, HEADS, HEAD_DIM)
    )
    delta_rows = jnp.einsum("phd,hpd->hp", attend_back.astype(jnp.float32), attended)
    all_keys, all_values, all_docs = (
        lax.all_gather(key_rows, "seq", axis=0, tiled=True),
        lax.all_gather(value_rows, "seq", axis=0, tiled=True),
        lax.all_gather(patch_docs, "seq", axis=0, tiled=True),
    )
    total_keys = all_keys.shape[0]
    span_rows = block_rows(total_keys)
    number = total_keys // span_rows
    key_blocks = all_keys.reshape(number, span_rows, HEADS, HEAD_DIM)
    value_blocks = all_values.reshape(number, span_rows, HEADS, HEAD_DIM)
    doc_blocks = all_docs.reshape(number, span_rows)
    firsts = span_rows * jnp.arange(number, dtype=jnp.int32)
    query_start = jnp.zeros((patch_dev, HEADS, HEAD_DIM), jnp.float32)

    def backstep(query_back, section):
        block_keys, block_values, block_docs, block_first = section
        scores = (
            jnp.einsum("phd,khd->hpk", queries, block_keys, preferred_element_type=jnp.float32)
            * SCORE_SCALE
        )
        key_pos = spread_positions(block_first, span_rows, patch_dev, devices)
        allowed = (patch_docs[:, None] == block_docs[None, :]) & (
            key_pos[None, :] <= patch_pos[:, None]
        )
        probs = jnp.where(allowed[None], jnp.exp(scores - log_total[..., None]), 0.0)
        prob_back = jnp.einsum(
            "phd,khd->hpk", attend_back, block_values, preferred_element_type=jnp.float32
        )
        score_back = (probs * (prob_back - delta_rows[..., None])).astype(jnp.bfloat16)
        query_back = (
            query_back
            + jnp.einsum("hpk,khd->phd", score_back, block_keys, preferred_element_type=jnp.float32)
            * SCORE_SCALE
        )
        keys_part = (
            jnp.einsum("hpk,phd->khd", score_back, queries, preferred_element_type=jnp.float32)
            * SCORE_SCALE
        )
        values_part = jnp.einsum(
            "hpk,phd->khd",
            probs.astype(jnp.bfloat16),
            attend_back,
            preferred_element_type=jnp.float32,
        )
        return (
            query_back,
            (
                keys_part.reshape(span_rows, model_width),
                values_part.reshape(span_rows, model_width),
            ),
        )

    query_back, (keys_back, values_back) = lax.scan(
        backstep, query_start, (key_blocks, value_blocks, doc_blocks, firsts)
    )
    keys_own, values_own = (
        lax.psum_scatter(
            keys_back.reshape(total_keys, model_width).astype(jnp.bfloat16),
            "seq",
            scatter_dimension=0,
            tiled=True,
        ).astype(jnp.float32),
        lax.psum_scatter(
            values_back.reshape(total_keys, model_width).astype(jnp.bfloat16),
            "seq",
            scatter_dimension=0,
            tiled=True,
        ).astype(jnp.float32),
    )
    triple_back = jnp.concatenate(
        [query_back.reshape(patch_dev, model_width), keys_own, values_own], axis=1
    ).astype(jnp.bfloat16)
    triple_grad = outer_sum(first_low, triple_back)
    first_back = back_product(triple_back, triple_full)
    _, first_pull = jax.vjp(normalize, widened, gain_one)
    first_part, first_gain = first_pull(first_back)
    base_low = (lower_back + first_part).astype(jnp.bfloat16)
    widen_grad = outer_sum(patch_rows, base_low)
    patch_back = back_product(base_low, widen_full).astype(jnp.bfloat16)
    grad_slots = jnp.where(
        valid_slot[:, None], jnp.take(patch_back, target, axis=0, mode="clip"), 0
    )
    grad_rows = lax.all_to_all(grad_slots, "seq", split_axis=0, concat_axis=0, tiled=True)
    coming = jnp.take(grad_rows, target_slot, axis=0, mode="clip").astype(jnp.float32)
    grad_block = cotangent_rows.astype(jnp.float32) + jnp.where(
        start_flags[:, None] == 1, coming, 0.0
    )
    gains_grad = jnp.stack([first_gain, second_gain], axis=0)
    reduced = (
        lax.psum_scatter(widen_grad, ("seq", "dp"), scatter_dimension=0, tiled=True),
        lax.psum_scatter(triple_grad, ("seq", "dp"), scatter_dimension=0, tiled=True),
        lax.psum_scatter(mixing_grad, ("seq", "dp"), scatter_dimension=0, tiled=True),
        lax.psum_scatter(expand_grad, ("seq", "dp"), scatter_dimension=0, tiled=True),
        lax.psum_scatter(shrink_grad, ("seq", "dp"), scatter_dimension=0, tiled=True),
        lax.psum_scatter(narrow_grad, ("seq", "dp"), scatter_dimension=0, tiled=True),
        lax.psum_scatter(gains_grad, ("seq", "dp"), scatter_dimension=1, tiled=True),
    )
    local_squares = jnp.float32(0.0)
    for member in reduced:
        local_squares = local_squares + jnp.sum(member * member)
    norm_squared = lax.psum(local_squares, ("seq", "dp"))
    grad_norm = jnp.sqrt(norm_squared)
    factor = CLIP_NORM / jnp.maximum(grad_norm, CLIP_NORM)
    masters = (
        widen_master,
        triple_master,
        mixing_master,
        expand_master,
        shrink_master,
        narrow_master,
        gains_master,
    )
    firsts_old = (
        widen_first,
        triple_first,
        mixing_first,
        expand_first,
        shrink_first,
        narrow_first,
        gains_first,
    )
    seconds_old = (
        widen_second,
        triple_second,
        mixing_second,
        expand_second,
        shrink_second,
        narrow_second,
        gains_second,
    )
    rates = (
        2.0 * D_BYTE ** (-0.5),
        2.0 * D ** (-0.5),
        0.4,
        2.0 * D ** (-0.5),
        2.0 * FF ** (-0.5),
        2.0 * D ** (-0.5),
        0.6,
    )
    decays = (DECAY_RATE, DECAY_RATE, DECAY_RATE, DECAY_RATE, DECAY_RATE, DECAY_RATE, 0.0)
    updates = [
        adam_update(
            masters[index],
            firsts_old[index],
            seconds_old[index],
            reduced[index],
            factor,
            rates[index],
            decays[index],
        )
        for index in range(7)
    ]
    return (
        new_block.astype(jnp.bfloat16)[None],
        grad_block.astype(jnp.bfloat16)[None],
        grad_norm,
        updates[0][0],
        updates[0][1],
        updates[0][2],
        updates[1][0],
        updates[1][1],
        updates[1][2],
        updates[2][0],
        updates[2][1],
        updates[2][2],
        updates[3][0],
        updates[3][1],
        updates[3][2],
        updates[4][0],
        updates[4][1],
        updates[4][2],
        updates[5][0],
        updates[5][1],
        updates[5][2],
        updates[6][0],
        updates[6][1],
        updates[6][2],
    )


PLANES = 4
TEAM = 8
CORE_BIT, Y_BIT, X_BIT = 1, 2, 4
AXES = ("z", "x", "y", "c")
TEAM_AXES = ("x", "y", "c")
LOW = jnp.bfloat16
WIDE = jnp.float32
VMEM_LIMIT = 56 * 1024 * 1024
LOG2_E = 1.4426950408889634
GELU_A = 0.7978845608028654
GELU_B = 0.044715


def plane_fits(mesh):
    return mesh.shape["seq"] == 2 * PLANES and mesh.shape["dp"] == PLANES


def flip(value, bit):
    pairs = [(place, place ^ bit) for place in range(PLANES * TEAM)]
    return lax.ppermute(value, AXES, pairs)


def shift_plane(value, hop):
    pairs = [
        (plane * TEAM + t, (plane + hop) % PLANES * TEAM + t)
        for plane in range(PLANES)
        for t in range(TEAM)
    ]
    return lax.ppermute(value, AXES, pairs)


SEQUENCE_OF_PLANE = (2, 0, 1, 3)


def source_of(plane, t):
    return (plane + t // 2 % 2 + 2 * (t % 2) + 2 * PLANES) % PLANES * 2 + t // 4


def byte_pairs():
    return [
        (source_of(plane, t) * PLANES + SEQUENCE_OF_PLANE[plane], plane * TEAM + t)
        for plane in range(PLANES)
        for t in range(TEAM)
    ]


def to_plane(value):
    return lax.ppermute(value, AXES, byte_pairs())


def from_plane(value):
    return lax.ppermute(value, AXES, [(there, here) for here, there in byte_pairs()])


def team_gather(block, cut=None, before_relay=lambda own: ()):
    cut = block.shape[0] // 2 if cut is None else cut
    from_x = flip(block, X_BIT)
    from_y = flip(block, Y_BIT)
    from_core = flip(block, CORE_BIT)
    from_x, from_y = after((from_x, from_y), *before_relay(from_core))
    to_x, to_y = from_y[:cut], from_x[cut:]
    upper = flip(to_x, X_BIT)
    lower = flip(to_y, Y_BIT)
    y_core = flip(from_y, CORE_BIT)
    x_core = flip(from_x, CORE_BIT)
    return [
        block,
        from_core,
        from_y,
        y_core,
        from_x,
        x_core,
        upper,
        lower,
        flip(upper, CORE_BIT),
        flip(lower, CORE_BIT),
    ], (to_x, to_y)


PIECES = 10


def piece(refs, m):
    if m < 6:
        return refs[m][...]
    return jnp.concatenate([refs[2 * m - 6][...], refs[2 * m - 5][...]], axis=0)


def team_scatter(far_send, far_keep, x_send, x_keep, y_send, y_keep, own_send, own_keep):
    def pair(send, keep):
        return keep.astype(WIDE) + flip(send, CORE_BIT).astype(WIDE)

    far = pair(far_send, far_keep).astype(LOW)
    cut = far.shape[0] // 2
    upper = flip(far[:cut], X_BIT).astype(WIDE)
    lower = flip(far[cut:], Y_BIT).astype(WIDE)
    to_x, to_y = pair(x_send, x_keep), pair(y_send, y_keep)
    to_x = jnp.concatenate([to_x[:cut], to_x[cut:] + lower], axis=0).astype(LOW)
    to_y = jnp.concatenate([to_y[:cut] + upper, to_y[cut:]], axis=0).astype(LOW)
    terms = (own_keep, flip(own_send, CORE_BIT), flip(to_x, X_BIT), flip(to_y, Y_BIT))
    return terms, (to_x, to_y)


def put_terms(outs, m, value):
    outs[7 - m][...] = value.astype(LOW)


def term_shapes(rows, width):
    return (jax.ShapeDtypeStruct((rows, width), LOW),) * TEAM


def add_terms(refs, lanes=slice(None)):
    total = refs[0][:, lanes].astype(WIDE)
    for ref in refs[1:]:
        total = total + ref[:, lanes].astype(WIDE)
    return total


def after(value, *earlier):
    return lax.optimization_barrier((value,) + earlier)[0]


def plane_gather_small(block):
    return [block] + [shift_plane(block, hop) for hop in (1, 2, 3)]


def plane_scatter_small(stack):
    back = lax.all_to_all(stack.astype(LOW), "z", split_axis=0, concat_axis=0, tiled=True)
    return jnp.sum(back.astype(WIDE), axis=0)


def team_exchange(value):
    return lax.all_to_all(value, TEAM_AXES, split_axis=0, concat_axis=0, tiled=True)


def pick(value, place, axis):
    return lax.dynamic_index_in_dim(value, place, axis, False)


def in_vmem():
    return pl.BlockSpec(memory_space=pltpu.VMEM)


def in_smem():
    return pl.BlockSpec(memory_space=pltpu.SMEM)


def params():
    return pltpu.CompilerParams(vmem_limit_bytes=VMEM_LIMIT)


def estimate(microseconds):
    return pl.CostEstimate(
        flops=int(microseconds * 8e8), bytes_accessed=int(microseconds * 2e6), transcendentals=0
    )


def nn(left, right):
    return lax.dot_general(left, right, (((1,), (0,)), ((), ())), preferred_element_type=WIDE)


def nt(left, right):
    return lax.dot_general(left, right, (((1,), (1,)), ((), ())), preferred_element_type=WIDE)


def tn(left, right):
    return lax.dot_general(left, right, (((0,), (0,)), ((), ())), preferred_element_type=WIDE)


def slot_matrix(flags, slots):
    amount = flags.shape[1]
    row = lax.broadcasted_iota(jnp.int32, (amount, amount), 0)
    column = lax.broadcasted_iota(jnp.int32, (amount, amount), 1)
    before = jnp.where(row < column, 1.0, 0.0).astype(LOW)
    rank = nn(jnp.broadcast_to(flags, (8, amount)).astype(LOW), before)[:1]
    rank = jnp.where(flags > 0.5, rank, -1.0)
    slot = lax.broadcasted_iota(jnp.int32, (slots, amount), 0).astype(WIDE)
    return jnp.where(slot == rank, 1.0, 0.0).astype(LOW)


def pack_kernel(starts_ref, docs_ref, rows_ref, cotangent_ref, rows_out, chosen_out):
    capacity = chosen_out.shape[0]
    width = rows_out.shape[1]
    flags = starts_ref[...].astype(WIDE)
    chosen = slot_matrix(flags, 384)
    amount = jnp.sum(flags)
    docs = nt(jnp.broadcast_to(docs_ref[...].astype(WIDE), (16, flags.shape[1])).astype(LOW), chosen)
    docs = jnp.concatenate([docs, jnp.zeros((16, width - 384), WIDE)], axis=1)
    row = lax.broadcasted_iota(jnp.int32, (16, width), 0)
    high = jnp.floor(amount * 0.5)
    meta = jnp.where(row == 0, docs, jnp.where(row == 1, high, amount - 2.0 * high))
    chosen = chosen[:capacity]
    chosen_out[...] = chosen
    rows_out[:16] = meta.astype(LOW)
    rows_out[16 : 16 + capacity] = nn(chosen, rows_ref[...]).astype(LOW)
    rows_out[16 + capacity :] = nn(chosen, cotangent_ref[...]).astype(LOW)


def pack(starts, docs, rows, cotangent_rows, capacity):
    amount, width = rows.shape
    return pl.pallas_call(
        pack_kernel,
        out_shape=(
            jax.ShapeDtypeStruct((2 * capacity + 16, width), LOW),
            jax.ShapeDtypeStruct((capacity, amount), LOW),
        ),
        in_specs=[in_vmem()] * 4,
        out_specs=(in_vmem(), in_vmem()),
        compiler_params=params(),
        cost_estimate=estimate(5),
        name="pack",
    )(starts, docs, rows, cotangent_rows)


def unpack_kernel(chosen_ref, rows_ref, cotangent_ref, back_ref, rows_out, cotangent_out):
    width = rows_ref.shape[1]
    added = tn(chosen_ref[...], back_ref[...])
    rows_out[...] = (rows_ref[...].astype(WIDE) + added[:, :width]).astype(LOW)
    cotangent_out[...] = (cotangent_ref[...].astype(WIDE) + added[:, width:]).astype(LOW)


def unpack(chosen, rows, cotangent_rows, back):
    return pl.pallas_call(
        unpack_kernel,
        out_shape=(jax.ShapeDtypeStruct(rows.shape, LOW),) * 2,
        in_specs=[in_vmem()] * 4,
        out_specs=(in_vmem(),) * 2,
        compiler_params=params(),
        cost_estimate=estimate(5),
        name="unpack",
    )(chosen, rows, cotangent_rows, back)


def window_matrix(first, amount, capacity):
    target = lax.broadcasted_iota(jnp.int32, (capacity + 16, capacity), 0)
    source = lax.broadcasted_iota(jnp.int32, (capacity + 16, capacity), 1)
    moved = (target == source + first % 16) & (source < amount)
    return jnp.where(moved, 1.0, 0.0).astype(LOW)


def widen_kernel(place_ref, *refs):
    pieces = refs[:PIECES]
    widen_out, gains_out, narrow_out = refs[PIECES : PIECES + 3]
    widen_wide, gains = refs[PIECES + 3 :]
    plane, t = place_ref[0], place_ref[1]
    shards = PLANES * TEAM
    shard = widen_out.shape[0] // shards
    model = widen_out.shape[1]
    width = model // 2
    gain_shard = model // shards
    for m in range(TEAM):
        low = piece(pieces, m)
        here = low.astype(WIDE)
        for hop in range(PLANES):
            place = (plane - hop + PLANES) % PLANES * TEAM + (t ^ m)
            at = pl.ds(pl.multiple_of(place * shard, 8), shard)
            base = hop * (64 + gain_shard)
            narrow_at = pl.ds(pl.multiple_of(place * gain_shard, 16), gain_shard)
            narrow_out[narrow_at] = low[base + 64 : base + 64 + gain_shard]
            widen_wide[at, :width] = here[base : base + shard]
            widen_wide[at, width:] = here[base + 32 : base + 32 + shard]
            gains[0, pl.ds(place, 1)] = here[base + shard : base + shard + 1, :128]
            gains[1, pl.ds(place, 1)] = here[base + shard + 1 : base + shard + 2, :128]
    widen_out[...] = widen_wide[...].astype(LOW)
    column = lax.broadcasted_iota(jnp.int32, (shards, model), 1)
    owner = lax.broadcasted_iota(jnp.int32, (shards, model), 0)
    owned = (column >= owner * gain_shard) & (column < (owner + 1) * gain_shard)
    inside = jnp.sum(jnp.where(owned, column - owner * gain_shard, 0).astype(WIDE), axis=0, keepdims=True)
    row = lax.broadcasted_iota(jnp.int32, (128, model), 0).astype(WIDE)
    owned = jnp.where(owned, 1.0, 0.0).astype(LOW)
    for k in range(2):
        spread = tn(gains[k].astype(LOW), owned)
        line = jnp.sum(jnp.where(row == inside, spread, 0.0), axis=0, keepdims=True)
        gains_out[k * 8 : k * 8 + 8] = jnp.broadcast_to(line, (8, model))


def widen_whole(place, pieces, shard, model):
    return pl.pallas_call(
        widen_kernel,
        out_shape=(
            jax.ShapeDtypeStruct((shard * PLANES * TEAM, model), LOW),
            jax.ShapeDtypeStruct((16, model), WIDE),
            jax.ShapeDtypeStruct((model, pieces[0].shape[1]), LOW),
        ),
        in_specs=[in_smem()] + [in_vmem()] * PIECES,
        out_specs=(in_vmem(),) * 3,
        scratch_shapes=[
            pltpu.VMEM((shard * PLANES * TEAM, model), WIDE),
            pltpu.VMEM((2, PLANES * TEAM, 128), WIDE),
        ],
        compiler_params=params(),
        cost_estimate=estimate(5),
        name="widen_whole",
    )(place, *pieces)


def enter_kernel(capacity, place_ref, gains_ref, widen_ref, *refs):
    pieces = refs[:PIECES]
    low_out, own_wide, own_rows, doc_column, doc_row, spans = refs[PIECES : PIECES + 6]
    rows, docs = refs[PIECES + 6 :]
    plane, t = place_ref[0], place_ref[1]
    member_rows = own_rows.shape[0]
    total = low_out.shape[0]

    metas = [pieces[m][:16] for m in range(6)] + [pieces[6][:16], pieces[8][:16]]
    blocks = [piece(pieces, m)[16 : 16 + capacity] for m in range(TEAM)]
    amounts, sources = [], []
    for m in range(TEAM):
        meta = metas[m].astype(WIDE)
        row = lax.broadcasted_iota(jnp.int32, meta.shape, 0)
        lane = lax.broadcasted_iota(jnp.int32, meta.shape, 1)
        picked = jnp.where(lane == 0, jnp.where(row == 1, 2.0 * meta, jnp.where(row == 2, meta, 0.0)), 0.0)
        amounts.append(jnp.sum(picked).astype(jnp.int32))
        sources.append(source_of(plane, t ^ m))
    firsts = []
    for m in range(TEAM):
        first = jnp.int32(0)
        for other in range(TEAM):
            if other != m:
                first = first + jnp.where(sources[other] < sources[m], amounts[other], 0)
        firsts.append(first)
        spans[m] = first
        spans[TEAM + m] = amounts[m]

    rows[...] = jnp.zeros_like(rows)
    docs[...] = jnp.zeros_like(docs)
    for m in range(TEAM):
        moving = window_matrix(firsts[m], amounts[m], capacity)
        at = pl.ds(pl.multiple_of(firsts[m] // 16 * 16, 16), capacity + 16)
        rows[at] = rows[at] + nn(moving, blocks[m]).astype(LOW)
        names = metas[m][:1, :384]
        names = jnp.broadcast_to(names, (128, 384))[:, :capacity]
        docs[at] = docs[at] + nt(moving, names)

    doc_column[...] = docs[:total]
    select = jnp.where(lax.broadcasted_iota(jnp.int32, (8, 128), 1) == 0, 1.0, 0.0).astype(LOW)
    doc_row[...] = nt(select, docs[:total].astype(LOW))
    own_rows[...] = rows[pl.ds(pl.multiple_of(t * member_rows, 16), member_rows)]

    def one(k, carry):
        at = pl.ds(pl.multiple_of(k * 2 * member_rows, 16), 2 * member_rows)
        wide = nn(rows[at], widen_ref[...])
        inverse = lax.rsqrt(jnp.mean(wide * wide, axis=-1, keepdims=True) + NORM_EPS)
        low_out[at] = (wide * inverse * gains_ref[:1]).astype(LOW)
        return carry

    lax.fori_loop(0, TEAM // 2, one, 0)
    own_wide[...] = nn(own_rows[...], widen_ref[...])


def enter(place, gains, widen_full, pieces, capacity, member_rows):
    width, model = widen_full.shape
    total = member_rows * TEAM
    padded = total + capacity + 16
    return pl.pallas_call(
        lambda *refs: enter_kernel(capacity, *refs),
        out_shape=(
            jax.ShapeDtypeStruct((total, model), LOW),
            jax.ShapeDtypeStruct((member_rows, model), WIDE),
            jax.ShapeDtypeStruct((member_rows, width), LOW),
            jax.ShapeDtypeStruct((total, 128), WIDE),
            jax.ShapeDtypeStruct((8, total), WIDE),
            jax.ShapeDtypeStruct((2 * TEAM,), jnp.int32),
        ),
        in_specs=[in_smem(), in_vmem(), in_vmem()] + [in_vmem()] * PIECES,
        out_specs=(in_vmem(),) * 5 + (in_smem(),),
        scratch_shapes=[
            pltpu.VMEM((padded, width), LOW),
            pltpu.VMEM((padded, 128), WIDE),
        ],
        compiler_params=params(),
        cost_estimate=estimate(14),
        name="enter",
    )(place, gains, widen_full, *pieces)


def cotangent_kernel(capacity, place_ref, spans_ref, narrow_ref, *refs):
    pieces = refs[:PIECES]
    low_out, own_wide, all_rows = refs[PIECES : PIECES + 3]
    (rows,) = refs[PIECES + 3 :]
    t = place_ref[1]
    member_rows = own_wide.shape[0]
    rows[...] = jnp.zeros_like(rows)
    for m in range(TEAM):
        first = spans_ref[m]
        moving = window_matrix(first, spans_ref[TEAM + m], capacity)
        at = pl.ds(pl.multiple_of(first // 16 * 16, 16), capacity + 16)
        rows[at] = rows[at] + nn(moving, piece(pieces, m)[16 + capacity :]).astype(LOW)
    all_rows[...] = rows[: all_rows.shape[0]]

    def one(k, carry):
        first = pl.multiple_of((t ^ (2 * k)) * member_rows, 16)
        second = pl.multiple_of((t ^ (2 * k + 1)) * member_rows, 16)
        here = jnp.concatenate(
            [rows[pl.ds(first, member_rows)], rows[pl.ds(second, member_rows)]], axis=0
        )
        at = pl.ds(pl.multiple_of(k * 2 * member_rows, 16), 2 * member_rows)
        low_out[at] = nt(here, narrow_ref[...]).astype(LOW)
        return carry

    lax.fori_loop(0, TEAM // 2, one, 0)
    own_wide[...] = nt(
        rows[pl.ds(pl.multiple_of(t * member_rows, 16), member_rows)], narrow_ref[...]
    )


def cotangent(place, spans, narrow_full, pieces, capacity, member_rows):
    model, width = narrow_full.shape
    total = member_rows * TEAM
    return pl.pallas_call(
        lambda *refs: cotangent_kernel(capacity, *refs),
        out_shape=(
            jax.ShapeDtypeStruct((total, model), LOW),
            jax.ShapeDtypeStruct((member_rows, model), WIDE),
            jax.ShapeDtypeStruct((total, width), LOW),
        ),
        in_specs=[in_smem(), in_smem()] + [in_vmem()] * (1 + PIECES),
        out_specs=(in_vmem(),) * 3,
        scratch_shapes=[pltpu.VMEM((total + capacity + 16, width), LOW)],
        compiler_params=params(),
        cost_estimate=estimate(13),
        name="cotangent",
    )(place, spans, narrow_full, *pieces)


def leave_kernel(place_ref, spans_ref, *refs):
    pieces, out_ref, total = refs[:PIECES], refs[PIECES], refs[PIECES + 1]
    t = place_ref[1]
    first = spans_ref[0]
    capacity = out_ref.shape[0]
    total[...] = jnp.zeros_like(total)
    for m in range(TEAM):
        rows = pieces[0].shape[0]
        offset = (t ^ m) * rows - first

        @pl.when((offset < capacity) & (offset + rows > 0))
        def _(m=m, offset=offset, rows=rows):
            target = lax.broadcasted_iota(jnp.int32, (capacity, rows), 0)
            source = lax.broadcasted_iota(jnp.int32, (capacity, rows), 1) + offset
            total[...] += nn(jnp.where(target == source, 1.0, 0.0).astype(LOW), piece(pieces, m))

    out_ref[...] = total[...].astype(LOW)


def leave(place, spans, pieces, capacity):
    width = pieces[0].shape[1]
    return pl.pallas_call(
        leave_kernel,
        out_shape=jax.ShapeDtypeStruct((capacity, width), LOW),
        in_specs=[in_smem(), in_smem()] + [in_vmem()] * PIECES,
        out_specs=in_vmem(),
        scratch_shapes=[pltpu.VMEM((capacity, width), WIDE)],
        compiler_params=params(),
        cost_estimate=estimate(2),
        name="leave",
    )(place, spans, *pieces)


def norm_kernel(wide_ref, gains_ref, *refs):
    resid_out, low_out = refs[4:]
    resid = wide_ref[...] + add_terms(refs[:4])
    resid_out[...] = resid
    inverse = lax.rsqrt(jnp.mean(resid * resid, axis=-1, keepdims=True) + NORM_EPS)
    low_out[...] = (resid * inverse * gains_ref[8:9]).astype(LOW)


def add_and_norm(wide, gains, terms):
    return pl.pallas_call(
        norm_kernel,
        out_shape=(
            jax.ShapeDtypeStruct(wide.shape, WIDE),
            jax.ShapeDtypeStruct(wide.shape, LOW),
        ),
        in_specs=[in_vmem()] * 6,
        out_specs=(in_vmem(),) * 2,
        compiler_params=params(),
        cost_estimate=estimate(2),
        name="add_and_norm",
    )(wide, gains, *terms)


def norm_back(resid, gain, incoming):
    inverse = lax.rsqrt(jnp.mean(resid * resid, axis=-1, keepdims=True) + NORM_EPS)
    scaled = incoming * gain
    along = jnp.mean(scaled * resid, axis=-1, keepdims=True)
    back = inverse * scaled - resid * (inverse * inverse * inverse * along)
    return back, jnp.sum(incoming * resid * inverse, axis=0, keepdims=True)


def second_back_kernel(resid_ref, gains_ref, upper_ref, *refs):
    lower_out, low_out, gain_out = refs[4:]
    back, gain_back = norm_back(
        resid_ref[...], gains_ref[8:9], add_terms(refs[:4], slice(resid_ref.shape[1]))
    )
    lower = upper_ref[...] + back
    lower_out[...] = lower
    low_out[...] = lower.astype(LOW)
    gain_out[...] = jnp.broadcast_to(gain_back, gain_out.shape)


def second_norm_back(resid, gains, upper, terms):
    rows, model = resid.shape
    return pl.pallas_call(
        second_back_kernel,
        out_shape=(
            jax.ShapeDtypeStruct((rows, model), WIDE),
            jax.ShapeDtypeStruct((rows, model), LOW),
            jax.ShapeDtypeStruct((8, model), WIDE),
        ),
        in_specs=[in_vmem()] * 7,
        out_specs=(in_vmem(),) * 3,
        compiler_params=params(),
        cost_estimate=estimate(2),
        name="second_norm_back",
    )(resid, gains, upper, *terms)


def first_back_kernel(
    place_ref, wide_ref, gains_ref, lower_ref, rows_ref, widen_ref, second_gain_ref, narrow_ref, *refs
):
    patch_out = refs[4]
    outs = refs[5:13]
    grad = refs[13]
    t = place_ref[1]
    back, first_gain = norm_back(wide_ref[...], gains_ref[:1], add_terms(refs[:4]))
    low = (lower_ref[...] + back).astype(LOW)
    grad[...] = tn(rows_ref[...], low)
    shard = grad.shape[0] // (PLANES * TEAM)
    row = lax.broadcasted_iota(jnp.int32, (16, grad.shape[1]), 0)
    gain_rows = jnp.where(row == 0, first_gain, jnp.where(row == 1, second_gain_ref[:1], 0.0))
    for m in (7, 6, 5, 3, 4, 2, 1, 0):
        parts = [
            grad[pl.ds(pl.multiple_of((plane * TEAM + (t ^ m)) * shard, 8), shard)]
            for plane in range(PLANES)
        ]
        put_terms(outs, m, jnp.concatenate(parts + [gain_rows], axis=0))
    width = narrow_ref.shape[1]
    patch_out[:, :width] = narrow_ref[...]
    patch_out[:, width:] = nt(low, widen_ref[...]).astype(LOW)


def first_norm_back(place, wide, gains, lower, rows, widen_full, second_gain, narrow_low, terms):
    model = wide.shape[1]
    width = widen_full.shape[0]
    return pl.pallas_call(
        first_back_kernel,
        out_shape=(jax.ShapeDtypeStruct((rows.shape[0], 2 * width), LOW),)
        + term_shapes(width // TEAM + 16, model),
        in_specs=[in_smem()] + [in_vmem()] * 11,
        out_specs=(in_vmem(),) * 9,
        scratch_shapes=[pltpu.VMEM((width, model), WIDE)],
        compiler_params=params(),
        cost_estimate=estimate(5),
        name="first_norm_back",
    )(place, wide, gains, lower, rows, widen_full, second_gain, narrow_low, *terms)


def exit_kernel(resid_ref, narrow_ref, *refs):
    low_out, narrow_out = refs[4:]
    model = resid_ref.shape[1]
    wide = resid_ref[...] + add_terms(refs[:4], slice(model, 2 * model))
    low = wide.astype(LOW)
    shard = low_out.shape[2] // PLANES
    for m in range(TEAM):
        parts = [
            wide[:, (plane * TEAM + m) * shard : (plane * TEAM + m + 1) * shard]
            for plane in range(PLANES)
        ]
        low_out[m] = jnp.concatenate(parts, axis=1).astype(LOW)
    narrow_out[...] = nn(low, narrow_ref[...]).astype(LOW)


def exit_block(resid, narrow_full, terms):
    rows, model = resid.shape
    return pl.pallas_call(
        exit_kernel,
        out_shape=(
            jax.ShapeDtypeStruct((TEAM, rows, model // TEAM), LOW),
            jax.ShapeDtypeStruct((rows, narrow_full.shape[1]), LOW),
        ),
        in_specs=[in_vmem()] * 6,
        out_specs=(in_vmem(),) * 2,
        compiler_params=params(),
        cost_estimate=estimate(4),
        name="exit_block",
    )(resid, narrow_full, *terms)


def forward_terms_kernel(left_ref, right_ref, *outs):
    rows = left_ref.shape[0] // TEAM
    for k in (3, 2, 1, 0):
        product = nn(left_ref[2 * k * rows : (2 * k + 2) * rows], right_ref[...])
        put_terms(outs, 2 * k + 1, product[rows:])
        put_terms(outs, 2 * k, product[:rows])


def forward_terms(left, right):
    return pl.pallas_call(
        forward_terms_kernel,
        out_shape=term_shapes(left.shape[0] // TEAM, right.shape[1]),
        in_specs=[in_vmem()] * 2,
        out_specs=(in_vmem(),) * 8,
        compiler_params=params(),
        cost_estimate=estimate(6),
        name="forward_terms",
    )(left, right)


def feed_kernel(expand_ref, shrink_ref, back_ref, *refs):
    pieces = refs[:PIECES]
    second_out, active_out, expand_out = refs[PIECES : PIECES + 3]
    outs = refs[PIECES + 3 :]
    rows = back_ref.shape[0] // TEAM
    for k in (3, 2, 1, 0):
        at = slice(2 * k * rows, (2 * k + 2) * rows)
        low = jnp.concatenate([piece(pieces, 2 * k), piece(pieces, 2 * k + 1)], axis=0)
        second_out[at] = low
        value = nn(low, expand_ref[...])
        square = value * value
        bend = jnp.tanh(GELU_A * (value + GELU_B * square * value))
        active_out[at] = (0.5 * value * (1.0 + bend)).astype(LOW)
        slope = 0.5 * (1.0 + bend) + 0.5 * value * (1.0 - bend * bend) * (
            GELU_A * (1.0 + 3.0 * GELU_B * square)
        )
        back = (slope * nt(back_ref[at], shrink_ref[...])).astype(LOW)
        expand_out[at] = back
        product = jnp.concatenate(
            [nt(back, expand_ref[...]).astype(LOW), nn(active_out[at], shrink_ref[...]).astype(LOW)],
            axis=1,
        )
        put_terms(outs, 2 * k + 1, product[rows:])
        put_terms(outs, 2 * k, product[:rows])


def feed(expand_own, shrink_own, shrink_back, pieces):
    total, model = shrink_back.shape
    hidden = expand_own.shape[1]
    return pl.pallas_call(
        feed_kernel,
        out_shape=(
            jax.ShapeDtypeStruct((total, model), LOW),
            jax.ShapeDtypeStruct((total, hidden), LOW),
            jax.ShapeDtypeStruct((total, hidden), LOW),
        )
        + term_shapes(total // TEAM, 2 * model),
        in_specs=[in_vmem()] * (3 + PIECES),
        out_specs=(in_vmem(),) * 11,
        compiler_params=params(),
        cost_estimate=estimate(18),
        name="feed",
    )(expand_own, shrink_own, shrink_back, *pieces)


def attend_kernel(
    own,
    tile,
    place_ref,
    first_ref,
    triple_ref,
    doc_column,
    doc_row,
    projected_ref,
    flat_out,
    low_out,
    total_out,
    queries,
    keys,
    values,
    attended,
):
    t = place_ref[1]
    rows = first_ref.shape[0]
    member_rows = rows // TEAM
    width = own * HEAD_DIM

    def project(k, carry):
        at = pl.ds(pl.multiple_of(k * 2 * member_rows, 16), 2 * member_rows)
        projected_ref[at] = nn(first_ref[at], triple_ref[...]).astype(LOW)
        return carry

    lax.fori_loop(0, TEAM // 2, project, 0)
    for h in range(own):
        lanes = slice(h * HEAD_DIM, (h + 1) * HEAD_DIM)
        queries[h] = projected_ref[:, :width][:, lanes]
        keys[h] = projected_ref[:, width : 2 * width][:, lanes]
        values[h] = jnp.transpose(
            projected_ref[:, 2 * width :][:, lanes].astype(WIDE)
        ).astype(LOW)
    total_out[...] = jnp.zeros_like(total_out)
    scale = SCORE_SCALE * LOG2_E
    causal = lax.broadcasted_iota(jnp.int32, (tile, tile), 0) <= lax.broadcasted_iota(
        jnp.int32, (tile, tile), 1
    )

    def one_query(j, carry):
        at_query = pl.ds(pl.multiple_of(j * tile, tile), tile)
        query_docs = doc_row[:1, at_query]

        def one_key(i, status, diagonal):
            at_key = pl.ds(pl.multiple_of(i * tile, tile), tile)
            allowed = doc_column[at_key, :1] == query_docs
            if diagonal:
                allowed = allowed & causal
            result = []
            for h in range(own):
                scores = nt(keys[h, at_key], queries[h, at_query]) * scale
                masked = jnp.where(allowed, scores, MASK_FILL)
                best = jnp.max(masked, axis=0, keepdims=True)
                if diagonal:
                    top = best
                    weights = jnp.exp2(masked - top)
                    summed = jnp.sum(weights, axis=0, keepdims=True)
                    out = nn(values[h, :, at_key], weights.astype(LOW))
                else:
                    old_top, old_sum, old_out = status[h]
                    top = jnp.maximum(old_top, best)
                    weights = jnp.exp2(masked - top)
                    rescale = jnp.exp2(old_top - top)
                    summed = old_sum * rescale + jnp.sum(weights, axis=0, keepdims=True)
                    out = old_out * rescale + nn(values[h, :, at_key], weights.astype(LOW))
                result.append((top, summed, out))
            return tuple(result)

        status = one_key(j, None, True)
        status = lax.fori_loop(0, j, lambda i, now: one_key(i, now, False), status)
        for h in range(own):
            top, summed, out = status[h]
            done = out / summed
            flat_out[h * HEAD_DIM : (h + 1) * HEAD_DIM, at_query] = done
            total_out[h : h + 1, at_query] = top + jnp.log2(summed)
        return carry

    lax.fori_loop(0, rows // tile, one_query, 0)
    attended[...] = jnp.transpose(flat_out[...]).astype(LOW)
    for k in (3, 2, 1, 0):
        pair = jnp.concatenate(
            [
                attended[pl.ds(pl.multiple_of((t ^ m) * member_rows, 16), member_rows)]
                for m in (2 * k, 2 * k + 1)
            ],
            axis=0,
        )
        low_out[2 * k * member_rows : (2 * k + 2) * member_rows] = pair


def attend_team(place, first_low, triple_own, doc_column, doc_row, own):
    rows, model = first_low.shape
    width = own * HEAD_DIM
    tile = rows // 2
    return pl.pallas_call(
        lambda *refs: attend_kernel(own, tile, *refs),
        out_shape=(
            jax.ShapeDtypeStruct((rows, 3 * width), LOW),
            jax.ShapeDtypeStruct((width, rows), WIDE),
            jax.ShapeDtypeStruct((rows, width), LOW),
            jax.ShapeDtypeStruct((8, rows), WIDE),
        ),
        in_specs=[in_smem()] + [in_vmem()] * 4,
        out_specs=(in_vmem(),) * 4,
        scratch_shapes=[
            pltpu.VMEM((own, rows, HEAD_DIM), LOW),
            pltpu.VMEM((own, rows, HEAD_DIM), LOW),
            pltpu.VMEM((own, HEAD_DIM, rows), LOW),
            pltpu.VMEM((rows, width), LOW),
        ],
        compiler_params=params(),
        cost_estimate=estimate(20),
        name="attend",
    )(place, first_low, triple_own, doc_column, doc_row)


def attend_back_setup(own, projected_ref, flat_ref, back_ref, scratch):
    queries, keys, values, backs, keys_flat, backs_flat, deltas = scratch
    width = own * HEAD_DIM
    for h in range(own):
        lanes = slice(h * HEAD_DIM, (h + 1) * HEAD_DIM)
        key = projected_ref[:, width : 2 * width][:, lanes]
        back = back_ref[:, lanes]
        back_flat = jnp.transpose(back.astype(WIDE))
        queries[h] = projected_ref[:, :width][:, lanes]
        keys[h] = key
        values[h] = projected_ref[:, 2 * width :][:, lanes]
        backs[h] = back
        keys_flat[h] = jnp.transpose(key.astype(WIDE)).astype(LOW)
        backs_flat[h] = back_flat.astype(LOW)
        deltas[h : h + 1] = jnp.sum(back_flat * flat_ref[lanes], axis=0, keepdims=True)


def attend_back_tile(own, tile, i, total_ref, doc_column, doc_row, scratch, query_back):
    queries, keys, values, backs, keys_flat, backs_flat, deltas = scratch
    rows = queries.shape[1]
    scale = SCORE_SCALE * LOG2_E
    causal = lax.broadcasted_iota(jnp.int32, (tile, tile), 0) <= lax.broadcasted_iota(
        jnp.int32, (tile, tile), 1
    )
    at_key = slice(i * tile, (i + 1) * tile)
    status = [None] * own
    for j in range(i, rows // tile):
        at_query = slice(j * tile, (j + 1) * tile)
        allowed = doc_column[at_key, :1] == doc_row[:1, at_query]
        if i == j:
            allowed = allowed & causal
        for h in range(own):
            scores = nt(keys[h, at_key], queries[h, at_query]) * scale
            probs = jnp.where(allowed, jnp.exp2(scores - total_ref[h : h + 1, at_query]), 0.0)
            prob_back = nn(values[h, at_key], backs_flat[h, :, at_query])
            score_back = (probs * (prob_back - deltas[h : h + 1, at_query])).astype(LOW)
            value_part = nn(probs.astype(LOW), backs[h, at_query])
            key_part = nn(score_back, queries[h, at_query])
            query_part = nn(keys_flat[h, :, at_key], score_back)
            if i == 0:
                query_back[h, :, at_query] = query_part
            else:
                query_back[h, :, at_query] += query_part
            if status[h] is None:
                status[h] = (key_part, value_part)
            else:
                status[h] = (status[h][0] + key_part, status[h][1] + value_part)
    return jnp.concatenate(
        [status[h][0] * SCORE_SCALE for h in range(own)] + [status[h][1] for h in range(own)],
        axis=1,
    ).astype(LOW)


def attend_back_first_kernel(
    own,
    tile,
    place_ref,
    projected_ref,
    flat_ref,
    total_ref,
    doc_column,
    doc_row,
    back_ref,
    tile_out,
    query_back,
    *scratch,
):
    attend_back_setup(own, projected_ref, flat_ref, back_ref, scratch)
    for i in range(tile_out.shape[0] // tile):
        tile_out[i * tile : (i + 1) * tile] = attend_back_tile(
            own, tile, i, total_ref, doc_column, doc_row, scratch, query_back
        )


def attend_back_rest_kernel(
    own,
    tile,
    place_ref,
    projected_ref,
    flat_ref,
    total_ref,
    doc_column,
    doc_row,
    back_ref,
    tile_ref,
    earlier_ref,
    triple_ref,
    out_ref,
    *refs,
):
    outs, query_back, scratch = refs[:8], refs[8], refs[9:]
    t = place_ref[1]
    rows = projected_ref.shape[0]
    member_rows = rows // TEAM
    width = own * HEAD_DIM
    attend_back_setup(own, projected_ref, flat_ref, back_ref, scratch)
    query_back[...] = earlier_ref[...]
    done = tile_ref.shape[0]
    out_ref[:done, width:] = tile_ref[...]
    for i in range(done // tile, rows // tile):
        out_ref[i * tile : (i + 1) * tile, width:] = attend_back_tile(
            own, tile, i, total_ref, doc_column, doc_row, scratch, query_back
        )
    flat = jnp.concatenate([query_back[h] for h in range(own)], axis=0) * SCORE_SCALE
    out_ref[:, :width] = jnp.transpose(flat).astype(LOW)
    for k in (3, 2, 1, 0):
        pair = jnp.concatenate(
            [
                out_ref[pl.ds(pl.multiple_of((t ^ m) * member_rows, 16), member_rows)]
                for m in (2 * k, 2 * k + 1)
            ],
            axis=0,
        )
        product = nt(pair, triple_ref[...])
        put_terms(outs, 2 * k + 1, product[member_rows:])
        put_terms(outs, 2 * k, product[:member_rows])


def attend_back_scratch(own, rows):
    tall = pltpu.VMEM((own, rows, HEAD_DIM), LOW)
    long = pltpu.VMEM((own, HEAD_DIM, rows), LOW)
    return [tall, tall, tall, tall, long, long, pltpu.VMEM((8, rows), WIDE)]


def attend_back_first(place, projected, flat, totals, doc_column, doc_row, back, own):
    rows = projected.shape[0]
    tile = rows // 3
    return pl.pallas_call(
        lambda *refs: attend_back_first_kernel(own, tile, *refs),
        out_shape=(
            jax.ShapeDtypeStruct((2 * tile, 2 * own * HEAD_DIM), LOW),
            jax.ShapeDtypeStruct((own, HEAD_DIM, rows), WIDE),
        ),
        in_specs=[in_smem()] + [in_vmem()] * 6,
        out_specs=(in_vmem(),) * 2,
        scratch_shapes=attend_back_scratch(own, rows),
        compiler_params=params(),
        cost_estimate=estimate(12),
        name="attend_back_first",
    )(place, projected, flat, totals, doc_column, doc_row, back)


def attend_back_rest(
    place, projected, flat, totals, doc_column, doc_row, back, first_tile, query_back, triple_own, own
):
    rows = projected.shape[0]
    tile = rows // 3
    return pl.pallas_call(
        lambda *refs: attend_back_rest_kernel(own, tile, *refs),
        out_shape=(jax.ShapeDtypeStruct(projected.shape, LOW),)
        + term_shapes(rows // TEAM, triple_own.shape[0]),
        in_specs=[in_smem()] + [in_vmem()] * 9,
        out_specs=(in_vmem(),) * 9,
        scratch_shapes=[pltpu.VMEM((own, HEAD_DIM, rows), WIDE)] + attend_back_scratch(own, rows),
        compiler_params=params(),
        cost_estimate=estimate(18),
        name="attend_back_rest",
    )(
        place,
        projected,
        flat,
        totals,
        doc_column,
        doc_row,
        back,
        first_tile,
        query_back,
        triple_own,
    )


def mixing_send_kernel(place_ref, *refs):
    stack_ref, out_ref = refs
    out_ref[...] = jnp.zeros_like(out_ref)
    x = place_ref[1] // 4
    for source in range(PLANES):
        out_ref[2 * source + x] = stack_ref[source]


def mixing_send(place, stack):
    rows, width = stack.shape[1:]
    return pl.pallas_call(
        mixing_send_kernel,
        out_shape=jax.ShapeDtypeStruct((TEAM, rows, width), LOW),
        in_specs=[in_smem(), in_vmem()],
        out_specs=in_vmem(),
        compiler_params=params(),
        cost_estimate=estimate(2),
        name="mixing_send",
    )(place, stack)


def mixing_exchange(sent, core):
    rows, width = sent.shape[1:]
    return lax.dynamic_slice_in_dim(
        team_exchange(sent), core * PLANES, PLANES, 0
    ).reshape(PLANES * rows, width)


def mixing_return(sent, x):
    back = team_exchange(sent)
    return pick(back.reshape((PLANES, 2) + back.shape[1:]), x, 1)


def mix_back_kernel(place_ref, mixing_ref, attended_ref, *refs):
    pieces = refs[:PIECES]
    back_ref, mixing_out, mixed = refs[PIECES:]
    t = place_ref[1]
    member_rows = back_ref.shape[0] // TEAM
    for k in range(TEAM // 2):
        pair = jnp.concatenate([piece(pieces, 2 * k), piece(pieces, 2 * k + 1)], axis=0)
        mixed[2 * k * member_rows : (2 * k + 2) * member_rows] = pair
        back = nt(pair, mixing_ref[...]).astype(LOW)
        for m in (2 * k, 2 * k + 1):
            at = pl.ds(pl.multiple_of((t ^ m) * member_rows, 16), member_rows)
            back_ref[at] = back[(m - 2 * k) * member_rows : (m - 2 * k + 1) * member_rows]
    gradient = tn(attended_ref[...], mixed[...]).astype(LOW)
    mixing_out[...] = jnp.zeros_like(mixing_out)
    rows = gradient.shape[0] // PLANES
    for k in range(PLANES):
        mixing_out[t % 2 * PLANES + k] = gradient[k * rows : (k + 1) * rows]


def mix_back(place, mixing_own, attended, pieces):
    rows, width = attended.shape
    model = mixing_own.shape[1]
    return pl.pallas_call(
        mix_back_kernel,
        out_shape=(
            jax.ShapeDtypeStruct((rows, width), LOW),
            jax.ShapeDtypeStruct((TEAM, width // PLANES, model), LOW),
        ),
        in_specs=[in_smem()] + [in_vmem()] * (2 + PIECES),
        out_specs=(in_vmem(),) * 2,
        scratch_shapes=[pltpu.VMEM((rows, model), LOW)],
        compiler_params=params(),
        cost_estimate=estimate(5),
        name="mix_back",
    )(place, mixing_own, attended, *pieces)


def columns_kernel_of(piece_width, in_ref, out_ref, square_ref):
    total = jnp.zeros((1, 1), WIDE)
    for group in range(in_ref.shape[2] // piece_width):
        for pair in range(TEAM // 2):
            lanes = slice(group * piece_width, (group + 1) * piece_width)
            value = jnp.concatenate(
                [in_ref[2 * pair][:, lanes].astype(WIDE), in_ref[2 * pair + 1][:, lanes].astype(WIDE)],
                axis=1,
            )
            first = (group * TEAM + 2 * pair) * piece_width
            out_ref[:, first : first + 2 * piece_width] = value
            total = total + jnp.sum(value * value, axis=(0, 1), keepdims=True)
    square_ref[...] = jnp.broadcast_to(total, square_ref.shape)


def to_columns(value, piece_width):
    members, rows, width = value.shape
    out, square = pl.pallas_call(
        lambda *refs: columns_kernel_of(piece_width, *refs),
        out_shape=(
            jax.ShapeDtypeStruct((rows, members * width), WIDE),
            jax.ShapeDtypeStruct((8, 128), WIDE),
        ),
        in_specs=[in_vmem()],
        out_specs=(in_vmem(),) * 2,
        compiler_params=params(),
        cost_estimate=estimate(2),
        name="to_columns",
    )(value)
    return out, square[0, 0]


def adam_kernel(rates, factor_ref, *refs):
    number = len(rates)
    factor = factor_ref[0]
    for index in range(number):
        gradient, master, first, second = (refs[k * number + index][...] for k in range(4))
        weight, moment, square = adam_update(
            master, first, second, gradient, factor, rates[index], DECAY_RATE
        )
        refs[4 * number + 3 * index][...] = weight
        refs[4 * number + 3 * index + 1][...] = moment
        refs[4 * number + 3 * index + 2][...] = square


def adam_all(factor, gradients, masters, firsts, seconds, rates):
    steps = 6

    def block(array):
        rows, columns = array.shape
        return pl.BlockSpec((rows, columns // steps), lambda step: (0, step))

    blocks = [block(master) for master in masters]
    return pl.pallas_call(
        lambda *refs: adam_kernel(rates, *refs),
        grid=(steps,),
        out_shape=[
            jax.ShapeDtypeStruct(master.shape, WIDE) for master in masters for _ in range(3)
        ],
        in_specs=[in_smem()] + blocks * 4,
        out_specs=[one for one in blocks for _ in range(3)],
        compiler_params=params(),
        cost_estimate=estimate(10),
        name="adam_all",
    )(factor, *gradients, *masters, *firsts, *seconds)


def per_member(
    byte_rows,
    starts,
    doc_ids,
    out_cotangent,
    widen_master,
    widen_first,
    widen_second,
    triple_master,
    triple_first,
    triple_second,
    mixing_master,
    mixing_first,
    mixing_second,
    expand_master,
    expand_first,
    expand_second,
    shrink_master,
    shrink_first,
    shrink_second,
    narrow_master,
    narrow_first,
    narrow_second,
    gains_master,
    gains_first,
    gains_second,
):
    plane = lax.axis_index("z")
    x, y, core = lax.axis_index("x"), lax.axis_index("y"), lax.axis_index("c")
    t = 4 * x + 2 * y + core
    place = jnp.stack([plane, t]).astype(jnp.int32)
    byte_block, cotangent_rows = byte_rows[0], out_cotangent[0]
    bytes_dev, byte_width = byte_block.shape
    model = triple_master.shape[1] // 3
    hidden = expand_master.shape[1]
    shard = triple_master.shape[0]
    widen_shard = widen_master.shape[0]
    member_rows = 3 * bytes_dev // 16
    capacity = member_rows + member_rows // 2
    total = TEAM * member_rows
    own = HEADS // TEAM
    own_width = model // TEAM
    own_hidden = hidden // TEAM
    piece_hidden = own_hidden // PLANES

    widen_low = widen_master.astype(LOW)
    gains_low = gains_master.astype(LOW)
    gain_rows = jnp.pad(gains_low, ((0, 32 - widen_shard - 2), (0, byte_width - shard)))
    small = jnp.concatenate(
        [
            widen_low[:, :byte_width],
            gain_rows,
            widen_low[:, byte_width:],
            jnp.zeros((32 - widen_shard, byte_width), LOW),
            narrow_master.astype(LOW),
        ],
        axis=0,
    )
    small = plane_gather_small(small)
    row_buffer, chosen = pack(
        after(starts, small[1]), doc_ids, byte_block, cotangent_rows, capacity
    )
    packed = row_buffer
    row_buffer = to_plane(row_buffer)
    small, small_marks = team_gather(jnp.concatenate(small, axis=0))
    widen_full, gains_full, narrow_full = widen_whole(place, small, widen_shard, model)
    triple_own = triple_master.astype(LOW).reshape(shard, 3, TEAM, own_width)
    triple_own = jnp.transpose(triple_own, (2, 0, 1, 3)).reshape(TEAM, shard, 3 * own_width)
    triple_own = team_exchange(triple_own)
    mixing_rows = shard * model // (3 * own_width)
    triple_sent = jnp.concatenate(
        [
            after(triple_own, row_buffer, small[2], small[4]).reshape(TEAM * shard, 3 * own_width),
            mixing_master.astype(LOW).reshape(mixing_rows, 3 * own_width),
        ],
        axis=0,
    )
    gathered = lax.all_gather(triple_sent, "z", axis=0)
    triple_own = gathered[:, : TEAM * shard].reshape(model, 3 * own_width)
    mixing_stack = gathered[:, TEAM * shard :].reshape(PLANES, shard, model)
    expand_own = after(expand_master, triple_sent).astype(LOW)
    expand_own = expand_own.reshape(shard, PLANES, TEAM, piece_hidden)
    expand_own = jnp.transpose(expand_own, (2, 0, 1, 3)).reshape(TEAM, shard, own_hidden)
    expand_own = team_exchange(expand_own).reshape(TEAM * shard, own_hidden)
    shrink_low = shrink_master.astype(LOW)
    fed = lax.all_gather(
        jnp.concatenate(
            [expand_own, shrink_low[:, :own_hidden], shrink_low[:, own_hidden:]], axis=0
        ),
        "z",
        axis=0,
    )
    expand_own = fed[:, : TEAM * shard].reshape(model, own_hidden)
    shrink_own = jnp.concatenate(
        [
            fed[:, TEAM * shard : TEAM * shard + piece_hidden],
            fed[:, TEAM * shard + piece_hidden :],
        ],
        axis=2,
    ).reshape(own_hidden, model)
    entering, enter_marks = team_gather(after(row_buffer, *small_marks))
    first_low, widened, patch_rows, doc_column, doc_row, spans = enter(
        place,
        gains_full,
        widen_full,
        entering,
        capacity,
        member_rows,
    )
    mixing_sent = mixing_send(place, mixing_stack)
    mixing_own = mixing_exchange(mixing_sent, core)

    projected, flat, attended_low, totals = attend_team(
        after(place, mixing_sent), first_low, triple_own, doc_column, doc_row, own
    )
    terms, marks = team_scatter(*forward_terms(attended_low, mixing_own))
    shrink_back, upper_back, narrow_back = cotangent(
        after(place, *marks), spans, narrow_full, entering, capacity, member_rows
    )
    resid_one, second_own = add_and_norm(after(widened, shrink_back), gains_full, terms)

    second_pieces, _ = team_gather(second_own)
    second_low, active_low, expand_back, *terms = feed(
        expand_own, shrink_own, shrink_back, second_pieces
    )
    terms, marks = team_scatter(*terms)
    shrink_grad = tn(after(active_low, *marks), shrink_back).astype(LOW)
    shrink_sum = lax.psum_scatter(shrink_grad, "z", scatter_dimension=0, tiled=True)
    lower_back, mixed_own, second_gain = second_norm_back(
        after(resid_one, shrink_grad), gains_full, upper_back, terms
    )
    exit_out = []

    def leave_forward(own):
        exit_out.extend(exit_block(after(resid_one, own), narrow_full, terms))
        return exit_out[:1]

    mixed, mixed_marks = team_gather(mixed_own, None, leave_forward)
    resid_low, narrow_low = exit_out
    resid_low = team_exchange(resid_low).reshape(total, own_width)
    expand_grad = tn(after(second_low, *mixed_marks), expand_back).astype(LOW)
    expand_sum = lax.psum_scatter(expand_grad, "z", scatter_dimension=0, tiled=True)

    attend_back, mixing_grad = mix_back(
        after(place, expand_grad), mixing_own, attended_low, mixed
    )
    narrow_grad = tn(resid_low, after(narrow_back, attend_back)).astype(LOW)
    attention = (projected, flat, totals, doc_column, doc_row, attend_back)
    first_tile, query_back = attend_back_first(
        after(place, shrink_sum, narrow_grad), *attention, own
    )
    mixing_stack = mixing_return(mixing_grad, x)
    both = plane_scatter_small(
        jnp.concatenate(
            [mixing_stack, after(narrow_grad, first_tile).reshape(PLANES, shard, byte_width)],
            axis=2,
        )
    )
    mixing_sum, narrow_sum = both[:, :model], both[:, model:]
    triple_back, *terms = attend_back_rest(
        after(place, mixing_stack), *attention, first_tile, query_back, triple_own, own
    )
    first_terms, marks = team_scatter(*terms)
    triple_grad = tn(after(first_low, expand_sum, *marks), triple_back).astype(LOW)
    triple_sum = lax.psum_scatter(triple_grad, "z", scatter_dimension=0, tiled=True)

    back_rows, *terms = first_norm_back(
        after(place, triple_grad, mixing_sum),
        widened,
        gains_full,
        lower_back,
        patch_rows,
        widen_full,
        second_gain,
        narrow_low,
        first_terms,
    )
    expand_sum = team_exchange(
        after(expand_sum, back_rows).reshape(TEAM, shard, own_hidden)
    )
    terms, marks = team_scatter(*terms)
    widen_ready = sum(term.astype(WIDE) for term in terms)
    widen_ready = after(widen_ready, expand_sum)
    gains_ready = widen_ready[PLANES * widen_shard :][:8]
    widen_sum = plane_scatter_small(
        jnp.concatenate(
            [
                widen_ready[: PLANES * widen_shard].reshape(PLANES, widen_shard, model),
                jnp.broadcast_to(gains_ready, (PLANES, 8, model)),
            ],
            axis=1,
        )
    )
    gains_sum = lax.dynamic_slice(
        widen_sum[widen_shard : widen_shard + 2], (0, (plane * TEAM + t) * shard), (2, shard)
    )
    widen_sum = widen_sum[:widen_shard]
    back_rows, _ = team_gather(after(back_rows, terms[2]))
    back_buffer = from_plane(leave(place, spans, back_rows, capacity))
    new_block, grad_block = unpack(chosen, byte_block, cotangent_rows, back_buffer)

    triple_sum = team_exchange(triple_sum.reshape(TEAM, shard, 3 * own_width))
    triple_sum, triple_square = to_columns(triple_sum, own_width)
    expand_sum, expand_square = to_columns(expand_sum, piece_hidden)
    shrink_sum = shrink_sum.astype(WIDE)

    reduced = (widen_sum, triple_sum, mixing_sum, expand_sum, shrink_sum, narrow_sum, gains_sum)
    squares = triple_square + expand_square
    for gradient in (widen_sum, mixing_sum, shrink_sum, narrow_sum, gains_sum):
        squares = squares + jnp.sum(gradient * gradient)
    squares = jnp.full((8, 128), squares, WIDE)
    for bit in (CORE_BIT, Y_BIT, X_BIT, TEAM, 2 * TEAM):
        squares = squares + flip(squares, bit)
    grad_norm = jnp.sqrt(squares[0, 0])
    factor = CLIP_NORM / jnp.maximum(grad_norm, CLIP_NORM)
    rates = (
        2.0 * D_BYTE ** (-0.5),
        2.0 * D ** (-0.5),
        0.4,
        2.0 * D ** (-0.5),
        2.0 * FF ** (-0.5),
        2.0 * D ** (-0.5),
    )
    updated = adam_all(
        factor.reshape(1),
        reduced[:6],
        (widen_master, triple_master, mixing_master, expand_master, shrink_master, narrow_master),
        (widen_first, triple_first, mixing_first, expand_first, shrink_first, narrow_first),
        (widen_second, triple_second, mixing_second, expand_second, shrink_second, narrow_second),
        rates,
    )
    gains = adam_update(gains_master, gains_first, gains_second, gains_sum, factor, 0.6, 0.0)
    return (new_block[None], grad_block[None], grad_norm, *updated, *gains)


def plane_solution(mesh):
    fine = Mesh(mesh.devices.reshape(PLANES, 2, 2, 2), AXES)
    byte_spec = P(("y", "c"), ("z", "x"))
    rows_spec = P(AXES, None)
    gains_spec = P(None, AXES)
    return jax.shard_map(
        per_member,
        mesh=fine,
        in_specs=(byte_spec,) * 4 + (rows_spec,) * 18 + (gains_spec,) * 3,
        out_specs=(byte_spec,) * 2 + (P(),) + (rows_spec,) * 18 + (gains_spec,) * 3,
        check_vma=False,
    )


def solution(mesh):
    if plane_fits(mesh):
        return plane_solution(mesh)
    placed = (
        P("dp", "seq", None),
        P("dp", "seq"),
        P("dp", "seq"),
        P("dp", "seq", None),
        P(("seq", "dp"), None),
        P(("seq", "dp"), None),
        P(("seq", "dp"), None),
        P(("seq", "dp"), None),
        P(("seq", "dp"), None),
        P(("seq", "dp"), None),
        P(("seq", "dp"), None),
        P(("seq", "dp"), None),
        P(("seq", "dp"), None),
        P(("seq", "dp"), None),
        P(("seq", "dp"), None),
        P(("seq", "dp"), None),
        P(("seq", "dp"), None),
        P(("seq", "dp"), None),
        P(("seq", "dp"), None),
        P(("seq", "dp"), None),
        P(("seq", "dp"), None),
        P(("seq", "dp"), None),
        P(None, ("seq", "dp")),
        P(None, ("seq", "dp")),
        P(None, ("seq", "dp")),
    )
    return jax.shard_map(
        per_device,
        mesh=mesh,
        in_specs=placed,
        out_specs=(
            P("dp", "seq", None),
            P("dp", "seq", None),
            P(),
            P(("seq", "dp"), None),
            P(("seq", "dp"), None),
            P(("seq", "dp"), None),
            P(("seq", "dp"), None),
            P(("seq", "dp"), None),
            P(("seq", "dp"), None),
            P(("seq", "dp"), None),
            P(("seq", "dp"), None),
            P(("seq", "dp"), None),
            P(("seq", "dp"), None),
            P(("seq", "dp"), None),
            P(("seq", "dp"), None),
            P(("seq", "dp"), None),
            P(("seq", "dp"), None),
            P(("seq", "dp"), None),
            P(("seq", "dp"), None),
            P(("seq", "dp"), None),
            P(("seq", "dp"), None),
            P(None, ("seq", "dp")),
            P(None, ("seq", "dp")),
            P(None, ("seq", "dp")),
        ),
        check_vma=False,
    )
```
